32 devices in a mesh: win: 2 (over y), chan: 16 (over z, x, core), tm: 1.
Axes of the slice: x: 2, y: 2, z: 4, core: 2. Of those that a mesh axis runs over, the one named last changes fastest.
Arguments:
- records: float32 [1024, 32768], P(('win', 'chan'), 'tm'), parts along dimension 0, may hold values from -1000 to 1000
- dead_mask: int32 [1024], P(('win', 'chan')), parts along dimension 0, may hold values 0 or 1
- offsets: int32 [16], P('win'), parts along dimension 0, may hold values from 0 to 511, as said below
Outputs:
- correlations: bfloat16 [32, 1024, 256], P('tm', ('win', 'chan')), parts along dimension 1
The draws below stay inside these ranges and needn't reach their ends.
There are 2 independent parts, one for each index of `win`. The reference program is written for one: setup_inputs(seed, part) draws one part's arguments, and reference() takes and returns one part's arrays. A program takes and returns all parts, laid end to end along the dimension named above; each array names one. Nothing has to cross between parts.
Inputs may be any that keep to these rules, and one draw needn't show every extreme that they name: `dead_mask`: 1 marks a dead channel. Window w begins at sample w * 4096 + offsets[w]; some window has offset 512 - 1.
All inputs are finite; a program needn't handle non-finite values. No bound on the sum of `dead_mask` on one device may be relied on, other than what follows from the above.
Results may differ from the reference program's by a relative error of at most 0.0033.
Values may be sent and summed in bfloat16 or wider, within the bound.
No kernel may reach another device: no remote copies, remote signals or barrier semaphores. Data moves between devices by JAX's collectives and lax.ppermute only.
A program may use at most 64 MiB of HBM per device.

```python
import math
import jax
import jax.numpy as jnp
from jax import lax

L = 8192
HOP = 4096
JIT = 512
H = 128
K0 = 32
NF = 256
WB = 64
NLAG = 32
NPART = 256
NCH = 512
NS = 32768
NWIN = 8


TWO_PI = 2.0 * math.pi


def draw_records(key, part):
    key_list = jax.random.split(jax.random.fold_in(key, 11), 6)
    chan_pos = jnp.arange(NCH, dtype=jnp.float32)[:, None]
    time_pos = jnp.arange(NS, dtype=jnp.float32)[None, :]
    noise_part = jnp.clip(jax.random.normal(key_list[0], (NCH, NS), jnp.float32), -6.0, 6.0)
    spread = 1.2
    channel_gains = jnp.exp(jax.random.uniform(key_list[1], (NCH, 1), jnp.float32, -2.3, 2.3))
    blocks_count = (NS + 31) // 32
    envelope = jnp.exp(jax.random.uniform(key_list[2], (1, blocks_count), jnp.float32, -spread, spread))
    envelope = jnp.repeat(envelope, 32, axis=1)[:, :NS]
    frequencies = jax.random.uniform(key_list[3], (3,), jnp.float32, K0 / L, (K0 + NF) / L)
    delays = jax.random.uniform(key_list[4], (3,), jnp.float32, 0.1, 0.5)
    phases = jax.random.uniform(key_list[5], (3,), jnp.float32, 0.0, 6.28)
    wave_field = jnp.zeros((NCH, NS), jnp.float32)
    for wave_index in range(3):
        wave_field = wave_field + jnp.sin(TWO_PI * frequencies[wave_index] * (time_pos - delays[wave_index] * chan_pos) + phases[wave_index])
    return (channel_gains * envelope * (noise_part + 0.7 * wave_field)).astype(jnp.float32)


def draw_offsets(key, part):
    first_key = jax.random.fold_in(key, 21)
    second_key = jax.random.fold_in(key, 22)
    values = jax.random.randint(first_key, (NWIN,), 0, JIT, dtype=jnp.int32)
    chosen = jax.random.randint(second_key, (), 0, NWIN, dtype=jnp.int32)
    return jnp.where(jnp.arange(NWIN, dtype=jnp.int32) == chosen, JIT - 1, values).astype(jnp.int32)


def touch_ends(values, stream_key, low, largest):
    spot = [jax.random.randint(jax.random.fold_in(stream_key, axis), (), 0, length) for axis, length in enumerate(values.shape)]
    longest = values.shape.index(max(values.shape))
    next_to = spot[:longest] + [(spot[longest] + 1) % values.shape[longest]] + spot[longest + 1:]
    return values.at[tuple(spot)].set(low).at[tuple(next_to)].set(largest)


def setup_inputs(seed: int = 0, part: int = 0) -> dict:
    seeds = jax.random.split(jax.random.key(seed), 4)
    part_splits = jax.random.split(jax.random.fold_in(seeds[3], part), 4)
    return {
        "records": draw_records(jax.random.fold_in(jax.random.fold_in(seeds[3], part), 71), part),
        "dead_mask": touch_ends((jax.random.randint(part_splits[1], (NCH,), 0, 16) < 1).astype(jnp.int32), jax.random.fold_in(part_splits[1], 1), 0, 1),
        "offsets": draw_offsets(jax.random.fold_in(jax.random.fold_in(seeds[3], part), 71), part),
    }


EPS = 1e-05
TWO_PI = 2.0 * math.pi

def reference(records, dead_mask, offsets):
    channels = records.shape[0]
    live_samples = records * (1 - dead_mask).astype(jnp.float32)[:, None]
    box_sum = lax.reduce_window(jnp.abs(live_samples), jnp.float32(0.0), lax.add, (1, 2 * H + 1), (1, 1), ((0, 0), (H, H)))
    mean_level = box_sum / (2 * H + 1)
    normalised = live_samples / (mean_level + EPS)
    padded = jnp.pad(normalised, ((0, 0), (0, L)))
    taper_weights = 0.5 - 0.5 * jnp.cos(jnp.arange(L, dtype=jnp.int32).astype(jnp.float32) * (TWO_PI / L))
    bin_index = jnp.arange(NF, dtype=jnp.int32)
    freq_bins = K0 + bin_index
    band_matrix = (jnp.abs(bin_index[:, None] - bin_index[None, :]) <= WB).astype(jnp.float32)
    band_counts = lax.optimization_barrier(jnp.sum(band_matrix, axis=0))

    def spectrum(window_id):
        start = (window_id * HOP + offsets[window_id]).astype(jnp.int32)
        segment = lax.dynamic_slice_in_dim(padded, start, L, 1) * taper_weights
        full_spec = jnp.fft.rfft(segment, axis=1)[:, K0:K0 + NF]
        spec_real = jnp.real(full_spec).astype(jnp.float32)
        spec_imag = jnp.imag(full_spec).astype(jnp.float32)
        magnitude = jnp.sqrt(spec_real * spec_real + spec_imag * spec_imag + 1e-12)
        smoothed = jnp.dot(magnitude, band_matrix, precision=lax.Precision.HIGHEST, preferred_element_type=jnp.float32) / band_counts
        white_real = (spec_real / (smoothed + EPS)).astype(jnp.bfloat16)
        white_imag = (spec_imag / (smoothed + EPS)).astype(jnp.bfloat16)
        return (white_real, white_imag)
    white_real, white_imag = lax.map(spectrum, jnp.arange(NWIN, dtype=jnp.int32))
    real_cw = jnp.transpose(white_real, (1, 0, 2))
    imag_cw = jnp.transpose(white_imag, (1, 0, 2))
    features = jnp.stack([real_cw, imag_cw], axis=1).reshape(channels, 2 * NWIN * NF)
    padded_features = jnp.concatenate([features, jnp.zeros((NPART, 2 * NWIN * NF), jnp.bfloat16)], axis=0)
    own_real = real_cw.astype(jnp.float32)
    own_imag = imag_cw.astype(jnp.float32)
    lag_values = jnp.arange(NLAG, dtype=jnp.int32) - NLAG // 2
    lag_angle = jnp.mod(lag_values[:, None] * freq_bins[None, :], L).astype(jnp.float32) * (TWO_PI / L)
    cos_lag = jnp.cos(lag_angle)[:, None, None, :]
    sin_lag = jnp.sin(lag_angle)[:, None, None, :]
    norm_scale = 1.0 / math.sqrt(2.0 * NF * NWIN)
    block_rows = math.gcd(channels, 128)
    col_count = block_rows + NPART

    def block_corr(block_id):
        begin = (block_id * block_rows).astype(jnp.int32)
        block_real = lax.dynamic_slice_in_dim(own_real, begin, block_rows, 0)[None]
        block_imag = lax.dynamic_slice_in_dim(own_imag, begin, block_rows, 0)[None]
        rotated_real = block_real * cos_lag - block_imag * sin_lag
        rotated_imag = block_real * sin_lag + block_imag * cos_lag
        lag_rows = jnp.stack([rotated_real, rotated_imag], axis=2).astype(jnp.bfloat16).reshape(NLAG * block_rows, 2 * NWIN * NF)
        partners = lax.dynamic_slice_in_dim(padded_features, begin, col_count, 0)
        products = jnp.dot(lag_rows.astype(jnp.float32), partners.astype(jnp.float32).T, preferred_element_type=jnp.float32) * norm_scale
        flattened = products.reshape(NLAG, block_rows * col_count)[:, 1:]
        flattened = jnp.pad(flattened, ((0, 0), (0, block_rows + 1)))
        return flattened.reshape(NLAG, block_rows, col_count + 1)[:, :, :NPART].astype(jnp.bfloat16)
    lag_blocks = lax.map(block_corr, jnp.arange(channels // block_rows, dtype=jnp.int32))
    return jnp.transpose(lag_blocks, (1, 0, 2, 3)).reshape(NLAG, channels, NPART)
```

```python
import functools
import math

import jax
import jax.numpy as jnp
import ml_dtypes
import numpy as np
from jax import lax
from jax.experimental import pallas as pl
from jax.experimental.pallas import tpu as pltpu
from jax.sharding import PartitionSpec as P

L = 8192
HOP = 4096
H = 128
K0 = 32
NF = 256
WB = 64
NLAG = 32
NPART = 256
EDGE = 512
STEP = 256
EPS = 1e-05
TWO_PI = 2.0 * math.pi
BF16 = jnp.bfloat16
F32 = jnp.float32


def split_table(table):
    high = table.astype(ml_dtypes.bfloat16)
    low = (table - high.astype(np.float64)).astype(ml_dtypes.bfloat16)
    return high, low


@functools.cache
def fourier_tables():
    samples = np.arange(HOP)[:, None]
    bins = K0 + np.arange(NF)[None, :]
    angle = (samples * bins % L) * (TWO_PI / L)
    inner = np.concatenate([np.cos(angle), -np.sin(angle)], axis=1)
    outer = np.zeros((HOP, 128))
    for lane, k, wave in ((0, K0 - 1, np.cos), (64, K0 - 1, np.sin), (127, K0 + NF, np.cos), (63, K0 + NF, np.sin)):
        sign = 1.0 if wave is np.cos else -1.0
        outer[:, lane] = sign * wave((samples[:, 0] * k % L) * (TWO_PI / L))
    high, low = split_table(inner)
    return np.concatenate([high, outer.astype(ml_dtypes.bfloat16)], axis=1), low


@functools.cache
def small_tables():
    lane = np.arange(2 * H + STEP)[:, None]
    place = np.arange(STEP)[None, :]
    level_band = ((lane >= place) & (lane <= place + 2 * H)).astype(ml_dtypes.bfloat16)
    bins = np.arange(NF)
    smooth_band = np.abs(bins[:, None] - bins[None, :]) <= WB
    inverse_count = (1.0 / smooth_band.sum(axis=0)).astype(np.float32)[None, :]
    return level_band, smooth_band.astype(ml_dtypes.bfloat16), inverse_count


@functools.cache
def lag_tables():
    lags = np.arange(NLAG)[:, None] - NLAG // 2
    angle = (lags * (K0 + np.arange(NF))[None, :] % L) * (TWO_PI / L)
    return np.cos(angle).astype(np.float32), np.sin(angle).astype(np.float32)


def split(value):
    high = value.astype(BF16)
    return high, (value - high.astype(F32)).astype(BF16)


def dot(a, b):
    return jnp.dot(a, b, preferred_element_type=F32)


def spectra_kernel(
    halves, own, has_halo,
    x_hbm, high_hbm, low_hbm, dead, offs, level_band, smooth_band, inverse_count,
    out, x, abs_high, abs_low, norm_high, norm_low, edge_high, edge_low, high, low, sems,
):
    channels = x.shape[0]
    width = halves * HOP
    copies = []
    if has_halo:
        copies.append(pltpu.make_async_copy(x_hbm, x, sems.at[0]))
    else:
        x[:, :H] = jnp.zeros((channels, H), F32)
        x[:, H + width:] = jnp.zeros((channels, H), F32)
        for j in range(halves):
            copies.append(
                pltpu.make_async_copy(
                    x_hbm.at[:, pl.ds(j * HOP, HOP)], x.at[:, pl.ds(H + j * HOP, HOP)], sems.at[j]
                )
            )
    high_copy = pltpu.make_async_copy(high_hbm, high, sems.at[halves])
    low_copy = pltpu.make_async_copy(low_hbm, low, sems.at[halves + 1])
    for copy in copies:
        copy.start()
    high_copy.start()
    low_copy.start()

    def take_abs(begin, count):
        a_high, a_low = split(jnp.abs(x[:, begin:begin + count]))
        abs_high[:, begin:begin + count] = a_high
        abs_low[:, begin:begin + count] = a_low

    take_after = 1024
    if has_halo:
        copies[0].wait()
    take_abs(0, H)
    for j in range(halves):
        if not has_halo:
            copies[j].wait()
        for part in range(HOP // take_after):
            take_abs(H + j * HOP + part * take_after, take_after)
    take_abs(H + width, H)

    offsets = offs[...]
    for b in range(HOP // STEP):
        def rows(ref, begin, count):
            return jnp.concatenate(
                [ref[:, begin + j * HOP:begin + j * HOP + count] for j in range(halves)], axis=0
            )

        level = dot(rows(abs_high, b * STEP, STEP + 2 * H), level_band[...])
        level = level + dot(rows(abs_low, b * STEP, STEP + 2 * H), level_band[...])
        normal = rows(x, H + b * STEP, STEP) / (level * (1.0 / (2 * H + 1)) + EPS)
        n_high, n_low = split(normal)
        norm_high[:, b * STEP:(b + 1) * STEP] = n_high
        norm_low[:, b * STEP:(b + 1) * STEP] = n_low
        if b * STEP < EDGE:
            lane = lax.broadcasted_iota(jnp.int32, (channels, STEP), 1) + b * STEP
            parts = []
            for w in range(own):
                mine = normal[w * channels:(w + 1) * channels]
                other = (
                    normal[(w + 2) * channels:(w + 3) * channels]
                    if w + 2 < halves else jnp.zeros_like(mine)
                )
                parts.append(jnp.where(lane >= offsets[w:w + 1, :], mine, other))
            e_high, e_low = split(jnp.concatenate(parts, axis=0))
            edge_high[:, b * STEP:(b + 1) * STEP] = e_high
            edge_low[:, b * STEP:(b + 1) * STEP] = e_low

    high_copy.wait()
    low_copy.wait()

    def transform(a_high, a_low, begin, end):
        first = dot(a_high, high[begin:end, :])
        second = dot(a_low, high[begin:end, :2 * NF]) + dot(a_high, low[begin:end, :])
        return first[:, :2 * NF] + second, first[:, 2 * NF:]

    bulk, bulk_outer = transform(norm_high[:, EDGE:], norm_low[:, EDGE:], EDGE, HOP)
    full, full_outer = transform(norm_high[:, :EDGE], norm_low[:, :EDGE], 0, EDGE)
    edge, edge_outer = transform(edge_high[...], edge_low[...], 0, EDGE)

    lane = lax.broadcasted_iota(jnp.int32, (1, NF), 1)
    outer_lane = lax.broadcasted_iota(jnp.int32, (1, 128), 1)
    outer_bin = jnp.where((outer_lane == 0) | (outer_lane == 64), K0 - 1, K0 + NF)

    def turn(bins):
        angle = jnp.bitwise_and(bins * offsets, L - 1).astype(F32) * (TWO_PI / L)
        return jnp.cos(angle), jnp.sin(angle)

    cos_turn, sin_turn = turn(lane + K0)
    cos_outer, sin_outer = turn(outer_bin)
    sign = 1.0 - 2.0 * jnp.bitwise_and(lane + K0, 1).astype(F32)
    sign2 = jnp.concatenate([sign, sign], axis=1)
    sign_outer = 1.0 - 2.0 * jnp.bitwise_and(outer_bin, 1).astype(F32)
    live = 1.0 - dead[...].astype(F32)

    reals, imags, magnitudes = [], [], []
    for w in range(own):
        here = slice(w * channels, (w + 1) * channels)
        after = slice((w + 1) * channels, (w + 2) * channels)
        spec = bulk[here] + edge[here]
        outer = bulk_outer[here] + edge_outer[here]
        if w + 1 < halves:
            spec = spec + (bulk[after] + full[after]) * sign2
            outer = outer + (bulk_outer[after] + full_outer[after]) * sign_outer
        spec = spec * live
        outer = outer * live
        c, s = cos_turn[w:w + 1], sin_turn[w:w + 1]
        c_outer, s_outer = cos_outer[w:w + 1], sin_outer[w:w + 1]
        outer_imag = pltpu.roll(outer, 64, 1)

        def hann(inner, ends):
            ends = jnp.concatenate([ends, ends], axis=1)
            before = jnp.where(lane == 0, ends, pltpu.roll(inner, 1, 1))
            behind = jnp.where(lane == NF - 1, ends, pltpu.roll(inner, NF - 1, 1))
            return 0.5 * inner - 0.25 * (before + behind)

        real = hann(
            spec[:, :NF] * c - spec[:, NF:] * s, outer * c_outer - outer_imag * s_outer
        )
        imag = hann(
            spec[:, :NF] * s + spec[:, NF:] * c, outer * s_outer + outer_imag * c_outer
        )
        reals.append(real)
        imags.append(imag)
        magnitudes.append(jnp.sqrt(real * real + imag * imag + 1e-12))
    m_high, m_low = split(jnp.concatenate(magnitudes, axis=0))
    smooth = (dot(m_high, smooth_band[...]) + dot(m_low, smooth_band[...])) * inverse_count[...]
    scale = 1.0 / (smooth + EPS)
    for w in range(own):
        here = slice(w * channels, (w + 1) * channels)
        out[w, :, :NF] = (reals[w] * scale[here]).astype(BF16)
        out[w, :, NF:] = (imags[w] * scale[here]).astype(BF16)


def correlate_kernel(
    blocks, lags, norm_scale,
    place, gathered, cos_lag, sin_lag, out, partners, rotated, total, sems,
):
    me = place[0]
    windows, _, features = partners.shape
    channels = out.shape[1]
    count = gathered.shape[0]

    def copy(d):
        return pltpu.make_async_copy(
            gathered.at[me + d], partners.at[:, pl.ds(d * channels, channels), :], sems.at[d]
        )

    for d in range(blocks + 1):
        @pl.when(me + d < count)
        def _(d=d):
            copy(d).start()

        @pl.when(me + d >= count)
        def _(d=d):
            partners[:, d * channels:(d + 1) * channels, :] = jnp.zeros(
                (windows, channels, features), BF16
            )
    for d in range(blocks + 1):
        @pl.when(me + d < count)
        def _(d=d):
            copy(d).wait()

    row = lax.broadcasted_iota(jnp.int32, (channels, channels), 0)
    column = lax.broadcasted_iota(jnp.int32, (channels, channels), 1)
    flip = (row + column == channels - 1).astype(F32).astype(BF16)

    @pl.loop(0, windows)
    def _(w):
        own = dot(flip, partners[w, :channels, :])
        real, imag = own[:, :NF], own[:, NF:]
        for t in range(lags):
            c, s = cos_lag[t:t + 1, :], sin_lag[t:t + 1, :]
            rotated[t * channels:(t + 1) * channels, :NF] = (real * c - imag * s).astype(BF16)
            rotated[t * channels:(t + 1) * channels, NF:] = (real * s + imag * c).astype(BF16)
        product = lax.dot_general(
            rotated[...], partners[w], (((1,), (1,)), ((), ())), preferred_element_type=F32
        )

        @pl.when(w == 0)
        def _():
            total[...] = product

        @pl.when(w > 0)
        def _():
            total[...] += product

    @pl.loop(0, lags)
    def _(t):
        rows = total[pl.ds(t * channels, channels), :] * norm_scale
        first = jnp.where(row + column < channels, rows[:, NPART:], rows[:, :channels])
        cyclic = jnp.concatenate([first, rows[:, channels:NPART]], axis=1)
        cyclic = pltpu.roll(cyclic, NPART - channels, 1, stride=1, stride_axis=0)
        out[t] = dot(flip, cyclic.astype(BF16)).astype(BF16)


def shifted(value, steps):
    if steps == 0:
        return value
    count = lax.axis_size("chan")
    return lax.ppermute(value, "chan", [(i, i - steps) for i in range(steps, count)])


def local(records, dead_mask, offsets):
    channels, samples = records.shape
    tm_count = lax.axis_size("tm")
    tm_index = lax.axis_index("tm")
    chan_count = lax.axis_size("chan")
    own = samples // HOP
    windows = own * tm_count
    has_halo = tm_count > 1
    halves = own
    if has_halo:
        reach = 2 * HOP + H
        left = lax.ppermute(
            records[:, samples - H:], "tm", [(i, i + 1) for i in range(tm_count - 1)]
        )
        right = lax.ppermute(
            records[:, :reach], "tm", [(i + 1, i) for i in range(tm_count - 1)]
        )
        records = jnp.concatenate([left, records, right], axis=1)
        halves = own + 2
    high, low = (jnp.asarray(t) for t in fourier_tables())
    level_band, smooth_band, inverse_count = (jnp.asarray(t) for t in small_tables())
    own_offsets = lax.dynamic_slice_in_dim(offsets, tm_index * own, own, 0).reshape(own, 1)
    rows = halves * channels
    padded = halves * HOP + 2 * H
    vmem = pl.BlockSpec(memory_space=pltpu.VMEM)
    hbm = pl.BlockSpec(memory_space=pl.ANY)
    params = pltpu.CompilerParams(vmem_limit_bytes=56 * 1024 * 1024)
    spectra = pl.pallas_call(
        functools.partial(spectra_kernel, halves, own, has_halo),
        name="spectra",
        out_shape=jax.ShapeDtypeStruct((own, channels, 2 * NF), BF16),
        in_specs=[hbm, hbm, hbm, vmem, vmem, vmem, vmem, vmem],
        out_specs=vmem,
        scratch_shapes=[
            pltpu.VMEM((channels, padded), F32),
            pltpu.VMEM((channels, padded), BF16),
            pltpu.VMEM((channels, padded), BF16),
            pltpu.VMEM((rows, HOP), BF16),
            pltpu.VMEM((rows, HOP), BF16),
            pltpu.VMEM((own * channels, EDGE), BF16),
            pltpu.VMEM((own * channels, EDGE), BF16),
            pltpu.VMEM(high.shape, BF16),
            pltpu.VMEM(low.shape, BF16),
            pltpu.SemaphoreType.DMA((halves + 2,)),
        ],
        compiler_params=params,
    )(records, high, low, dead_mask.reshape(channels, 1), own_offsets,
      level_band, smooth_band, inverse_count)

    blocks = NPART // channels
    if has_halo:
        spectra = lax.all_gather(spectra, "tm", axis=0, tiled=True)
    if chan_count <= 2 * blocks:
        gathered = lax.all_gather(spectra, "chan")
        place = lax.axis_index("chan").astype(jnp.int32).reshape(1)
    else:
        gathered = jnp.stack([shifted(spectra, d) for d in range(blocks + 1)])
        place = jnp.zeros((1,), jnp.int32)
    lags = NLAG // tm_count
    cos_lag, sin_lag = (
        lax.dynamic_slice_in_dim(jnp.asarray(t), tm_index * lags, lags, 0) for t in lag_tables()
    )
    columns = (blocks + 1) * channels
    return pl.pallas_call(
        functools.partial(
            correlate_kernel, blocks, lags, 1.0 / math.sqrt(2.0 * NF * windows)
        ),
        name="correlate",
        out_shape=jax.ShapeDtypeStruct((lags, channels, NPART), BF16),
        in_specs=[pl.BlockSpec(memory_space=pltpu.SMEM), hbm, vmem, vmem],
        out_specs=vmem,
        scratch_shapes=[
            pltpu.VMEM((windows, columns, 2 * NF), BF16),
            pltpu.VMEM((lags * channels, 2 * NF), BF16),
            pltpu.VMEM((lags * channels, columns), F32),
            pltpu.SemaphoreType.DMA((blocks + 1,)),
        ],
        compiler_params=params,
    )(place, gathered, cos_lag, sin_lag)


def solution(mesh):
    return jax.shard_map(
        local,
        mesh=mesh,
        in_specs=(P(("win", "chan"), "tm"), P(("win", "chan")), P("win")),
        out_specs=P("tm", ("win", "chan"), None),
        check_vma=False,
    )
```

```python
import functools
import math

import jax
import jax.numpy as jnp
import ml_dtypes
import numpy as np
from jax import lax
from jax.experimental import pallas as pl
from jax.experimental.pallas import tpu as pltpu
from jax.sharding import PartitionSpec as P

L = 8192
HOP = 4096
H = 128
K0 = 32
NF = 256
WB = 64
NLAG = 32
NPART = 256
EDGE = 512
STEP = 256
EPS = 1e-05
TWO_PI = 2.0 * math.pi
BF16 = jnp.bfloat16
F32 = jnp.float32


def split_table(table):
    high = table.astype(ml_dtypes.bfloat16)
    low = (table - high.astype(np.float64)).astype(ml_dtypes.bfloat16)
    return high, low


@functools.cache
def fourier_tables():
    samples = np.arange(HOP)[:, None]
    bins = K0 + np.arange(NF)[None, :]
    angle = (samples * bins % L) * (TWO_PI / L)
    inner = np.concatenate([np.cos(angle), -np.sin(angle)], axis=1)
    outer = np.zeros((HOP, 128))
    for lane, k, wave in ((0, K0 - 1, np.cos), (64, K0 - 1, np.sin), (127, K0 + NF, np.cos), (63, K0 + NF, np.sin)):
        sign = 1.0 if wave is np.cos else -1.0
        outer[:, lane] = sign * wave((samples[:, 0] * k % L) * (TWO_PI / L))
    high, low = split_table(inner)
    return np.concatenate([high, outer.astype(ml_dtypes.bfloat16)], axis=1), low


@functools.cache
def small_tables():
    lane = np.arange(2 * H + STEP)[:, None]
    place = np.arange(STEP)[None, :]
    level_band = ((lane >= place) & (lane <= place + 2 * H)).astype(ml_dtypes.bfloat16)
    bins = np.arange(NF)
    smooth_band = np.abs(bins[:, None] - bins[None, :]) <= WB
    inverse_count = (1.0 / smooth_band.sum(axis=0)).astype(np.float32)[None, :]
    return level_band, smooth_band.astype(ml_dtypes.bfloat16), inverse_count


@functools.cache
def lag_tables():
    lags = np.arange(NLAG)[:, None] - NLAG // 2
    angle = (lags * (K0 + np.arange(NF))[None, :] % L) * (TWO_PI / L)
    return np.cos(angle).astype(np.float32), np.sin(angle).astype(np.float32)


def split(value):
    high = value.astype(BF16)
    return high, (value - high.astype(F32)).astype(BF16)


def dot(a, b):
    return jnp.dot(a, b, preferred_element_type=F32)


def spectra_kernel(
    halves, own, has_halo,
    x_hbm, high_hbm, low_hbm, dead, offs, level_band, smooth_band, inverse_count,
    out, x, abs_high, abs_low, norm_high, norm_low, edge_high, edge_low, high, low, sems,
):
    channels = x.shape[0]
    width = halves * HOP
    copies = []
    if has_halo:
        copies.append(pltpu.make_async_copy(x_hbm, x, sems.at[0]))
    else:
        x[:, :H] = jnp.zeros((channels, H), F32)
        x[:, H + width:] = jnp.zeros((channels, H), F32)
        for j in range(halves):
            copies.append(
                pltpu.make_async_copy(
                    x_hbm.at[:, pl.ds(j * HOP, HOP)], x.at[:, pl.ds(H + j * HOP, HOP)], sems.at[j]
                )
            )
    high_copy = pltpu.make_async_copy(high_hbm, high, sems.at[halves])
    low_copy = pltpu.make_async_copy(low_hbm, low, sems.at[halves + 1])
    for copy in copies:
        copy.start()
    high_copy.start()
    low_copy.start()

    def take_abs(begin, count):
        a_high, a_low = split(jnp.abs(x[:, begin:begin + count]))
        abs_high[:, begin:begin + count] = a_high
        abs_low[:, begin:begin + count] = a_low

    take_after = 1024
    if has_halo:
        copies[0].wait()
    take_abs(0, H)
    for j in range(halves):
        if not has_halo:
            copies[j].wait()
        for part in range(HOP // take_after):
            take_abs(H + j * HOP + part * take_after, take_after)
    take_abs(H + width, H)

    window = lax.broadcasted_iota(jnp.int32, (own, 1), 0)
    offsets = sum(jnp.where(window == w, offs[w], 0) for w in range(own))
    for b in range(HOP // STEP):
        def rows(ref, begin, count):
            return jnp.concatenate(
                [ref[:, begin + j * HOP:begin + j * HOP + count] for j in range(halves)], axis=0
            )

        level = dot(rows(abs_high, b * STEP, STEP + 2 * H), level_band[...])
        level = level + dot(rows(abs_low, b * STEP, STEP + 2 * H), level_band[...])
        normal = rows(x, H + b * STEP, STEP) / (level * (1.0 / (2 * H + 1)) + EPS)
        n_high, n_low = split(normal)
        norm_high[:, b * STEP:(b + 1) * STEP] = n_high
        norm_low[:, b * STEP:(b + 1) * STEP] = n_low
        if b * STEP < EDGE:
            lane = lax.broadcasted_iota(jnp.int32, (channels, STEP), 1) + b * STEP
            parts = []
            for w in range(own):
                mine = normal[w * channels:(w + 1) * channels]
                other = (
                    normal[(w + 2) * channels:(w + 3) * channels]
                    if w + 2 < halves else jnp.zeros_like(mine)
                )
                parts.append(jnp.where(lane >= offs[w], mine, other))
            e_high, e_low = split(jnp.concatenate(parts, axis=0))
            edge_high[:, b * STEP:(b + 1) * STEP] = e_high
            edge_low[:, b * STEP:(b + 1) * STEP] = e_low

    high_copy.wait()
    low_copy.wait()

    def transform(a_high, a_low, begin, end):
        first = dot(a_high, high[begin:end, :])
        second = dot(a_low, high[begin:end, :2 * NF]) + dot(a_high, low[begin:end, :])
        return first[:, :2 * NF] + second, first[:, 2 * NF:]

    bulk, bulk_outer = transform(norm_high[:, EDGE:], norm_low[:, EDGE:], EDGE, HOP)
    full, full_outer = transform(norm_high[:, :EDGE], norm_low[:, :EDGE], 0, EDGE)
    edge, edge_outer = transform(edge_high[...], edge_low[...], 0, EDGE)

    lane = lax.broadcasted_iota(jnp.int32, (1, NF), 1)
    outer_lane = lax.broadcasted_iota(jnp.int32, (1, 128), 1)
    outer_bin = jnp.where((outer_lane == 0) | (outer_lane == 64), K0 - 1, K0 + NF)

    def turn(bins):
        angle = jnp.bitwise_and(bins * offsets, L - 1).astype(F32) * (TWO_PI / L)
        return jnp.cos(angle), jnp.sin(angle)

    cos_turn, sin_turn = turn(lane + K0)
    cos_outer, sin_outer = turn(outer_bin)
    sign = 1.0 - 2.0 * jnp.bitwise_and(lane + K0, 1).astype(F32)
    sign2 = jnp.concatenate([sign, sign], axis=1)
    sign_outer = 1.0 - 2.0 * jnp.bitwise_and(outer_bin, 1).astype(F32)
    channel = lax.broadcasted_iota(jnp.int32, (channels, 1), 0)
    live = 1.0 - sum(jnp.where(channel == i, dead[i], 0) for i in range(channels)).astype(F32)

    reals, imags, magnitudes = [], [], []
    for w in range(own):
        here = slice(w * channels, (w + 1) * channels)
        after = slice((w + 1) * channels, (w + 2) * channels)
        spec = bulk[here] + edge[here]
        outer = bulk_outer[here] + edge_outer[here]
        if w + 1 < halves:
            spec = spec + (bulk[after] + full[after]) * sign2
            outer = outer + (bulk_outer[after] + full_outer[after]) * sign_outer
        spec = spec * live
        outer = outer * live
        c, s = cos_turn[w:w + 1], sin_turn[w:w + 1]
        c_outer, s_outer = cos_outer[w:w + 1], sin_outer[w:w + 1]
        outer_imag = pltpu.roll(outer, 64, 1)

        def hann(inner, ends):
            ends = jnp.concatenate([ends, ends], axis=1)
            before = jnp.where(lane == 0, ends, pltpu.roll(inner, 1, 1))
            behind = jnp.where(lane == NF - 1, ends, pltpu.roll(inner, NF - 1, 1))
            return 0.5 * inner - 0.25 * (before + behind)

        real = hann(
            spec[:, :NF] * c - spec[:, NF:] * s, outer * c_outer - outer_imag * s_outer
        )
        imag = hann(
            spec[:, :NF] * s + spec[:, NF:] * c, outer * s_outer + outer_imag * c_outer
        )
        reals.append(real)
        imags.append(imag)
        magnitudes.append(jnp.sqrt(real * real + imag * imag + 1e-12))
    m_high, m_low = split(jnp.concatenate(magnitudes, axis=0))
    smooth = (dot(m_high, smooth_band[...]) + dot(m_low, smooth_band[...])) * inverse_count[...]
    scale = 1.0 / (smooth + EPS)
    for w in range(own):
        here = slice(w * channels, (w + 1) * channels)
        begin = w * 2 * NF
        out[:, begin:begin + NF] = (reals[w] * scale[here]).astype(BF16)
        out[:, begin + NF:begin + 2 * NF] = (imags[w] * scale[here]).astype(BF16)


def rotate_and_multiply(windows, lags, group, own, flipped, cos_lag, sin_lag, rotated, partners, finish):
    channels = own.shape[0]
    row = lax.broadcasted_iota(jnp.int32, (channels, channels), 0)
    column = lax.broadcasted_iota(jnp.int32, (channels, channels), 1)
    flip = (row + column == channels - 1).astype(F32).astype(BF16)
    flipped[...] = dot(flip, own[...])

    def rotate(g):
        target = rotated[g % 2]
        for w in range(windows):
            begin = w * 2 * NF
            real, imag = flipped[:, begin:begin + NF], flipped[:, begin + NF:begin + 2 * NF]
            for i in range(group):
                t = g * group + i
                c, s = cos_lag[t:t + 1, :], sin_lag[t:t + 1, :]
                here = slice(i * channels, (i + 1) * channels)
                target[here, begin:begin + NF] = (real * c - imag * s).astype(BF16)
                target[here, begin + NF:begin + 2 * NF] = (real * s + imag * c).astype(BF16)

    rotate(0)
    for g in range(lags // group):
        product = lax.dot_general(
            rotated[g % 2][...], partners[...], (((1,), (1,)), ((), ())),
            preferred_element_type=F32,
        )
        if g + 1 < lags // group:
            rotate(g + 1)
        finish(g, product, flip, row + column < channels)


def fill_slots(channels, partners, present, absent, sems):
    def place(slot):
        return pl.ds(pl.multiple_of(slot * channels, channels), channels)

    for slot in absent:
        partners[place(slot), :] = jnp.zeros((channels, partners.shape[1]), BF16)
    copies = [
        pltpu.make_async_copy(source, partners.at[place(slot), :], sems.at[i])
        for i, (source, slot) in enumerate(present)
    ]
    for copy in copies:
        copy.start()
    return copies


def early_kernel(
    windows, lags, group,
    place, own, ahead, swapped, cos_lag, sin_lag, out, partners, flipped, even, odd, sems,
):
    channels = own.shape[0]
    core = lax.rem(place[0], 2)

    @pl.when(core == 0)
    def _():
        copies = fill_slots(
            channels, partners,
            [(own, 0), (swapped.at[0], 1), (ahead, 4), (swapped.at[1], 5)], (2, 3, 6, 7), sems,
        )
        for copy in copies:
            copy.wait()

    @pl.when(core == 1)
    def _():
        copies = fill_slots(
            channels, partners,
            [(own, 0), (ahead, 4), (swapped.at[1], 3)], (1, 2, 5, 6, 7), sems,
        )
        for copy in copies:
            copy.wait()

    def finish(g, product, flip, low):
        out[g * group * channels:(g + 1) * group * channels, :] = product

    rotate_and_multiply(
        windows, lags, group, own, flipped, cos_lag, sin_lag, (even, odd), partners, finish
    )


def late_kernel(
    windows, lags, group, norm_scale,
    place, own, early, far, cross, other, swapped, last, cos_lag, sin_lag,
    out, partners, flipped, even, odd, sems,
):
    channels = own.shape[0]
    core = lax.rem(place[0], 2)
    side = lax.rem(place[0] // 2, 2)
    cross_slot = 6 - 4 * side
    other_slot = 8 - cross_slot
    step = 1 - 2 * core
    blocks = [(far, 0), (cross, cross_slot), (other, other_slot),
              (swapped.at[1], cross_slot + step), (last, other_slot + step)]

    @pl.when(core == 0)
    def _():
        for copy in fill_slots(channels, partners, blocks, (1, 4, 5), sems):
            copy.wait()

    @pl.when(core == 1)
    def _():
        for copy in fill_slots(channels, partners, blocks + [(swapped.at[0], 7)], (3, 4), sems):
            copy.wait()

    def finish(g, product, flip, low):
        for i in range(group):
            t = g * group + i
            late = product[i * channels:(i + 1) * channels, :]
            before = early[t * channels:(t + 1) * channels, :]
            both = late + before
            first = jnp.where(low, late[:, :channels], before[:, :channels])
            cyclic = jnp.concatenate([first, both[:, channels:]], axis=1) * norm_scale
            cyclic = pltpu.roll(cyclic, NPART - channels, 1, stride=1, stride_axis=0)
            out[t] = dot(flip, cyclic.astype(BF16)).astype(BF16)

    rotate_and_multiply(
        windows, lags, group, own, flipped, cos_lag, sin_lag, (even, odd), partners, finish
    )


def exchange(value, pairs):
    count = lax.axis_size("chan")
    return lax.ppermute(value, "chan", [(i, j) for i, j in pairs if max(i, j) < count])


def local(records, dead_mask, offsets):
    channels, samples = records.shape
    tm_count = lax.axis_size("tm")
    tm_index = lax.axis_index("tm")
    chan_count = lax.axis_size("chan")
    own = samples // HOP
    windows = own * tm_count
    has_halo = tm_count > 1
    halves = own
    if has_halo:
        reach = 2 * HOP + H
        left = lax.ppermute(
            records[:, samples - H:], "tm", [(i, i + 1) for i in range(tm_count - 1)]
        )
        right = lax.ppermute(
            records[:, :reach], "tm", [(i + 1, i) for i in range(tm_count - 1)]
        )
        records = jnp.concatenate([left, records, right], axis=1)
        halves = own + 2
    high, low = (jnp.asarray(t) for t in fourier_tables())
    level_band, smooth_band, inverse_count = (jnp.asarray(t) for t in small_tables())
    own_offsets = lax.dynamic_slice_in_dim(offsets, tm_index * own, own, 0)
    rows = halves * channels
    padded = halves * HOP + 2 * H
    vmem = pl.BlockSpec(memory_space=pltpu.VMEM)
    smem = pl.BlockSpec(memory_space=pltpu.SMEM)
    hbm = pl.BlockSpec(memory_space=pl.ANY)
    params = pltpu.CompilerParams(vmem_limit_bytes=56 * 1024 * 1024)
    spectra = pl.pallas_call(
        functools.partial(spectra_kernel, halves, own, has_halo),
        name="spectra",
        out_shape=jax.ShapeDtypeStruct((channels, own * 2 * NF), BF16),
        in_specs=[hbm, hbm, hbm, smem, smem, vmem, vmem, vmem],
        out_specs=vmem,
        scratch_shapes=[
            pltpu.VMEM((channels, padded), F32),
            pltpu.VMEM((channels, padded), BF16),
            pltpu.VMEM((channels, padded), BF16),
            pltpu.VMEM((rows, HOP), BF16),
            pltpu.VMEM((rows, HOP), BF16),
            pltpu.VMEM((own * channels, EDGE), BF16),
            pltpu.VMEM((own * channels, EDGE), BF16),
            pltpu.VMEM(high.shape, BF16),
            pltpu.VMEM(low.shape, BF16),
            pltpu.SemaphoreType.DMA((halves + 2,)),
        ],
        compiler_params=params,
    )(records, high, low, dead_mask, own_offsets, level_band, smooth_band, inverse_count)
    if has_halo:
        spectra = lax.all_gather(spectra, "tm", axis=1, tiled=True)

    lags = NLAG // tm_count
    group = min(8, lags)
    cos_lag, sin_lag = (
        lax.dynamic_slice_in_dim(jnp.asarray(t), tm_index * lags, lags, 0) for t in lag_tables()
    )
    place = lax.axis_index("chan").astype(jnp.int32).reshape(1)
    features = spectra.shape[1]
    scratch = [
        pltpu.VMEM((NPART, features), BF16),
        pltpu.VMEM((channels, features), F32),
        pltpu.VMEM((group * channels, features), BF16),
        pltpu.VMEM((group * channels, features), BF16),
        pltpu.SemaphoreType.DMA((6,)),
    ]
    cost = pl.CostEstimate(
        flops=2 * lags * channels * features * NPART, bytes_accessed=4 * 1024 * 1024,
        transcendentals=0,
    )

    every = range(chan_count)
    down = [(i, i - 4) for i in every if i >= 4]
    across = [(i, i ^ 2) for i in every]
    cores = [(i, i ^ 1) for i in every]
    ahead = exchange(spectra, down)
    near_swapped = exchange(jnp.stack([spectra, ahead]), cores)
    far = exchange(ahead, down)
    cross = exchange(ahead, across)
    side = lax.rem(lax.axis_index("chan") // 2, 2)
    other = exchange(jnp.where(side == 0, far, spectra), across)
    far_swapped = exchange(jnp.stack([far, cross]), cores)
    last = exchange(other, cores)
    early = pl.pallas_call(
        functools.partial(early_kernel, windows, lags, group),
        name="early_correlate",
        out_shape=jax.ShapeDtypeStruct((lags * channels, NPART), F32),
        in_specs=[smem, vmem, hbm, hbm, vmem, vmem],
        out_specs=vmem,
        scratch_shapes=scratch,
        compiler_params=params,
        cost_estimate=cost,
    )(place, spectra, ahead, near_swapped, cos_lag, sin_lag)
    return pl.pallas_call(
        functools.partial(
            late_kernel, windows, lags, group, 1.0 / math.sqrt(2.0 * NF * windows)
        ),
        name="late_correlate",
        out_shape=jax.ShapeDtypeStruct((lags, channels, NPART), BF16),
        in_specs=[smem, vmem, vmem, hbm, hbm, hbm, hbm, hbm, vmem, vmem],
        out_specs=vmem,
        scratch_shapes=scratch,
        compiler_params=params,
        cost_estimate=cost,
    )(place, spectra, early, far, cross, other, far_swapped, last, cos_lag, sin_lag)


def solution(mesh):
    return jax.shard_map(
        local,
        mesh=mesh,
        in_specs=(P(("win", "chan"), "tm"), P(("win", "chan")), P("win")),
        out_specs=P("tm", ("win", "chan"), None),
        check_vma=False,
    )
```

```python
import functools
import math

import jax
import jax.numpy as jnp
import ml_dtypes
import numpy as np
from jax import lax
from jax.experimental import pallas as pl
from jax.experimental.pallas import tpu as pltpu
from jax.sharding import PartitionSpec as P

L = 8192
HOP = 4096
H = 128
K0 = 32
NF = 256
WB = 64
NLAG = 32
NPART = 256
EDGE = 512
STEP = 256
GROUP = 512
CHUNKS = 2
EPS = 1e-05
TWO_PI = 2.0 * math.pi
BF16 = jnp.bfloat16
F32 = jnp.float32


def split_table(table):
    high = table.astype(ml_dtypes.bfloat16)
    low = (table - high.astype(np.float64)).astype(ml_dtypes.bfloat16)
    return high, low


@functools.cache
def fourier_tables():
    samples = np.arange(HOP)[:, None]
    bins = K0 + np.arange(NF)[None, :]
    angle = (samples * bins % L) * (TWO_PI / L)
    inner = np.concatenate([np.cos(angle), -np.sin(angle)], axis=1)
    outer = np.zeros((HOP, 128))
    for lane, k, wave in ((0, K0 - 1, np.cos), (64, K0 - 1, np.sin), (127, K0 + NF, np.cos), (63, K0 + NF, np.sin)):
        sign = 1.0 if wave is np.cos else -1.0
        outer[:, lane] = sign * wave((samples[:, 0] * k % L) * (TWO_PI / L))
    high, low = split_table(inner)
    return np.concatenate([high, outer.astype(ml_dtypes.bfloat16)], axis=1), low


@functools.cache
def small_tables():
    lane = np.arange(2 * H + STEP)[:, None]
    place = np.arange(STEP)[None, :]
    level_band = ((lane >= place) & (lane <= place + 2 * H)).astype(ml_dtypes.bfloat16)
    bins = np.arange(NF)
    smooth_band = np.abs(bins[:, None] - bins[None, :]) <= WB
    inverse_count = (1.0 / smooth_band.sum(axis=0)).astype(np.float32)[None, :]
    return level_band, smooth_band.astype(ml_dtypes.bfloat16), inverse_count


@functools.cache
def lag_tables():
    lags = np.arange(NLAG)[:, None] - NLAG // 2
    angle = (lags * (K0 + np.arange(NF))[None, :] % L) * (TWO_PI / L)
    return np.cos(angle).astype(np.float32), np.sin(angle).astype(np.float32)


def split(value):
    high = value.astype(BF16)
    return high, (value - high.astype(F32)).astype(BF16)


def dot(a, b):
    return jnp.dot(a, b, preferred_element_type=F32)


def spectra_kernel(
    first, own, bulk, edges, halo,
    x_hbm, high_hbm, low_hbm, dead, offs, level_band, smooth_band, inverse_count,
    out, x, absolute, total, total_outer, high, low, x_sems, table_sems,
):
    channels = x.shape[0]
    groups = HOP // GROUP
    base = first * HOP + halo
    pieces = {}
    count = 0

    def add(group, begin, length):
        nonlocal count
        pieces.setdefault(group, []).append(
            (pltpu.make_async_copy(
                x_hbm.at[:, pl.ds(base + begin, length)],
                x.at[:, pl.ds(H + begin, length)],
                x_sems.at[count],
            ), H + begin, length)
        )
        count += 1

    zeros = []
    if base >= H:
        add(groups - 1, -H, H)
    else:
        zeros.append(0)
    for j in range(bulk):
        for g in range(groups):
            add(g, j * HOP + g * GROUP, GROUP)
    for j in range(bulk, edges):
        add(0, j * HOP, EDGE + H)
    if edges == bulk:
        zeros.append(H + bulk * HOP)
    for begin in zeros:
        absolute[:, begin:begin + H] = jnp.zeros((channels, H), BF16)

    def table_copies(g):
        here = pl.ds(g * GROUP, GROUP)
        return (
            pltpu.make_async_copy(high_hbm.at[here, :], high.at[here, :], table_sems.at[2 * g]),
            pltpu.make_async_copy(low_hbm.at[here, :], low.at[here, :], table_sems.at[2 * g + 1]),
        )

    def start(g):
        for copy, _, _ in pieces[g]:
            copy.start()

    def start_table(g):
        for copy in table_copies(g):
            copy.start()

    start(groups - 1)
    start(0)
    start(1)
    start_table(0)
    for g in range(2, groups - 1):
        start(g)
        start_table(g - 1)
    start_table(groups - 2)
    start_table(groups - 1)

    def arrive(g):
        for copy, begin, length in pieces[g]:
            copy.wait()
            absolute[:, begin:begin + length] = jnp.abs(x[:, begin:begin + length]).astype(BF16)

    def normal(begin, halves):
        def rows(ref, start, length):
            return jnp.concatenate(
                [ref[:, start + j * HOP:start + j * HOP + length] for j in range(halves)], axis=0
            )

        level = dot(rows(absolute, begin, STEP + 2 * H), level_band[...])
        return rows(x, H + begin, STEP) / (level * (1.0 / (2 * H + 1)) + EPS)

    def transform(value, g):
        a_high, a_low = split(value)
        here = slice(g * GROUP, (g + 1) * GROUP)
        first_part = dot(a_high, high[here, :])
        second = dot(a_low, high[here, :2 * NF]) + dot(a_high, low[here, :])
        return first_part[:, :2 * NF] + second, first_part[:, 2 * NF:]

    arrive(groups - 1)
    arrive(0)
    for g in range(groups):
        if g + 1 < groups - 1:
            arrive(g + 1)
        halves = edges if g == 0 else bulk
        value = jnp.concatenate(
            [normal(g * GROUP + part * STEP, halves) for part in range(GROUP // STEP)], axis=1
        )
        for copy in table_copies(g):
            copy.wait()
        if g == 0:
            lane = lax.broadcasted_iota(jnp.int32, (channels, EDGE), 1)
            parts = []
            for w in range(own):
                mine = value[w * channels:(w + 1) * channels]
                other = (
                    value[(w + 2) * channels:(w + 3) * channels]
                    if w + 2 < halves else jnp.zeros_like(mine)
                )
                parts.append(jnp.where(lane >= offs[w], mine, other))
            edge, edge_outer = transform(jnp.concatenate(parts, axis=0), g)
            full, full_outer = transform(value[:bulk * channels], g)
        else:
            inner, outer = transform(value, g)
            if g == 1:
                total[...] = inner
                total_outer[...] = outer
            else:
                total[...] += inner
                total_outer[...] += outer

    window = lax.broadcasted_iota(jnp.int32, (own, 1), 0)
    offsets = sum(jnp.where(window == w, offs[w], 0) for w in range(own))
    lane = lax.broadcasted_iota(jnp.int32, (1, NF), 1)
    outer_lane = lax.broadcasted_iota(jnp.int32, (1, 128), 1)
    outer_bin = jnp.where((outer_lane == 0) | (outer_lane == 64), K0 - 1, K0 + NF)

    def turn(bins):
        angle = jnp.bitwise_and(bins * offsets, L - 1).astype(F32) * (TWO_PI / L)
        return jnp.cos(angle), jnp.sin(angle)

    cos_turn, sin_turn = turn(lane + K0)
    cos_outer, sin_outer = turn(outer_bin)
    sign = 1.0 - 2.0 * jnp.bitwise_and(lane + K0, 1).astype(F32)
    sign2 = jnp.concatenate([sign, sign], axis=1)
    sign_outer = 1.0 - 2.0 * jnp.bitwise_and(outer_bin, 1).astype(F32)
    channel = lax.broadcasted_iota(jnp.int32, (channels, 1), 0)
    live = 1.0 - sum(jnp.where(channel == i, dead[i], 0) for i in range(channels)).astype(F32)

    reals, imags, magnitudes = [], [], []
    for w in range(own):
        here = slice(w * channels, (w + 1) * channels)
        after = slice((w + 1) * channels, (w + 2) * channels)
        spec = total[here, :] + edge[here]
        outer = total_outer[here, :] + edge_outer[here]
        if w + 1 < bulk:
            spec = spec + (total[after, :] + full[after]) * sign2
            outer = outer + (total_outer[after, :] + full_outer[after]) * sign_outer
        spec = spec * live
        outer = outer * live
        c, s = cos_turn[w:w + 1], sin_turn[w:w + 1]
        c_outer, s_outer = cos_outer[w:w + 1], sin_outer[w:w + 1]
        outer_imag = pltpu.roll(outer, 64, 1)

        def hann(inner, ends):
            ends = jnp.concatenate([ends, ends], axis=1)
            before = jnp.where(lane == 0, ends, pltpu.roll(inner, 1, 1))
            behind = jnp.where(lane == NF - 1, ends, pltpu.roll(inner, NF - 1, 1))
            return 0.5 * inner - 0.25 * (before + behind)

        real = hann(
            spec[:, :NF] * c - spec[:, NF:] * s, outer * c_outer - outer_imag * s_outer
        )
        imag = hann(
            spec[:, :NF] * s + spec[:, NF:] * c, outer * s_outer + outer_imag * c_outer
        )
        reals.append(real)
        imags.append(imag)
        magnitudes.append(jnp.sqrt(real * real + imag * imag + 1e-12))
    m_high, m_low = split(jnp.concatenate(magnitudes, axis=0))
    smooth = (dot(m_high, smooth_band[...]) + dot(m_low, smooth_band[...])) * inverse_count[...]
    scale = 1.0 / (smooth + EPS)
    for w in range(own):
        here = slice(w * channels, (w + 1) * channels)
        begin = w * 2 * NF
        out[:, begin:begin + NF] = (reals[w] * scale[here]).astype(BF16)
        out[:, begin + NF:begin + 2 * NF] = (imags[w] * scale[here]).astype(BF16)


def flip_matrix(channels):
    row = lax.broadcasted_iota(jnp.int32, (channels, channels), 0)
    column = lax.broadcasted_iota(jnp.int32, (channels, channels), 1)
    return (row + column == channels - 1).astype(F32).astype(BF16)


def rotate_kernel(lags, own, cos_lag, sin_lag, out):
    channels, features = own.shape
    flip = flip_matrix(channels)
    for begin in range(0, features, 2 * NF):
        flipped = dot(flip, own[:, begin:begin + 2 * NF])
        real, imag = flipped[:, :NF], flipped[:, NF:]
        for t in range(lags):
            c, s = cos_lag[t:t + 1, :], sin_lag[t:t + 1, :]
            here = slice(t * channels, (t + 1) * channels)
            out[here, begin:begin + NF] = (real * c - imag * s).astype(BF16)
            out[here, begin + NF:begin + 2 * NF] = (real * s + imag * c).astype(BF16)


def fill_slots(channels, partners, present, absent, sems):
    def place(slot):
        return pl.ds(pl.multiple_of(slot * channels, channels), channels)

    for slot in absent:
        partners[place(slot), :] = jnp.zeros((channels, partners.shape[1]), BF16)
    copies = [
        pltpu.make_async_copy(source, partners.at[place(slot), :], sems.at[i])
        for i, (source, slot) in enumerate(present)
    ]
    for copy in copies:
        copy.start()
    return copies


def early_slots(place, channels, blocks, partners, sems):
    core = lax.rem(place[0], 2)
    own, own_swapped, ahead, ahead_swapped = blocks

    @pl.when(core == 0)
    def _():
        for copy in fill_slots(
            channels, partners,
            [(own, 0), (own_swapped, 1), (ahead, 4), (ahead_swapped, 5)], (2, 3, 6, 7), sems,
        ):
            copy.wait()

    @pl.when(core == 1)
    def _():
        for copy in fill_slots(
            channels, partners,
            [(own, 0), (ahead, 4), (ahead_swapped, 3)], (1, 2, 5, 6, 7), sems,
        ):
            copy.wait()


def late_slots(place, channels, blocks, partners, sems):
    core = lax.rem(place[0], 2)
    side = lax.rem(place[0] // 2, 2)
    far, far_swapped, cross, cross_swapped, other, other_swapped = blocks
    cross_slot = 6 - 4 * side
    other_slot = 8 - cross_slot
    step = 1 - 2 * core
    both = [(far, 0), (cross, cross_slot), (other, other_slot),
            (cross_swapped, cross_slot + step), (other_swapped, other_slot + step)]

    @pl.when(core == 0)
    def _():
        for copy in fill_slots(channels, partners, both, (1, 4, 5), sems):
            copy.wait()

    @pl.when(core == 1)
    def _():
        for copy in fill_slots(channels, partners, both + [(far_swapped, 7)], (3, 4), sems):
            copy.wait()


def product_kernel(late, last, norm_scale, lags, channels, rows, has_before, place, rotated_hbm, *refs):
    refs = list(refs)
    before_hbm = refs.pop(0) if has_before else None
    block_count = 6 if late else 4
    blocks, refs = refs[:block_count], refs[block_count:]
    out, partners, rotated, before, slot_sems, sems = refs
    count = lags * channels // rows
    copies = []
    for g in range(count):
        here = pl.ds(g * rows, rows)
        copies.append([
            pltpu.make_async_copy(rotated_hbm.at[here, :], rotated.at[here, :], sems.at[2 * g])
        ])
        if has_before:
            copies[-1].append(
                pltpu.make_async_copy(before_hbm.at[here, :], before.at[here, :], sems.at[2 * g + 1])
            )
    for group in copies:
        for copy in group:
            copy.start()
    (late_slots if late else early_slots)(place, channels, blocks, partners, slot_sems)

    row = lax.broadcasted_iota(jnp.int32, (channels, NPART), 0)
    column = lax.broadcasted_iota(jnp.int32, (channels, NPART), 1)
    low = row + column < channels
    keep = (low | (column >= channels)) if late else jnp.logical_not(low)
    flip = flip_matrix(channels)
    for g in range(count):
        for copy in copies[g]:
            copy.wait()
        product = lax.dot_general(
            rotated[g * rows:(g + 1) * rows, :], partners[...], (((1,), (1,)), ((), ())),
            preferred_element_type=F32,
        )
        for i in range(rows // channels):
            here = slice(g * rows + i * channels, g * rows + (i + 1) * channels)
            value = jnp.where(keep, product[i * channels:(i + 1) * channels, :], 0.0)
            if has_before:
                value = value + before[here, :]
            if last:
                cyclic = pltpu.roll(
                    value * norm_scale, NPART - channels, 1, stride=1, stride_axis=0
                )
                out[here.start // channels] = dot(flip, cyclic.astype(BF16)).astype(BF16)
            else:
                out[here, :] = value


def exchange(value, pairs):
    return lax.ppermute(value, "chan", pairs)


def local(records, dead_mask, offsets):
    channels, samples = records.shape
    tm_count = lax.axis_size("tm")
    tm_index = lax.axis_index("tm")
    chan_count = lax.axis_size("chan")
    own = samples // HOP
    windows = own * tm_count
    halves = own
    halo = 0
    if tm_count > 1:
        reach = 2 * HOP + H
        left = lax.ppermute(
            records[:, samples - H:], "tm", [(i, i + 1) for i in range(tm_count - 1)]
        )
        right = lax.ppermute(
            records[:, :reach], "tm", [(i + 1, i) for i in range(tm_count - 1)]
        )
        records = jnp.concatenate([left, records, right], axis=1)
        halves = own + 2
        halo = H
    high, low = (jnp.asarray(t) for t in fourier_tables())
    level_band, smooth_band, inverse_count = (jnp.asarray(t) for t in small_tables())
    own_offsets = lax.dynamic_slice_in_dim(offsets, tm_index * own, own, 0)
    vmem = pl.BlockSpec(memory_space=pltpu.VMEM)
    smem = pl.BlockSpec(memory_space=pltpu.SMEM)
    hbm = pl.BlockSpec(memory_space=pl.ANY)
    params = pltpu.CompilerParams(vmem_limit_bytes=40 * 1024 * 1024)

    def spectra_of(first, count):
        bulk = min(count + 1, halves - first)
        edges = min(count + 2, halves - first)
        spectra = pl.pallas_call(
            functools.partial(spectra_kernel, first, count, bulk, edges, halo),
            name="spectra",
            out_shape=jax.ShapeDtypeStruct((channels, count * 2 * NF), BF16),
            in_specs=[hbm, hbm, hbm, smem, smem, vmem, vmem, vmem],
            out_specs=vmem,
            scratch_shapes=[
                pltpu.VMEM((channels, edges * HOP + 2 * H), F32),
                pltpu.VMEM((channels, edges * HOP + 2 * H), BF16),
                pltpu.VMEM((bulk * channels, 2 * NF), F32),
                pltpu.VMEM((bulk * channels, 128), F32),
                pltpu.VMEM(high.shape, BF16),
                pltpu.VMEM(low.shape, BF16),
                pltpu.SemaphoreType.DMA((bulk * (HOP // GROUP) + 3,)),
                pltpu.SemaphoreType.DMA((2 * (HOP // GROUP),)),
            ],
            compiler_params=params,
            cost_estimate=pl.CostEstimate(
                flops=7_000_000_000 // CHUNKS, bytes_accessed=8 * 1024 * 1024, transcendentals=0
            ),
        )(records, high, low, dead_mask, own_offsets[first:first + count],
          level_band, smooth_band, inverse_count)
        if tm_count > 1:
            spectra = lax.all_gather(spectra, "tm", axis=1, tiled=True)
        return spectra

    lags = NLAG // tm_count
    rows = min(256, lags * channels)
    cos_lag, sin_lag = (
        lax.dynamic_slice_in_dim(jnp.asarray(t), tm_index * lags, lags, 0) for t in lag_tables()
    )
    place = lax.axis_index("chan").astype(jnp.int32).reshape(1)
    norm_scale = 1.0 / math.sqrt(2.0 * NF * windows)

    def rotate(spectra):
        features = spectra.shape[1]
        return pl.pallas_call(
            functools.partial(rotate_kernel, lags),
            name="rotate",
            out_shape=jax.ShapeDtypeStruct((lags * channels, features), BF16),
            in_specs=[vmem, vmem, vmem],
            out_specs=vmem,
            compiler_params=params,
            cost_estimate=pl.CostEstimate(
                flops=2_000_000_000, bytes_accessed=4 * 1024 * 1024, transcendentals=0
            ),
        )(spectra, cos_lag, sin_lag)

    def product(rotated, blocks, before, late, last):
        features = rotated.shape[1]
        operands = [place, rotated] + ([] if before is None else [before]) + list(blocks)
        return pl.pallas_call(
            functools.partial(
                product_kernel, late, last, norm_scale, lags, channels, rows, before is not None
            ),
            name="late_product" if late else "early_product",
            out_shape=(
                jax.ShapeDtypeStruct((lags, channels, NPART), BF16) if last
                else jax.ShapeDtypeStruct((lags * channels, NPART), F32)
            ),
            in_specs=[smem] + [hbm] * (len(operands) - 1),
            out_specs=vmem,
            scratch_shapes=[
                pltpu.VMEM((NPART, features), BF16),
                pltpu.VMEM((lags * channels, features), BF16),
                pltpu.VMEM((lags * channels, NPART), F32),
                pltpu.SemaphoreType.DMA((6,)),
                pltpu.SemaphoreType.DMA((2 * (lags * channels // rows),)),
            ],
            compiler_params=params,
            cost_estimate=pl.CostEstimate(
                flops=2 * lags * channels * features * NPART, bytes_accessed=6 * 1024 * 1024,
                transcendentals=0,
            ),
        )(*operands)

    every = range(chan_count)
    down = [(i, i - 4) for i in every if i >= 4]
    across = [(i, i ^ 2) for i in every]
    cores = [(i, i ^ 1) for i in every]
    side = lax.rem(lax.axis_index("chan") // 2, 2)

    def gather(spectra):
        ahead = exchange(spectra, down)
        far = exchange(ahead, down)
        cross = exchange(ahead, across)
        other = exchange(jnp.where(side == 0, far, spectra), across)
        early = (spectra, exchange(spectra, cores), ahead, exchange(ahead, cores))
        late = (far, exchange(far, cores), cross, exchange(cross, cores),
                other, exchange(other, cores))
        return early, late

    per_chunk = own // CHUNKS
    chunks = [spectra_of(i * per_chunk, per_chunk) for i in range(CHUNKS)]
    moved = [gather(spectra) for spectra in chunks]
    rotated = [rotate(spectra) for spectra in chunks]
    total = None
    for i in range(CHUNKS):
        total = product(rotated[i], moved[i][0], total, False, False)
    for i in range(CHUNKS):
        total = product(rotated[i], moved[i][1], total, True, i == CHUNKS - 1)
    return total


def solution(mesh):
    return jax.shard_map(
        local,
        mesh=mesh,
        in_specs=(P(("win", "chan"), "tm"), P(("win", "chan")), P("win")),
        out_specs=P("tm", ("win", "chan"), None),
        check_vma=False,
    )
```

```python
import functools
import math

import jax
import jax.numpy as jnp
import ml_dtypes
import numpy as np
from jax import lax
from jax.experimental import pallas as pl
from jax.experimental.pallas import tpu as pltpu
from jax.sharding import PartitionSpec as P

L = 8192
HOP = 4096
H = 128
K0 = 32
NF = 256
WB = 64
NLAG = 32
NPART = 256
EDGE = 512
STEP = 256
GROUP = 512
EPS = 1e-05
TWO_PI = 2.0 * math.pi
BF16 = jnp.bfloat16
F32 = jnp.float32


def split_table(table):
    high = table.astype(ml_dtypes.bfloat16)
    low = (table - high.astype(np.float64)).astype(ml_dtypes.bfloat16)
    return high, low


@functools.cache
def fourier_tables():
    samples = np.arange(GROUP)[:, None]
    bins = K0 + np.arange(NF)[None, :]
    angle = (samples * bins % L) * (TWO_PI / L)
    inner = np.concatenate([np.cos(angle), -np.sin(angle)], axis=1)
    outer = np.zeros((GROUP, 128))
    for lane, k, wave in ((0, K0 - 1, np.cos), (64, K0 - 1, np.sin), (127, K0 + NF, np.cos), (63, K0 + NF, np.sin)):
        sign = 1.0 if wave is np.cos else -1.0
        outer[:, lane] = sign * wave((samples[:, 0] * k % L) * (TWO_PI / L))
    high, low = split_table(inner)
    return np.concatenate([high, outer.astype(ml_dtypes.bfloat16)], axis=1), low


@functools.cache
def group_turns():
    bins = K0 + np.arange(NF)
    outer_bins = np.where(np.isin(np.arange(128), (0, 64)), K0 - 1, K0 + NF)
    outer_sign = np.where(np.isin(np.arange(128), (0, 127)), -1.0, 1.0)
    every = np.concatenate([bins, bins, outer_bins])
    sign = np.concatenate([-np.ones(NF), np.ones(NF), outer_sign])
    angle = (np.arange(HOP // GROUP)[:, None] * GROUP * every[None, :] % L) * (TWO_PI / L)
    return np.cos(angle).astype(np.float32), (sign * np.sin(angle)).astype(np.float32)


@functools.cache
def small_tables():
    lane = np.arange(2 * H + STEP)[:, None]
    place = np.arange(STEP)[None, :]
    level_band = ((lane >= place) & (lane <= place + 2 * H)).astype(ml_dtypes.bfloat16)
    bins = np.arange(NF)
    smooth_band = np.abs(bins[:, None] - bins[None, :]) <= WB
    inverse_count = (1.0 / smooth_band.sum(axis=0)).astype(np.float32)[None, :]
    return level_band, smooth_band.astype(ml_dtypes.bfloat16), inverse_count


@functools.cache
def lag_tables():
    lags = np.arange(NLAG)[:, None] - NLAG // 2
    angle = (lags * (K0 + np.arange(NF))[None, :] % L) * (TWO_PI / L)
    return np.cos(angle).astype(np.float32), np.sin(angle).astype(np.float32)


def split(value):
    high = value.astype(BF16)
    return high, (value - high.astype(F32)).astype(BF16)


def dot(a, b):
    return jnp.dot(a, b, preferred_element_type=F32)


def spectra_kernel(
    halves, own, halo,
    x_hbm, high, low, turn_same, turn_swap, dead, offs, level_band, smooth_band, inverse_count,
    out, x, absolute, norm_high, norm_low, parts, sems,
):
    channels = x.shape[0]
    groups = HOP // GROUP
    bulk = min(own + 1, halves)
    edges = min(own + 2, halves)
    width = halves * HOP
    copies = []
    if halo:
        copies.append((pltpu.make_async_copy(x_hbm, x, sems.at[0]), 0, width + 2 * H))
    else:
        for begin in (0, H + width):
            absolute[:, begin:begin + H] = jnp.zeros((channels, H), BF16)
        for j in range(halves):
            copies.append((
                pltpu.make_async_copy(
                    x_hbm.at[:, pl.ds(j * HOP, HOP)], x.at[:, pl.ds(H + j * HOP, HOP)], sems.at[j]
                ), H + j * HOP, HOP,
            ))
    for copy, _, _ in copies:
        copy.start()
    for copy, begin, length in copies:
        copy.wait()
        absolute[:, begin:begin + length] = jnp.abs(x[:, begin:begin + length]).astype(BF16)

    def rows(ref, begin, length, count):
        return [ref[:, begin + j * HOP:begin + j * HOP + length] for j in range(count)]

    def store(place, value):
        here = slice(place, place + value.shape[0])
        norm_high[here, :], norm_low[here, :] = split(value)

    def normalise(group_ids, place):
        blocks = [(g, g * GROUP + part * STEP) for g in group_ids for part in range(GROUP // STEP)]
        counts = [edges if g == 0 else bulk for g, _ in blocks]
        level = dot(
            jnp.concatenate(
                [r for (_, begin), n in zip(blocks, counts)
                 for r in rows(absolute, begin, STEP + 2 * H, n)], axis=0
            ), level_band[...],
        ) * (1.0 / (2 * H + 1)) + EPS
        values = []
        at = 0
        for (_, begin), n in zip(blocks, counts):
            samples = jnp.concatenate(rows(x, H + begin, STEP, n), axis=0)
            values.append(samples / level[at:at + n * channels])
            at += n * channels
        begins = {}
        for index, g in enumerate(group_ids):
            value = jnp.concatenate(values[2 * index:2 * index + 2], axis=1)
            if g == 0:
                lane = lax.broadcasted_iota(jnp.int32, (channels, EDGE), 1)
                merged = []
                for w in range(own):
                    mine = value[w * channels:(w + 1) * channels]
                    other = (
                        value[(w + 2) * channels:(w + 3) * channels]
                        if w + 2 < edges else jnp.zeros_like(mine)
                    )
                    merged.append(jnp.where(lane >= offs[w], mine, other))
                begins["edge"] = place
                store(place, jnp.concatenate(merged, axis=0))
                place += own * channels
                value = value[:bulk * channels]
            begins[g] = place
            store(place, value)
            place += bulk * channels
        return begins, place

    def transform(begin, end):
        first = dot(norm_high[begin:end, :], high[...])
        second = dot(norm_low[begin:end, :], high[:, :2 * NF])
        second = second + dot(norm_high[begin:end, :], low[...])
        parts[begin:end, :2 * NF] = first[:, :2 * NF] + second
        parts[begin:end, 2 * NF:] = first[:, 2 * NF:]

    begins = {}
    place = 0
    half = groups // 2
    for batch in (range(half), range(half, groups)):
        start = place
        found, place = normalise(list(batch), place)
        begins.update(found)
        transform(start, place)

    def piece(name, j):
        return parts[begins[name] + j * channels:begins[name] + (j + 1) * channels, :]

    def bulk_of(j):
        same = jnp.zeros((channels, parts.shape[1]), F32)
        swap = same
        for g in range(1, groups):
            value = piece(g, j)
            same = same + value * turn_same[g:g + 1, :]
            swap = swap + value * turn_swap[g:g + 1, :]
        return same + jnp.concatenate(
            [swap[:, NF:2 * NF], swap[:, :NF], pltpu.roll(swap[:, 2 * NF:], 64, 1)], axis=1
        )

    window = lax.broadcasted_iota(jnp.int32, (own, 1), 0)
    offsets = sum(jnp.where(window == w, offs[w], 0) for w in range(own))
    lane = lax.broadcasted_iota(jnp.int32, (1, NF), 1)
    outer_lane = lax.broadcasted_iota(jnp.int32, (1, 128), 1)
    outer_bin = jnp.where((outer_lane == 0) | (outer_lane == 64), K0 - 1, K0 + NF)

    def turn(bins):
        angle = jnp.bitwise_and(bins * offsets, L - 1).astype(F32) * (TWO_PI / L)
        return jnp.cos(angle), jnp.sin(angle)

    cos_turn, sin_turn = turn(lane + K0)
    cos_outer, sin_outer = turn(outer_bin)
    sign = 1.0 - 2.0 * jnp.bitwise_and(lane + K0, 1).astype(F32)
    sign_outer = 1.0 - 2.0 * jnp.bitwise_and(outer_bin, 1).astype(F32)
    channel = lax.broadcasted_iota(jnp.int32, (channels, 1), 0)
    live = 1.0 - sum(jnp.where(channel == i, dead[i], 0) for i in range(channels)).astype(F32)

    signs = jnp.concatenate([sign, sign, sign_outer], axis=1)
    reals, imags, magnitudes = [], [], []
    following = bulk_of(0)
    for w in range(own):
        spec = following + piece("edge", w)
        if w + 1 < bulk:
            following = bulk_of(w + 1)
            spec = spec + (following + piece(0, w + 1)) * signs
        spec = spec * live
        outer = spec[:, 2 * NF:]
        c, s = cos_turn[w:w + 1], sin_turn[w:w + 1]
        c_outer, s_outer = cos_outer[w:w + 1], sin_outer[w:w + 1]
        outer_imag = pltpu.roll(outer, 64, 1)

        def hann(inner, ends):
            ends = jnp.concatenate([ends, ends], axis=1)
            before = jnp.where(lane == 0, ends, pltpu.roll(inner, 1, 1))
            behind = jnp.where(lane == NF - 1, ends, pltpu.roll(inner, NF - 1, 1))
            return 0.5 * inner - 0.25 * (before + behind)

        real = hann(
            spec[:, :NF] * c - spec[:, NF:2 * NF] * s, outer * c_outer - outer_imag * s_outer
        )
        imag = hann(
            spec[:, :NF] * s + spec[:, NF:2 * NF] * c, outer * s_outer + outer_imag * c_outer
        )
        reals.append(real)
        imags.append(imag)
        magnitudes.append(jnp.sqrt(real * real + imag * imag + 1e-12))
    m_high, m_low = split(jnp.concatenate(magnitudes, axis=0))
    smooth = (dot(m_high, smooth_band[...]) + dot(m_low, smooth_band[...])) * inverse_count[...]
    scale = 1.0 / (smooth + EPS)
    for w in range(own):
        here = slice(w * channels, (w + 1) * channels)
        begin = w * 2 * NF
        out[:, begin:begin + NF] = (reals[w] * scale[here]).astype(BF16)
        out[:, begin + NF:begin + 2 * NF] = (imags[w] * scale[here]).astype(BF16)


def flip_matrix(channels):
    row = lax.broadcasted_iota(jnp.int32, (channels, channels), 0)
    column = lax.broadcasted_iota(jnp.int32, (channels, channels), 1)
    return (row + column == channels - 1).astype(F32).astype(BF16)


def rotate_kernel(lags, own, cos_lag, sin_lag, out):
    channels, features = own.shape
    flip = flip_matrix(channels)
    for begin in range(0, features, 2 * NF):
        flipped = dot(flip, own[:, begin:begin + 2 * NF])
        real, imag = flipped[:, :NF], flipped[:, NF:]
        for t in range(lags):
            c, s = cos_lag[t:t + 1, :], sin_lag[t:t + 1, :]
            here = slice(t * channels, (t + 1) * channels)
            out[here, begin:begin + NF] = (real * c - imag * s).astype(BF16)
            out[here, begin + NF:begin + 2 * NF] = (real * s + imag * c).astype(BF16)


def fill_slots(channels, partners, present, absent, sems):
    def place(slot):
        return pl.ds(pl.multiple_of(slot * channels, channels), channels)

    for slot in absent:
        partners[place(slot), :] = jnp.zeros((channels, partners.shape[1]), BF16)
    copies = [
        pltpu.make_async_copy(source, partners.at[place(slot), :], sems.at[i])
        for i, (source, slot) in enumerate(present)
    ]
    for copy in copies:
        copy.start()
    return copies


def early_slots(place, channels, blocks, partners, sems):
    core = lax.rem(place[0], 2)
    own, own_swapped, ahead, ahead_swapped = blocks

    @pl.when(core == 0)
    def _():
        for copy in fill_slots(
            channels, partners,
            [(own, 0), (own_swapped, 1), (ahead, 4), (ahead_swapped, 5)], (2, 3, 6, 7), sems,
        ):
            copy.wait()

    @pl.when(core == 1)
    def _():
        for copy in fill_slots(
            channels, partners,
            [(own, 0), (ahead, 4), (ahead_swapped, 3)], (1, 2, 5, 6, 7), sems,
        ):
            copy.wait()


def late_slots(place, channels, blocks, partners, sems):
    core = lax.rem(place[0], 2)
    side = lax.rem(place[0] // 2, 2)
    far, far_swapped, cross, cross_swapped, other, other_swapped = blocks
    cross_slot = 6 - 4 * side
    other_slot = 8 - cross_slot
    step = 1 - 2 * core
    both = [(far, 0), (cross, cross_slot), (other, other_slot),
            (cross_swapped, cross_slot + step), (other_swapped, other_slot + step)]

    @pl.when(core == 0)
    def _():
        for copy in fill_slots(channels, partners, both, (1, 4, 5), sems):
            copy.wait()

    @pl.when(core == 1)
    def _():
        for copy in fill_slots(channels, partners, both + [(far_swapped, 7)], (3, 4), sems):
            copy.wait()


def product_kernel(late, last, norm_scale, lags, channels, rows, has_before, place, rotated_hbm, *refs):
    refs = list(refs)
    before_hbm = refs.pop(0) if has_before else None
    block_count = 6 if late else 4
    blocks, refs = refs[:block_count], refs[block_count:]
    out, partners, partners_turned, rotated, before, slot_sems, sems = refs
    count = lags * channels // rows
    copies = []
    for g in range(count):
        here = pl.ds(g * rows, rows)
        copies.append([
            pltpu.make_async_copy(rotated_hbm.at[here, :], rotated.at[here, :], sems.at[2 * g])
        ])
        if has_before:
            copies[-1].append(
                pltpu.make_async_copy(before_hbm.at[here, :], before.at[here, :], sems.at[2 * g + 1])
            )
    for group in copies:
        for copy in group:
            copy.start()
    (late_slots if late else early_slots)(place, channels, blocks, partners, slot_sems)

    for begin in range(0, partners.shape[1], 2 * NF):
        partners_turned[begin:begin + 2 * NF, :] = partners[:, begin:begin + 2 * NF].T
    row = lax.broadcasted_iota(jnp.int32, (channels, NPART), 0)
    column = lax.broadcasted_iota(jnp.int32, (channels, NPART), 1)
    low = row + column < channels
    keep = (low | (column >= channels)) if late else jnp.logical_not(low)
    flip = flip_matrix(channels)
    for g in range(count):
        for copy in copies[g]:
            copy.wait()
        product = dot(rotated[g * rows:(g + 1) * rows, :], partners_turned[...])
        for i in range(rows // channels):
            here = slice(g * rows + i * channels, g * rows + (i + 1) * channels)
            value = jnp.where(keep, product[i * channels:(i + 1) * channels, :], 0.0)
            if has_before:
                value = value + before[here, :]
            if last:
                cyclic = pltpu.roll(
                    value * norm_scale, NPART - channels, 1, stride=1, stride_axis=0
                )
                out[here.start // channels] = dot(flip, cyclic.astype(BF16)).astype(BF16)
            else:
                out[here, :] = value


def exchange(value, pairs):
    return lax.ppermute(value, "chan", pairs)


def local(records, dead_mask, offsets):
    channels, samples = records.shape
    tm_count = lax.axis_size("tm")
    tm_index = lax.axis_index("tm")
    chan_count = lax.axis_size("chan")
    own = samples // HOP
    windows = own * tm_count
    halves = own
    halo = 0
    if tm_count > 1:
        reach = 2 * HOP + H
        left = lax.ppermute(
            records[:, samples - H:], "tm", [(i, i + 1) for i in range(tm_count - 1)]
        )
        right = lax.ppermute(
            records[:, :reach], "tm", [(i + 1, i) for i in range(tm_count - 1)]
        )
        records = jnp.concatenate([left, records, right], axis=1)
        halves = own + 2
        halo = H
    high, low = (jnp.asarray(t) for t in fourier_tables())
    turn_same, turn_swap = (jnp.asarray(t) for t in group_turns())
    level_band, smooth_band, inverse_count = (jnp.asarray(t) for t in small_tables())
    own_offsets = lax.dynamic_slice_in_dim(offsets, tm_index * own, own, 0)
    vmem = pl.BlockSpec(memory_space=pltpu.VMEM)
    smem = pl.BlockSpec(memory_space=pltpu.SMEM)
    hbm = pl.BlockSpec(memory_space=pl.ANY)
    params = pltpu.CompilerParams(vmem_limit_bytes=48 * 1024 * 1024)

    bulk = min(own + 1, halves)
    part_rows = (own + bulk * (HOP // GROUP)) * channels
    spectra = pl.pallas_call(
        functools.partial(spectra_kernel, halves, own, halo),
        name="spectra",
        out_shape=jax.ShapeDtypeStruct((channels, own * 2 * NF), BF16),
        in_specs=[hbm, vmem, vmem, vmem, vmem, smem, smem, vmem, vmem, vmem],
        out_specs=vmem,
        scratch_shapes=[
            pltpu.VMEM((channels, halves * HOP + 2 * H), F32),
            pltpu.VMEM((channels, halves * HOP + 2 * H), BF16),
            pltpu.VMEM((part_rows, GROUP), BF16),
            pltpu.VMEM((part_rows, GROUP), BF16),
            pltpu.VMEM((part_rows, 2 * NF + 128), F32),
            pltpu.SemaphoreType.DMA((halves,)),
        ],
        compiler_params=params,
        cost_estimate=pl.CostEstimate(
            flops=7_000_000_000, bytes_accessed=8 * 1024 * 1024, transcendentals=0
        ),
    )(records, high, low, turn_same, turn_swap, dead_mask, own_offsets,
      level_band, smooth_band, inverse_count)
    if tm_count > 1:
        spectra = lax.all_gather(spectra, "tm", axis=1, tiled=True)

    lags = NLAG // tm_count
    rows = min(256, lags * channels)
    cos_lag, sin_lag = (
        lax.dynamic_slice_in_dim(jnp.asarray(t), tm_index * lags, lags, 0) for t in lag_tables()
    )
    place = lax.axis_index("chan").astype(jnp.int32).reshape(1)
    norm_scale = 1.0 / math.sqrt(2.0 * NF * windows)

    def rotate(spectra):
        features = spectra.shape[1]
        return pl.pallas_call(
            functools.partial(rotate_kernel, lags),
            name="rotate",
            out_shape=jax.ShapeDtypeStruct((lags * channels, features), BF16),
            in_specs=[vmem, vmem, vmem],
            out_specs=vmem,
            compiler_params=params,
            cost_estimate=pl.CostEstimate(
                flops=4_000_000_000, bytes_accessed=8 * 1024 * 1024, transcendentals=0
            ),
        )(spectra, cos_lag, sin_lag)

    def product(rotated, blocks, before, late, last):
        features = rotated.shape[1]
        operands = [place, rotated] + ([] if before is None else [before]) + list(blocks)
        return pl.pallas_call(
            functools.partial(
                product_kernel, late, last, norm_scale, lags, channels, rows, before is not None
            ),
            name="late_product" if late else "early_product",
            out_shape=(
                jax.ShapeDtypeStruct((lags, channels, NPART), BF16) if last
                else jax.ShapeDtypeStruct((lags * channels, NPART), F32)
            ),
            in_specs=[smem] + [hbm] * (len(operands) - 1),
            out_specs=vmem,
            scratch_shapes=[
                pltpu.VMEM((NPART, features), BF16),
                pltpu.VMEM((features, NPART), BF16),
                pltpu.VMEM((lags * channels, features), BF16),
                pltpu.VMEM((lags * channels, NPART), F32),
                pltpu.SemaphoreType.DMA((6,)),
                pltpu.SemaphoreType.DMA((2 * (lags * channels // rows),)),
            ],
            compiler_params=params,
            cost_estimate=pl.CostEstimate(
                flops=2 * lags * channels * features * NPART, bytes_accessed=6 * 1024 * 1024,
                transcendentals=0,
            ),
        )(*operands)

    every = range(chan_count)
    down = [(i, i - 4) for i in every if i >= 4]
    down_2 = [(i, i - 2) for i in every if i >= 2]
    across = [(i, i ^ 2) for i in every]
    cores = [(i, i ^ 1) for i in every]
    side = lax.rem(lax.axis_index("chan") // 2, 2)

    ahead = exchange(spectra, down)
    own_swapped = exchange(spectra, [(i, j) for i, j in cores if j < i])
    rotated = rotate(spectra)
    ahead, rotated = lax.optimization_barrier((ahead, rotated))
    other = exchange(jnp.where(side == 0, ahead, spectra), down_2)
    cross = exchange(ahead, across)
    far = exchange(ahead, down)
    ahead_swapped = exchange(ahead, cores)
    early = product(rotated, (spectra, own_swapped, ahead, ahead_swapped), None, False, False)
    other, early = lax.optimization_barrier((other, early))
    far_swapped = exchange(far, [(i, j) for i, j in cores if j > i])
    blocks = (far, far_swapped, cross, exchange(cross, cores), other, exchange(other, cores))
    return product(rotated, blocks, early, True, True)


def solution(mesh):
    return jax.shard_map(
        local,
        mesh=mesh,
        in_specs=(P(("win", "chan"), "tm"), P(("win", "chan")), P("win")),
        out_specs=P("tm", ("win", "chan"), None),
        check_vma=False,
    )
```

```python
import functools
import math

import jax
import jax.numpy as jnp
import ml_dtypes
import numpy as np
from jax import lax
from jax.experimental import pallas as pl
from jax.experimental.pallas import tpu as pltpu
from jax.sharding import PartitionSpec as P

L = 8192
HOP = 4096
H = 128
K0 = 32
NF = 256
WB = 64
NLAG = 32
NPART = 256
EDGE = 512
STEP = 256
GROUP = 512
TABLES = 7
EPS = 1e-05
TWO_PI = 2.0 * math.pi
BF16 = jnp.bfloat16
F32 = jnp.float32


def split_table(table):
    high = table.astype(ml_dtypes.bfloat16)
    low = (table - high.astype(np.float64)).astype(ml_dtypes.bfloat16)
    return high, low


@functools.cache
def fourier_tables():
    samples = np.arange(GROUP)[:, None]
    bins = K0 + np.arange(NF)[None, :]
    angle = (samples * bins % L) * (TWO_PI / L)
    inner = np.concatenate([np.cos(angle), -np.sin(angle)], axis=1)
    outer = np.zeros((GROUP, 128))
    for lane, k, wave in ((0, K0 - 1, np.cos), (64, K0 - 1, np.sin), (127, K0 + NF, np.cos), (63, K0 + NF, np.sin)):
        sign = 1.0 if wave is np.cos else -1.0
        outer[:, lane] = sign * wave((samples[:, 0] * k % L) * (TWO_PI / L))
    high, low = split_table(inner)
    return np.concatenate([high, outer.astype(ml_dtypes.bfloat16)], axis=1), low


@functools.cache
def group_turns():
    bins = K0 + np.arange(NF)
    outer_bins = np.where(np.isin(np.arange(128), (0, 64)), K0 - 1, K0 + NF)
    outer_sign = np.where(np.isin(np.arange(128), (0, 127)), -1.0, 1.0)
    every = np.concatenate([bins, bins, outer_bins])
    sign = np.concatenate([-np.ones(NF), np.ones(NF), outer_sign])
    angle = (np.arange(HOP // GROUP)[:, None] * GROUP * every[None, :] % L) * (TWO_PI / L)
    return np.cos(angle).astype(np.float32), (sign * np.sin(angle)).astype(np.float32)


@functools.cache
def small_tables():
    lane = np.arange(2 * H + STEP)[:, None]
    place = np.arange(STEP)[None, :]
    level_band = ((lane >= place) & (lane <= place + 2 * H)).astype(ml_dtypes.bfloat16)
    bins = np.arange(NF)
    smooth_band = np.abs(bins[:, None] - bins[None, :]) <= WB
    inverse_count = (1.0 / smooth_band.sum(axis=0)).astype(np.float32)[None, :]
    return level_band, smooth_band.astype(ml_dtypes.bfloat16), inverse_count


@functools.cache
def lag_tables():
    lags = np.arange(NLAG)[:, None] - NLAG // 2
    angle = (lags * (K0 + np.arange(NF))[None, :] % L) * (TWO_PI / L)
    return np.cos(angle).astype(np.float32), np.sin(angle).astype(np.float32)


def split(value):
    high = value.astype(BF16)
    return high, (value - high.astype(F32)).astype(BF16)


def dot(a, b):
    return jnp.dot(a, b, preferred_element_type=F32)


def spectra_kernel(
    halves, own, halo,
    dead, offs, x_hbm, *refs,
):
    tables, refs = refs[:TABLES], refs[TABLES:]
    out, x, absolute, norm_high, norm_low, parts, sems, table_sems = refs[:8]
    held = refs[8:]
    level_band, high, low, turn_same, turn_swap, smooth_band, inverse_count = held
    channels = x.shape[0]
    groups = HOP // GROUP
    bulk = min(own + 1, halves)
    edges = min(own + 2, halves)
    width = halves * HOP
    copies = []
    if halo:
        copies.append((pltpu.make_async_copy(x_hbm, x, sems.at[0]), 0, width + 2 * H))
    else:
        for begin in (0, H + width):
            absolute[:, begin:begin + H] = jnp.zeros((channels, H), BF16)
        for j in range(halves):
            copies.append((
                pltpu.make_async_copy(
                    x_hbm.at[:, pl.ds(j * HOP, HOP)], x.at[:, pl.ds(H + j * HOP, HOP)], sems.at[j]
                ), H + j * HOP, HOP,
            ))
    for copy, _, _ in copies:
        copy.start()
    table_copies = [
        pltpu.make_async_copy(table, place, table_sems.at[i])
        for i, (table, place) in enumerate(zip(tables, held))
    ]
    for copy in table_copies:
        copy.start()
    for copy, begin, length in copies:
        copy.wait()
        absolute[:, begin:begin + length] = jnp.abs(x[:, begin:begin + length]).astype(BF16)

    for copy in table_copies:
        copy.wait()

    def rows(ref, begin, length, count):
        return [ref[:, begin + j * HOP:begin + j * HOP + length] for j in range(count)]

    def store(place, value):
        here = slice(place, place + value.shape[0])
        norm_high[here, :], norm_low[here, :] = split(value)

    def normalise(group_ids, place):
        blocks = [(g, g * GROUP + part * STEP) for g in group_ids for part in range(GROUP // STEP)]
        counts = [edges if g == 0 else bulk for g, _ in blocks]
        level = dot(
            jnp.concatenate(
                [r for (_, begin), n in zip(blocks, counts)
                 for r in rows(absolute, begin, STEP + 2 * H, n)], axis=0
            ), level_band[...],
        ) * (1.0 / (2 * H + 1)) + EPS
        values = []
        at = 0
        for (_, begin), n in zip(blocks, counts):
            samples = jnp.concatenate(rows(x, H + begin, STEP, n), axis=0)
            values.append(samples / level[at:at + n * channels])
            at += n * channels
        begins = {}
        for index, g in enumerate(group_ids):
            value = jnp.concatenate(values[2 * index:2 * index + 2], axis=1)
            if g == 0:
                lane = lax.broadcasted_iota(jnp.int32, (channels, EDGE), 1)
                merged = []
                for w in range(own):
                    mine = value[w * channels:(w + 1) * channels]
                    other = (
                        value[(w + 2) * channels:(w + 3) * channels]
                        if w + 2 < edges else jnp.zeros_like(mine)
                    )
                    merged.append(jnp.where(lane >= offs[w], mine, other))
                begins["edge"] = place
                store(place, jnp.concatenate(merged, axis=0))
                place += own * channels
                value = value[:bulk * channels]
            begins[g] = place
            store(place, value)
            place += bulk * channels
        return begins, place

    def transform(begin, end):
        first = dot(norm_high[begin:end, :], high[...])
        second = dot(norm_low[begin:end, :], high[:, :2 * NF])
        second = second + dot(norm_high[begin:end, :], low[...])
        parts[begin:end, :2 * NF] = first[:, :2 * NF] + second
        parts[begin:end, 2 * NF:] = first[:, 2 * NF:]

    begins = {}
    place = 0
    half = groups // 2
    for batch in (range(half), range(half, groups)):
        start = place
        found, place = normalise(list(batch), place)
        begins.update(found)
        transform(start, place)

    def piece(name, j):
        return parts[begins[name] + j * channels:begins[name] + (j + 1) * channels, :]

    def bulk_of(j):
        same = jnp.zeros((channels, parts.shape[1]), F32)
        swap = same
        for g in range(1, groups):
            value = piece(g, j)
            same = same + value * turn_same[g:g + 1, :]
            swap = swap + value * turn_swap[g:g + 1, :]
        return same + jnp.concatenate(
            [swap[:, NF:2 * NF], swap[:, :NF], pltpu.roll(swap[:, 2 * NF:], 64, 1)], axis=1
        )

    window = lax.broadcasted_iota(jnp.int32, (own, 1), 0)
    offsets = sum(jnp.where(window == w, offs[w], 0) for w in range(own))
    lane = lax.broadcasted_iota(jnp.int32, (1, NF), 1)
    outer_lane = lax.broadcasted_iota(jnp.int32, (1, 128), 1)
    outer_bin = jnp.where((outer_lane == 0) | (outer_lane == 64), K0 - 1, K0 + NF)

    def turn(bins):
        angle = jnp.bitwise_and(bins * offsets, L - 1).astype(F32) * (TWO_PI / L)
        return jnp.cos(angle), jnp.sin(angle)

    cos_turn, sin_turn = turn(lane + K0)
    cos_outer, sin_outer = turn(outer_bin)
    sign = 1.0 - 2.0 * jnp.bitwise_and(lane + K0, 1).astype(F32)
    sign_outer = 1.0 - 2.0 * jnp.bitwise_and(outer_bin, 1).astype(F32)
    channel = lax.broadcasted_iota(jnp.int32, (channels, 1), 0)
    live = 1.0 - sum(jnp.where(channel == i, dead[i], 0) for i in range(channels)).astype(F32)

    signs = jnp.concatenate([sign, sign, sign_outer], axis=1)
    reals, imags, magnitudes = [], [], []
    following = bulk_of(0)
    for w in range(own):
        spec = following + piece("edge", w)
        if w + 1 < bulk:
            following = bulk_of(w + 1)
            spec = spec + (following + piece(0, w + 1)) * signs
        spec = spec * live
        outer = spec[:, 2 * NF:]
        c, s = cos_turn[w:w + 1], sin_turn[w:w + 1]
        c_outer, s_outer = cos_outer[w:w + 1], sin_outer[w:w + 1]
        outer_imag = pltpu.roll(outer, 64, 1)

        def hann(inner, ends):
            ends = jnp.concatenate([ends, ends], axis=1)
            before = jnp.where(lane == 0, ends, pltpu.roll(inner, 1, 1))
            behind = jnp.where(lane == NF - 1, ends, pltpu.roll(inner, NF - 1, 1))
            return 0.5 * inner - 0.25 * (before + behind)

        real = hann(
            spec[:, :NF] * c - spec[:, NF:2 * NF] * s, outer * c_outer - outer_imag * s_outer
        )
        imag = hann(
            spec[:, :NF] * s + spec[:, NF:2 * NF] * c, outer * s_outer + outer_imag * c_outer
        )
        reals.append(real)
        imags.append(imag)
        magnitudes.append(jnp.sqrt(real * real + imag * imag + 1e-12))
    m_high, m_low = split(jnp.concatenate(magnitudes, axis=0))
    smooth = (dot(m_high, smooth_band[...]) + dot(m_low, smooth_band[...])) * inverse_count[...]
    scale = 1.0 / (smooth + EPS)
    flip = flip_matrix(channels)
    for w in range(own):
        here = slice(w * channels, (w + 1) * channels)
        white = jnp.concatenate([reals[w] * scale[here], imags[w] * scale[here]], axis=1)
        out[:, w * 2 * NF:(w + 1) * 2 * NF] = dot(flip, white.astype(BF16)).astype(BF16)


def flip_matrix(channels):
    row = lax.broadcasted_iota(jnp.int32, (channels, channels), 0)
    column = lax.broadcasted_iota(jnp.int32, (channels, channels), 1)
    return (row + column == channels - 1).astype(F32).astype(BF16)


def rotate_kernel(lags, own, cos_lag, sin_lag, out):
    channels = own.shape[0]
    straight = dot(flip_matrix(channels), own[...])
    real, imag = straight[:, :NF], straight[:, NF:]
    for t in range(lags):
        c, s = cos_lag[t:t + 1, :], sin_lag[t:t + 1, :]
        here = slice(t * channels, (t + 1) * channels)
        out[here, :NF] = (real * c - imag * s).astype(BF16)
        out[here, NF:] = (real * s + imag * c).astype(BF16)


def fill_slots(channels, partners, present, absent, sems):
    last = NPART // channels - 1

    def place(slot):
        return pl.ds(pl.multiple_of((last - slot) * channels, channels), channels)

    copies = [
        pltpu.make_async_copy(source, partners.at[place(slot), :], sems.at[i])
        for i, (source, slot) in enumerate(present)
    ]
    for copy in copies:
        copy.start()
    for slot in absent:
        partners[place(slot), :] = jnp.zeros((channels, partners.shape[1]), BF16)
    for copy in copies:
        copy.wait()


def early_slots(place, channels, blocks, partners, sems):
    core = lax.rem(place[0], 2)
    own, own_swapped, ahead = blocks

    @pl.when(core == 0)
    def _():
        present = [(own, 0), (own_swapped, 1), (ahead, 4)]
        fill_slots(channels, partners, present, (2, 3, 5, 6, 7), sems)

    @pl.when(core == 1)
    def _():
        fill_slots(channels, partners, [(own, 0), (ahead, 4)], (1, 2, 3, 5, 6, 7), sems)


def late_slots(place, channels, blocks, partners, sems):
    core = lax.rem(place[0], 2)
    side = lax.rem(place[0] // 2, 2)
    ahead_swapped, far, far_swapped, cross, cross_swapped, other, other_swapped = blocks
    cross_slot = 6 - 4 * side
    other_slot = 8 - cross_slot
    step = 1 - 2 * core
    both = [(far, 0), (cross, cross_slot), (other, other_slot), (ahead_swapped, 4 + step),
            (cross_swapped, cross_slot + step), (other_swapped, other_slot + step)]

    @pl.when(core == 0)
    def _():
        fill_slots(channels, partners, both, (1, 4), sems)

    @pl.when(core == 1)
    def _():
        fill_slots(channels, partners, both + [(far_swapped, 7)], (4,), sems)


def product_kernel(late, norm_scale, place, rotated, *refs):
    refs = list(refs)
    before = refs.pop(0) if late else None
    out, partners, total, sems = refs[-4:]
    blocks = refs[:-4]
    channels = blocks[0].shape[0]
    (late_slots if late else early_slots)(place, channels, blocks, partners, sems)
    rows, features = rotated.shape
    chunk = 2 * 2 * NF
    for begin in range(0, features, chunk):
        turned = partners[:, begin:begin + chunk].T
        product = dot(rotated[:, begin:begin + chunk], turned)
        if begin == 0:
            total[...] = product
        else:
            total[...] += product

    row = lax.broadcasted_iota(jnp.int32, (channels, NPART), 0)
    column = lax.broadcasted_iota(jnp.int32, (channels, NPART), 1)
    low = row + column >= NPART - 1
    keep = (low | (column < NPART - channels)) if late else jnp.logical_not(low)
    sheared = []
    for begin in range(0, rows, channels):
        here = slice(begin, begin + channels)
        value = jnp.where(keep, total[here, :], 0.0)
        if late:
            value = (value + before[here, :]) * norm_scale
            sheared.append(pltpu.roll(value, 1, 1, stride=1, stride_axis=0).astype(BF16))
        else:
            out[here, :] = value
    if late:
        sheared = jnp.concatenate(sheared, axis=0)
        out[...] = dot(sheared, flip_matrix(NPART)).astype(BF16)


def exchange(value, pairs):
    return lax.ppermute(value, "chan", pairs)


def local(records, dead_mask, offsets):
    channels, samples = records.shape
    tm_count = lax.axis_size("tm")
    tm_index = lax.axis_index("tm")
    chan_count = lax.axis_size("chan")
    own = samples // HOP
    windows = own * tm_count
    halves = own
    halo = 0
    if tm_count > 1:
        reach = 2 * HOP + H
        left = lax.ppermute(
            records[:, samples - H:], "tm", [(i, i + 1) for i in range(tm_count - 1)]
        )
        right = lax.ppermute(
            records[:, :reach], "tm", [(i + 1, i) for i in range(tm_count - 1)]
        )
        records = jnp.concatenate([left, records, right], axis=1)
        halves = own + 2
        halo = H
    level_band, smooth_band, inverse_count = small_tables()
    tables = (level_band, *fourier_tables(), *group_turns(), smooth_band, inverse_count)
    tables = [jnp.asarray(t) for t in tables]
    own_offsets = lax.dynamic_slice_in_dim(offsets, tm_index * own, own, 0)
    vmem = pl.BlockSpec(memory_space=pltpu.VMEM)
    smem = pl.BlockSpec(memory_space=pltpu.SMEM)
    hbm = pl.BlockSpec(memory_space=pl.ANY)
    far_memory = pl.BlockSpec(memory_space=pltpu.HBM)
    params = pltpu.CompilerParams(vmem_limit_bytes=24 * 1024 * 1024)

    bulk = min(own + 1, halves)
    part_rows = (own + bulk * (HOP // GROUP)) * channels
    spectra = pl.pallas_call(
        functools.partial(spectra_kernel, halves, own, halo),
        name="spectra",
        out_shape=jax.ShapeDtypeStruct((channels, own * 2 * NF), BF16),
        in_specs=[smem, smem] + [far_memory] * (1 + TABLES),
        out_specs=vmem,
        scratch_shapes=[
            pltpu.VMEM((channels, halves * HOP + 2 * H), F32),
            pltpu.VMEM((channels, halves * HOP + 2 * H), BF16),
            pltpu.VMEM((part_rows, GROUP), BF16),
            pltpu.VMEM((part_rows, GROUP), BF16),
            pltpu.VMEM((part_rows, 2 * NF + 128), F32),
            pltpu.SemaphoreType.DMA((halves,)),
            pltpu.SemaphoreType.DMA((TABLES,)),
        ] + [pltpu.VMEM(t.shape, t.dtype) for t in tables],
        compiler_params=pltpu.CompilerParams(vmem_limit_bytes=60 * 1024 * 1024),
        cost_estimate=pl.CostEstimate(
            flops=7_000_000_000, bytes_accessed=8 * 1024 * 1024, transcendentals=0
        ),
    )(dead_mask, own_offsets, records, *tables)
    if tm_count > 1:
        spectra = lax.all_gather(spectra, "tm", axis=1, tiled=True)

    lags = NLAG // tm_count
    cos_lag, sin_lag = (
        lax.dynamic_slice_in_dim(jnp.asarray(t), tm_index * lags, lags, 0) for t in lag_tables()
    )
    place = lax.axis_index("chan").astype(jnp.int32).reshape(1)
    norm_scale = 1.0 / math.sqrt(2.0 * NF * windows)

    features = spectra.shape[1]
    rotated = pl.pallas_call(
        functools.partial(rotate_kernel, lags),
        name="rotate",
        grid=(windows,),
        out_shape=jax.ShapeDtypeStruct((lags * channels, features), BF16),
        in_specs=[
            pl.BlockSpec((channels, 2 * NF), lambda w: (0, w)),
            pl.BlockSpec((lags, NF), lambda w: (0, 0)),
            pl.BlockSpec((lags, NF), lambda w: (0, 0)),
        ],
        out_specs=pl.BlockSpec((lags * channels, 2 * NF), lambda w: (0, w)),
        compiler_params=params,
        cost_estimate=pl.CostEstimate(
            flops=4_000_000_000, bytes_accessed=8 * 1024 * 1024, transcendentals=0
        ),
    )(spectra, cos_lag, sin_lag)

    def product(blocks, before):
        late = before is not None
        operands = [place, rotated] + ([before] if late else []) + list(blocks)
        return pl.pallas_call(
            functools.partial(product_kernel, late, norm_scale),
            name="late_product" if late else "early_product",
            out_shape=jax.ShapeDtypeStruct((lags * channels, NPART), BF16 if late else F32),
            in_specs=[smem, vmem] + ([vmem] if late else []) + [hbm] * len(blocks),
            out_specs=vmem,
            scratch_shapes=[
                pltpu.VMEM((NPART, features), BF16),
                pltpu.VMEM((lags * channels, NPART), F32),
                pltpu.SemaphoreType.DMA((len(blocks),)),
            ],
            compiler_params=params,
            cost_estimate=pl.CostEstimate(
                flops=2 * lags * channels * features * NPART, bytes_accessed=6 * 1024 * 1024,
                transcendentals=0,
            ),
        )(*operands)

    every = range(chan_count)
    down = [(i, i - 4) for i in every if i >= 4]
    down_2 = [(i, i - 2) for i in every if i >= 2]
    across = [(i, i ^ 2) for i in every]
    cores = [(i, i ^ 1) for i in every]
    side = lax.rem(lax.axis_index("chan") // 2, 2)

    ahead = exchange(spectra, down)
    own_swapped = exchange(spectra, [(i, j) for i, j in cores if j < i])
    ahead, rotated = lax.optimization_barrier((ahead, rotated))
    other = exchange(jnp.where(side == 0, ahead, spectra), down_2)
    cross = exchange(ahead, across)
    far = exchange(ahead, down)
    early = product((spectra, own_swapped, ahead), None)
    ahead, other, early = lax.optimization_barrier((ahead, other, early))
    far_swapped = exchange(far, [(i, j) for i, j in cores if j > i])
    blocks = (exchange(ahead, cores), far, far_swapped, cross, exchange(cross, cores),
              other, exchange(other, cores))
    return product(blocks, early).reshape(lags, channels, NPART)


def solution(mesh):
    return jax.shard_map(
        local,
        mesh=mesh,
        in_specs=(P(("win", "chan"), "tm"), P(("win", "chan")), P("win")),
        out_specs=P("tm", ("win", "chan"), None),
        check_vma=False,
    )
```

```python
import functools
import math

import jax
import jax.numpy as jnp
import ml_dtypes
import numpy as np
from jax import lax
from jax.experimental import pallas as pl
from jax.experimental.pallas import tpu as pltpu
from jax.sharding import PartitionSpec as P

L = 8192
HOP = 4096
H = 128
K0 = 32
NF = 256
WB = 64
NLAG = 32
NPART = 256
EDGE = 512
STEP = 256
GROUP = 512
TABLES = 7
EPS = 1e-05
TWO_PI = 2.0 * math.pi
BF16 = jnp.bfloat16
F32 = jnp.float32


def split_table(table):
    high = table.astype(ml_dtypes.bfloat16)
    low = (table - high.astype(np.float64)).astype(ml_dtypes.bfloat16)
    return high, low


@functools.cache
def fourier_tables():
    samples = np.arange(GROUP)[:, None]
    bins = K0 + np.arange(NF)[None, :]
    angle = (samples * bins % L) * (TWO_PI / L)
    inner = np.concatenate([np.cos(angle), -np.sin(angle)], axis=1)
    outer = np.zeros((GROUP, 128))
    for lane, k, wave in ((0, K0 - 1, np.cos), (64, K0 - 1, np.sin), (127, K0 + NF, np.cos), (63, K0 + NF, np.sin)):
        sign = 1.0 if wave is np.cos else -1.0
        outer[:, lane] = sign * wave((samples[:, 0] * k % L) * (TWO_PI / L))
    high, low = split_table(inner)
    return np.concatenate([high, outer.astype(ml_dtypes.bfloat16)], axis=1), low


@functools.cache
def group_turns():
    bins = K0 + np.arange(NF)
    outer_bins = np.where(np.isin(np.arange(128), (0, 64)), K0 - 1, K0 + NF)
    outer_sign = np.where(np.isin(np.arange(128), (0, 127)), -1.0, 1.0)
    every = np.concatenate([bins, bins, outer_bins])
    sign = np.concatenate([-np.ones(NF), np.ones(NF), outer_sign])
    angle = (np.arange(HOP // GROUP)[:, None] * GROUP * every[None, :] % L) * (TWO_PI / L)
    return np.cos(angle).astype(np.float32), (sign * np.sin(angle)).astype(np.float32)


@functools.cache
def small_tables():
    lane = np.arange(2 * H + STEP)[:, None]
    place = np.arange(STEP)[None, :]
    level_band = ((lane >= place) & (lane <= place + 2 * H)).astype(ml_dtypes.bfloat16)
    bins = np.arange(NF)
    smooth_band = np.abs(bins[:, None] - bins[None, :]) <= WB
    inverse_count = (1.0 / smooth_band.sum(axis=0)).astype(np.float32)[None, :]
    return level_band, smooth_band.astype(ml_dtypes.bfloat16), inverse_count


@functools.cache
def lag_tables():
    lags = np.arange(NLAG)[:, None] - NLAG // 2
    angle = (lags * (K0 + np.arange(NF))[None, :] % L) * (TWO_PI / L)
    return np.cos(angle).astype(np.float32), np.sin(angle).astype(np.float32)


def split(value):
    high = value.astype(BF16)
    return high, (value - high.astype(F32)).astype(BF16)


def dot(a, b):
    return jnp.dot(a, b, preferred_element_type=F32)


def spectra_kernel(
    halves, own, halo,
    dead, offs, x_hbm, *refs,
):
    tables, refs = refs[:TABLES], refs[TABLES:]
    out, x, absolute, norm_high, norm_low, parts, sems, table_sems = refs[:8]
    held = refs[8:]
    level_band, high, low, turn_same, turn_swap, smooth_band, inverse_count = held
    channels = x.shape[0]
    groups = HOP // GROUP
    bulk = min(own + 1, halves)
    edges = min(own + 2, halves)
    width = halves * HOP
    half = groups // 2 * GROUP
    firsts, seconds = [], []
    for begin in (() if halo else (0, H + width)):
        absolute[:, begin:begin + H] = jnp.zeros((channels, H), BF16)
    for j in range(halves):
        begin = j * HOP - (H if j or halo else 0)
        firsts.append((begin, j * HOP + half + H))
        end = (j + 1) * HOP - H if j + 1 < halves else width + halo
        seconds.append((j * HOP + half + H, end))
    copies = [
        pltpu.make_async_copy(
            x_hbm.at[:, pl.ds(halo + begin, end - begin)], x.at[:, pl.ds(H + begin, end - begin)],
            sems.at[i],
        )
        for i, (begin, end) in enumerate(firsts + seconds)
    ]
    table_copies = [
        pltpu.make_async_copy(table, place, table_sems.at[i])
        for i, (table, place) in enumerate(zip(tables, held))
    ]
    for copy in copies[:halves] + table_copies + copies[halves:]:
        copy.start()

    def arrive(ids):
        for i in ids:
            copies[i].wait()
            begin, end = (firsts + seconds)[i]
            here = slice(H + begin, H + end)
            absolute[:, here] = jnp.abs(x[:, here]).astype(BF16)

    def rows(ref, begin, length, count):
        return [ref[:, begin + j * HOP:begin + j * HOP + length] for j in range(count)]

    def store(place, value):
        here = slice(place, place + value.shape[0])
        norm_high[here, :], norm_low[here, :] = split(value)

    def normalise(group_ids, place):
        blocks = [(g, g * GROUP + part * STEP) for g in group_ids for part in range(GROUP // STEP)]
        counts = [edges if g == 0 else bulk for g, _ in blocks]
        level = dot(
            jnp.concatenate(
                [r for (_, begin), n in zip(blocks, counts)
                 for r in rows(absolute, begin, STEP + 2 * H, n)], axis=0
            ), level_band[...],
        ) * (1.0 / (2 * H + 1)) + EPS
        values = []
        at = 0
        for (_, begin), n in zip(blocks, counts):
            samples = jnp.concatenate(rows(x, H + begin, STEP, n), axis=0)
            values.append(samples / level[at:at + n * channels])
            at += n * channels
        begins = {}
        for index, g in enumerate(group_ids):
            value = jnp.concatenate(values[2 * index:2 * index + 2], axis=1)
            if g == 0:
                lane = lax.broadcasted_iota(jnp.int32, (channels, EDGE), 1)
                merged = []
                for w in range(own):
                    mine = value[w * channels:(w + 1) * channels]
                    other = (
                        value[(w + 2) * channels:(w + 3) * channels]
                        if w + 2 < edges else jnp.zeros_like(mine)
                    )
                    merged.append(jnp.where(lane >= offs[w], mine, other))
                begins["edge"] = place
                store(place, jnp.concatenate(merged, axis=0))
                place += own * channels
                value = value[:bulk * channels]
            begins[g] = place
            store(place, value)
            place += bulk * channels
        return begins, place

    def transform(begin, end):
        first = dot(norm_high[begin:end, :], high[...])
        second = dot(norm_low[begin:end, :], high[:, :2 * NF])
        second = second + dot(norm_high[begin:end, :], low[...])
        parts[begin:end, :2 * NF] = first[:, :2 * NF] + second
        parts[begin:end, 2 * NF:] = first[:, 2 * NF:]

    begins = {}
    place = 0
    for batch in (range(groups // 2), range(groups // 2, groups)):
        arrive(range(halves) if batch.start == 0 else range(halves, 2 * halves))
        if batch.start == 0:
            for copy in table_copies:
                copy.wait()
        start = place
        found, place = normalise(list(batch), place)
        begins.update(found)
        transform(start, place)

    def piece(name, j):
        return parts[begins[name] + j * channels:begins[name] + (j + 1) * channels, :]

    def bulk_of(j):
        same = jnp.zeros((channels, parts.shape[1]), F32)
        swap = same
        for g in range(1, groups):
            value = piece(g, j)
            same = same + value * turn_same[g:g + 1, :]
            swap = swap + value * turn_swap[g:g + 1, :]
        return same + jnp.concatenate(
            [swap[:, NF:2 * NF], swap[:, :NF], pltpu.roll(swap[:, 2 * NF:], 64, 1)], axis=1
        )

    window = lax.broadcasted_iota(jnp.int32, (own, 1), 0)
    offsets = sum(jnp.where(window == w, offs[w], 0) for w in range(own))
    lane = lax.broadcasted_iota(jnp.int32, (1, NF), 1)
    outer_lane = lax.broadcasted_iota(jnp.int32, (1, 128), 1)
    outer_bin = jnp.where((outer_lane == 0) | (outer_lane == 64), K0 - 1, K0 + NF)

    def turn(bins):
        angle = jnp.bitwise_and(bins * offsets, L - 1).astype(F32) * (TWO_PI / L)
        return jnp.cos(angle), jnp.sin(angle)

    cos_turn, sin_turn = turn(lane + K0)
    cos_outer, sin_outer = turn(outer_bin)
    sign = 1.0 - 2.0 * jnp.bitwise_and(lane + K0, 1).astype(F32)
    sign_outer = 1.0 - 2.0 * jnp.bitwise_and(outer_bin, 1).astype(F32)
    channel = lax.broadcasted_iota(jnp.int32, (channels, 1), 0)
    live = 1.0 - sum(jnp.where(channel == i, dead[i], 0) for i in range(channels)).astype(F32)

    signs = jnp.concatenate([sign, sign, sign_outer], axis=1)
    reals, imags, magnitudes = [], [], []
    following = bulk_of(0)
    for w in range(own):
        spec = following + piece("edge", w)
        if w + 1 < bulk:
            following = bulk_of(w + 1)
            spec = spec + (following + piece(0, w + 1)) * signs
        spec = spec * live
        outer = spec[:, 2 * NF:]
        c, s = cos_turn[w:w + 1], sin_turn[w:w + 1]
        c_outer, s_outer = cos_outer[w:w + 1], sin_outer[w:w + 1]
        outer_imag = pltpu.roll(outer, 64, 1)

        def hann(inner, ends):
            ends = jnp.concatenate([ends, ends], axis=1)
            before = jnp.where(lane == 0, ends, pltpu.roll(inner, 1, 1))
            behind = jnp.where(lane == NF - 1, ends, pltpu.roll(inner, NF - 1, 1))
            return 0.5 * inner - 0.25 * (before + behind)

        real = hann(
            spec[:, :NF] * c - spec[:, NF:2 * NF] * s, outer * c_outer - outer_imag * s_outer
        )
        imag = hann(
            spec[:, :NF] * s + spec[:, NF:2 * NF] * c, outer * s_outer + outer_imag * c_outer
        )
        reals.append(real)
        imags.append(imag)
        magnitudes.append(jnp.sqrt(real * real + imag * imag + 1e-12))
    m_high, m_low = split(jnp.concatenate(magnitudes, axis=0))
    smooth = (dot(m_high, smooth_band[...]) + dot(m_low, smooth_band[...])) * inverse_count[...]
    scale = 1.0 / (smooth + EPS)
    flip = flip_matrix(channels)
    for w in range(own):
        here = slice(w * channels, (w + 1) * channels)
        white = jnp.concatenate([reals[w] * scale[here], imags[w] * scale[here]], axis=1)
        out[:, w * 2 * NF:(w + 1) * 2 * NF] = dot(flip, white.astype(BF16)).astype(BF16)


def flip_matrix(channels):
    row = lax.broadcasted_iota(jnp.int32, (channels, channels), 0)
    column = lax.broadcasted_iota(jnp.int32, (channels, channels), 1)
    return (row + column == channels - 1).astype(F32).astype(BF16)


def rotate_kernel(lags, own, cos_lag, sin_lag, out):
    channels = own.shape[0]
    straight = dot(flip_matrix(channels), own[...])
    real, imag = straight[:, :NF], straight[:, NF:]
    for t in range(lags):
        c, s = cos_lag[t:t + 1, :], sin_lag[t:t + 1, :]
        here = slice(t * channels, (t + 1) * channels)
        out[here, :NF] = (real * c - imag * s).astype(BF16)
        out[here, NF:] = (real * s + imag * c).astype(BF16)


def fill_slots(channels, partners, present, absent, sems):
    last = NPART // channels - 1

    def place(slot):
        return pl.ds(pl.multiple_of((last - slot) * channels, channels), channels)

    copies = [
        pltpu.make_async_copy(source, partners.at[place(slot), :], sems.at[i])
        for i, (source, slot) in enumerate(present)
    ]
    for copy in copies:
        copy.start()
    for slot in absent:
        partners[place(slot), :] = jnp.zeros((channels, partners.shape[1]), BF16)
    for copy in copies:
        copy.wait()


def early_slots(place, channels, blocks, partners, sems):
    core = lax.rem(place[0], 2)
    own, own_swapped, ahead = blocks

    @pl.when(core == 0)
    def _():
        present = [(own, 0), (own_swapped, 1), (ahead, 4)]
        fill_slots(channels, partners, present, (2, 3, 5, 6, 7), sems)

    @pl.when(core == 1)
    def _():
        fill_slots(channels, partners, [(own, 0), (ahead, 4)], (1, 2, 3, 5, 6, 7), sems)


def late_slots(place, channels, blocks, partners, sems):
    core = lax.rem(place[0], 2)
    side = lax.rem(place[0] // 2, 2)
    ahead_swapped, far, far_swapped, cross, cross_swapped, other, other_swapped = blocks
    cross_slot = 6 - 4 * side
    other_slot = 8 - cross_slot
    step = 1 - 2 * core
    both = [(far, 0), (cross, cross_slot), (other, other_slot), (ahead_swapped, 4 + step),
            (cross_swapped, cross_slot + step), (other_swapped, other_slot + step)]

    @pl.when(core == 0)
    def _():
        fill_slots(channels, partners, both, (1, 4), sems)

    @pl.when(core == 1)
    def _():
        fill_slots(channels, partners, both + [(far_swapped, 7)], (4,), sems)


def product_kernel(late, norm_scale, place, rotated, *refs):
    refs = list(refs)
    before = refs.pop(0) if late else None
    out, partners, total, sems = refs[-4:]
    blocks = refs[:-4]
    channels = blocks[0].shape[0]
    (late_slots if late else early_slots)(place, channels, blocks, partners, sems)
    rows, features = rotated.shape
    chunk = 2 * 2 * NF
    for begin in range(0, features, chunk):
        turned = partners[:, begin:begin + chunk].T
        product = dot(rotated[:, begin:begin + chunk], turned)
        if begin == 0:
            total[...] = product
        else:
            total[...] += product

    row = lax.broadcasted_iota(jnp.int32, (channels, NPART), 0)
    column = lax.broadcasted_iota(jnp.int32, (channels, NPART), 1)
    low = row + column >= NPART - 1
    keep = (low | (column < NPART - channels)) if late else jnp.logical_not(low)
    sheared = []
    for begin in range(0, rows, channels):
        here = slice(begin, begin + channels)
        value = jnp.where(keep, total[here, :], 0.0)
        if late:
            value = (value + before[here, :]) * norm_scale
            sheared.append(pltpu.roll(value, 1, 1, stride=1, stride_axis=0).astype(BF16))
        else:
            out[here, :] = value
    if late:
        sheared = jnp.concatenate(sheared, axis=0)
        out[...] = dot(sheared, flip_matrix(NPART)).astype(BF16)


def exchange(value, pairs):
    return lax.ppermute(value, "chan", pairs)


def local(records, dead_mask, offsets):
    channels, samples = records.shape
    tm_count = lax.axis_size("tm")
    tm_index = lax.axis_index("tm")
    chan_count = lax.axis_size("chan")
    own = samples // HOP
    windows = own * tm_count
    halves = own
    halo = 0
    if tm_count > 1:
        reach = 2 * HOP + H
        left = lax.ppermute(
            records[:, samples - H:], "tm", [(i, i + 1) for i in range(tm_count - 1)]
        )
        right = lax.ppermute(
            records[:, :reach], "tm", [(i + 1, i) for i in range(tm_count - 1)]
        )
        records = jnp.concatenate([left, records, right], axis=1)
        halves = own + 2
        halo = H
    level_band, smooth_band, inverse_count = small_tables()
    tables = (level_band, *fourier_tables(), *group_turns(), smooth_band, inverse_count)
    tables = [jnp.asarray(t) for t in tables]
    own_offsets = lax.dynamic_slice_in_dim(offsets, tm_index * own, own, 0)
    vmem = pl.BlockSpec(memory_space=pltpu.VMEM)
    smem = pl.BlockSpec(memory_space=pltpu.SMEM)
    hbm = pl.BlockSpec(memory_space=pl.ANY)
    far_memory = pl.BlockSpec(memory_space=pltpu.HBM)
    params = pltpu.CompilerParams(vmem_limit_bytes=24 * 1024 * 1024)

    bulk = min(own + 1, halves)
    part_rows = (own + bulk * (HOP // GROUP)) * channels
    spectra = pl.pallas_call(
        functools.partial(spectra_kernel, halves, own, halo),
        name="spectra",
        out_shape=jax.ShapeDtypeStruct((channels, own * 2 * NF), BF16),
        in_specs=[smem, smem] + [far_memory] * (1 + TABLES),
        out_specs=vmem,
        scratch_shapes=[
            pltpu.VMEM((channels, halves * HOP + 2 * H), F32),
            pltpu.VMEM((channels, halves * HOP + 2 * H), BF16),
            pltpu.VMEM((part_rows, GROUP), BF16),
            pltpu.VMEM((part_rows, GROUP), BF16),
            pltpu.VMEM((part_rows, 2 * NF + 128), F32),
            pltpu.SemaphoreType.DMA((2 * halves,)),
            pltpu.SemaphoreType.DMA((TABLES,)),
        ] + [pltpu.VMEM(t.shape, t.dtype) for t in tables],
        compiler_params=pltpu.CompilerParams(vmem_limit_bytes=60 * 1024 * 1024),
        cost_estimate=pl.CostEstimate(
            flops=7_000_000_000, bytes_accessed=8 * 1024 * 1024, transcendentals=0
        ),
    )(dead_mask, own_offsets, records, *tables)
    if tm_count > 1:
        spectra = lax.all_gather(spectra, "tm", axis=1, tiled=True)

    lags = NLAG // tm_count
    cos_lag, sin_lag = (
        lax.dynamic_slice_in_dim(jnp.asarray(t), tm_index * lags, lags, 0) for t in lag_tables()
    )
    place = lax.axis_index("chan").astype(jnp.int32).reshape(1)
    norm_scale = 1.0 / math.sqrt(2.0 * NF * windows)

    features = spectra.shape[1]
    rotated = pl.pallas_call(
        functools.partial(rotate_kernel, lags),
        name="rotate",
        grid=(windows,),
        out_shape=jax.ShapeDtypeStruct((lags * channels, features), BF16),
        in_specs=[
            pl.BlockSpec((channels, 2 * NF), lambda w: (0, w)),
            pl.BlockSpec((lags, NF), lambda w: (0, 0)),
            pl.BlockSpec((lags, NF), lambda w: (0, 0)),
        ],
        out_specs=pl.BlockSpec((lags * channels, 2 * NF), lambda w: (0, w)),
        compiler_params=params,
        cost_estimate=pl.CostEstimate(
            flops=4_000_000_000, bytes_accessed=8 * 1024 * 1024, transcendentals=0
        ),
    )(spectra, cos_lag, sin_lag)

    def product(blocks, before):
        late = before is not None
        operands = [place, rotated] + ([before] if late else []) + list(blocks)
        return pl.pallas_call(
            functools.partial(product_kernel, late, norm_scale),
            name="late_product" if late else "early_product",
            out_shape=jax.ShapeDtypeStruct((lags * channels, NPART), BF16 if late else F32),
            in_specs=[smem, vmem] + ([vmem] if late else []) + [hbm] * len(blocks),
            out_specs=vmem,
            scratch_shapes=[
                pltpu.VMEM((NPART, features), BF16),
                pltpu.VMEM((lags * channels, NPART), F32),
                pltpu.SemaphoreType.DMA((len(blocks),)),
            ],
            compiler_params=params,
            cost_estimate=pl.CostEstimate(
                flops=2 * lags * channels * features * NPART, bytes_accessed=6 * 1024 * 1024,
                transcendentals=0,
            ),
        )(*operands)

    every = range(chan_count)
    down = [(i, i - 4) for i in every if i >= 4]
    down_2 = [(i, i - 2) for i in every if i >= 2]
    across = [(i, i ^ 2) for i in every]
    cores = [(i, i ^ 1) for i in every]
    side = lax.rem(lax.axis_index("chan") // 2, 2)

    ahead = exchange(spectra, down)
    kept, rotated = lax.optimization_barrier((spectra, rotated))
    own_swapped = exchange(kept, [(i, j) for i, j in cores if j < i])
    ahead, rotated = lax.optimization_barrier((ahead, rotated))
    other = exchange(jnp.where(side == 0, ahead, spectra), down_2)
    cross = exchange(ahead, across)
    far = exchange(ahead, down)
    early = product((spectra, own_swapped, ahead), None)
    ahead, early = lax.optimization_barrier((ahead, early))
    ahead_swapped = exchange(ahead, cores)
    other, ahead_swapped = lax.optimization_barrier((other, ahead_swapped))
    far_swapped = exchange(far, [(i, j) for i, j in cores if j > i])
    blocks = (ahead_swapped, far, far_swapped, cross, exchange(cross, cores),
              other, exchange(other, cores))
    return product(blocks, early).reshape(lags, channels, NPART)


def solution(mesh):
    return jax.shard_map(
        local,
        mesh=mesh,
        in_specs=(P(("win", "chan"), "tm"), P(("win", "chan")), P("win")),
        out_specs=P("tm", ("win", "chan"), None),
        check_vma=False,
    )
```

```python
import functools
import math

import jax
import jax.numpy as jnp
import ml_dtypes
import numpy as np
from jax import lax
from jax.experimental import pallas as pl
from jax.experimental.pallas import tpu as pltpu
from jax.sharding import PartitionSpec as P

L = 8192
HOP = 4096
H = 128
K0 = 32
NF = 256
WB = 64
NLAG = 32
NPART = 256
EDGE = 512
STEP = 256
GROUP = 512
EPS = 1e-05
TWO_PI = 2.0 * math.pi
BF16 = jnp.bfloat16
F32 = jnp.float32


def split_table(table):
    high = table.astype(ml_dtypes.bfloat16)
    low = (table - high.astype(np.float64)).astype(ml_dtypes.bfloat16)
    return high, low


@functools.cache
def fourier_tables():
    samples = np.arange(GROUP)[:, None]
    bins = K0 + np.arange(NF)[None, :]
    angle = (samples * bins % L) * (TWO_PI / L)
    inner = np.concatenate([np.cos(angle), -np.sin(angle)], axis=1)
    outer = np.zeros((GROUP, 128))
    for lane, k, wave in ((0, K0 - 1, np.cos), (64, K0 - 1, np.sin), (127, K0 + NF, np.cos), (63, K0 + NF, np.sin)):
        sign = 1.0 if wave is np.cos else -1.0
        outer[:, lane] = sign * wave((samples[:, 0] * k % L) * (TWO_PI / L))
    high, low = split_table(inner)
    return np.concatenate([high, outer.astype(ml_dtypes.bfloat16)], axis=1), low


@functools.cache
def packed_tables():
    lane = np.arange(2 * H + STEP)[:, None]
    place = np.arange(STEP)[None, :]
    level_band = ((lane >= place) & (lane <= place + 2 * H)).astype(ml_dtypes.bfloat16)
    bins = np.arange(NF)
    smooth_band = np.zeros((GROUP, NF), ml_dtypes.bfloat16)
    smooth_band[:NF] = np.abs(bins[:, None] - bins[None, :]) <= WB
    return np.concatenate([*fourier_tables(), level_band, smooth_band], axis=1)


@functools.cache
def lag_tables():
    lags = np.arange(NLAG)[:, None] - NLAG // 2
    angle = (lags * (K0 + np.arange(NF))[None, :] % L) * (TWO_PI / L)
    return np.cos(angle).astype(np.float32), np.sin(angle).astype(np.float32)


def split(value):
    high = value.astype(BF16)
    return high, (value - high.astype(F32)).astype(BF16)


def dot(a, b):
    return jnp.dot(a, b, preferred_element_type=F32)


def spectra_kernel(
    halves, own, halo,
    dead, offs, x, table_hbm, out, absolute, norm_high, norm_low, parts, table, sem,
):
    table_copy = pltpu.make_async_copy(table_hbm, table, sem)
    table_copy.start()
    channels = x.shape[0]
    groups = HOP // GROUP
    bulk = min(own + 1, halves)
    edges = min(own + 2, halves)
    width = halves * HOP
    if not halo:
        for begin in (0, H + width):
            absolute[:, begin:begin + H] = jnp.zeros((channels, H), BF16)
    for begin in range(0, x.shape[1], GROUP):
        end = min(begin + GROUP, x.shape[1])
        absolute[:, H - halo + begin:H - halo + end] = jnp.abs(x[:, begin:end]).astype(BF16)

    begin = 2 * NF + 128
    high = table.at[:, :begin]
    low = table.at[:, begin:begin + 2 * NF]
    level_band = table.at[:, begin + 2 * NF:begin + 2 * NF + STEP]
    smooth_band = table.at[:NF, begin + 2 * NF + STEP:]
    lane = lax.broadcasted_iota(jnp.int32, (1, parts.shape[1]), 1)
    outer_place = lane - 2 * NF
    outer_first = (outer_place == 0) | (outer_place == 64)
    every_bin = jnp.where(
        lane < 2 * NF, jnp.bitwise_and(lane, NF - 1) + K0, jnp.where(outer_first, K0 - 1, K0 + NF)
    )
    real_place = (lane < NF) | (outer_place == 0) | (outer_place == 127)
    group = lax.broadcasted_iota(jnp.int32, (groups, 1), 0) * GROUP
    angle = jnp.bitwise_and(group * every_bin, L - 1).astype(F32) * (TWO_PI / L)
    turn_same = jnp.cos(angle)
    turn_swap = jnp.sin(angle) * jnp.where(real_place, -1.0, 1.0)
    bin_index = lax.broadcasted_iota(jnp.int32, (1, NF), 1)
    below, above = jnp.minimum(bin_index, WB), jnp.minimum(NF - 1 - bin_index, WB)
    inverse_count = 1.0 / (below + above + 1).astype(F32)
    table_copy.wait()

    def rows(ref, begin, length, count):
        return [ref[:, begin + j * HOP:begin + j * HOP + length] for j in range(count)]

    def store(place, value):
        here = slice(place, place + value.shape[0])
        norm_high[here, :], norm_low[here, :] = split(value)

    def normalise(group_ids, place):
        blocks = [(g, g * GROUP + part * STEP) for g in group_ids for part in range(GROUP // STEP)]
        counts = [edges if g == 0 else bulk for g, _ in blocks]
        level = dot(
            jnp.concatenate(
                [r for (_, begin), n in zip(blocks, counts)
                 for r in rows(absolute, begin, STEP + 2 * H, n)], axis=0
            ), level_band[...],
        ) * (1.0 / (2 * H + 1)) + EPS
        values = []
        at = 0
        for (_, begin), n in zip(blocks, counts):
            samples = jnp.concatenate(rows(x, halo + begin, STEP, n), axis=0)
            values.append(samples / level[at:at + n * channels])
            at += n * channels
        begins = {}
        for index, g in enumerate(group_ids):
            value = jnp.concatenate(values[2 * index:2 * index + 2], axis=1)
            if g == 0:
                lane = lax.broadcasted_iota(jnp.int32, (channels, EDGE), 1)
                merged = []
                for w in range(own):
                    mine = value[w * channels:(w + 1) * channels]
                    other = (
                        value[(w + 2) * channels:(w + 3) * channels]
                        if w + 2 < edges else jnp.zeros_like(mine)
                    )
                    merged.append(jnp.where(lane >= offs[w], mine, other))
                begins["edge"] = place
                store(place, jnp.concatenate(merged, axis=0))
                place += own * channels
                value = value[:bulk * channels]
            begins[g] = place
            store(place, value)
            place += bulk * channels
        return begins, place

    def transform(begin, end):
        first = dot(norm_high[begin:end, :], high[...])
        second = dot(norm_low[begin:end, :], high[:, :2 * NF])
        second = second + dot(norm_high[begin:end, :], low[...])
        parts[begin:end, :2 * NF] = first[:, :2 * NF] + second
        parts[begin:end, 2 * NF:] = first[:, 2 * NF:]

    begins = {}
    place = 0
    half = groups // 2
    for batch in (range(half), range(half, groups)):
        start = place
        found, place = normalise(list(batch), place)
        begins.update(found)
        transform(start, place)

    def piece(name, j):
        return parts[begins[name] + j * channels:begins[name] + (j + 1) * channels, :]

    def bulk_of(j):
        same = jnp.zeros((channels, parts.shape[1]), F32)
        swap = same
        for g in range(1, groups):
            value = piece(g, j)
            same = same + value * turn_same[g:g + 1, :]
            swap = swap + value * turn_swap[g:g + 1, :]
        return same + jnp.concatenate(
            [swap[:, NF:2 * NF], swap[:, :NF], pltpu.roll(swap[:, 2 * NF:], 64, 1)], axis=1
        )

    window = lax.broadcasted_iota(jnp.int32, (own, 1), 0)
    offsets = sum(jnp.where(window == w, offs[w], 0) for w in range(own))
    lane = lax.broadcasted_iota(jnp.int32, (1, NF), 1)
    outer_lane = lax.broadcasted_iota(jnp.int32, (1, 128), 1)
    outer_bin = jnp.where((outer_lane == 0) | (outer_lane == 64), K0 - 1, K0 + NF)

    def turn(bins):
        angle = jnp.bitwise_and(bins * offsets, L - 1).astype(F32) * (TWO_PI / L)
        return jnp.cos(angle), jnp.sin(angle)

    cos_turn, sin_turn = turn(lane + K0)
    cos_outer, sin_outer = turn(outer_bin)
    sign = 1.0 - 2.0 * jnp.bitwise_and(lane + K0, 1).astype(F32)
    sign_outer = 1.0 - 2.0 * jnp.bitwise_and(outer_bin, 1).astype(F32)
    channel = lax.broadcasted_iota(jnp.int32, (channels, 1), 0)
    live = 1.0 - sum(jnp.where(channel == i, dead[i], 0) for i in range(channels)).astype(F32)

    signs = jnp.concatenate([sign, sign, sign_outer], axis=1)
    reals, imags, magnitudes = [], [], []
    following = bulk_of(0)
    for w in range(own):
        spec = following + piece("edge", w)
        if w + 1 < bulk:
            following = bulk_of(w + 1)
            spec = spec + (following + piece(0, w + 1)) * signs
        spec = spec * live
        outer = spec[:, 2 * NF:]
        c, s = cos_turn[w:w + 1], sin_turn[w:w + 1]
        c_outer, s_outer = cos_outer[w:w + 1], sin_outer[w:w + 1]
        outer_imag = pltpu.roll(outer, 64, 1)

        def hann(inner, ends):
            ends = jnp.concatenate([ends, ends], axis=1)
            before = jnp.where(lane == 0, ends, pltpu.roll(inner, 1, 1))
            behind = jnp.where(lane == NF - 1, ends, pltpu.roll(inner, NF - 1, 1))
            return 0.5 * inner - 0.25 * (before + behind)

        real = hann(
            spec[:, :NF] * c - spec[:, NF:2 * NF] * s, outer * c_outer - outer_imag * s_outer
        )
        imag = hann(
            spec[:, :NF] * s + spec[:, NF:2 * NF] * c, outer * s_outer + outer_imag * c_outer
        )
        reals.append(real)
        imags.append(imag)
        magnitudes.append(jnp.sqrt(real * real + imag * imag + 1e-12))
    m_high, m_low = split(jnp.concatenate(magnitudes, axis=0))
    smooth = (dot(m_high, smooth_band[...]) + dot(m_low, smooth_band[...])) * inverse_count
    scale = 1.0 / (smooth + EPS)
    flip = flip_matrix(channels)
    for w in range(own):
        here = slice(w * channels, (w + 1) * channels)
        white = jnp.concatenate([reals[w] * scale[here], imags[w] * scale[here]], axis=1)
        out[:, w * 2 * NF:(w + 1) * 2 * NF] = dot(flip, white.astype(BF16)).astype(BF16)


def flip_matrix(channels):
    row = lax.broadcasted_iota(jnp.int32, (channels, channels), 0)
    column = lax.broadcasted_iota(jnp.int32, (channels, channels), 1)
    return (row + column == channels - 1).astype(F32).astype(BF16)


def rotate_kernel(lags, own, cos_lag, sin_lag, out):
    channels = own.shape[0]
    straight = dot(flip_matrix(channels), own[...])
    real, imag = straight[:, :NF], straight[:, NF:]
    for t in range(lags):
        c, s = cos_lag[t:t + 1, :], sin_lag[t:t + 1, :]
        here = slice(t * channels, (t + 1) * channels)
        out[here, :NF] = (real * c - imag * s).astype(BF16)
        out[here, NF:] = (real * s + imag * c).astype(BF16)


def fill_slots(channels, partners, present, absent, sems):
    last = NPART // channels - 1

    def place(slot):
        return pl.ds(pl.multiple_of((last - slot) * channels, channels), channels)

    copies = [
        pltpu.make_async_copy(source, partners.at[place(slot), :], sems.at[i])
        for i, (source, slot) in enumerate(present)
    ]
    for copy in copies:
        copy.start()
    for slot in absent:
        partners[place(slot), :] = jnp.zeros((channels, partners.shape[1]), BF16)
    for copy in copies:
        copy.wait()


def early_slots(place, channels, blocks, partners, sems):
    own, ahead = blocks
    fill_slots(channels, partners, [(own, 0), (ahead, 4)], (1, 2, 3, 5, 6, 7), sems)


def late_slots(place, channels, blocks, partners, sems):
    core = lax.rem(place[0], 2)
    side = lax.rem(place[0] // 2, 2)
    (own_swapped, ahead_swapped, far, far_swapped, cross, cross_swapped, other,
     other_swapped) = blocks
    cross_slot = 6 - 4 * side
    other_slot = 8 - cross_slot
    step = 1 - 2 * core
    both = [(far, 0), (cross, cross_slot), (other, other_slot), (ahead_swapped, 4 + step),
            (cross_swapped, cross_slot + step), (other_swapped, other_slot + step)]

    @pl.when(core == 0)
    def _():
        fill_slots(channels, partners, both + [(own_swapped, 1)], (4,), sems)

    @pl.when(core == 1)
    def _():
        fill_slots(channels, partners, both + [(far_swapped, 7)], (4,), sems)


def product_kernel(late, norm_scale, place, rotated, *refs):
    refs = list(refs)
    before = refs.pop(0) if late else None
    out, partners, total, sems = refs[-4:]
    blocks = refs[:-4]
    channels = blocks[0].shape[0]
    (late_slots if late else early_slots)(place, channels, blocks, partners, sems)
    rows, features = rotated.shape
    chunk = 2 * 2 * NF
    for begin in range(0, features, chunk):
        turned = partners[:, begin:begin + chunk].T
        product = dot(rotated[:, begin:begin + chunk], turned)
        if begin == 0:
            total[...] = product
        else:
            total[...] += product

    row = lax.broadcasted_iota(jnp.int32, (channels, NPART), 0)
    column = lax.broadcasted_iota(jnp.int32, (channels, NPART), 1)
    low = row + column >= NPART - 1
    keep = (low | (column < NPART - channels)) if late else jnp.logical_not(low)
    sheared = []
    for begin in range(0, rows, channels):
        here = slice(begin, begin + channels)
        value = jnp.where(keep, total[here, :], 0.0)
        if late:
            value = (value + before[here, :]) * norm_scale
            sheared.append(pltpu.roll(value, 1, 1, stride=1, stride_axis=0).astype(BF16))
        else:
            out[here, :] = value
    if late:
        sheared = jnp.concatenate(sheared, axis=0)
        out[...] = dot(sheared, flip_matrix(NPART)).astype(BF16)


def exchange(value, pairs):
    return lax.ppermute(value, "chan", pairs)


def local(records, dead_mask, offsets):
    channels, samples = records.shape
    tm_count = lax.axis_size("tm")
    tm_index = lax.axis_index("tm")
    chan_count = lax.axis_size("chan")
    own = samples // HOP
    windows = own * tm_count
    halves = own
    halo = 0
    if tm_count > 1:
        reach = 2 * HOP + H
        left = lax.ppermute(
            records[:, samples - H:], "tm", [(i, i + 1) for i in range(tm_count - 1)]
        )
        right = lax.ppermute(
            records[:, :reach], "tm", [(i + 1, i) for i in range(tm_count - 1)]
        )
        records = jnp.concatenate([left, records, right], axis=1)
        halves = own + 2
        halo = H
    table = jnp.asarray(packed_tables())
    own_offsets = lax.dynamic_slice_in_dim(offsets, tm_index * own, own, 0)
    vmem = pl.BlockSpec(memory_space=pltpu.VMEM)
    smem = pl.BlockSpec(memory_space=pltpu.SMEM)
    hbm = pl.BlockSpec(memory_space=pl.ANY)
    params = pltpu.CompilerParams(vmem_limit_bytes=24 * 1024 * 1024)

    bulk = min(own + 1, halves)
    part_rows = (own + bulk * (HOP // GROUP)) * channels
    spectra = pl.pallas_call(
        functools.partial(spectra_kernel, halves, own, halo),
        name="spectra",
        out_shape=jax.ShapeDtypeStruct((channels, own * 2 * NF), BF16),
        in_specs=[smem, smem, vmem, hbm],
        out_specs=vmem,
        scratch_shapes=[
            pltpu.VMEM((channels, halves * HOP + 2 * H), BF16),
            pltpu.VMEM((part_rows, GROUP), BF16),
            pltpu.VMEM((part_rows, GROUP), BF16),
            pltpu.VMEM((part_rows, 2 * NF + 128), F32),
            pltpu.VMEM(table.shape, BF16),
            pltpu.SemaphoreType.DMA,
        ],
        compiler_params=pltpu.CompilerParams(vmem_limit_bytes=60 * 1024 * 1024),
        cost_estimate=pl.CostEstimate(
            flops=7_000_000_000, bytes_accessed=8 * 1024 * 1024, transcendentals=0
        ),
    )(dead_mask, own_offsets, records, table)
    if tm_count > 1:
        spectra = lax.all_gather(spectra, "tm", axis=1, tiled=True)

    lags = NLAG // tm_count
    cos_lag, sin_lag = (
        lax.dynamic_slice_in_dim(jnp.asarray(t), tm_index * lags, lags, 0) for t in lag_tables()
    )
    place = lax.axis_index("chan").astype(jnp.int32).reshape(1)
    norm_scale = 1.0 / math.sqrt(2.0 * NF * windows)

    features = spectra.shape[1]
    rotated = pl.pallas_call(
        functools.partial(rotate_kernel, lags),
        name="rotate",
        grid=(windows,),
        out_shape=jax.ShapeDtypeStruct((lags * channels, features), BF16),
        in_specs=[
            pl.BlockSpec((channels, 2 * NF), lambda w: (0, w)),
            pl.BlockSpec((lags, NF), lambda w: (0, 0)),
            pl.BlockSpec((lags, NF), lambda w: (0, 0)),
        ],
        out_specs=pl.BlockSpec((lags * channels, 2 * NF), lambda w: (0, w)),
        compiler_params=params,
        cost_estimate=pl.CostEstimate(
            flops=4_000_000_000, bytes_accessed=8 * 1024 * 1024, transcendentals=0
        ),
    )(spectra, cos_lag, sin_lag)

    def product(blocks, before):
        late = before is not None
        operands = [place, rotated] + ([before] if late else []) + list(blocks)
        return pl.pallas_call(
            functools.partial(product_kernel, late, norm_scale),
            name="late_product" if late else "early_product",
            out_shape=jax.ShapeDtypeStruct((lags * channels, NPART), BF16 if late else F32),
            in_specs=[smem, vmem] + ([vmem] if late else []) + [hbm] * len(blocks),
            out_specs=vmem,
            scratch_shapes=[
                pltpu.VMEM((NPART, features), BF16),
                pltpu.VMEM((lags * channels, NPART), F32),
                pltpu.SemaphoreType.DMA((len(blocks),)),
            ],
            compiler_params=params,
            cost_estimate=pl.CostEstimate(
                flops=2 * lags * channels * features * NPART, bytes_accessed=6 * 1024 * 1024,
                transcendentals=0,
            ),
        )(*operands)

    every = range(chan_count)
    down = [(i, i - 4) for i in every if i >= 4]
    down_2 = [(i, i - 2) for i in every if i >= 2]
    across = [(i, i ^ 2) for i in every]
    cores = [(i, i ^ 1) for i in every]
    side = lax.rem(lax.axis_index("chan") // 2, 2)

    ahead = exchange(spectra, down)
    ahead, rotated = lax.optimization_barrier((ahead, rotated))
    other = exchange(jnp.where(side == 0, ahead, spectra), down_2)
    cross = exchange(ahead, across)
    far = exchange(ahead, down)
    early = product((spectra, ahead), None)
    kept, ahead, other, early = lax.optimization_barrier((spectra, ahead, other, early))
    own_swapped = exchange(kept, [(i, j) for i, j in cores if j < i])
    ahead_swapped = exchange(ahead, cores)
    cross, own_swapped, ahead_swapped = lax.optimization_barrier(
        (cross, own_swapped, ahead_swapped)
    )
    far_swapped = exchange(far, [(i, j) for i, j in cores if j > i])
    blocks = (own_swapped, ahead_swapped, far, far_swapped, cross, exchange(cross, cores),
              other, exchange(other, cores))
    return product(blocks, early).reshape(lags, channels, NPART)


def solution(mesh):
    return jax.shard_map(
        local,
        mesh=mesh,
        in_specs=(P(("win", "chan"), "tm"), P(("win", "chan")), P("win")),
        out_specs=P("tm", ("win", "chan"), None),
        check_vma=False,
    )
```

```python
import functools
import math

import jax
import jax.numpy as jnp
import ml_dtypes
import numpy as np
from jax import lax
from jax.experimental import pallas as pl
from jax.experimental.pallas import tpu as pltpu
from jax.sharding import PartitionSpec as P

L = 8192
HOP = 4096
H = 128
K0 = 32
NF = 256
WB = 64
NLAG = 32
NPART = 256
EDGE = 512
STEP = 256
GROUP = 512
EPS = 1e-05
TWO_PI = 2.0 * math.pi
BF16 = jnp.bfloat16
F32 = jnp.float32


def split_table(table):
    high = table.astype(ml_dtypes.bfloat16)
    low = (table - high.astype(np.float64)).astype(ml_dtypes.bfloat16)
    return high, low


@functools.cache
def fourier_tables():
    samples = np.arange(GROUP)[:, None]
    bins = K0 + np.arange(NF)[None, :]
    angle = (samples * bins % L) * (TWO_PI / L)
    inner = np.concatenate([np.cos(angle), -np.sin(angle)], axis=1)
    outer = np.zeros((GROUP, 128))
    for lane, k, wave in ((0, K0 - 1, np.cos), (64, K0 - 1, np.sin), (127, K0 + NF, np.cos), (63, K0 + NF, np.sin)):
        sign = 1.0 if wave is np.cos else -1.0
        outer[:, lane] = sign * wave((samples[:, 0] * k % L) * (TWO_PI / L))
    high, low = split_table(inner)
    return np.concatenate([high, outer.astype(ml_dtypes.bfloat16)], axis=1), low


@functools.cache
def packed_tables():
    high, low = fourier_tables()
    lane = np.arange(2 * H + STEP)[:, None]
    place = np.arange(STEP)[None, :]
    level_band = (lane >= place) & (lane <= place + 2 * H)
    bins = np.arange(NF)
    smooth_band = np.abs(bins[:, None] - bins[None, :]) <= WB
    inner = np.concatenate([high[:, :2 * NF], high[:, :2 * NF], low], axis=0)
    side = np.zeros((3 * GROUP, STEP), ml_dtypes.bfloat16)
    side[:GROUP, :128] = high[:, 2 * NF:]
    side[GROUP:2 * GROUP] = level_band
    side[2 * GROUP:2 * GROUP + NF] = smooth_band
    return np.concatenate([inner, side], axis=1)


@functools.cache
def lag_tables():
    lags = np.arange(NLAG)[:, None] - NLAG // 2
    angle = (lags * (K0 + np.arange(NF))[None, :] % L) * (TWO_PI / L)
    return np.cos(angle).astype(np.float32), np.sin(angle).astype(np.float32)


def split(value):
    high = value.astype(BF16)
    return high, (value - high.astype(F32)).astype(BF16)


def inverse(value):
    guess = pl.reciprocal(value, approx=True)
    return guess * (2.0 - value * guess)


def dot(a, b):
    return jnp.dot(a, b, preferred_element_type=F32)


def spectra_kernel(
    halves, own, halo,
    dead, offs, x, table_hbm, out, absolute, norm, parts, table, sem,
):
    table_copy = pltpu.make_async_copy(table_hbm, table, sem)
    table_copy.start()
    channels = x.shape[0]
    groups = HOP // GROUP
    bulk = min(own + 1, halves)
    edges = min(own + 2, halves)
    width = halves * HOP
    if not halo:
        for begin in (0, H + width):
            absolute[:, begin:begin + H] = jnp.zeros((channels, H), BF16)
    for begin in range(0, x.shape[1], GROUP):
        end = min(begin + GROUP, x.shape[1])
        absolute[:, H - halo + begin:H - halo + end] = jnp.abs(x[:, begin:end]).astype(BF16)

    fourier = table.at[:, :2 * NF]
    outer_table = table.at[:GROUP, 2 * NF:2 * NF + 128]
    level_band = table.at[GROUP:2 * GROUP, 2 * NF:]
    smooth_band = table.at[2 * GROUP:2 * GROUP + NF, 2 * NF:]
    lane = lax.broadcasted_iota(jnp.int32, (1, parts.shape[1]), 1)
    outer_place = lane - 2 * NF
    outer_first = (outer_place == 0) | (outer_place == 64)
    every_bin = jnp.where(
        lane < 2 * NF, jnp.bitwise_and(lane, NF - 1) + K0, jnp.where(outer_first, K0 - 1, K0 + NF)
    )
    real_place = (lane < NF) | (outer_place == 0) | (outer_place == 127)
    group = lax.broadcasted_iota(jnp.int32, (groups, 1), 0) * GROUP
    angle = jnp.bitwise_and(group * every_bin, L - 1).astype(F32) * (TWO_PI / L)
    turn_same = jnp.cos(angle)
    turn_swap = jnp.sin(angle) * jnp.where(real_place, -1.0, 1.0)
    bin_index = lax.broadcasted_iota(jnp.int32, (1, NF), 1)
    below, above = jnp.minimum(bin_index, WB), jnp.minimum(NF - 1 - bin_index, WB)
    inverse_count = 1.0 / (below + above + 1).astype(F32)
    table_copy.wait()

    def rows(ref, begin, length, count):
        return [ref[:, begin + j * HOP:begin + j * HOP + length] for j in range(count)]

    def store(place, value):
        here = slice(place, place + value.shape[0])
        high, low = split(value)
        norm[here, :] = jnp.concatenate([high, low, high], axis=1)

    def normalise(group_ids, place):
        blocks = [(g, g * GROUP + part * STEP) for g in group_ids for part in range(GROUP // STEP)]
        counts = [edges if g == 0 else bulk for g, _ in blocks]
        level = dot(
            jnp.concatenate(
                [r for (_, begin), n in zip(blocks, counts)
                 for r in rows(absolute, begin, STEP + 2 * H, n)], axis=0
            ), level_band[...],
        ) * (1.0 / (2 * H + 1)) + EPS
        values = []
        at = 0
        for (_, begin), n in zip(blocks, counts):
            samples = jnp.concatenate(rows(x, halo + begin, STEP, n), axis=0)
            values.append(samples * inverse(level[at:at + n * channels]))
            at += n * channels
        begins = {}
        for index, g in enumerate(group_ids):
            value = jnp.concatenate(values[2 * index:2 * index + 2], axis=1)
            if g == 0:
                lane = lax.broadcasted_iota(jnp.int32, (channels, EDGE), 1)
                merged = []
                for w in range(own):
                    mine = value[w * channels:(w + 1) * channels]
                    other = (
                        value[(w + 2) * channels:(w + 3) * channels]
                        if w + 2 < edges else jnp.zeros_like(mine)
                    )
                    merged.append(jnp.where(lane >= offs[w], mine, other))
                begins["edge"] = place
                store(place, jnp.concatenate(merged, axis=0))
                place += own * channels
                value = value[:bulk * channels]
            begins[g] = place
            store(place, value)
            place += bulk * channels
        return begins, place

    def transform(begin, end):
        parts[begin:end, :2 * NF] = dot(norm[begin:end, :], fourier[...])
        parts[begin:end, 2 * NF:] = dot(norm[begin:end, :GROUP], outer_table[...])

    begins = {}
    place = 0
    half = groups // 2
    for batch in (range(half), range(half, groups)):
        start = place
        found, place = normalise(list(batch), place)
        begins.update(found)
        transform(start, place)

    def piece(name, j):
        return parts[begins[name] + j * channels:begins[name] + (j + 1) * channels, :]

    def bulk_of(j):
        same = jnp.zeros((channels, parts.shape[1]), F32)
        swap = same
        for g in range(1, groups):
            value = piece(g, j)
            same = same + value * turn_same[g:g + 1, :]
            swap = swap + value * turn_swap[g:g + 1, :]
        return same + jnp.concatenate(
            [swap[:, NF:2 * NF], swap[:, :NF], pltpu.roll(swap[:, 2 * NF:], 64, 1)], axis=1
        )

    window = lax.broadcasted_iota(jnp.int32, (own, 1), 0)
    offsets = sum(jnp.where(window == w, offs[w], 0) for w in range(own))
    lane = lax.broadcasted_iota(jnp.int32, (1, NF), 1)
    outer_lane = lax.broadcasted_iota(jnp.int32, (1, 128), 1)
    outer_bin = jnp.where((outer_lane == 0) | (outer_lane == 64), K0 - 1, K0 + NF)

    def turn(bins):
        angle = jnp.bitwise_and(bins * offsets, L - 1).astype(F32) * (TWO_PI / L)
        return jnp.cos(angle), jnp.sin(angle)

    cos_turn, sin_turn = turn(lane + K0)
    cos_outer, sin_outer = turn(outer_bin)
    sign = 1.0 - 2.0 * jnp.bitwise_and(lane + K0, 1).astype(F32)
    sign_outer = 1.0 - 2.0 * jnp.bitwise_and(outer_bin, 1).astype(F32)
    channel = lax.broadcasted_iota(jnp.int32, (channels, 1), 0)
    live = 1.0 - sum(jnp.where(channel == i, dead[i], 0) for i in range(channels)).astype(F32)

    signs = jnp.concatenate([sign, sign, sign_outer], axis=1)
    reals, imags, magnitudes = [], [], []
    following = bulk_of(0)
    for w in range(own):
        spec = following + piece("edge", w)
        if w + 1 < bulk:
            following = bulk_of(w + 1)
            spec = spec + (following + piece(0, w + 1)) * signs
        spec = spec * live
        outer = spec[:, 2 * NF:]
        c, s = cos_turn[w:w + 1], sin_turn[w:w + 1]
        c_outer, s_outer = cos_outer[w:w + 1], sin_outer[w:w + 1]
        outer_imag = pltpu.roll(outer, 64, 1)

        def hann(inner, ends):
            ends = jnp.concatenate([ends, ends], axis=1)
            before = jnp.where(lane == 0, ends, pltpu.roll(inner, 1, 1))
            behind = jnp.where(lane == NF - 1, ends, pltpu.roll(inner, NF - 1, 1))
            return 0.5 * inner - 0.25 * (before + behind)

        real = hann(
            spec[:, :NF] * c - spec[:, NF:2 * NF] * s, outer * c_outer - outer_imag * s_outer
        )
        imag = hann(
            spec[:, :NF] * s + spec[:, NF:2 * NF] * c, outer * s_outer + outer_imag * c_outer
        )
        reals.append(real)
        imags.append(imag)
        magnitudes.append(jnp.sqrt(real * real + imag * imag + 1e-12))
    m_high, m_low = split(jnp.concatenate(magnitudes, axis=0))
    smooth = (dot(m_high, smooth_band[...]) + dot(m_low, smooth_band[...])) * inverse_count
    scale = 1.0 / (smooth + EPS)
    flip = flip_matrix(channels)
    for w in range(own):
        here = slice(w * channels, (w + 1) * channels)
        white = jnp.concatenate([reals[w] * scale[here], imags[w] * scale[here]], axis=1)
        out[:, w * 2 * NF:(w + 1) * 2 * NF] = dot(flip, white.astype(BF16)).astype(BF16)


def flip_matrix(channels):
    row = lax.broadcasted_iota(jnp.int32, (channels, channels), 0)
    column = lax.broadcasted_iota(jnp.int32, (channels, channels), 1)
    return (row + column == channels - 1).astype(F32).astype(BF16)


def rotate_kernel(lags, own, cos_lag, sin_lag, out, tick):
    tick[...] = jnp.zeros_like(tick)
    channels = own.shape[0]
    straight = dot(flip_matrix(channels), own[...])
    real, imag = straight[:, :NF], straight[:, NF:]
    for t in range(lags):
        c, s = cos_lag[t:t + 1, :], sin_lag[t:t + 1, :]
        here = slice(t * channels, (t + 1) * channels)
        out[here, :NF] = (real * c - imag * s).astype(BF16)
        out[here, NF:] = (real * s + imag * c).astype(BF16)


def fill_slots(channels, partners, present, absent, sems):
    last = NPART // channels - 1

    def place(slot):
        return pl.ds(pl.multiple_of((last - slot) * channels, channels), channels)

    copies = [
        pltpu.make_async_copy(source, partners.at[place(slot), :], sems.at[i])
        for i, (source, slot) in enumerate(present)
    ]
    for copy in copies:
        copy.start()
    for slot in absent:
        partners[place(slot), :] = jnp.zeros((channels, partners.shape[1]), BF16)
    for copy in copies:
        copy.wait()


def early_slots(place, channels, blocks, partners, sems):
    own, ahead, _ = blocks
    fill_slots(channels, partners, [(own, 0), (ahead, 4)], (1, 2, 3, 5, 6, 7), sems)


def late_slots(place, channels, blocks, partners, sems):
    core = lax.rem(place[0], 2)
    side = lax.rem(place[0] // 2, 2)
    (own_swapped, ahead_swapped, far, far_swapped, cross, cross_swapped, other,
     other_swapped) = blocks
    cross_slot = 6 - 4 * side
    other_slot = 8 - cross_slot
    step = 1 - 2 * core
    both = [(far, 0), (cross, cross_slot), (other, other_slot), (ahead_swapped, 4 + step),
            (cross_swapped, cross_slot + step), (other_swapped, other_slot + step)]

    @pl.when(core == 0)
    def _():
        fill_slots(channels, partners, both + [(own_swapped, 1)], (4,), sems)

    @pl.when(core == 1)
    def _():
        fill_slots(channels, partners, both + [(far_swapped, 7)], (4,), sems)


def product_kernel(late, norm_scale, place, rotated, *refs):
    refs = list(refs)
    before = refs.pop(0) if late else None
    out, partners, total, sems = refs[-4:]
    blocks = refs[:-4]
    channels = blocks[0].shape[0]
    (late_slots if late else early_slots)(place, channels, blocks, partners, sems)
    rows, features = rotated.shape
    chunk = 2 * 2 * NF
    for begin in range(0, features, chunk):
        turned = partners[:, begin:begin + chunk].T
        product = dot(rotated[:, begin:begin + chunk], turned)
        if begin == 0:
            total[...] = product
        else:
            total[...] += product

    row = lax.broadcasted_iota(jnp.int32, (channels, NPART), 0)
    column = lax.broadcasted_iota(jnp.int32, (channels, NPART), 1)
    low = row + column >= NPART - 1
    keep = (low | (column < NPART - channels)) if late else jnp.logical_not(low)
    sheared = []
    for begin in range(0, rows, channels):
        here = slice(begin, begin + channels)
        value = jnp.where(keep, total[here, :], 0.0)
        if late:
            value = (value + before[here, :]) * norm_scale
            sheared.append(pltpu.roll(value, 1, 1, stride=1, stride_axis=0).astype(BF16))
        else:
            out[here, :] = value
    if late:
        sheared = jnp.concatenate(sheared, axis=0)
        out[...] = dot(sheared, flip_matrix(NPART)).astype(BF16)


def exchange(value, pairs):
    return lax.ppermute(value, "chan", pairs)


def local(records, dead_mask, offsets):
    channels, samples = records.shape
    tm_count = lax.axis_size("tm")
    tm_index = lax.axis_index("tm")
    chan_count = lax.axis_size("chan")
    own = samples // HOP
    windows = own * tm_count
    halves = own
    halo = 0
    if tm_count > 1:
        reach = 2 * HOP + H
        left = lax.ppermute(
            records[:, samples - H:], "tm", [(i, i + 1) for i in range(tm_count - 1)]
        )
        right = lax.ppermute(
            records[:, :reach], "tm", [(i + 1, i) for i in range(tm_count - 1)]
        )
        records = jnp.concatenate([left, records, right], axis=1)
        halves = own + 2
        halo = H
    table = jnp.asarray(packed_tables())
    own_offsets = lax.dynamic_slice_in_dim(offsets, tm_index * own, own, 0)
    vmem = pl.BlockSpec(memory_space=pltpu.VMEM)
    smem = pl.BlockSpec(memory_space=pltpu.SMEM)
    hbm = pl.BlockSpec(memory_space=pl.ANY)
    params = pltpu.CompilerParams(vmem_limit_bytes=24 * 1024 * 1024)

    bulk = min(own + 1, halves)
    part_rows = (own + bulk * (HOP // GROUP)) * channels
    spectra = pl.pallas_call(
        functools.partial(spectra_kernel, halves, own, halo),
        name="spectra",
        out_shape=jax.ShapeDtypeStruct((channels, own * 2 * NF), BF16),
        in_specs=[smem, smem, vmem, hbm],
        out_specs=vmem,
        scratch_shapes=[
            pltpu.VMEM((channels, halves * HOP + 2 * H), BF16),
            pltpu.VMEM((part_rows, 3 * GROUP), BF16),
            pltpu.VMEM((part_rows, 2 * NF + 128), F32),
            pltpu.VMEM(table.shape, BF16),
            pltpu.SemaphoreType.DMA,
        ],
        compiler_params=pltpu.CompilerParams(vmem_limit_bytes=55 * 1024 * 1024),
        cost_estimate=pl.CostEstimate(
            flops=7_000_000_000, bytes_accessed=8 * 1024 * 1024, transcendentals=0
        ),
    )(dead_mask, own_offsets, records, table)
    if tm_count > 1:
        spectra = lax.all_gather(spectra, "tm", axis=1, tiled=True)

    lags = NLAG // tm_count
    cos_lag, sin_lag = (
        lax.dynamic_slice_in_dim(jnp.asarray(t), tm_index * lags, lags, 0) for t in lag_tables()
    )
    place = lax.axis_index("chan").astype(jnp.int32).reshape(1)
    norm_scale = 1.0 / math.sqrt(2.0 * NF * windows)

    features = spectra.shape[1]
    rotated, tick = pl.pallas_call(
        functools.partial(rotate_kernel, lags),
        name="rotate",
        grid=(windows,),
        out_shape=(
            jax.ShapeDtypeStruct((lags * channels, features), BF16),
            jax.ShapeDtypeStruct((8, 128), F32),
        ),
        in_specs=[
            pl.BlockSpec((channels, 2 * NF), lambda w: (0, w)),
            pl.BlockSpec((lags, NF), lambda w: (0, 0)),
            pl.BlockSpec((lags, NF), lambda w: (0, 0)),
        ],
        out_specs=(
            pl.BlockSpec((lags * channels, 2 * NF), lambda w: (0, w)),
            pl.BlockSpec((8, 128), lambda w: (0, 0)),
        ),
        compiler_params=params,
        cost_estimate=pl.CostEstimate(
            flops=4_000_000_000, bytes_accessed=8 * 1024 * 1024, transcendentals=0
        ),
    )(spectra, cos_lag, sin_lag)

    def product(blocks, before):
        late = before is not None
        operands = [place, rotated] + ([before] if late else []) + list(blocks)
        return pl.pallas_call(
            functools.partial(product_kernel, late, norm_scale),
            name="late_product" if late else "early_product",
            out_shape=jax.ShapeDtypeStruct((lags * channels, NPART), BF16 if late else F32),
            in_specs=[smem, vmem] + ([vmem] if late else []) + [hbm] * len(blocks),
            out_specs=vmem,
            scratch_shapes=[
                pltpu.VMEM((NPART, features), BF16),
                pltpu.VMEM((lags * channels, NPART), F32),
                pltpu.SemaphoreType.DMA((len(blocks),)),
            ],
            compiler_params=params,
            cost_estimate=pl.CostEstimate(
                flops=2 * lags * channels * features * NPART, bytes_accessed=6 * 1024 * 1024,
                transcendentals=0,
            ),
        )(*operands)

    every = range(chan_count)
    down = [(i, i - 4) for i in every if i >= 4]
    to_low_side = [(i, i - 2) for i in every if i & 2]
    to_high_side = [(i, i - 2) for i in every if i >= 4 and not i & 2]
    across = [(i, i ^ 2) for i in every]
    cores = [(i, i ^ 1) for i in every]
    side = lax.rem(lax.axis_index("chan") // 2, 2)

    ahead = exchange(spectra, down)
    later, tick = lax.optimization_barrier((spectra, tick))
    beside = exchange(later, to_low_side)
    ahead, rotated = lax.optimization_barrier((ahead, rotated))
    other = jnp.where(side == 0, beside, exchange(ahead, to_high_side))
    cross = exchange(ahead, across)
    far = exchange(ahead, down)
    early = product((spectra, ahead, tick), None)
    kept, ahead, other, early = lax.optimization_barrier((spectra, ahead, other, early))
    own_swapped = exchange(kept, [(i, j) for i, j in cores if j < i])
    ahead_swapped = exchange(ahead, cores)
    cross, own_swapped, ahead_swapped = lax.optimization_barrier(
        (cross, own_swapped, ahead_swapped)
    )
    far_swapped = exchange(far, [(i, j) for i, j in cores if j > i])
    blocks = (own_swapped, ahead_swapped, far, far_swapped, cross, exchange(cross, cores),
              other, exchange(other, cores))
    return product(blocks, early).reshape(lags, channels, NPART)


def solution(mesh):
    return jax.shard_map(
        local,
        mesh=mesh,
        in_specs=(P(("win", "chan"), "tm"), P(("win", "chan")), P("win")),
        out_specs=P("tm", ("win", "chan"), None),
        check_vma=False,
    )
```

```python
import functools
import math

import jax
import jax.numpy as jnp
import ml_dtypes
import numpy as np
from jax import lax
from jax.experimental import pallas as pl
from jax.experimental.pallas import tpu as pltpu
from jax.sharding import PartitionSpec as P

L = 8192
HOP = 4096
H = 128
K0 = 32
NF = 256
WB = 64
NLAG = 32
NPART = 256
EDGE = 512
STEP = 256
GROUP = 512
EPS = 1e-05
TWO_PI = 2.0 * math.pi
BF16 = jnp.bfloat16
F32 = jnp.float32


def split_table(table):
    high = table.astype(ml_dtypes.bfloat16)
    low = (table - high.astype(np.float64)).astype(ml_dtypes.bfloat16)
    return high, low


@functools.cache
def fourier_tables():
    samples = np.arange(GROUP)[:, None]
    bins = K0 + np.arange(NF)[None, :]
    angle = (samples * bins % L) * (TWO_PI / L)
    inner = np.concatenate([np.cos(angle), -np.sin(angle)], axis=1)
    outer = np.zeros((GROUP, 128))
    for lane, k, wave in ((0, K0 - 1, np.cos), (64, K0 - 1, np.sin), (127, K0 + NF, np.cos), (63, K0 + NF, np.sin)):
        sign = 1.0 if wave is np.cos else -1.0
        outer[:, lane] = sign * wave((samples[:, 0] * k % L) * (TWO_PI / L))
    high, low = split_table(inner)
    return np.concatenate([high, outer.astype(ml_dtypes.bfloat16)], axis=1), low


@functools.cache
def packed_tables():
    lane = np.arange(2 * H + STEP)[:, None]
    place = np.arange(STEP)[None, :]
    level_band = ((lane >= place) & (lane <= place + 2 * H)).astype(ml_dtypes.bfloat16)
    bins = np.arange(NF)
    smooth_band = np.zeros((GROUP, NF), ml_dtypes.bfloat16)
    smooth_band[:NF] = np.abs(bins[:, None] - bins[None, :]) <= WB
    return np.concatenate([*fourier_tables(), level_band, smooth_band], axis=1)


@functools.cache
def lag_tables():
    lags = np.arange(NLAG)[:, None] - NLAG // 2
    angle = (lags * (K0 + np.arange(NF))[None, :] % L) * (TWO_PI / L)
    return np.cos(angle).astype(np.float32), np.sin(angle).astype(np.float32)


def split(value):
    high = value.astype(BF16)
    return high, (value - high.astype(F32)).astype(BF16)


def inverse(value):
    guess = pl.reciprocal(value, approx=True)
    return guess * (2.0 - value * guess)


def dot(a, b):
    return jnp.dot(a, b, preferred_element_type=F32)


def spectra_kernel(
    halves, own, halo,
    dead, offs, x, table_hbm, out, absolute, norm_high, norm_low, parts, table, sem,
):
    table_copy = pltpu.make_async_copy(table_hbm, table, sem)
    table_copy.start()
    channels = x.shape[0]
    groups = HOP // GROUP
    bulk = min(own + 1, halves)
    edges = min(own + 2, halves)
    width = halves * HOP
    if not halo:
        for begin in (0, H + width):
            absolute[:, begin:begin + H] = jnp.zeros((channels, H), BF16)
    for begin in range(0, x.shape[1], GROUP):
        end = min(begin + GROUP, x.shape[1])
        absolute[:, H - halo + begin:H - halo + end] = jnp.abs(x[:, begin:end]).astype(BF16)

    begin = 2 * NF + 128
    high = table.at[:, :begin]
    low = table.at[:, begin:begin + 2 * NF]
    level_band = table.at[:, begin + 2 * NF:begin + 2 * NF + STEP]
    smooth_band = table.at[:NF, begin + 2 * NF + STEP:]
    lane = lax.broadcasted_iota(jnp.int32, (1, parts.shape[1]), 1)
    outer_place = lane - 2 * NF
    outer_first = (outer_place == 0) | (outer_place == 64)
    every_bin = jnp.where(
        lane < 2 * NF, jnp.bitwise_and(lane, NF - 1) + K0, jnp.where(outer_first, K0 - 1, K0 + NF)
    )
    real_place = (lane < NF) | (outer_place == 0) | (outer_place == 127)
    group = lax.broadcasted_iota(jnp.int32, (groups, 1), 0) * GROUP
    angle = jnp.bitwise_and(group * every_bin, L - 1).astype(F32) * (TWO_PI / L)
    turn_same = jnp.cos(angle)
    turn_swap = jnp.sin(angle) * jnp.where(real_place, -1.0, 1.0)
    bin_index = lax.broadcasted_iota(jnp.int32, (1, NF), 1)
    below, above = jnp.minimum(bin_index, WB), jnp.minimum(NF - 1 - bin_index, WB)
    inverse_count = 1.0 / (below + above + 1).astype(F32)
    table_copy.wait()

    def rows(ref, begin, length, count):
        return [ref[:, begin + j * HOP:begin + j * HOP + length] for j in range(count)]

    def store(place, value):
        here = slice(place, place + value.shape[0])
        norm_high[here, :], norm_low[here, :] = split(value)

    def normalise(group_ids, place):
        blocks = [(g, g * GROUP + part * STEP) for g in group_ids for part in range(GROUP // STEP)]
        counts = [edges if g == 0 else bulk for g, _ in blocks]
        level = dot(
            jnp.concatenate(
                [r for (_, begin), n in zip(blocks, counts)
                 for r in rows(absolute, begin, STEP + 2 * H, n)], axis=0
            ), level_band[...],
        ) * (1.0 / (2 * H + 1)) + EPS
        values = []
        at = 0
        for (_, begin), n in zip(blocks, counts):
            samples = jnp.concatenate(rows(x, halo + begin, STEP, n), axis=0)
            values.append(samples * inverse(level[at:at + n * channels]))
            at += n * channels
        begins = {}
        for index, g in enumerate(group_ids):
            value = jnp.concatenate(values[2 * index:2 * index + 2], axis=1)
            if g == 0:
                lane = lax.broadcasted_iota(jnp.int32, (channels, EDGE), 1)
                merged = []
                for w in range(own):
                    mine = value[w * channels:(w + 1) * channels]
                    other = (
                        value[(w + 2) * channels:(w + 3) * channels]
                        if w + 2 < edges else jnp.zeros_like(mine)
                    )
                    merged.append(jnp.where(lane >= offs[w], mine, other))
                begins["edge"] = place
                store(place, jnp.concatenate(merged, axis=0))
                place += own * channels
                value = value[:bulk * channels]
            begins[g] = place
            store(place, value)
            place += bulk * channels
        return begins, place

    def transform(begin, end):
        first = dot(norm_high[begin:end, :], high[...])
        second = dot(norm_low[begin:end, :], high[:, :2 * NF])
        second = second + dot(norm_high[begin:end, :], low[...])
        parts[begin:end, :2 * NF] = first[:, :2 * NF] + second
        parts[begin:end, 2 * NF:] = first[:, 2 * NF:]

    begins = {}
    place = 0
    waiting = None
    for g in range(0, groups, 2):
        start = place
        found, place = normalise([g, g + 1], place)
        begins.update(found)
        if waiting:
            transform(*waiting)
        waiting = (start, place)
    transform(*waiting)

    def piece(name, j):
        return parts[begins[name] + j * channels:begins[name] + (j + 1) * channels, :]

    def bulk_of(j):
        same = jnp.zeros((channels, parts.shape[1]), F32)
        swap = same
        for g in range(1, groups):
            value = piece(g, j)
            same = same + value * turn_same[g:g + 1, :]
            swap = swap + value * turn_swap[g:g + 1, :]
        return same + jnp.concatenate(
            [swap[:, NF:2 * NF], swap[:, :NF], pltpu.roll(swap[:, 2 * NF:], 64, 1)], axis=1
        )

    window = lax.broadcasted_iota(jnp.int32, (own, 1), 0)
    offsets = sum(jnp.where(window == w, offs[w], 0) for w in range(own))
    lane = lax.broadcasted_iota(jnp.int32, (1, NF), 1)
    outer_lane = lax.broadcasted_iota(jnp.int32, (1, 128), 1)
    outer_bin = jnp.where((outer_lane == 0) | (outer_lane == 64), K0 - 1, K0 + NF)

    def turn(bins):
        angle = jnp.bitwise_and(bins * offsets, L - 1).astype(F32) * (TWO_PI / L)
        return jnp.cos(angle), jnp.sin(angle)

    cos_turn, sin_turn = turn(lane + K0)
    cos_outer, sin_outer = turn(outer_bin)
    sign = 1.0 - 2.0 * jnp.bitwise_and(lane + K0, 1).astype(F32)
    sign_outer = 1.0 - 2.0 * jnp.bitwise_and(outer_bin, 1).astype(F32)
    channel = lax.broadcasted_iota(jnp.int32, (channels, 1), 0)
    live = 1.0 - sum(jnp.where(channel == i, dead[i], 0) for i in range(channels)).astype(F32)

    signs = jnp.concatenate([sign, sign, sign_outer], axis=1)
    reals, imags, magnitudes = [], [], []
    following = bulk_of(0)
    for w in range(own):
        spec = following + piece("edge", w)
        if w + 1 < bulk:
            following = bulk_of(w + 1)
            spec = spec + (following + piece(0, w + 1)) * signs
        spec = spec * live
        outer = spec[:, 2 * NF:]
        c, s = cos_turn[w:w + 1], sin_turn[w:w + 1]
        c_outer, s_outer = cos_outer[w:w + 1], sin_outer[w:w + 1]
        outer_imag = pltpu.roll(outer, 64, 1)

        def hann(inner, ends):
            ends = jnp.concatenate([ends, ends], axis=1)
            before = jnp.where(lane == 0, ends, pltpu.roll(inner, 1, 1))
            behind = jnp.where(lane == NF - 1, ends, pltpu.roll(inner, NF - 1, 1))
            return 0.5 * inner - 0.25 * (before + behind)

        real = hann(
            spec[:, :NF] * c - spec[:, NF:2 * NF] * s, outer * c_outer - outer_imag * s_outer
        )
        imag = hann(
            spec[:, :NF] * s + spec[:, NF:2 * NF] * c, outer * s_outer + outer_imag * c_outer
        )
        reals.append(real)
        imags.append(imag)
        magnitudes.append(jnp.sqrt(real * real + imag * imag + 1e-12))
    m_high, m_low = split(jnp.concatenate(magnitudes, axis=0))
    smooth = (dot(m_high, smooth_band[...]) + dot(m_low, smooth_band[...])) * inverse_count
    scale = 1.0 / (smooth + EPS)
    flip = flip_matrix(channels)
    for w in range(own):
        here = slice(w * channels, (w + 1) * channels)
        white = jnp.concatenate([reals[w] * scale[here], imags[w] * scale[here]], axis=1)
        out[:, w * 2 * NF:(w + 1) * 2 * NF] = dot(flip, white.astype(BF16)).astype(BF16)


def flip_matrix(channels):
    row = lax.broadcasted_iota(jnp.int32, (channels, channels), 0)
    column = lax.broadcasted_iota(jnp.int32, (channels, channels), 1)
    return (row + column == channels - 1).astype(F32).astype(BF16)


def rotate_kernel(lags, own, cos_lag, sin_lag, out):
    channels = own.shape[0]
    straight = dot(flip_matrix(channels), own[...])
    real, imag = straight[:, :NF], straight[:, NF:]
    for t in range(lags):
        c, s = cos_lag[t:t + 1, :], sin_lag[t:t + 1, :]
        here = slice(t * channels, (t + 1) * channels)
        out[here, :NF] = (real * c - imag * s).astype(BF16)
        out[here, NF:] = (real * s + imag * c).astype(BF16)


def hand_on_kernel(own, rotated, out):
    out[...] = own[...]


def fill_slots(channels, partners, present, absent, sems):
    last = NPART // channels - 1

    def place(slot):
        return pl.ds(pl.multiple_of((last - slot) * channels, channels), channels)

    copies = [
        pltpu.make_async_copy(source, partners.at[place(slot), :], sems.at[i])
        for i, (source, slot) in enumerate(present)
    ]
    for copy in copies:
        copy.start()
    for slot in absent:
        partners[place(slot), :] = jnp.zeros((channels, partners.shape[1]), BF16)
    for copy in copies:
        copy.wait()


def early_slots(place, channels, blocks, partners, sems):
    own, ahead = blocks
    fill_slots(channels, partners, [(own, 0), (ahead, 4)], (1, 2, 3, 5, 6, 7), sems)


def late_slots(place, channels, blocks, partners, sems):
    core = lax.rem(place[0], 2)
    side = lax.rem(place[0] // 2, 2)
    (own_swapped, ahead_swapped, far, far_swapped, cross, cross_swapped, other,
     other_swapped) = blocks
    cross_slot = 6 - 4 * side
    other_slot = 8 - cross_slot
    step = 1 - 2 * core
    both = [(far, 0), (cross, cross_slot), (other, other_slot), (ahead_swapped, 4 + step),
            (cross_swapped, cross_slot + step), (other_swapped, other_slot + step)]

    @pl.when(core == 0)
    def _():
        fill_slots(channels, partners, both + [(own_swapped, 1)], (4,), sems)

    @pl.when(core == 1)
    def _():
        fill_slots(channels, partners, both + [(far_swapped, 7)], (4,), sems)


def product_kernel(late, norm_scale, place, rotated, *refs):
    refs = list(refs)
    before = refs.pop(0) if late else None
    out, partners, total, sems = refs[-4:]
    blocks = refs[:-4]
    channels = blocks[0].shape[0]
    (late_slots if late else early_slots)(place, channels, blocks, partners, sems)
    rows, features = rotated.shape
    chunk = 2 * 2 * NF
    for begin in range(0, features, chunk):
        turned = partners[:, begin:begin + chunk].T
        product = dot(rotated[:, begin:begin + chunk], turned)
        if begin == 0:
            total[...] = product
        else:
            total[...] += product

    row = lax.broadcasted_iota(jnp.int32, (channels, NPART), 0)
    column = lax.broadcasted_iota(jnp.int32, (channels, NPART), 1)
    low = row + column >= NPART - 1
    keep = (low | (column < NPART - channels)) if late else jnp.logical_not(low)
    sheared = []
    for begin in range(0, rows, channels):
        here = slice(begin, begin + channels)
        value = jnp.where(keep, total[here, :], 0.0)
        if late:
            value = (value + before[here, :]) * norm_scale
            sheared.append(pltpu.roll(value, 1, 1, stride=1, stride_axis=0).astype(BF16))
        else:
            out[here, :] = value
    if late:
        sheared = jnp.concatenate(sheared, axis=0)
        out[...] = dot(sheared, flip_matrix(NPART)).astype(BF16)


def exchange(value, pairs):
    return lax.ppermute(value, "chan", pairs)


def local(records, dead_mask, offsets):
    channels, samples = records.shape
    tm_count = lax.axis_size("tm")
    tm_index = lax.axis_index("tm")
    chan_count = lax.axis_size("chan")
    own = samples // HOP
    windows = own * tm_count
    halves = own
    halo = 0
    if tm_count > 1:
        reach = 2 * HOP + H
        left = lax.ppermute(
            records[:, samples - H:], "tm", [(i, i + 1) for i in range(tm_count - 1)]
        )
        right = lax.ppermute(
            records[:, :reach], "tm", [(i + 1, i) for i in range(tm_count - 1)]
        )
        records = jnp.concatenate([left, records, right], axis=1)
        halves = own + 2
        halo = H
    table = jnp.asarray(packed_tables())
    own_offsets = lax.dynamic_slice_in_dim(offsets, tm_index * own, own, 0)
    vmem = pl.BlockSpec(memory_space=pltpu.VMEM)
    smem = pl.BlockSpec(memory_space=pltpu.SMEM)
    hbm = pl.BlockSpec(memory_space=pl.ANY)
    params = pltpu.CompilerParams(vmem_limit_bytes=24 * 1024 * 1024)

    bulk = min(own + 1, halves)
    part_rows = (own + bulk * (HOP // GROUP)) * channels
    spectra = pl.pallas_call(
        functools.partial(spectra_kernel, halves, own, halo),
        name="spectra",
        out_shape=jax.ShapeDtypeStruct((channels, own * 2 * NF), BF16),
        in_specs=[smem, smem, vmem, hbm],
        out_specs=vmem,
        scratch_shapes=[
            pltpu.VMEM((channels, halves * HOP + 2 * H), BF16),
            pltpu.VMEM((part_rows, GROUP), BF16),
            pltpu.VMEM((part_rows, GROUP), BF16),
            pltpu.VMEM((part_rows, 2 * NF + 128), F32),
            pltpu.VMEM(table.shape, BF16),
            pltpu.SemaphoreType.DMA,
        ],
        compiler_params=pltpu.CompilerParams(vmem_limit_bytes=55 * 1024 * 1024),
        cost_estimate=pl.CostEstimate(
            flops=7_000_000_000, bytes_accessed=8 * 1024 * 1024, transcendentals=0
        ),
    )(dead_mask, own_offsets, records, table)
    if tm_count > 1:
        spectra = lax.all_gather(spectra, "tm", axis=1, tiled=True)

    lags = NLAG // tm_count
    cos_lag, sin_lag = (
        lax.dynamic_slice_in_dim(jnp.asarray(t), tm_index * lags, lags, 0) for t in lag_tables()
    )
    place = lax.axis_index("chan").astype(jnp.int32).reshape(1)
    norm_scale = 1.0 / math.sqrt(2.0 * NF * windows)

    features = spectra.shape[1]
    rotated = pl.pallas_call(
        functools.partial(rotate_kernel, lags),
        name="rotate",
        grid=(windows,),
        out_shape=jax.ShapeDtypeStruct((lags * channels, features), BF16),
        in_specs=[
            pl.BlockSpec((channels, 2 * NF), lambda w: (0, w)),
            pl.BlockSpec((lags, NF), lambda w: (0, 0)),
            pl.BlockSpec((lags, NF), lambda w: (0, 0)),
        ],
        out_specs=pl.BlockSpec((lags * channels, 2 * NF), lambda w: (0, w)),
        compiler_params=params,
        cost_estimate=pl.CostEstimate(
            flops=4_000_000_000, bytes_accessed=8 * 1024 * 1024, transcendentals=0
        ),
    )(spectra, cos_lag, sin_lag)

    def product(blocks, before):
        late = before is not None
        operands = [place, rotated] + ([before] if late else []) + list(blocks)
        return pl.pallas_call(
            functools.partial(product_kernel, late, norm_scale),
            name="late_product" if late else "early_product",
            out_shape=jax.ShapeDtypeStruct((lags * channels, NPART), BF16 if late else F32),
            in_specs=[smem, vmem] + ([vmem] if late else []) + [hbm] * len(blocks),
            out_specs=vmem,
            scratch_shapes=[
                pltpu.VMEM((NPART, features), BF16),
                pltpu.VMEM((lags * channels, NPART), F32),
                pltpu.SemaphoreType.DMA((len(blocks),)),
            ],
            compiler_params=params,
            cost_estimate=pl.CostEstimate(
                flops=2 * lags * channels * features * NPART, bytes_accessed=6 * 1024 * 1024,
                transcendentals=0,
            ),
        )(*operands)

    every = range(chan_count)
    down = [(i, i - 4) for i in every if i >= 4]
    to_low_side = [(i, i - 2) for i in every if i & 2]
    to_high_side = [(i, i - 2) for i in every if i >= 4 and not i & 2]
    across = [(i, i ^ 2) for i in every]
    cores = [(i, i ^ 1) for i in every]
    side = lax.rem(lax.axis_index("chan") // 2, 2)

    ahead = exchange(spectra, down)
    handed_on = pl.pallas_call(
        hand_on_kernel,
        name="hand_on",
        out_shape=jax.ShapeDtypeStruct(spectra.shape, BF16),
        in_specs=[vmem, hbm],
        out_specs=vmem,
        compiler_params=params,
    )(spectra, rotated)
    beside = exchange(handed_on, to_low_side)
    ahead, rotated = lax.optimization_barrier((ahead, rotated))
    other = jnp.where(side == 0, beside, exchange(ahead, to_high_side))
    cross = exchange(ahead, across)
    far = exchange(ahead, down)
    early = product((spectra, ahead), None)
    kept, ahead, other, early = lax.optimization_barrier((spectra, ahead, other, early))
    own_swapped = exchange(kept, [(i, j) for i, j in cores if j < i])
    ahead_swapped = exchange(ahead, cores)
    cross, own_swapped, ahead_swapped = lax.optimization_barrier(
        (cross, own_swapped, ahead_swapped)
    )
    far_swapped = exchange(far, [(i, j) for i, j in cores if j > i])
    blocks = (own_swapped, ahead_swapped, far, far_swapped, cross, exchange(cross, cores),
              other, exchange(other, cores))
    return product(blocks, early).reshape(lags, channels, NPART)


def solution(mesh):
    return jax.shard_map(
        local,
        mesh=mesh,
        in_specs=(P(("win", "chan"), "tm"), P(("win", "chan")), P("win")),
        out_specs=P("tm", ("win", "chan"), None),
        check_vma=False,
    )
```

```python
import functools
import math

import jax
import jax.numpy as jnp
import ml_dtypes
import numpy as np
from jax import lax
from jax.experimental import pallas as pl
from jax.experimental.pallas import tpu as pltpu
from jax.sharding import PartitionSpec as P

L = 8192
HOP = 4096
H = 128
K0 = 32
NF = 256
WB = 64
NLAG = 32
NPART = 256
EDGE = 512
STEP = 256
GROUP = 512
EPS = 1e-05
TWO_PI = 2.0 * math.pi
BF16 = jnp.bfloat16
F32 = jnp.float32


def split_table(table):
    high = table.astype(ml_dtypes.bfloat16)
    low = (table - high.astype(np.float64)).astype(ml_dtypes.bfloat16)
    return high, low


@functools.cache
def fourier_tables():
    samples = np.arange(GROUP)[:, None]
    bins = K0 + np.arange(NF)[None, :]
    angle = (samples * bins % L) * (TWO_PI / L)
    inner = np.concatenate([np.cos(angle), -np.sin(angle)], axis=1)
    outer = np.zeros((GROUP, 128))
    for lane, k, wave in ((0, K0 - 1, np.cos), (64, K0 - 1, np.sin), (127, K0 + NF, np.cos), (63, K0 + NF, np.sin)):
        sign = 1.0 if wave is np.cos else -1.0
        outer[:, lane] = sign * wave((samples[:, 0] * k % L) * (TWO_PI / L))
    high, low = split_table(inner)
    return np.concatenate([high, outer.astype(ml_dtypes.bfloat16)], axis=1), low


@functools.cache
def packed_tables():
    return np.concatenate(fourier_tables(), axis=1)


@functools.cache
def lag_tables():
    lags = np.arange(NLAG)[:, None] - NLAG // 2
    angle = (lags * (K0 + np.arange(NF))[None, :] % L) * (TWO_PI / L)
    return np.cos(angle).astype(np.float32), np.sin(angle).astype(np.float32)


def split(value):
    high = value.astype(BF16)
    return high, (value - high.astype(F32)).astype(BF16)


def inverse(value):
    guess = pl.reciprocal(value, approx=True)
    return guess * (2.0 - value * guess)


def dot(a, b):
    return jnp.dot(a, b, preferred_element_type=F32)


def spectra_kernel(
    halves, own, halo,
    dead, offs, x_hbm, table_hbm, out, x, absolute, norm_high, norm_low, parts, table, sems,
):
    channels = x.shape[0]
    groups = HOP // GROUP
    bulk = min(own + 1, halves)
    edges = min(own + 2, halves)
    width = halves * HOP
    middle = HOP // 2 + H
    firsts, seconds = [], []
    for j in range(halves):
        firsts.append((j * HOP - (H if j or halo else 0), j * HOP + middle))
        seconds.append((j * HOP + middle, (j + 1) * HOP - H if j + 1 < halves else width + halo))
    copies = [
        pltpu.make_async_copy(
            x_hbm.at[:, pl.ds(halo + begin, end - begin)], x.at[:, pl.ds(H + begin, end - begin)],
            sems.at[i],
        )
        for i, (begin, end) in enumerate(firsts + seconds)
    ]
    table_copy = pltpu.make_async_copy(table_hbm, table, sems.at[2 * halves])
    for copy in copies[:halves] + [table_copy] + copies[halves:]:
        copy.start()
    if not halo:
        for begin in (0, H + width):
            absolute[:, begin:begin + H] = jnp.zeros((channels, H), BF16)

    def arrive(ids):
        for i in ids:
            copies[i].wait()
        for i in ids:
            begin, end = (firsts + seconds)[i]
            here = slice(H + begin, H + end)
            absolute[:, here] = jnp.abs(x[:, here]).astype(BF16)

    high = table.at[:, :2 * NF + 128]
    low = table.at[:, 2 * NF + 128:]
    from_lane = lax.broadcasted_iota(jnp.int32, (2 * H + STEP, STEP), 0)
    to_lane = lax.broadcasted_iota(jnp.int32, (2 * H + STEP, STEP), 1)
    level_band = ((from_lane >= to_lane) & (from_lane <= to_lane + 2 * H)).astype(F32).astype(BF16)
    from_bin = lax.broadcasted_iota(jnp.int32, (NF, NF), 0)
    to_bin = lax.broadcasted_iota(jnp.int32, (NF, NF), 1)
    smooth_band = (jnp.abs(from_bin - to_bin) <= WB).astype(F32).astype(BF16)
    lane = lax.broadcasted_iota(jnp.int32, (1, parts.shape[1]), 1)
    outer_place = lane - 2 * NF
    outer_first = (outer_place == 0) | (outer_place == 64)
    every_bin = jnp.where(
        lane < 2 * NF, jnp.bitwise_and(lane, NF - 1) + K0, jnp.where(outer_first, K0 - 1, K0 + NF)
    )
    real_place = (lane < NF) | (outer_place == 0) | (outer_place == 127)
    group = lax.broadcasted_iota(jnp.int32, (groups, 1), 0) * GROUP
    angle = jnp.bitwise_and(group * every_bin, L - 1).astype(F32) * (TWO_PI / L)
    turn_same = jnp.cos(angle)
    turn_swap = jnp.sin(angle) * jnp.where(real_place, -1.0, 1.0)
    bin_index = lax.broadcasted_iota(jnp.int32, (1, NF), 1)
    below, above = jnp.minimum(bin_index, WB), jnp.minimum(NF - 1 - bin_index, WB)
    inverse_count = 1.0 / (below + above + 1).astype(F32)

    def rows(ref, begin, length, count):
        return [ref[:, begin + j * HOP:begin + j * HOP + length] for j in range(count)]

    def store(place, value):
        here = slice(place, place + value.shape[0])
        norm_high[here, :], norm_low[here, :] = split(value)

    def normalise(group_ids, place):
        blocks = [(g, g * GROUP + part * STEP) for g in group_ids for part in range(GROUP // STEP)]
        counts = [edges if g == 0 else bulk for g, _ in blocks]
        level = dot(
            jnp.concatenate(
                [r for (_, begin), n in zip(blocks, counts)
                 for r in rows(absolute, begin, STEP + 2 * H, n)], axis=0
            ), level_band,
        ) * (1.0 / (2 * H + 1)) + EPS
        values = []
        at = 0
        for (_, begin), n in zip(blocks, counts):
            samples = jnp.concatenate(rows(x, H + begin, STEP, n), axis=0)
            values.append(samples * inverse(level[at:at + n * channels]))
            at += n * channels
        begins = {}
        for index, g in enumerate(group_ids):
            value = jnp.concatenate(values[2 * index:2 * index + 2], axis=1)
            if g == 0:
                lane = lax.broadcasted_iota(jnp.int32, (channels, EDGE), 1)
                merged = []
                for w in range(own):
                    mine = value[w * channels:(w + 1) * channels]
                    other = (
                        value[(w + 2) * channels:(w + 3) * channels]
                        if w + 2 < edges else jnp.zeros_like(mine)
                    )
                    merged.append(jnp.where(lane >= offs[w], mine, other))
                begins["edge"] = place
                store(place, jnp.concatenate(merged, axis=0))
                place += own * channels
                value = value[:bulk * channels]
            begins[g] = place
            store(place, value)
            place += bulk * channels
        return begins, place

    def transform(begin, end):
        first = dot(norm_high[begin:end, :], high[...])
        second = dot(norm_low[begin:end, :], high[:, :2 * NF])
        second = second + dot(norm_high[begin:end, :], low[...])
        parts[begin:end, :2 * NF] = first[:, :2 * NF] + second
        parts[begin:end, 2 * NF:] = first[:, 2 * NF:]

    begins = {}
    place = 0
    waiting = None
    arrive(range(halves))
    table_copy.wait()
    for g in range(0, groups, 2):
        if g == groups // 2:
            arrive(range(halves, 2 * halves))
        start = place
        found, place = normalise([g, g + 1], place)
        begins.update(found)
        if waiting:
            transform(*waiting)
        waiting = (start, place)
    transform(*waiting)

    def piece(name, j):
        return parts[begins[name] + j * channels:begins[name] + (j + 1) * channels, :]

    def bulk_of(j):
        same = jnp.zeros((channels, parts.shape[1]), F32)
        swap = same
        for g in range(1, groups):
            value = piece(g, j)
            same = same + value * turn_same[g:g + 1, :]
            swap = swap + value * turn_swap[g:g + 1, :]
        return same + jnp.concatenate(
            [swap[:, NF:2 * NF], swap[:, :NF], pltpu.roll(swap[:, 2 * NF:], 64, 1)], axis=1
        )

    window = lax.broadcasted_iota(jnp.int32, (own, 1), 0)
    offsets = sum(jnp.where(window == w, offs[w], 0) for w in range(own))
    lane = lax.broadcasted_iota(jnp.int32, (1, NF), 1)
    outer_lane = lax.broadcasted_iota(jnp.int32, (1, 128), 1)
    outer_bin = jnp.where((outer_lane == 0) | (outer_lane == 64), K0 - 1, K0 + NF)

    def turn(bins):
        angle = jnp.bitwise_and(bins * offsets, L - 1).astype(F32) * (TWO_PI / L)
        return jnp.cos(angle), jnp.sin(angle)

    cos_turn, sin_turn = turn(lane + K0)
    cos_outer, sin_outer = turn(outer_bin)
    sign = 1.0 - 2.0 * jnp.bitwise_and(lane + K0, 1).astype(F32)
    sign_outer = 1.0 - 2.0 * jnp.bitwise_and(outer_bin, 1).astype(F32)
    channel = lax.broadcasted_iota(jnp.int32, (channels, 1), 0)
    live = 1.0 - sum(jnp.where(channel == i, dead[i], 0) for i in range(channels)).astype(F32)

    signs = jnp.concatenate([sign, sign, sign_outer], axis=1)
    reals, imags, magnitudes = [], [], []
    following = bulk_of(0)
    for w in range(own):
        spec = following + piece("edge", w)
        if w + 1 < bulk:
            following = bulk_of(w + 1)
            spec = spec + (following + piece(0, w + 1)) * signs
        spec = spec * live
        outer = spec[:, 2 * NF:]
        c, s = cos_turn[w:w + 1], sin_turn[w:w + 1]
        c_outer, s_outer = cos_outer[w:w + 1], sin_outer[w:w + 1]
        outer_imag = pltpu.roll(outer, 64, 1)

        def hann(inner, ends):
            ends = jnp.concatenate([ends, ends], axis=1)
            before = jnp.where(lane == 0, ends, pltpu.roll(inner, 1, 1))
            behind = jnp.where(lane == NF - 1, ends, pltpu.roll(inner, NF - 1, 1))
            return 0.5 * inner - 0.25 * (before + behind)

        real = hann(
            spec[:, :NF] * c - spec[:, NF:2 * NF] * s, outer * c_outer - outer_imag * s_outer
        )
        imag = hann(
            spec[:, :NF] * s + spec[:, NF:2 * NF] * c, outer * s_outer + outer_imag * c_outer
        )
        reals.append(real)
        imags.append(imag)
        magnitudes.append(jnp.sqrt(real * real + imag * imag + 1e-12))
    m_high, m_low = split(jnp.concatenate(magnitudes, axis=0))
    smooth = (dot(m_high, smooth_band) + dot(m_low, smooth_band)) * inverse_count
    scale = 1.0 / (smooth + EPS)
    flip = flip_matrix(channels)
    for w in range(own):
        here = slice(w * channels, (w + 1) * channels)
        white = jnp.concatenate([reals[w] * scale[here], imags[w] * scale[here]], axis=1)
        out[:, w * 2 * NF:(w + 1) * 2 * NF] = dot(flip, white.astype(BF16)).astype(BF16)


def flip_matrix(channels):
    row = lax.broadcasted_iota(jnp.int32, (channels, channels), 0)
    column = lax.broadcasted_iota(jnp.int32, (channels, channels), 1)
    return (row + column == channels - 1).astype(F32).astype(BF16)


def rotate_kernel(lags, own, cos_lag, sin_lag, out):
    channels = own.shape[0]
    straight = dot(flip_matrix(channels), own[...])
    real, imag = straight[:, :NF], straight[:, NF:]
    for t in range(lags):
        c, s = cos_lag[t:t + 1, :], sin_lag[t:t + 1, :]
        here = slice(t * channels, (t + 1) * channels)
        out[here, :NF] = (real * c - imag * s).astype(BF16)
        out[here, NF:] = (real * s + imag * c).astype(BF16)


def fill_slots(channels, partners, present, absent, sems):
    last = NPART // channels - 1

    def place(slot):
        return pl.ds(pl.multiple_of((last - slot) * channels, channels), channels)

    copies = [
        pltpu.make_async_copy(source, partners.at[place(slot), :], sems.at[i])
        for i, (source, slot) in enumerate(present)
    ]
    for copy in copies:
        copy.start()
    for slot in absent:
        partners[place(slot), :] = jnp.zeros((channels, partners.shape[1]), BF16)
    for copy in copies:
        copy.wait()


def early_slots(place, channels, blocks, partners, sems):
    own, ahead = blocks
    fill_slots(channels, partners, [(own, 0), (ahead, 4)], (1, 2, 3, 5, 6, 7), sems)


def late_slots(place, channels, blocks, partners, sems):
    core = lax.rem(place[0], 2)
    side = lax.rem(place[0] // 2, 2)
    (own_swapped, ahead_swapped, far, far_swapped, cross, cross_swapped, other,
     other_swapped) = blocks
    cross_slot = 6 - 4 * side
    other_slot = 8 - cross_slot
    step = 1 - 2 * core
    both = [(far, 0), (cross, cross_slot), (other, other_slot), (ahead_swapped, 4 + step),
            (cross_swapped, cross_slot + step), (other_swapped, other_slot + step)]

    @pl.when(core == 0)
    def _():
        fill_slots(channels, partners, both + [(own_swapped, 1)], (4,), sems)

    @pl.when(core == 1)
    def _():
        fill_slots(channels, partners, both + [(far_swapped, 7)], (4,), sems)


def product_kernel(late, norm_scale, place, rotated, *refs):
    refs = list(refs)
    before = refs.pop(0) if late else None
    out, partners, total, sems = refs[-4:]
    blocks = refs[:-4]
    channels = blocks[0].shape[0]
    (late_slots if late else early_slots)(place, channels, blocks, partners, sems)
    rows, features = rotated.shape
    chunk = 2 * 2 * NF
    for begin in range(0, features, chunk):
        turned = partners[:, begin:begin + chunk].T
        product = dot(rotated[:, begin:begin + chunk], turned)
        if begin == 0:
            total[...] = product
        else:
            total[...] += product

    row = lax.broadcasted_iota(jnp.int32, (channels, NPART), 0)
    column = lax.broadcasted_iota(jnp.int32, (channels, NPART), 1)
    low = row + column >= NPART - 1
    keep = (low | (column < NPART - channels)) if late else jnp.logical_not(low)
    sheared = []
    for begin in range(0, rows, channels):
        here = slice(begin, begin + channels)
        value = jnp.where(keep, total[here, :], 0.0)
        if late:
            value = (value + before[here, :]) * norm_scale
            sheared.append(pltpu.roll(value, 1, 1, stride=1, stride_axis=0).astype(BF16))
        else:
            out[here, :] = value
    if late:
        sheared = jnp.concatenate(sheared, axis=0)
        out[...] = dot(sheared, flip_matrix(NPART)).astype(BF16)


def exchange(value, pairs):
    return lax.ppermute(value, "chan", pairs)


def local(records, dead_mask, offsets):
    channels, samples = records.shape
    tm_count = lax.axis_size("tm")
    tm_index = lax.axis_index("tm")
    chan_count = lax.axis_size("chan")
    own = samples // HOP
    windows = own * tm_count
    halves = own
    halo = 0
    if tm_count > 1:
        reach = 2 * HOP + H
        left = lax.ppermute(
            records[:, samples - H:], "tm", [(i, i + 1) for i in range(tm_count - 1)]
        )
        right = lax.ppermute(
            records[:, :reach], "tm", [(i + 1, i) for i in range(tm_count - 1)]
        )
        records = jnp.concatenate([left, records, right], axis=1)
        halves = own + 2
        halo = H
    table = jnp.asarray(packed_tables())
    own_offsets = lax.dynamic_slice_in_dim(offsets, tm_index * own, own, 0)
    vmem = pl.BlockSpec(memory_space=pltpu.VMEM)
    smem = pl.BlockSpec(memory_space=pltpu.SMEM)
    hbm = pl.BlockSpec(memory_space=pl.ANY)
    params = pltpu.CompilerParams(vmem_limit_bytes=24 * 1024 * 1024)

    bulk = min(own + 1, halves)
    part_rows = (own + bulk * (HOP // GROUP)) * channels
    spectra = pl.pallas_call(
        functools.partial(spectra_kernel, halves, own, halo),
        name="spectra",
        out_shape=jax.ShapeDtypeStruct((channels, own * 2 * NF), BF16),
        in_specs=[smem, smem, hbm, hbm],
        out_specs=vmem,
        scratch_shapes=[
            pltpu.VMEM((channels, halves * HOP + 2 * H), F32),
            pltpu.VMEM((channels, halves * HOP + 2 * H), BF16),
            pltpu.VMEM((part_rows, GROUP), BF16),
            pltpu.VMEM((part_rows, GROUP), BF16),
            pltpu.VMEM((part_rows, 2 * NF + 128), F32),
            pltpu.VMEM(table.shape, BF16),
            pltpu.SemaphoreType.DMA((2 * halves + 1,)),
        ],
        compiler_params=pltpu.CompilerParams(vmem_limit_bytes=60 * 1024 * 1024),
        cost_estimate=pl.CostEstimate(
            flops=7_000_000_000, bytes_accessed=8 * 1024 * 1024, transcendentals=0
        ),
    )(dead_mask, own_offsets, records, table)
    if tm_count > 1:
        spectra = lax.all_gather(spectra, "tm", axis=1, tiled=True)

    lags = NLAG // tm_count
    cos_lag, sin_lag = (
        lax.dynamic_slice_in_dim(jnp.asarray(t), tm_index * lags, lags, 0) for t in lag_tables()
    )
    place = lax.axis_index("chan").astype(jnp.int32).reshape(1)
    norm_scale = 1.0 / math.sqrt(2.0 * NF * windows)

    features = spectra.shape[1]
    rotated = pl.pallas_call(
        functools.partial(rotate_kernel, lags),
        name="rotate",
        grid=(windows,),
        out_shape=jax.ShapeDtypeStruct((lags * channels, features), BF16),
        in_specs=[
            pl.BlockSpec((channels, 2 * NF), lambda w: (0, w)),
            pl.BlockSpec((lags, NF), lambda w: (0, 0)),
            pl.BlockSpec((lags, NF), lambda w: (0, 0)),
        ],
        out_specs=pl.BlockSpec((lags * channels, 2 * NF), lambda w: (0, w)),
        compiler_params=params,
        cost_estimate=pl.CostEstimate(
            flops=4_000_000_000, bytes_accessed=8 * 1024 * 1024, transcendentals=0
        ),
    )(spectra, cos_lag, sin_lag)

    def product(blocks, before):
        late = before is not None
        operands = [place, rotated] + ([before] if late else []) + list(blocks)
        return pl.pallas_call(
            functools.partial(product_kernel, late, norm_scale),
            name="late_product" if late else "early_product",
            out_shape=jax.ShapeDtypeStruct((lags * channels, NPART), BF16 if late else F32),
            in_specs=[smem, vmem] + ([vmem] if late else []) + [hbm] * len(blocks),
            out_specs=vmem,
            scratch_shapes=[
                pltpu.VMEM((NPART, features), BF16),
                pltpu.VMEM((lags * channels, NPART), F32),
                pltpu.SemaphoreType.DMA((len(blocks),)),
            ],
            compiler_params=params,
            cost_estimate=pl.CostEstimate(
                flops=2 * lags * channels * features * NPART, bytes_accessed=6 * 1024 * 1024,
                transcendentals=0,
            ),
        )(*operands)

    every = range(chan_count)
    down = [(i, i - 4) for i in every if i >= 4]
    down_2 = [(i, i - 2) for i in every if i >= 2]
    across = [(i, i ^ 2) for i in every]
    cores = [(i, i ^ 1) for i in every]
    side = lax.rem(lax.axis_index("chan") // 2, 2)

    ahead = exchange(spectra, down)
    ahead, rotated = lax.optimization_barrier((ahead, rotated))
    other = exchange(jnp.where(side == 0, ahead, spectra), down_2)
    cross = exchange(ahead, across)
    far = exchange(ahead, down)
    early = product((spectra, ahead), None)
    kept, ahead, other, early = lax.optimization_barrier((spectra, ahead, other, early))
    own_swapped = exchange(kept, [(i, j) for i, j in cores if j < i])
    ahead_swapped = exchange(ahead, cores)
    cross, own_swapped, ahead_swapped = lax.optimization_barrier(
        (cross, own_swapped, ahead_swapped)
    )
    far_swapped = exchange(far, [(i, j) for i, j in cores if j > i])
    blocks = (own_swapped, ahead_swapped, far, far_swapped, cross, exchange(cross, cores),
              other, exchange(other, cores))
    return product(blocks, early).reshape(lags, channels, NPART)


def solution(mesh):
    return jax.shard_map(
        local,
        mesh=mesh,
        in_specs=(P(("win", "chan"), "tm"), P(("win", "chan")), P("win")),
        out_specs=P("tm", ("win", "chan"), None),
        check_vma=False,
    )
```

```python
import functools
import math

import jax
import jax.numpy as jnp
import ml_dtypes
import numpy as np
from jax import lax
from jax.experimental import pallas as pl
from jax.experimental.pallas import tpu as pltpu
from jax.sharding import PartitionSpec as P

L = 8192
HOP = 4096
H = 128
K0 = 32
NF = 256
WB = 64
NLAG = 32
NPART = 256
EDGE = 512
STEP = 256
GROUP = 512
EPS = 1e-05
TWO_PI = 2.0 * math.pi
BF16 = jnp.bfloat16
F32 = jnp.float32


def split_table(table):
    high = table.astype(ml_dtypes.bfloat16)
    low = (table - high.astype(np.float64)).astype(ml_dtypes.bfloat16)
    return high, low


@functools.cache
def fourier_tables():
    samples = np.arange(GROUP)[:, None]
    bins = K0 + np.arange(NF)[None, :]
    angle = (samples * bins % L) * (TWO_PI / L)
    inner = np.concatenate([np.cos(angle), -np.sin(angle)], axis=1)
    outer = np.zeros((GROUP, 128))
    for lane, k, wave in ((0, K0 - 1, np.cos), (64, K0 - 1, np.sin), (127, K0 + NF, np.cos), (63, K0 + NF, np.sin)):
        sign = 1.0 if wave is np.cos else -1.0
        outer[:, lane] = sign * wave((samples[:, 0] * k % L) * (TWO_PI / L))
    high, low = split_table(inner)
    return np.concatenate([high, outer.astype(ml_dtypes.bfloat16)], axis=1), low


@functools.cache
def packed_tables():
    return np.concatenate(fourier_tables(), axis=1)


@functools.cache
def lag_tables():
    lags = np.arange(NLAG)[:, None] - NLAG // 2
    angle = (lags * (K0 + np.arange(NF))[None, :] % L) * (TWO_PI / L)
    return np.cos(angle).astype(np.float32), np.sin(angle).astype(np.float32)


def split(value):
    high = value.astype(BF16)
    return high, (value - high.astype(F32)).astype(BF16)


def inverse(value):
    guess = pl.reciprocal(value, approx=True)
    return guess * (2.0 - value * guess)


def dot(a, b):
    return jnp.dot(a, b, preferred_element_type=F32)


def spectra_kernel(
    halves, own, halo,
    dead, offs, x_hbm, table_hbm, out, x, absolute, norm_high, norm_low, parts, table, sems,
):
    channels = x.shape[0]
    groups = HOP // GROUP
    bulk = min(own + 1, halves)
    edges = min(own + 2, halves)
    width = halves * HOP
    middle = HOP // 2 + H
    firsts, seconds = [], []
    for j in range(halves):
        firsts.append((j * HOP - (H if j or halo else 0), j * HOP + middle))
        seconds.append((j * HOP + middle, (j + 1) * HOP - H if j + 1 < halves else width + halo))
    copies = [
        pltpu.make_async_copy(
            x_hbm.at[:, pl.ds(halo + begin, end - begin)], x.at[:, pl.ds(H + begin, end - begin)],
            sems.at[i],
        )
        for i, (begin, end) in enumerate(firsts + seconds)
    ]
    table_copy = pltpu.make_async_copy(table_hbm, table, sems.at[2 * halves])
    for copy in copies[:halves] + [table_copy] + copies[halves:]:
        copy.start()
    if not halo:
        for begin in (0, H + width):
            absolute[:, begin:begin + H] = jnp.zeros((channels, H), BF16)

    def arrive(ids):
        for i in ids:
            copies[i].wait()
        for i in ids:
            begin, end = (firsts + seconds)[i]
            here = slice(H + begin, H + end)
            absolute[:, here] = jnp.abs(x[:, here]).astype(BF16)

    high = table.at[:, :2 * NF + 128]
    low = table.at[:, 2 * NF + 128:]
    from_lane = lax.broadcasted_iota(jnp.int32, (2 * H + STEP, STEP), 0)
    to_lane = lax.broadcasted_iota(jnp.int32, (2 * H + STEP, STEP), 1)
    level_band = ((from_lane >= to_lane) & (from_lane <= to_lane + 2 * H)).astype(F32).astype(BF16)
    from_bin = lax.broadcasted_iota(jnp.int32, (NF, NF), 0)
    to_bin = lax.broadcasted_iota(jnp.int32, (NF, NF), 1)
    smooth_band = (jnp.abs(from_bin - to_bin) <= WB).astype(F32).astype(BF16)
    lane = lax.broadcasted_iota(jnp.int32, (1, parts.shape[1]), 1)
    outer_place = lane - 2 * NF
    outer_first = (outer_place == 0) | (outer_place == 64)
    every_bin = jnp.where(
        lane < 2 * NF, jnp.bitwise_and(lane, NF - 1) + K0, jnp.where(outer_first, K0 - 1, K0 + NF)
    )
    real_place = (lane < NF) | (outer_place == 0) | (outer_place == 127)
    group = lax.broadcasted_iota(jnp.int32, (groups, 1), 0) * GROUP
    angle = jnp.bitwise_and(group * every_bin, L - 1).astype(F32) * (TWO_PI / L)
    turn_same = jnp.cos(angle)
    turn_swap = jnp.sin(angle) * jnp.where(real_place, -1.0, 1.0)
    bin_index = lax.broadcasted_iota(jnp.int32, (1, NF), 1)
    below, above = jnp.minimum(bin_index, WB), jnp.minimum(NF - 1 - bin_index, WB)
    inverse_count = 1.0 / (below + above + 1).astype(F32)

    def rows(ref, begin, length, count):
        return [ref[:, begin + j * HOP:begin + j * HOP + length] for j in range(count)]

    def store(place, value):
        here = slice(place, place + value.shape[0])
        norm_high[here, :], norm_low[here, :] = split(value)

    def normalise(group_ids, place):
        blocks = [(g, g * GROUP + part * STEP) for g in group_ids for part in range(GROUP // STEP)]
        counts = [edges if g == 0 else bulk for g, _ in blocks]
        level = dot(
            jnp.concatenate(
                [r for (_, begin), n in zip(blocks, counts)
                 for r in rows(absolute, begin, STEP + 2 * H, n)], axis=0
            ), level_band,
        ) * (1.0 / (2 * H + 1)) + EPS
        values = []
        at = 0
        for (_, begin), n in zip(blocks, counts):
            samples = jnp.concatenate(rows(x, H + begin, STEP, n), axis=0)
            values.append(samples * inverse(level[at:at + n * channels]))
            at += n * channels
        begins = {}
        for index, g in enumerate(group_ids):
            value = jnp.concatenate(values[2 * index:2 * index + 2], axis=1)
            if g == 0:
                lane = lax.broadcasted_iota(jnp.int32, (channels, EDGE), 1)
                merged = []
                for w in range(own):
                    mine = value[w * channels:(w + 1) * channels]
                    other = (
                        value[(w + 2) * channels:(w + 3) * channels]
                        if w + 2 < edges else jnp.zeros_like(mine)
                    )
                    merged.append(jnp.where(lane >= offs[w], mine, other))
                begins["edge"] = place
                store(place, jnp.concatenate(merged, axis=0))
                place += own * channels
                value = value[:bulk * channels]
            begins[g] = place
            store(place, value)
            place += bulk * channels
        return begins, place

    def transform(begin, end):
        first = dot(norm_high[begin:end, :], high[...])
        second = dot(norm_low[begin:end, :], high[:, :2 * NF])
        second = second + dot(norm_high[begin:end, :], low[...])
        parts[begin:end, :2 * NF] = first[:, :2 * NF] + second
        parts[begin:end, 2 * NF:] = first[:, 2 * NF:]

    begins = {}
    place = 0
    waiting = None
    arrive(range(halves))
    table_copy.wait()
    for g in range(0, groups, 2):
        if g == groups // 2:
            arrive(range(halves, 2 * halves))
        start = place
        found, place = normalise([g, g + 1], place)
        begins.update(found)
        if waiting:
            transform(*waiting)
        waiting = (start, place)
    transform(*waiting)

    def piece(name, j):
        return parts[begins[name] + j * channels:begins[name] + (j + 1) * channels, :]

    def bulk_of(j):
        same = jnp.zeros((channels, parts.shape[1]), F32)
        swap = same
        for g in range(1, groups):
            value = piece(g, j)
            same = same + value * turn_same[g:g + 1, :]
            swap = swap + value * turn_swap[g:g + 1, :]
        return same + jnp.concatenate(
            [swap[:, NF:2 * NF], swap[:, :NF], pltpu.roll(swap[:, 2 * NF:], 64, 1)], axis=1
        )

    window = lax.broadcasted_iota(jnp.int32, (own, 1), 0)
    offsets = sum(jnp.where(window == w, offs[w], 0) for w in range(own))
    lane = lax.broadcasted_iota(jnp.int32, (1, NF), 1)
    outer_lane = lax.broadcasted_iota(jnp.int32, (1, 128), 1)
    outer_bin = jnp.where((outer_lane == 0) | (outer_lane == 64), K0 - 1, K0 + NF)

    def turn(bins):
        angle = jnp.bitwise_and(bins * offsets, L - 1).astype(F32) * (TWO_PI / L)
        return jnp.cos(angle), jnp.sin(angle)

    cos_turn, sin_turn = turn(lane + K0)
    cos_outer, sin_outer = turn(outer_bin)
    sign = 1.0 - 2.0 * jnp.bitwise_and(lane + K0, 1).astype(F32)
    sign_outer = 1.0 - 2.0 * jnp.bitwise_and(outer_bin, 1).astype(F32)
    channel = lax.broadcasted_iota(jnp.int32, (channels, 1), 0)
    live = 1.0 - sum(jnp.where(channel == i, dead[i], 0) for i in range(channels)).astype(F32)

    signs = jnp.concatenate([sign, sign, sign_outer], axis=1)
    reals, imags, magnitudes = [], [], []
    following = bulk_of(0)
    for w in range(own):
        spec = following + piece("edge", w)
        if w + 1 < bulk:
            following = bulk_of(w + 1)
            spec = spec + (following + piece(0, w + 1)) * signs
        spec = spec * live
        outer = spec[:, 2 * NF:]
        c, s = cos_turn[w:w + 1], sin_turn[w:w + 1]
        c_outer, s_outer = cos_outer[w:w + 1], sin_outer[w:w + 1]
        outer_imag = pltpu.roll(outer, 64, 1)

        def hann(inner, ends):
            ends = jnp.concatenate([ends, ends], axis=1)
            before = jnp.where(lane == 0, ends, pltpu.roll(inner, 1, 1))
            behind = jnp.where(lane == NF - 1, ends, pltpu.roll(inner, NF - 1, 1))
            return 0.5 * inner - 0.25 * (before + behind)

        real = hann(
            spec[:, :NF] * c - spec[:, NF:2 * NF] * s, outer * c_outer - outer_imag * s_outer
        )
        imag = hann(
            spec[:, :NF] * s + spec[:, NF:2 * NF] * c, outer * s_outer + outer_imag * c_outer
        )
        reals.append(real)
        imags.append(imag)
        magnitudes.append(jnp.sqrt(real * real + imag * imag + 1e-12))
    m_high, m_low = split(jnp.concatenate(magnitudes, axis=0))
    smooth = (dot(m_high, smooth_band) + dot(m_low, smooth_band)) * inverse_count
    scale = 1.0 / (smooth + EPS)
    flip = flip_matrix(channels)
    for w in range(own):
        here = slice(w * channels, (w + 1) * channels)
        white = jnp.concatenate([reals[w] * scale[here], imags[w] * scale[here]], axis=1)
        out[:, w * 2 * NF:(w + 1) * 2 * NF] = dot(flip, white.astype(BF16)).astype(BF16)


def flip_matrix(channels):
    row = lax.broadcasted_iota(jnp.int32, (channels, channels), 0)
    column = lax.broadcasted_iota(jnp.int32, (channels, channels), 1)
    return (row + column == channels - 1).astype(F32).astype(BF16)


def rotate_kernel(lags, own, cos_lag, sin_lag, out):
    channels = own.shape[0]
    straight = dot(flip_matrix(channels), own[...])
    real, imag = straight[:, :NF], straight[:, NF:]
    for t in range(lags):
        c, s = cos_lag[t:t + 1, :], sin_lag[t:t + 1, :]
        here = slice(t * channels, (t + 1) * channels)
        out[here, :NF] = (real * c - imag * s).astype(BF16)
        out[here, NF:] = (real * s + imag * c).astype(BF16)


def put_slots(channels, partners, present, absent):
    last = NPART // channels - 1

    def place(slot):
        return pl.ds(pl.multiple_of((last - slot) * channels, channels), channels)

    for block, slot in present:
        partners[place(slot), :] = block[...]
    for slot in absent:
        partners[place(slot), :] = jnp.zeros((channels, partners.shape[1]), BF16)


def early_slots(place, channels, blocks, partners):
    own, ahead = blocks
    put_slots(channels, partners, [(own, 0), (ahead, 4)], (1, 2, 3, 5, 6, 7))


def late_slots(place, channels, blocks, partners):
    core = lax.rem(place[0], 2)
    side = lax.rem(place[0] // 2, 2)
    (own_swapped, ahead_swapped, far, far_swapped, cross, cross_swapped, other,
     other_swapped) = blocks
    cross_slot = 6 - 4 * side
    other_slot = 8 - cross_slot
    step = 1 - 2 * core
    both = [(far, 0), (cross, cross_slot), (other, other_slot), (ahead_swapped, 4 + step),
            (cross_swapped, cross_slot + step), (other_swapped, other_slot + step)]
    put_slots(channels, partners, both, (4,))

    @pl.when(core == 0)
    def _():
        put_slots(channels, partners, [(own_swapped, 1)], ())

    @pl.when(core == 1)
    def _():
        put_slots(channels, partners, [(far_swapped, 7)], ())


def product_kernel(late, norm_scale, place, rotated, *refs):
    refs = list(refs)
    before = refs.pop(0) if late else None
    out, partners, total = refs[-3:]
    blocks = refs[:-3]
    channels = blocks[0].shape[0]
    (late_slots if late else early_slots)(place, channels, blocks, partners)
    rows, features = rotated.shape
    chunk = 2 * 2 * NF
    for begin in range(0, features, chunk):
        turned = partners[:, begin:begin + chunk].T
        product = dot(rotated[:, begin:begin + chunk], turned)
        if begin == 0:
            total[...] = product
        else:
            total[...] += product

    row = lax.broadcasted_iota(jnp.int32, (channels, NPART), 0)
    column = lax.broadcasted_iota(jnp.int32, (channels, NPART), 1)
    low = row + column >= NPART - 1
    keep = (low | (column < NPART - channels)) if late else jnp.logical_not(low)
    sheared = []
    for begin in range(0, rows, channels):
        here = slice(begin, begin + channels)
        value = jnp.where(keep, total[here, :], 0.0)
        if late:
            value = (value + before[here, :]) * norm_scale
            sheared.append(pltpu.roll(value, 1, 1, stride=1, stride_axis=0).astype(BF16))
        else:
            out[here, :] = value
    if late:
        sheared = jnp.concatenate(sheared, axis=0)
        out[...] = dot(sheared, flip_matrix(NPART)).astype(BF16)


def exchange(value, pairs):
    return lax.ppermute(value, "chan", pairs)


def local(records, dead_mask, offsets):
    channels, samples = records.shape
    tm_count = lax.axis_size("tm")
    tm_index = lax.axis_index("tm")
    chan_count = lax.axis_size("chan")
    own = samples // HOP
    windows = own * tm_count
    halves = own
    halo = 0
    if tm_count > 1:
        reach = 2 * HOP + H
        left = lax.ppermute(
            records[:, samples - H:], "tm", [(i, i + 1) for i in range(tm_count - 1)]
        )
        right = lax.ppermute(
            records[:, :reach], "tm", [(i + 1, i) for i in range(tm_count - 1)]
        )
        records = jnp.concatenate([left, records, right], axis=1)
        halves = own + 2
        halo = H
    table = jnp.asarray(packed_tables())
    own_offsets = lax.dynamic_slice_in_dim(offsets, tm_index * own, own, 0)
    vmem = pl.BlockSpec(memory_space=pltpu.VMEM)
    smem = pl.BlockSpec(memory_space=pltpu.SMEM)
    hbm = pl.BlockSpec(memory_space=pl.ANY)
    params = pltpu.CompilerParams(vmem_limit_bytes=24 * 1024 * 1024)

    bulk = min(own + 1, halves)
    part_rows = (own + bulk * (HOP // GROUP)) * channels
    spectra = pl.pallas_call(
        functools.partial(spectra_kernel, halves, own, halo),
        name="spectra",
        out_shape=jax.ShapeDtypeStruct((channels, own * 2 * NF), BF16),
        in_specs=[smem, smem, hbm, hbm],
        out_specs=vmem,
        scratch_shapes=[
            pltpu.VMEM((channels, halves * HOP + 2 * H), F32),
            pltpu.VMEM((channels, halves * HOP + 2 * H), BF16),
            pltpu.VMEM((part_rows, GROUP), BF16),
            pltpu.VMEM((part_rows, GROUP), BF16),
            pltpu.VMEM((part_rows, 2 * NF + 128), F32),
            pltpu.VMEM(table.shape, BF16),
            pltpu.SemaphoreType.DMA((2 * halves + 1,)),
        ],
        compiler_params=pltpu.CompilerParams(vmem_limit_bytes=60 * 1024 * 1024),
        cost_estimate=pl.CostEstimate(
            flops=7_000_000_000, bytes_accessed=8 * 1024 * 1024, transcendentals=0
        ),
    )(dead_mask, own_offsets, records, table)
    if tm_count > 1:
        spectra = lax.all_gather(spectra, "tm", axis=1, tiled=True)

    lags = NLAG // tm_count
    cos_lag, sin_lag = (
        lax.dynamic_slice_in_dim(jnp.asarray(t), tm_index * lags, lags, 0) for t in lag_tables()
    )
    place = lax.axis_index("chan").astype(jnp.int32).reshape(1)
    norm_scale = 1.0 / math.sqrt(2.0 * NF * windows)

    features = spectra.shape[1]
    rotated = pl.pallas_call(
        functools.partial(rotate_kernel, lags),
        name="rotate",
        grid=(windows,),
        out_shape=jax.ShapeDtypeStruct((lags * channels, features), BF16),
        in_specs=[
            pl.BlockSpec((channels, 2 * NF), lambda w: (0, w)),
            pl.BlockSpec((lags, NF), lambda w: (0, 0)),
            pl.BlockSpec((lags, NF), lambda w: (0, 0)),
        ],
        out_specs=pl.BlockSpec((lags * channels, 2 * NF), lambda w: (0, w)),
        compiler_params=params,
        cost_estimate=pl.CostEstimate(
            flops=4_000_000_000, bytes_accessed=8 * 1024 * 1024, transcendentals=0
        ),
    )(spectra, cos_lag, sin_lag)

    def product(blocks, before):
        late = before is not None
        operands = [place, rotated] + ([before] if late else []) + list(blocks)
        return pl.pallas_call(
            functools.partial(product_kernel, late, norm_scale),
            name="late_product" if late else "early_product",
            out_shape=jax.ShapeDtypeStruct((lags * channels, NPART), BF16 if late else F32),
            in_specs=[smem] + [vmem] * (len(operands) - 1),
            out_specs=vmem,
            scratch_shapes=[
                pltpu.VMEM((NPART, features), BF16),
                pltpu.VMEM((lags * channels, NPART), F32),
            ],
            compiler_params=params,
            cost_estimate=pl.CostEstimate(
                flops=2 * lags * channels * features * NPART, bytes_accessed=6 * 1024 * 1024,
                transcendentals=0,
            ),
        )(*operands)

    every = range(chan_count)
    down = [(i, i - 4) for i in every if i >= 4]
    to_low_side = [(i, i - 2) for i in every if i & 2]
    to_high_side = [(i, i - 2) for i in every if i >= 4 and not i & 2]
    across = [(i, i ^ 2) for i in every]
    cores = [(i, i ^ 1) for i in every]
    side = lax.rem(lax.axis_index("chan") // 2, 2)

    ahead = exchange(spectra, down)
    beside = exchange(lax.optimization_barrier(spectra), to_low_side)
    ahead, rotated = lax.optimization_barrier((ahead, rotated))
    other = jnp.where(side == 0, beside, exchange(ahead, to_high_side))
    cross = exchange(ahead, across)
    far = exchange(ahead, down)
    early = product((spectra, ahead), None)
    kept, ahead, other, early = lax.optimization_barrier((spectra, ahead, other, early))
    own_swapped = exchange(kept, [(i, j) for i, j in cores if j < i])
    ahead_swapped = exchange(ahead, cores)
    cross, own_swapped, ahead_swapped = lax.optimization_barrier(
        (cross, own_swapped, ahead_swapped)
    )
    far_swapped = exchange(far, [(i, j) for i, j in cores if j > i])
    blocks = (own_swapped, ahead_swapped, far, far_swapped, cross, exchange(cross, cores),
              other, exchange(other, cores))
    return product(blocks, early).reshape(lags, channels, NPART)


def solution(mesh):
    return jax.shard_map(
        local,
        mesh=mesh,
        in_specs=(P(("win", "chan"), "tm"), P(("win", "chan")), P("win")),
        out_specs=P("tm", ("win", "chan"), None),
        check_vma=False,
    )
```

```python
import functools
import math

import jax
import jax.numpy as jnp
import ml_dtypes
import numpy as np
from jax import lax
from jax.experimental import pallas as pl
from jax.experimental.pallas import tpu as pltpu
from jax.sharding import PartitionSpec as P

L = 8192
HOP = 4096
H = 128
K0 = 32
NF = 256
WB = 64
NLAG = 32
NPART = 256
EDGE = 512
STEP = 256
GROUP = 512
EPS = 1e-05
TWO_PI = 2.0 * math.pi
BF16 = jnp.bfloat16
F32 = jnp.float32


def split_table(table):
    high = table.astype(ml_dtypes.bfloat16)
    low = (table - high.astype(np.float64)).astype(ml_dtypes.bfloat16)
    return high, low


@functools.cache
def fourier_tables():
    samples = np.arange(GROUP)[:, None]
    bins = K0 + np.arange(NF)[None, :]
    angle = (samples * bins % L) * (TWO_PI / L)
    inner = np.concatenate([np.cos(angle), -np.sin(angle)], axis=1)
    outer = np.zeros((GROUP, 128))
    for lane, k, wave in ((0, K0 - 1, np.cos), (64, K0 - 1, np.sin), (127, K0 + NF, np.cos), (63, K0 + NF, np.sin)):
        sign = 1.0 if wave is np.cos else -1.0
        outer[:, lane] = sign * wave((samples[:, 0] * k % L) * (TWO_PI / L))
    high, low = split_table(inner)
    return np.concatenate([high, outer.astype(ml_dtypes.bfloat16)], axis=1), low


@functools.cache
def packed_tables():
    return np.concatenate(fourier_tables(), axis=1)


@functools.cache
def lag_tables():
    lags = np.arange(NLAG)[:, None] - NLAG // 2
    angle = (lags * (K0 + np.arange(NF))[None, :] % L) * (TWO_PI / L)
    return np.cos(angle).astype(np.float32), np.sin(angle).astype(np.float32)


def split(value):
    high = value.astype(BF16)
    return high, (value - high.astype(F32)).astype(BF16)


def inverse(value):
    guess = pl.reciprocal(value, approx=True)
    return guess * (2.0 - value * guess)


def dot(a, b):
    return jnp.dot(a, b, preferred_element_type=F32)


def spectra_kernel(
    halves, own, halo,
    dead, offs, x_hbm, table_hbm, out, x, absolute, norm_high, norm_low, parts, table, sems,
):
    channels = x.shape[0]
    groups = HOP // GROUP
    bulk = min(own + 1, halves)
    edges = min(own + 2, halves)
    width = halves * HOP
    middle = HOP // 2 + H
    firsts, seconds = [], []
    for j in range(halves):
        firsts.append((j * HOP - (H if j or halo else 0), j * HOP + middle))
        seconds.append((j * HOP + middle, (j + 1) * HOP - H if j + 1 < halves else width + halo))
    copies = [
        pltpu.make_async_copy(
            x_hbm.at[:, pl.ds(halo + begin, end - begin)], x.at[:, pl.ds(H + begin, end - begin)],
            sems.at[i],
        )
        for i, (begin, end) in enumerate(firsts + seconds)
    ]
    table_copy = pltpu.make_async_copy(table_hbm, table, sems.at[2 * halves])
    for copy in copies[:halves] + [table_copy] + copies[halves:]:
        copy.start()
    if not halo:
        for begin in (0, H + width):
            absolute[:, begin:begin + H] = jnp.zeros((channels, H), BF16)

    def arrive(ids):
        for i in ids:
            copies[i].wait()
        for i in ids:
            begin, end = (firsts + seconds)[i]
            here = slice(H + begin, H + end)
            absolute[:, here] = jnp.abs(x[:, here]).astype(BF16)

    high = table.at[:, :2 * NF + 128]
    low = table.at[:, 2 * NF + 128:]
    from_lane = lax.broadcasted_iota(jnp.int32, (2 * H + STEP, STEP), 0)
    to_lane = lax.broadcasted_iota(jnp.int32, (2 * H + STEP, STEP), 1)
    level_band = ((from_lane >= to_lane) & (from_lane <= to_lane + 2 * H)).astype(F32).astype(BF16)
    from_bin = lax.broadcasted_iota(jnp.int32, (NF, NF), 0)
    to_bin = lax.broadcasted_iota(jnp.int32, (NF, NF), 1)
    smooth_band = (jnp.abs(from_bin - to_bin) <= WB).astype(F32).astype(BF16)
    lane = lax.broadcasted_iota(jnp.int32, (1, parts.shape[1]), 1)
    outer_place = lane - 2 * NF
    outer_first = (outer_place == 0) | (outer_place == 64)
    every_bin = jnp.where(
        lane < 2 * NF, jnp.bitwise_and(lane, NF - 1) + K0, jnp.where(outer_first, K0 - 1, K0 + NF)
    )
    real_place = (lane < NF) | (outer_place == 0) | (outer_place == 127)
    group = lax.broadcasted_iota(jnp.int32, (groups, 1), 0) * GROUP
    angle = jnp.bitwise_and(group * every_bin, L - 1).astype(F32) * (TWO_PI / L)
    turn_same = jnp.cos(angle)
    turn_swap = jnp.sin(angle) * jnp.where(real_place, -1.0, 1.0)
    bin_index = lax.broadcasted_iota(jnp.int32, (1, NF), 1)
    below, above = jnp.minimum(bin_index, WB), jnp.minimum(NF - 1 - bin_index, WB)
    inverse_count = 1.0 / (below + above + 1).astype(F32)

    def rows(ref, begin, length, count):
        return [ref[:, begin + j * HOP:begin + j * HOP + length] for j in range(count)]

    def store(place, value):
        here = slice(place, place + value.shape[0])
        norm_high[here, :], norm_low[here, :] = split(value)

    def normalise(group_ids, place):
        blocks = [(g, g * GROUP + part * STEP) for g in group_ids for part in range(GROUP // STEP)]
        counts = [edges if g == 0 else bulk for g, _ in blocks]
        level = dot(
            jnp.concatenate(
                [r for (_, begin), n in zip(blocks, counts)
                 for r in rows(absolute, begin, STEP + 2 * H, n)], axis=0
            ), level_band,
        ) * (1.0 / (2 * H + 1)) + EPS
        values = []
        at = 0
        for (_, begin), n in zip(blocks, counts):
            samples = jnp.concatenate(rows(x, H + begin, STEP, n), axis=0)
            values.append(samples * inverse(level[at:at + n * channels]))
            at += n * channels
        begins = {}
        for index, g in enumerate(group_ids):
            value = jnp.concatenate(values[2 * index:2 * index + 2], axis=1)
            if g == 0:
                lane = lax.broadcasted_iota(jnp.int32, (channels, EDGE), 1)
                merged = []
                for w in range(own):
                    mine = value[w * channels:(w + 1) * channels]
                    other = (
                        value[(w + 2) * channels:(w + 3) * channels]
                        if w + 2 < edges else jnp.zeros_like(mine)
                    )
                    merged.append(jnp.where(lane >= offs[w], mine, other))
                begins["edge"] = place
                store(place, jnp.concatenate(merged, axis=0))
                place += own * channels
                value = value[:bulk * channels]
            begins[g] = place
            store(place, value)
            place += bulk * channels
        return begins, place

    def transform(begin, end):
        first = dot(norm_high[begin:end, :], high[...])
        second = dot(norm_low[begin:end, :], high[:, :2 * NF])
        second = second + dot(norm_high[begin:end, :], low[...])
        parts[begin:end, :2 * NF] = first[:, :2 * NF] + second
        parts[begin:end, 2 * NF:] = first[:, 2 * NF:]

    begins = {}
    place = 0
    waiting = None
    arrive(range(halves))
    table_copy.wait()
    for g in range(0, groups, 2):
        if g == groups // 2:
            arrive(range(halves, 2 * halves))
        start = place
        found, place = normalise([g, g + 1], place)
        begins.update(found)
        if waiting:
            transform(*waiting)
        waiting = (start, place)
    transform(*waiting)

    def piece(name, j):
        return parts[begins[name] + j * channels:begins[name] + (j + 1) * channels, :]

    def bulk_of(j):
        same = jnp.zeros((channels, parts.shape[1]), F32)
        swap = same
        for g in range(1, groups):
            value = piece(g, j)
            same = same + value * turn_same[g:g + 1, :]
            swap = swap + value * turn_swap[g:g + 1, :]
        return same + jnp.concatenate(
            [swap[:, NF:2 * NF], swap[:, :NF], pltpu.roll(swap[:, 2 * NF:], 64, 1)], axis=1
        )

    window = lax.broadcasted_iota(jnp.int32, (own, 1), 0)
    offsets = sum(jnp.where(window == w, offs[w], 0) for w in range(own))
    lane = lax.broadcasted_iota(jnp.int32, (1, NF), 1)
    outer_lane = lax.broadcasted_iota(jnp.int32, (1, 128), 1)
    outer_bin = jnp.where((outer_lane == 0) | (outer_lane == 64), K0 - 1, K0 + NF)

    def turn(bins):
        angle = jnp.bitwise_and(bins * offsets, L - 1).astype(F32) * (TWO_PI / L)
        return jnp.cos(angle), jnp.sin(angle)

    cos_turn, sin_turn = turn(lane + K0)
    cos_outer, sin_outer = turn(outer_bin)
    sign = 1.0 - 2.0 * jnp.bitwise_and(lane + K0, 1).astype(F32)
    sign_outer = 1.0 - 2.0 * jnp.bitwise_and(outer_bin, 1).astype(F32)
    channel = lax.broadcasted_iota(jnp.int32, (channels, 1), 0)
    live = 1.0 - sum(jnp.where(channel == i, dead[i], 0) for i in range(channels)).astype(F32)

    signs = jnp.concatenate([sign, sign, sign_outer], axis=1)
    reals, imags, magnitudes = [], [], []
    following = bulk_of(0)
    for w in range(own):
        spec = following + piece("edge", w)
        if w + 1 < bulk:
            following = bulk_of(w + 1)
            spec = spec + (following + piece(0, w + 1)) * signs
        spec = spec * live
        outer = spec[:, 2 * NF:]
        c, s = cos_turn[w:w + 1], sin_turn[w:w + 1]
        c_outer, s_outer = cos_outer[w:w + 1], sin_outer[w:w + 1]
        outer_imag = pltpu.roll(outer, 64, 1)

        def hann(inner, ends):
            ends = jnp.concatenate([ends, ends], axis=1)
            before = jnp.where(lane == 0, ends, pltpu.roll(inner, 1, 1))
            behind = jnp.where(lane == NF - 1, ends, pltpu.roll(inner, NF - 1, 1))
            return 0.5 * inner - 0.25 * (before + behind)

        real = hann(
            spec[:, :NF] * c - spec[:, NF:2 * NF] * s, outer * c_outer - outer_imag * s_outer
        )
        imag = hann(
            spec[:, :NF] * s + spec[:, NF:2 * NF] * c, outer * s_outer + outer_imag * c_outer
        )
        reals.append(real)
        imags.append(imag)
        magnitudes.append(jnp.sqrt(real * real + imag * imag + 1e-12))
    m_high, m_low = split(jnp.concatenate(magnitudes, axis=0))
    smooth = (dot(m_high, smooth_band) + dot(m_low, smooth_band)) * inverse_count
    scale = 1.0 / (smooth + EPS)
    flip = flip_matrix(channels)
    for w in range(own):
        here = slice(w * channels, (w + 1) * channels)
        white = jnp.concatenate([reals[w] * scale[here], imags[w] * scale[here]], axis=1)
        out[:, w * 2 * NF:(w + 1) * 2 * NF] = dot(flip, white.astype(BF16)).astype(BF16)


def flip_matrix(channels):
    row = lax.broadcasted_iota(jnp.int32, (channels, channels), 0)
    column = lax.broadcasted_iota(jnp.int32, (channels, channels), 1)
    return (row + column == channels - 1).astype(F32).astype(BF16)


def rotate_kernel(lags, own, cos_lag, sin_lag, out):
    channels = own.shape[0]
    straight = dot(flip_matrix(channels), own[...])
    real, imag = straight[:, :NF], straight[:, NF:]
    for t in range(lags):
        c, s = cos_lag[t:t + 1, :], sin_lag[t:t + 1, :]
        here = slice(t * channels, (t + 1) * channels)
        out[here, :NF] = (real * c - imag * s).astype(BF16)
        out[here, NF:] = (real * s + imag * c).astype(BF16)


def put_slots(channels, partners, present, absent):
    last = NPART // channels - 1

    def place(slot):
        return pl.ds(pl.multiple_of((last - slot) * channels, channels), channels)

    for block, slot in present:
        partners[place(slot), :] = block[...]
    for slot in absent:
        partners[place(slot), :] = jnp.zeros((channels, partners.shape[1]), BF16)


def early_slots(place, channels, blocks, partners):
    own, ahead = blocks
    put_slots(channels, partners, [(own, 0), (ahead, 4)], (1, 2, 3, 5, 6, 7))


def late_slots(place, channels, blocks, partners):
    core = lax.rem(place[0], 2)
    side = lax.rem(place[0] // 2, 2)
    (own_swapped, ahead_swapped, far, far_swapped, cross, cross_swapped, other,
     other_swapped) = blocks
    cross_slot = 6 - 4 * side
    other_slot = 8 - cross_slot
    step = 1 - 2 * core
    both = [(far, 0), (cross, cross_slot), (other, other_slot), (ahead_swapped, 4 + step),
            (cross_swapped, cross_slot + step), (other_swapped, other_slot + step)]
    put_slots(channels, partners, both, (4,))

    @pl.when(core == 0)
    def _():
        put_slots(channels, partners, [(own_swapped, 1)], ())

    @pl.when(core == 1)
    def _():
        put_slots(channels, partners, [(far_swapped, 7)], ())


def product_kernel(late, norm_scale, place, rotated, *refs):
    refs = list(refs)
    before = refs.pop(0) if late else None
    out, partners, total = refs[-3:]
    blocks = refs[:-3]
    channels = blocks[0].shape[0]
    (late_slots if late else early_slots)(place, channels, blocks, partners)
    rows, features = rotated.shape
    chunk = 2 * 2 * NF
    for begin in range(0, features, chunk):
        turned = partners[:, begin:begin + chunk].T
        product = dot(rotated[:, begin:begin + chunk], turned)
        if begin == 0:
            total[...] = product
        else:
            total[...] += product

    row = lax.broadcasted_iota(jnp.int32, (channels, NPART), 0)
    column = lax.broadcasted_iota(jnp.int32, (channels, NPART), 1)
    low = row + column >= NPART - 1
    keep = (low | (column < NPART - channels)) if late else jnp.logical_not(low)
    sheared = []
    for begin in range(0, rows, channels):
        here = slice(begin, begin + channels)
        value = jnp.where(keep, total[here, :], 0.0)
        if late:
            value = (value + before[here, :]) * norm_scale
            sheared.append(pltpu.roll(value, 1, 1, stride=1, stride_axis=0).astype(BF16))
        else:
            out[here, :] = value
    if late:
        sheared = jnp.concatenate(sheared, axis=0)
        out[...] = dot(sheared, flip_matrix(NPART)).astype(BF16)


def exchange(value, pairs):
    return lax.ppermute(value, "chan", pairs)


def local(records, dead_mask, offsets):
    channels, samples = records.shape
    tm_count = lax.axis_size("tm")
    tm_index = lax.axis_index("tm")
    chan_count = lax.axis_size("chan")
    own = samples // HOP
    windows = own * tm_count
    halves = own
    halo = 0
    if tm_count > 1:
        reach = 2 * HOP + H
        left = lax.ppermute(
            records[:, samples - H:], "tm", [(i, i + 1) for i in range(tm_count - 1)]
        )
        right = lax.ppermute(
            records[:, :reach], "tm", [(i + 1, i) for i in range(tm_count - 1)]
        )
        records = jnp.concatenate([left, records, right], axis=1)
        halves = own + 2
        halo = H
    table = jnp.asarray(packed_tables())
    own_offsets = lax.dynamic_slice_in_dim(offsets, tm_index * own, own, 0)
    vmem = pl.BlockSpec(memory_space=pltpu.VMEM)
    smem = pl.BlockSpec(memory_space=pltpu.SMEM)
    hbm = pl.BlockSpec(memory_space=pl.ANY)
    params = pltpu.CompilerParams(vmem_limit_bytes=24 * 1024 * 1024)

    bulk = min(own + 1, halves)
    part_rows = (own + bulk * (HOP // GROUP)) * channels
    spectra = pl.pallas_call(
        functools.partial(spectra_kernel, halves, own, halo),
        name="spectra",
        out_shape=jax.ShapeDtypeStruct((channels, own * 2 * NF), BF16),
        in_specs=[smem, smem, hbm, hbm],
        out_specs=vmem,
        scratch_shapes=[
            pltpu.VMEM((channels, halves * HOP + 2 * H), F32),
            pltpu.VMEM((channels, halves * HOP + 2 * H), BF16),
            pltpu.VMEM((part_rows, GROUP), BF16),
            pltpu.VMEM((part_rows, GROUP), BF16),
            pltpu.VMEM((part_rows, 2 * NF + 128), F32),
            pltpu.VMEM(table.shape, BF16),
            pltpu.SemaphoreType.DMA((2 * halves + 1,)),
        ],
        compiler_params=pltpu.CompilerParams(vmem_limit_bytes=60 * 1024 * 1024),
        cost_estimate=pl.CostEstimate(
            flops=7_000_000_000, bytes_accessed=8 * 1024 * 1024, transcendentals=0
        ),
    )(dead_mask, own_offsets, records, table)
    if tm_count > 1:
        spectra = lax.all_gather(spectra, "tm", axis=1, tiled=True)

    lags = NLAG // tm_count
    cos_lag, sin_lag = (
        lax.dynamic_slice_in_dim(jnp.asarray(t), tm_index * lags, lags, 0) for t in lag_tables()
    )
    place = lax.axis_index("chan").astype(jnp.int32).reshape(1)
    norm_scale = 1.0 / math.sqrt(2.0 * NF * windows)

    features = spectra.shape[1]
    rotated = pl.pallas_call(
        functools.partial(rotate_kernel, lags),
        name="rotate",
        grid=(windows,),
        out_shape=jax.ShapeDtypeStruct((lags * channels, features), BF16),
        in_specs=[
            pl.BlockSpec((channels, 2 * NF), lambda w: (0, w)),
            pl.BlockSpec((lags, NF), lambda w: (0, 0)),
            pl.BlockSpec((lags, NF), lambda w: (0, 0)),
        ],
        out_specs=pl.BlockSpec((lags * channels, 2 * NF), lambda w: (0, w)),
        compiler_params=params,
        cost_estimate=pl.CostEstimate(
            flops=4_000_000_000, bytes_accessed=8 * 1024 * 1024, transcendentals=0
        ),
    )(spectra, cos_lag, sin_lag)

    def product(blocks, before):
        late = before is not None
        operands = [place, rotated] + ([before] if late else []) + list(blocks)
        return pl.pallas_call(
            functools.partial(product_kernel, late, norm_scale),
            name="late_product" if late else "early_product",
            out_shape=jax.ShapeDtypeStruct((lags * channels, NPART), BF16 if late else F32),
            in_specs=[smem] + [vmem] * (len(operands) - 1),
            out_specs=vmem,
            scratch_shapes=[
                pltpu.VMEM((NPART, features), BF16),
                pltpu.VMEM((lags * channels, NPART), F32),
            ],
            compiler_params=params,
            cost_estimate=pl.CostEstimate(
                flops=2 * lags * channels * features * NPART, bytes_accessed=6 * 1024 * 1024,
                transcendentals=0,
            ),
        )(*operands)

    every = range(chan_count)

    def reaches(i, levels):
        return (i // 4 + levels) * 4 < chan_count

    down = [(i, i - 4) for i in every if i >= 4]
    far_down = [(i, j) for i, j in down if reaches(i, 1)]
    down_2 = [(i, i - 2) for i in every if i >= 2 and (i & 2 or reaches(i, 1))]
    across = [(i, i ^ 2) for i in every if reaches(i, 1)]
    cores = [(i, i ^ 1) for i in every]
    side = lax.rem(lax.axis_index("chan") // 2, 2)

    ahead = exchange(spectra, down)
    ahead, rotated = lax.optimization_barrier((ahead, rotated))
    other = exchange(jnp.where(side == 0, ahead, spectra), down_2)
    cross = exchange(ahead, across)
    far = exchange(ahead, far_down)
    early = product((spectra, ahead), None)
    kept, ahead, other, early = lax.optimization_barrier((spectra, ahead, other, early))
    own_swapped = exchange(kept, [(i, j) for i, j in cores if j < i])
    ahead_swapped = exchange(ahead, [(i, j) for i, j in cores if reaches(i, 1)])
    cross, own_swapped, ahead_swapped = lax.optimization_barrier(
        (cross, own_swapped, ahead_swapped)
    )
    far_swapped = exchange(far, [(i, j) for i, j in cores if j > i and reaches(i, 2)])
    cross_swapped = exchange(cross, [(i, j) for i, j in cores if reaches(i, 1)])
    other_swapped = exchange(other, [(i, j) for i, j in cores if not i & 2 or reaches(i, 2)])
    blocks = (own_swapped, ahead_swapped, far, far_swapped, cross, cross_swapped,
              other, other_swapped)
    return product(blocks, early).reshape(lags, channels, NPART)


def solution(mesh):
    return jax.shard_map(
        local,
        mesh=mesh,
        in_specs=(P(("win", "chan"), "tm"), P(("win", "chan")), P("win")),
        out_specs=P("tm", ("win", "chan"), None),
        check_vma=False,
    )
```

```python
import functools
import math

import jax
import jax.numpy as jnp
import ml_dtypes
import numpy as np
from jax import lax
from jax.experimental import pallas as pl
from jax.experimental.pallas import tpu as pltpu
from jax.sharding import PartitionSpec as P

L = 8192
HOP = 4096
H = 128
K0 = 32
NF = 256
WB = 64
NLAG = 32
NPART = 256
EDGE = 512
STEP = 256
GROUP = 512
EPS = 1e-05
TWO_PI = 2.0 * math.pi
BF16 = jnp.bfloat16
F32 = jnp.float32


def split_table(table):
    high = table.astype(ml_dtypes.bfloat16)
    low = (table - high.astype(np.float64)).astype(ml_dtypes.bfloat16)
    return high, low


@functools.cache
def fourier_tables():
    samples = np.arange(GROUP)[:, None]
    bins = K0 + np.arange(NF)[None, :]
    angle = (samples * bins % L) * (TWO_PI / L)
    inner = np.concatenate([np.cos(angle), -np.sin(angle)], axis=1)
    outer = np.zeros((GROUP, 128))
    for lane, k, wave in ((0, K0 - 1, np.cos), (64, K0 - 1, np.sin), (127, K0 + NF, np.cos), (63, K0 + NF, np.sin)):
        sign = 1.0 if wave is np.cos else -1.0
        outer[:, lane] = sign * wave((samples[:, 0] * k % L) * (TWO_PI / L))
    high, low = split_table(inner)
    return np.concatenate([high, outer.astype(ml_dtypes.bfloat16)], axis=1), low


@functools.cache
def packed_tables():
    return np.concatenate(fourier_tables(), axis=1)


@functools.cache
def lag_tables():
    lags = np.arange(NLAG)[:, None] - NLAG // 2
    angle = (lags * (K0 + np.arange(NF))[None, :] % L) * (TWO_PI / L)
    return np.cos(angle).astype(np.float32), np.sin(angle).astype(np.float32)


def split(value):
    high = value.astype(BF16)
    return high, (value - high.astype(F32)).astype(BF16)


def inverse(value):
    guess = pl.reciprocal(value, approx=True)
    return guess * (2.0 - value * guess)


def dot(a, b):
    return jnp.dot(a, b, preferred_element_type=F32)


def spectra_kernel(
    halves, own, halo,
    dead, offs, x_hbm, table_hbm, out, x, absolute, norm_high, norm_low, parts, table, sems,
):
    channels = x.shape[0]
    groups = HOP // GROUP
    bulk = min(own + 1, halves)
    edges = min(own + 2, halves)
    width = halves * HOP
    middle = HOP // 2 + H
    firsts, seconds = [], []
    for j in range(halves):
        firsts.append((j * HOP - (H if j or halo else 0), j * HOP + middle))
        seconds.append((j * HOP + middle, (j + 1) * HOP - H if j + 1 < halves else width + halo))
    copies = [
        pltpu.make_async_copy(
            x_hbm.at[:, pl.ds(halo + begin, end - begin)], x.at[:, pl.ds(H + begin, end - begin)],
            sems.at[i],
        )
        for i, (begin, end) in enumerate(firsts + seconds)
    ]
    table_copy = pltpu.make_async_copy(table_hbm, table, sems.at[2 * halves])
    for copy in copies[:halves] + [table_copy] + copies[halves:]:
        copy.start()
    if not halo:
        for begin in (0, H + width):
            absolute[:, begin:begin + H] = jnp.zeros((channels, H), BF16)

    def arrive(ids):
        for i in ids:
            copies[i].wait()
        for i in ids:
            begin, end = (firsts + seconds)[i]
            here = slice(H + begin, H + end)
            absolute[:, here] = jnp.abs(x[:, here]).astype(BF16)

    high = table.at[:, :2 * NF + 128]
    low = table.at[:, 2 * NF + 128:]
    from_lane = lax.broadcasted_iota(jnp.int32, (2 * H + STEP, STEP), 0)
    to_lane = lax.broadcasted_iota(jnp.int32, (2 * H + STEP, STEP), 1)
    level_band = ((from_lane >= to_lane) & (from_lane <= to_lane + 2 * H)).astype(F32).astype(BF16)
    from_bin = lax.broadcasted_iota(jnp.int32, (NF, NF), 0)
    to_bin = lax.broadcasted_iota(jnp.int32, (NF, NF), 1)
    smooth_band = (jnp.abs(from_bin - to_bin) <= WB).astype(F32).astype(BF16)
    lane = lax.broadcasted_iota(jnp.int32, (1, parts.shape[1]), 1)
    outer_place = lane - 2 * NF
    outer_first = (outer_place == 0) | (outer_place == 64)
    every_bin = jnp.where(
        lane < 2 * NF, jnp.bitwise_and(lane, NF - 1) + K0, jnp.where(outer_first, K0 - 1, K0 + NF)
    )
    real_place = (lane < NF) | (outer_place == 0) | (outer_place == 127)
    group = lax.broadcasted_iota(jnp.int32, (groups, 1), 0) * GROUP
    angle = jnp.bitwise_and(group * every_bin, L - 1).astype(F32) * (TWO_PI / L)
    turn_same = jnp.cos(angle)
    turn_swap = jnp.sin(angle) * jnp.where(real_place, -1.0, 1.0)
    bin_index = lax.broadcasted_iota(jnp.int32, (1, NF), 1)
    below, above = jnp.minimum(bin_index, WB), jnp.minimum(NF - 1 - bin_index, WB)
    inverse_count = 1.0 / (below + above + 1).astype(F32)

    def rows(ref, begin, length, count):
        return [ref[:, begin + j * HOP:begin + j * HOP + length] for j in range(count)]

    def store(place, value):
        here = slice(place, place + value.shape[0])
        norm_high[here, :], norm_low[here, :] = split(value)

    def normalise(group_ids, place):
        blocks = [(g, g * GROUP + part * STEP) for g in group_ids for part in range(GROUP // STEP)]
        counts = [edges if g == 0 else bulk for g, _ in blocks]
        level = dot(
            jnp.concatenate(
                [r for (_, begin), n in zip(blocks, counts)
                 for r in rows(absolute, begin, STEP + 2 * H, n)], axis=0
            ), level_band,
        ) * (1.0 / (2 * H + 1)) + EPS
        values = []
        at = 0
        for (_, begin), n in zip(blocks, counts):
            samples = jnp.concatenate(rows(x, H + begin, STEP, n), axis=0)
            values.append(samples * inverse(level[at:at + n * channels]))
            at += n * channels
        begins = {}
        for index, g in enumerate(group_ids):
            value = jnp.concatenate(values[2 * index:2 * index + 2], axis=1)
            if g == 0:
                lane = lax.broadcasted_iota(jnp.int32, (channels, EDGE), 1)
                merged = []
                for w in range(own):
                    mine = value[w * channels:(w + 1) * channels]
                    other = (
                        value[(w + 2) * channels:(w + 3) * channels]
                        if w + 2 < edges else jnp.zeros_like(mine)
                    )
                    merged.append(jnp.where(lane >= offs[w], mine, other))
                begins["edge"] = place
                store(place, jnp.concatenate(merged, axis=0))
                place += own * channels
                value = value[:bulk * channels]
            begins[g] = place
            store(place, value)
            place += bulk * channels
        return begins, place

    def transform(begin, end):
        first = dot(norm_high[begin:end, :], high[...])
        second = dot(norm_low[begin:end, :], high[:, :2 * NF])
        second = second + dot(norm_high[begin:end, :], low[...])
        parts[begin:end, :2 * NF] = first[:, :2 * NF] + second
        parts[begin:end, 2 * NF:] = first[:, 2 * NF:]

    begins = {}
    place = 0
    waiting = None
    arrive(range(halves))
    table_copy.wait()
    for g in range(0, groups, 2):
        if g == groups // 2:
            arrive(range(halves, 2 * halves))
        start = place
        found, place = normalise([g, g + 1], place)
        begins.update(found)
        if waiting:
            transform(*waiting)
        waiting = (start, place)
    transform(*waiting)

    def piece(name, j):
        return parts[begins[name] + j * channels:begins[name] + (j + 1) * channels, :]

    def bulk_of(j):
        same = jnp.zeros((channels, parts.shape[1]), F32)
        swap = same
        for g in range(1, groups):
            value = piece(g, j)
            same = same + value * turn_same[g:g + 1, :]
            swap = swap + value * turn_swap[g:g + 1, :]
        return same + jnp.concatenate(
            [swap[:, NF:2 * NF], swap[:, :NF], pltpu.roll(swap[:, 2 * NF:], 64, 1)], axis=1
        )

    window = lax.broadcasted_iota(jnp.int32, (own, 1), 0)
    offsets = sum(jnp.where(window == w, offs[w], 0) for w in range(own))
    lane = lax.broadcasted_iota(jnp.int32, (1, NF), 1)
    outer_lane = lax.broadcasted_iota(jnp.int32, (1, 128), 1)
    outer_bin = jnp.where((outer_lane == 0) | (outer_lane == 64), K0 - 1, K0 + NF)

    def turn(bins):
        angle = jnp.bitwise_and(bins * offsets, L - 1).astype(F32) * (TWO_PI / L)
        return jnp.cos(angle), jnp.sin(angle)

    cos_turn, sin_turn = turn(lane + K0)
    cos_outer, sin_outer = turn(outer_bin)
    sign = 1.0 - 2.0 * jnp.bitwise_and(lane + K0, 1).astype(F32)
    sign_outer = 1.0 - 2.0 * jnp.bitwise_and(outer_bin, 1).astype(F32)
    channel = lax.broadcasted_iota(jnp.int32, (channels, 1), 0)
    live = 1.0 - sum(jnp.where(channel == i, dead[i], 0) for i in range(channels)).astype(F32)

    signs = jnp.concatenate([sign, sign, sign_outer], axis=1)
    reals, imags, magnitudes = [], [], []
    following = bulk_of(0)
    for w in range(own):
        spec = following + piece("edge", w)
        if w + 1 < bulk:
            following = bulk_of(w + 1)
            spec = spec + (following + piece(0, w + 1)) * signs
        spec = spec * live
        outer = spec[:, 2 * NF:]
        c, s = cos_turn[w:w + 1], sin_turn[w:w + 1]
        c_outer, s_outer = cos_outer[w:w + 1], sin_outer[w:w + 1]
        outer_imag = pltpu.roll(outer, 64, 1)

        def hann(inner, ends):
            ends = jnp.concatenate([ends, ends], axis=1)
            before = jnp.where(lane == 0, ends, pltpu.roll(inner, 1, 1))
            behind = jnp.where(lane == NF - 1, ends, pltpu.roll(inner, NF - 1, 1))
            return 0.5 * inner - 0.25 * (before + behind)

        real = hann(
            spec[:, :NF] * c - spec[:, NF:2 * NF] * s, outer * c_outer - outer_imag * s_outer
        )
        imag = hann(
            spec[:, :NF] * s + spec[:, NF:2 * NF] * c, outer * s_outer + outer_imag * c_outer
        )
        reals.append(real)
        imags.append(imag)
        magnitudes.append(jnp.sqrt(real * real + imag * imag + 1e-12))
    m_high, m_low = split(jnp.concatenate(magnitudes, axis=0))
    smooth = (dot(m_high, smooth_band) + dot(m_low, smooth_band)) * inverse_count
    scale = 1.0 / (smooth + EPS)
    flip = flip_matrix(channels)
    for w in range(own):
        here = slice(w * channels, (w + 1) * channels)
        white = jnp.concatenate([reals[w] * scale[here], imags[w] * scale[here]], axis=1)
        out[:, w * 2 * NF:(w + 1) * 2 * NF] = dot(flip, white.astype(BF16)).astype(BF16)


def flip_matrix(channels):
    row = lax.broadcasted_iota(jnp.int32, (channels, channels), 0)
    column = lax.broadcasted_iota(jnp.int32, (channels, channels), 1)
    return (row + column == channels - 1).astype(F32).astype(BF16)


def rotate_kernel(lags, own, cos_lag, sin_lag, out):
    channels = own.shape[0]
    straight = dot(flip_matrix(channels), own[...])
    real, imag = straight[:, :NF], straight[:, NF:]
    for t in range(lags):
        c, s = cos_lag[t:t + 1, :], sin_lag[t:t + 1, :]
        here = slice(t * channels, (t + 1) * channels)
        out[here, :NF] = (real * c - imag * s).astype(BF16)
        out[here, NF:] = (real * s + imag * c).astype(BF16)


def put_slots(channels, partners, present, absent):
    last = NPART // channels - 1
    nothing = jnp.zeros((channels, partners.shape[1]), BF16)

    def place(slot):
        return pl.ds(pl.multiple_of((last - slot) * channels, channels), channels)

    for block, slot, valid in present:
        partners[place(slot), :] = block[...]

        @pl.when(jnp.logical_not(valid))
        def _(slot=slot):
            partners[place(slot), :] = nothing

    for slot in absent:
        partners[place(slot), :] = nothing


def early_slots(me, count, channels, blocks, partners):
    own, ahead = blocks
    next_level = me // 4 + 1 < count // 4
    put_slots(
        channels, partners, [(own, 0, me >= 0), (ahead, 4, next_level)], (1, 2, 3, 5, 6, 7)
    )


def late_slots(me, count, channels, blocks, partners):
    core = lax.rem(me, 2)
    side = lax.rem(me // 2, 2)
    (own_swapped, ahead_swapped, far, far_swapped, cross, cross_swapped, other,
     other_swapped) = blocks
    cross_slot = 6 - 4 * side
    other_slot = 8 - cross_slot
    step = 1 - 2 * core
    next_level = me // 4 + 1 < count // 4
    second_level = me // 4 + 2 < count // 4
    other_there = (side == 0) | second_level
    put_slots(channels, partners, [
        (far, 0, second_level), (cross, cross_slot, next_level),
        (other, other_slot, other_there), (ahead_swapped, 4 + step, next_level),
        (cross_swapped, cross_slot + step, next_level),
        (other_swapped, other_slot + step, other_there),
    ], (4,))

    @pl.when(core == 0)
    def _():
        put_slots(channels, partners, [(own_swapped, 1, me >= 0)], ())

    @pl.when(core == 1)
    def _():
        put_slots(channels, partners, [(far_swapped, 7, second_level)], ())


def product_kernel(late, count, norm_scale, place, rotated, *refs):
    refs = list(refs)
    before = refs.pop(0) if late else None
    out, partners, total = refs[-3:]
    blocks = refs[:-3]
    channels = blocks[0].shape[0]
    (late_slots if late else early_slots)(place[0], count, channels, blocks, partners)
    rows, features = rotated.shape
    chunk = 2 * 2 * NF
    for begin in range(0, features, chunk):
        turned = partners[:, begin:begin + chunk].T
        product = dot(rotated[:, begin:begin + chunk], turned)
        if begin == 0:
            total[...] = product
        else:
            total[...] += product

    row = lax.broadcasted_iota(jnp.int32, (channels, NPART), 0)
    column = lax.broadcasted_iota(jnp.int32, (channels, NPART), 1)
    low = row + column >= NPART - 1
    keep = (low | (column < NPART - channels)) if late else jnp.logical_not(low)
    sheared = []
    for begin in range(0, rows, channels):
        here = slice(begin, begin + channels)
        value = jnp.where(keep, total[here, :], 0.0)
        if late:
            value = (value + before[here, :]) * norm_scale
            sheared.append(pltpu.roll(value, 1, 1, stride=1, stride_axis=0).astype(BF16))
        else:
            out[here, :] = value
    if late:
        sheared = jnp.concatenate(sheared, axis=0)
        out[...] = dot(sheared, flip_matrix(NPART)).astype(BF16)


def exchange(value, pairs):
    return lax.ppermute(value, "chan", pairs)


def local(records, dead_mask, offsets):
    channels, samples = records.shape
    tm_count = lax.axis_size("tm")
    tm_index = lax.axis_index("tm")
    chan_count = lax.axis_size("chan")
    own = samples // HOP
    windows = own * tm_count
    halves = own
    halo = 0
    if tm_count > 1:
        reach = 2 * HOP + H
        left = lax.ppermute(
            records[:, samples - H:], "tm", [(i, i + 1) for i in range(tm_count - 1)]
        )
        right = lax.ppermute(
            records[:, :reach], "tm", [(i + 1, i) for i in range(tm_count - 1)]
        )
        records = jnp.concatenate([left, records, right], axis=1)
        halves = own + 2
        halo = H
    table = jnp.asarray(packed_tables())
    own_offsets = lax.dynamic_slice_in_dim(offsets, tm_index * own, own, 0)
    vmem = pl.BlockSpec(memory_space=pltpu.VMEM)
    smem = pl.BlockSpec(memory_space=pltpu.SMEM)
    hbm = pl.BlockSpec(memory_space=pl.ANY)
    params = pltpu.CompilerParams(vmem_limit_bytes=24 * 1024 * 1024)

    bulk = min(own + 1, halves)
    part_rows = (own + bulk * (HOP // GROUP)) * channels
    spectra = pl.pallas_call(
        functools.partial(spectra_kernel, halves, own, halo),
        name="spectra",
        out_shape=jax.ShapeDtypeStruct((channels, own * 2 * NF), BF16),
        in_specs=[smem, smem, hbm, hbm],
        out_specs=vmem,
        scratch_shapes=[
            pltpu.VMEM((channels, halves * HOP + 2 * H), F32),
            pltpu.VMEM((channels, halves * HOP + 2 * H), BF16),
            pltpu.VMEM((part_rows, GROUP), BF16),
            pltpu.VMEM((part_rows, GROUP), BF16),
            pltpu.VMEM((part_rows, 2 * NF + 128), F32),
            pltpu.VMEM(table.shape, BF16),
            pltpu.SemaphoreType.DMA((2 * halves + 1,)),
        ],
        compiler_params=pltpu.CompilerParams(vmem_limit_bytes=60 * 1024 * 1024),
        cost_estimate=pl.CostEstimate(
            flops=7_000_000_000, bytes_accessed=8 * 1024 * 1024, transcendentals=0
        ),
    )(dead_mask, own_offsets, records, table)
    if tm_count > 1:
        spectra = lax.all_gather(spectra, "tm", axis=1, tiled=True)

    lags = NLAG // tm_count
    cos_lag, sin_lag = (
        lax.dynamic_slice_in_dim(jnp.asarray(t), tm_index * lags, lags, 0) for t in lag_tables()
    )
    place = lax.axis_index("chan").astype(jnp.int32).reshape(1)
    norm_scale = 1.0 / math.sqrt(2.0 * NF * windows)

    features = spectra.shape[1]
    rotated = pl.pallas_call(
        functools.partial(rotate_kernel, lags),
        name="rotate",
        grid=(windows,),
        out_shape=jax.ShapeDtypeStruct((lags * channels, features), BF16),
        in_specs=[
            pl.BlockSpec((channels, 2 * NF), lambda w: (0, w)),
            pl.BlockSpec((lags, NF), lambda w: (0, 0)),
            pl.BlockSpec((lags, NF), lambda w: (0, 0)),
        ],
        out_specs=pl.BlockSpec((lags * channels, 2 * NF), lambda w: (0, w)),
        compiler_params=params,
        cost_estimate=pl.CostEstimate(
            flops=4_000_000_000, bytes_accessed=8 * 1024 * 1024, transcendentals=0
        ),
    )(spectra, cos_lag, sin_lag)

    def product(blocks, before):
        late = before is not None
        operands = [place, rotated] + ([before] if late else []) + list(blocks)
        return pl.pallas_call(
            functools.partial(product_kernel, late, chan_count, norm_scale),
            name="late_product" if late else "early_product",
            out_shape=jax.ShapeDtypeStruct((lags * channels, NPART), BF16 if late else F32),
            in_specs=[smem] + [vmem] * (len(operands) - 1),
            out_specs=vmem,
            scratch_shapes=[
                pltpu.VMEM((NPART, features), BF16),
                pltpu.VMEM((lags * channels, NPART), F32),
            ],
            compiler_params=params,
            cost_estimate=pl.CostEstimate(
                flops=2 * lags * channels * features * NPART, bytes_accessed=6 * 1024 * 1024,
                transcendentals=0,
            ),
        )(*operands)

    every = range(chan_count)
    down = [(i, (i - 4) % chan_count) for i in every]
    down_2 = [(i, (i - 2) % chan_count) for i in every]
    across = [(i, i ^ 2) for i in every]
    cores = [(i, i ^ 1) for i in every]
    side = lax.rem(lax.axis_index("chan") // 2, 2)

    ahead = exchange(spectra, down)
    ahead, rotated = lax.optimization_barrier((ahead, rotated))
    other = exchange(jnp.where(side == 0, ahead, spectra), down_2)
    cross = exchange(ahead, across)
    far = exchange(ahead, down)
    early = product((spectra, ahead), None)
    kept, ahead, other, early = lax.optimization_barrier((spectra, ahead, other, early))
    own_swapped = exchange(kept, cores)
    ahead_swapped = exchange(ahead, cores)
    cross, own_swapped, ahead_swapped = lax.optimization_barrier(
        (cross, own_swapped, ahead_swapped)
    )
    blocks = (own_swapped, ahead_swapped, far, exchange(far, cores), cross,
              exchange(cross, cores), other, exchange(other, cores))
    return product(blocks, early).reshape(lags, channels, NPART)


def solution(mesh):
    return jax.shard_map(
        local,
        mesh=mesh,
        in_specs=(P(("win", "chan"), "tm"), P(("win", "chan")), P("win")),
        out_specs=P("tm", ("win", "chan"), None),
        check_vma=False,
    )
```

```python
import functools
import math

import jax
import jax.numpy as jnp
import ml_dtypes
import numpy as np
from jax import lax
from jax.experimental import pallas as pl
from jax.experimental.pallas import tpu as pltpu
from jax.sharding import PartitionSpec as P

L = 8192
HOP = 4096
H = 128
K0 = 32
NF = 256
WB = 64
NLAG = 32
NPART = 256
EDGE = 512
STEP = 256
GROUP = 512
EPS = 1e-05
TWO_PI = 2.0 * math.pi
BF16 = jnp.bfloat16
F32 = jnp.float32


def split_table(table):
    high = table.astype(ml_dtypes.bfloat16)
    low = (table - high.astype(np.float64)).astype(ml_dtypes.bfloat16)
    return high, low


@functools.cache
def fourier_tables():
    samples = np.arange(GROUP)[:, None]
    bins = K0 + np.arange(NF)[None, :]
    angle = (samples * bins % L) * (TWO_PI / L)
    inner = np.concatenate([np.cos(angle), -np.sin(angle)], axis=1)
    outer = np.zeros((GROUP, 128))
    for lane, k, wave in ((0, K0 - 1, np.cos), (64, K0 - 1, np.sin), (127, K0 + NF, np.cos), (63, K0 + NF, np.sin)):
        sign = 1.0 if wave is np.cos else -1.0
        outer[:, lane] = sign * wave((samples[:, 0] * k % L) * (TWO_PI / L))
    high, low = split_table(inner)
    return np.concatenate([high, outer.astype(ml_dtypes.bfloat16)], axis=1), low


@functools.cache
def packed_tables():
    return np.concatenate(fourier_tables(), axis=1)


@functools.cache
def lag_tables():
    lags = np.arange(NLAG)[:, None] - NLAG // 2
    angle = (lags * (K0 + np.arange(NF))[None, :] % L) * (TWO_PI / L)
    return np.cos(angle).astype(np.float32), np.sin(angle).astype(np.float32)


def split(value):
    high = value.astype(BF16)
    return high, (value - high.astype(F32)).astype(BF16)


def inverse(value):
    guess = pl.reciprocal(value, approx=True)
    return guess * (2.0 - value * guess)


def dot(a, b):
    return jnp.dot(a, b, preferred_element_type=F32)


def spectra_kernel(
    halves, own, halo,
    dead, offs, x_hbm, table_hbm, out, x, absolute, norm_high, norm_low, parts, table, sems,
):
    channels = x.shape[0]
    groups = HOP // GROUP
    bulk = min(own + 1, halves)
    edges = min(own + 2, halves)
    width = halves * HOP
    middle = HOP // 2 + H
    firsts, seconds = [], []
    for j in range(halves):
        firsts.append((j * HOP - (H if j or halo else 0), j * HOP + middle))
        seconds.append((j * HOP + middle, (j + 1) * HOP - H if j + 1 < halves else width + halo))
    copies = [
        pltpu.make_async_copy(
            x_hbm.at[:, pl.ds(halo + begin, end - begin)], x.at[:, pl.ds(H + begin, end - begin)],
            sems.at[i],
        )
        for i, (begin, end) in enumerate(firsts + seconds)
    ]
    table_copy = pltpu.make_async_copy(table_hbm, table, sems.at[2 * halves])
    for copy in copies[:halves] + [table_copy] + copies[halves:]:
        copy.start()
    if not halo:
        for begin in (0, H + width):
            absolute[:, begin:begin + H] = jnp.zeros((channels, H), BF16)

    def arrive(ids):
        for i in ids:
            copies[i].wait()
        for i in ids:
            begin, end = (firsts + seconds)[i]
            here = slice(H + begin, H + end)
            absolute[:, here] = jnp.abs(x[:, here]).astype(BF16)

    high = table.at[:, :2 * NF + 128]
    low = table.at[:, 2 * NF + 128:]
    from_lane = lax.broadcasted_iota(jnp.int32, (2 * H + STEP, STEP), 0)
    to_lane = lax.broadcasted_iota(jnp.int32, (2 * H + STEP, STEP), 1)
    level_band = ((from_lane >= to_lane) & (from_lane <= to_lane + 2 * H)).astype(F32).astype(BF16)
    from_bin = lax.broadcasted_iota(jnp.int32, (NF, NF), 0)
    to_bin = lax.broadcasted_iota(jnp.int32, (NF, NF), 1)
    smooth_band = (jnp.abs(from_bin - to_bin) <= WB).astype(F32).astype(BF16)
    lane = lax.broadcasted_iota(jnp.int32, (1, parts.shape[1]), 1)
    outer_place = lane - 2 * NF
    outer_first = (outer_place == 0) | (outer_place == 64)
    every_bin = jnp.where(
        lane < 2 * NF, jnp.bitwise_and(lane, NF - 1) + K0, jnp.where(outer_first, K0 - 1, K0 + NF)
    )
    real_place = (lane < NF) | (outer_place == 0) | (outer_place == 127)
    group = lax.broadcasted_iota(jnp.int32, (groups, 1), 0) * GROUP
    angle = jnp.bitwise_and(group * every_bin, L - 1).astype(F32) * (TWO_PI / L)
    turn_same = jnp.cos(angle)
    turn_swap = jnp.sin(angle) * jnp.where(real_place, -1.0, 1.0)
    bin_index = lax.broadcasted_iota(jnp.int32, (1, NF), 1)
    below, above = jnp.minimum(bin_index, WB), jnp.minimum(NF - 1 - bin_index, WB)
    inverse_count = 1.0 / (below + above + 1).astype(F32)

    def rows(ref, begin, length, count):
        return [ref[:, begin + j * HOP:begin + j * HOP + length] for j in range(count)]

    def store(place, value):
        here = slice(place, place + value.shape[0])
        norm_high[here, :], norm_low[here, :] = split(value)

    def normalise(group_ids, place):
        blocks = [(g, g * GROUP + part * STEP) for g in group_ids for part in range(GROUP // STEP)]
        counts = [edges if g == 0 else bulk for g, _ in blocks]
        level = dot(
            jnp.concatenate(
                [r for (_, begin), n in zip(blocks, counts)
                 for r in rows(absolute, begin, STEP + 2 * H, n)], axis=0
            ), level_band,
        ) * (1.0 / (2 * H + 1)) + EPS
        values = []
        at = 0
        for (_, begin), n in zip(blocks, counts):
            samples = jnp.concatenate(rows(x, H + begin, STEP, n), axis=0)
            values.append(samples * inverse(level[at:at + n * channels]))
            at += n * channels
        begins = {}
        for index, g in enumerate(group_ids):
            value = jnp.concatenate(values[2 * index:2 * index + 2], axis=1)
            if g == 0:
                lane = lax.broadcasted_iota(jnp.int32, (channels, EDGE), 1)
                merged = []
                for w in range(own):
                    mine = value[w * channels:(w + 1) * channels]
                    other = (
                        value[(w + 2) * channels:(w + 3) * channels]
                        if w + 2 < edges else jnp.zeros_like(mine)
                    )
                    merged.append(jnp.where(lane >= offs[w], mine, other))
                begins["edge"] = place
                store(place, jnp.concatenate(merged, axis=0))
                place += own * channels
                value = value[:bulk * channels]
            begins[g] = place
            store(place, value)
            place += bulk * channels
        return begins, place

    def transform(begin, end):
        first = dot(norm_high[begin:end, :], high[...])
        second = dot(norm_low[begin:end, :], high[:, :2 * NF])
        second = second + dot(norm_high[begin:end, :], low[...])
        parts[begin:end, :2 * NF] = first[:, :2 * NF] + second
        parts[begin:end, 2 * NF:] = first[:, 2 * NF:]

    begins = {}
    place = 0
    waiting = None
    arrive(range(halves))
    table_copy.wait()
    for g in range(0, groups, 2):
        if g == groups // 2:
            arrive(range(halves, 2 * halves))
        start = place
        found, place = normalise([g, g + 1], place)
        begins.update(found)
        if waiting:
            transform(*waiting)
        waiting = (start, place)
    transform(*waiting)

    def piece(name, j):
        return parts[begins[name] + j * channels:begins[name] + (j + 1) * channels, :]

    def bulk_of(j):
        same = jnp.zeros((channels, parts.shape[1]), F32)
        swap = same
        for g in range(1, groups):
            value = piece(g, j)
            same = same + value * turn_same[g:g + 1, :]
            swap = swap + value * turn_swap[g:g + 1, :]
        return same + jnp.concatenate(
            [swap[:, NF:2 * NF], swap[:, :NF], pltpu.roll(swap[:, 2 * NF:], 64, 1)], axis=1
        )

    window = lax.broadcasted_iota(jnp.int32, (own, 1), 0)
    offsets = sum(jnp.where(window == w, offs[w], 0) for w in range(own))
    lane = lax.broadcasted_iota(jnp.int32, (1, NF), 1)
    outer_lane = lax.broadcasted_iota(jnp.int32, (1, 128), 1)
    outer_bin = jnp.where((outer_lane == 0) | (outer_lane == 64), K0 - 1, K0 + NF)

    def turn(bins):
        angle = jnp.bitwise_and(bins * offsets, L - 1).astype(F32) * (TWO_PI / L)
        return jnp.cos(angle), jnp.sin(angle)

    cos_turn, sin_turn = turn(lane + K0)
    cos_outer, sin_outer = turn(outer_bin)
    sign = 1.0 - 2.0 * jnp.bitwise_and(lane + K0, 1).astype(F32)
    sign_outer = 1.0 - 2.0 * jnp.bitwise_and(outer_bin, 1).astype(F32)
    channel = lax.broadcasted_iota(jnp.int32, (channels, 1), 0)
    live = 1.0 - sum(jnp.where(channel == i, dead[i], 0) for i in range(channels)).astype(F32)

    signs = jnp.concatenate([sign, sign, sign_outer], axis=1)
    reals, imags, magnitudes = [], [], []
    following = bulk_of(0)
    for w in range(own):
        spec = following + piece("edge", w)
        if w + 1 < bulk:
            following = bulk_of(w + 1)
            spec = spec + (following + piece(0, w + 1)) * signs
        spec = spec * live
        outer = spec[:, 2 * NF:]
        c, s = cos_turn[w:w + 1], sin_turn[w:w + 1]
        c_outer, s_outer = cos_outer[w:w + 1], sin_outer[w:w + 1]
        outer_imag = pltpu.roll(outer, 64, 1)

        def hann(inner, ends):
            ends = jnp.concatenate([ends, ends], axis=1)
            before = jnp.where(lane == 0, ends, pltpu.roll(inner, 1, 1))
            behind = jnp.where(lane == NF - 1, ends, pltpu.roll(inner, NF - 1, 1))
            return 0.5 * inner - 0.25 * (before + behind)

        real = hann(
            spec[:, :NF] * c - spec[:, NF:2 * NF] * s, outer * c_outer - outer_imag * s_outer
        )
        imag = hann(
            spec[:, :NF] * s + spec[:, NF:2 * NF] * c, outer * s_outer + outer_imag * c_outer
        )
        reals.append(real)
        imags.append(imag)
        magnitudes.append(jnp.sqrt(real * real + imag * imag + 1e-12))
    m_high, m_low = split(jnp.concatenate(magnitudes, axis=0))
    smooth = (dot(m_high, smooth_band) + dot(m_low, smooth_band)) * inverse_count
    scale = 1.0 / (smooth + EPS)
    flip = flip_matrix(channels)
    for w in range(own):
        here = slice(w * channels, (w + 1) * channels)
        white = jnp.concatenate([reals[w] * scale[here], imags[w] * scale[here]], axis=1)
        out[:, w * 2 * NF:(w + 1) * 2 * NF] = dot(flip, white.astype(BF16)).astype(BF16)


def flip_matrix(channels):
    row = lax.broadcasted_iota(jnp.int32, (channels, channels), 0)
    column = lax.broadcasted_iota(jnp.int32, (channels, channels), 1)
    return (row + column == channels - 1).astype(F32).astype(BF16)


def rotate_kernel(lags, own, cos_lag, sin_lag, out):
    channels = own.shape[0]
    straight = dot(flip_matrix(channels), own[...])
    real, imag = straight[:, :NF], straight[:, NF:]
    for t in range(lags):
        c, s = cos_lag[t:t + 1, :], sin_lag[t:t + 1, :]
        here = slice(t * channels, (t + 1) * channels)
        out[here, :NF] = (real * c - imag * s).astype(BF16)
        out[here, NF:] = (real * s + imag * c).astype(BF16)


def put_slots(channels, partners, present, absent):
    last = NPART // channels - 1
    nothing = jnp.zeros((channels, partners.shape[1]), BF16)

    def place(slot):
        return pl.ds(pl.multiple_of((last - slot) * channels, channels), channels)

    for block, slot, valid in present:
        partners[place(slot), :] = block[...]

        @pl.when(jnp.logical_not(valid))
        def _(slot=slot):
            partners[place(slot), :] = nothing

    for slot in absent:
        partners[place(slot), :] = nothing


def early_slots(me, count, channels, blocks, partners):
    own, ahead = blocks
    next_level = me // 4 + 1 < count // 4
    put_slots(
        channels, partners, [(own, 0, me >= 0), (ahead, 4, next_level)], (1, 2, 3, 5, 6, 7)
    )


def late_slots(me, count, channels, blocks, partners):
    core = lax.rem(me, 2)
    side = lax.rem(me // 2, 2)
    (own_swapped, ahead_swapped, far, far_swapped, cross, cross_swapped, other,
     other_swapped) = blocks
    cross_slot = 6 - 4 * side
    other_slot = 8 - cross_slot
    step = 1 - 2 * core
    next_level = me // 4 + 1 < count // 4
    second_level = me // 4 + 2 < count // 4
    other_there = (side == 0) | second_level
    put_slots(channels, partners, [
        (far, 0, second_level), (cross, cross_slot, next_level),
        (other, other_slot, other_there), (ahead_swapped, 4 + step, next_level),
        (cross_swapped, cross_slot + step, next_level),
        (other_swapped, other_slot + step, other_there),
    ], (4,))

    @pl.when(core == 0)
    def _():
        put_slots(channels, partners, [(own_swapped, 1, me >= 0)], ())

    @pl.when(core == 1)
    def _():
        put_slots(channels, partners, [(far_swapped, 7, second_level)], ())


def product_kernel(late, count, norm_scale, place, rotated, *refs):
    refs = list(refs)
    before = refs.pop(0) if late else None
    out, partners, total = refs[-3:]
    blocks = refs[:-3]
    channels = blocks[0].shape[0]
    (late_slots if late else early_slots)(place[0], count, channels, blocks, partners)
    rows, features = rotated.shape
    chunk = 2 * 2 * NF
    for begin in range(0, features, chunk):
        turned = partners[:, begin:begin + chunk].T
        product = dot(rotated[:, begin:begin + chunk], turned)
        if begin == 0:
            total[...] = product
        else:
            total[...] += product

    row = lax.broadcasted_iota(jnp.int32, (channels, NPART), 0)
    column = lax.broadcasted_iota(jnp.int32, (channels, NPART), 1)
    low = row + column >= NPART - 1
    keep = (low | (column < NPART - channels)) if late else jnp.logical_not(low)
    sheared = []
    for begin in range(0, rows, channels):
        here = slice(begin, begin + channels)
        value = jnp.where(keep, total[here, :], 0.0)
        if late:
            value = (value + before[here, :]) * norm_scale
            sheared.append(pltpu.roll(value, 1, 1, stride=1, stride_axis=0).astype(BF16))
        else:
            out[here, :] = value
    if late:
        sheared = jnp.concatenate(sheared, axis=0)
        out[...] = dot(sheared, flip_matrix(NPART)).astype(BF16)


def exchange(value, pairs):
    return lax.ppermute(value, "chan", pairs)


def local(records, dead_mask, offsets):
    channels, samples = records.shape
    tm_count = lax.axis_size("tm")
    tm_index = lax.axis_index("tm")
    chan_count = lax.axis_size("chan")
    own = samples // HOP
    windows = own * tm_count
    halves = own
    halo = 0
    if tm_count > 1:
        reach = 2 * HOP + H
        left = lax.ppermute(
            records[:, samples - H:], "tm", [(i, i + 1) for i in range(tm_count - 1)]
        )
        right = lax.ppermute(
            records[:, :reach], "tm", [(i + 1, i) for i in range(tm_count - 1)]
        )
        records = jnp.concatenate([left, records, right], axis=1)
        halves = own + 2
        halo = H
    table = jnp.asarray(packed_tables())
    own_offsets = lax.dynamic_slice_in_dim(offsets, tm_index * own, own, 0)
    vmem = pl.BlockSpec(memory_space=pltpu.VMEM)
    smem = pl.BlockSpec(memory_space=pltpu.SMEM)
    hbm = pl.BlockSpec(memory_space=pl.ANY)
    params = pltpu.CompilerParams(vmem_limit_bytes=24 * 1024 * 1024)

    bulk = min(own + 1, halves)
    part_rows = (own + bulk * (HOP // GROUP)) * channels
    spectra = pl.pallas_call(
        functools.partial(spectra_kernel, halves, own, halo),
        name="spectra",
        out_shape=jax.ShapeDtypeStruct((channels, own * 2 * NF), BF16),
        in_specs=[smem, smem, hbm, hbm],
        out_specs=vmem,
        scratch_shapes=[
            pltpu.VMEM((channels, halves * HOP + 2 * H), F32),
            pltpu.VMEM((channels, halves * HOP + 2 * H), BF16),
            pltpu.VMEM((part_rows, GROUP), BF16),
            pltpu.VMEM((part_rows, GROUP), BF16),
            pltpu.VMEM((part_rows, 2 * NF + 128), F32),
            pltpu.VMEM(table.shape, BF16),
            pltpu.SemaphoreType.DMA((2 * halves + 1,)),
        ],
        compiler_params=pltpu.CompilerParams(vmem_limit_bytes=60 * 1024 * 1024),
        cost_estimate=pl.CostEstimate(
            flops=7_000_000_000, bytes_accessed=8 * 1024 * 1024, transcendentals=0
        ),
    )(dead_mask, own_offsets, records, table)
    if tm_count > 1:
        spectra = lax.all_gather(spectra, "tm", axis=1, tiled=True)

    lags = NLAG // tm_count
    cos_lag, sin_lag = (
        lax.dynamic_slice_in_dim(jnp.asarray(t), tm_index * lags, lags, 0) for t in lag_tables()
    )
    place = lax.axis_index("chan").astype(jnp.int32).reshape(1)
    norm_scale = 1.0 / math.sqrt(2.0 * NF * windows)

    features = spectra.shape[1]
    rotated = pl.pallas_call(
        functools.partial(rotate_kernel, lags),
        name="rotate",
        grid=(windows,),
        out_shape=jax.ShapeDtypeStruct((lags * channels, features), BF16),
        in_specs=[
            pl.BlockSpec((channels, 2 * NF), lambda w: (0, w)),
            pl.BlockSpec((lags, NF), lambda w: (0, 0)),
            pl.BlockSpec((lags, NF), lambda w: (0, 0)),
        ],
        out_specs=pl.BlockSpec((lags * channels, 2 * NF), lambda w: (0, w)),
        compiler_params=params,
        cost_estimate=pl.CostEstimate(
            flops=4_000_000_000, bytes_accessed=8 * 1024 * 1024, transcendentals=0
        ),
    )(spectra, cos_lag, sin_lag)

    def product(blocks, before):
        late = before is not None
        operands = [place, rotated] + ([before] if late else []) + list(blocks)
        return pl.pallas_call(
            functools.partial(product_kernel, late, chan_count, norm_scale),
            name="late_product" if late else "early_product",
            out_shape=jax.ShapeDtypeStruct((lags * channels, NPART), BF16 if late else F32),
            in_specs=[smem] + [vmem] * (len(operands) - 1),
            out_specs=vmem,
            scratch_shapes=[
                pltpu.VMEM((NPART, features), BF16),
                pltpu.VMEM((lags * channels, NPART), F32),
            ],
            compiler_params=params,
            cost_estimate=pl.CostEstimate(
                flops=2 * lags * channels * features * NPART, bytes_accessed=6 * 1024 * 1024,
                transcendentals=0,
            ),
        )(*operands)

    every = range(chan_count)
    down = [(i, (i - 4) % chan_count) for i in every]
    down_2 = [(i, (i - 2) % chan_count) for i in every]
    across = [(i, i ^ 2) for i in every]
    cores = [(i, i ^ 1) for i in every]
    side = lax.rem(lax.axis_index("chan") // 2, 2)

    ahead = exchange(spectra, down)
    ahead, rotated = lax.optimization_barrier((ahead, rotated))
    cross = exchange(ahead, across)
    other = exchange(jnp.where(side == 0, ahead, spectra), down_2)
    far = exchange(ahead, down)
    early = product((spectra, ahead), None)
    kept, ahead, cross, early = lax.optimization_barrier((spectra, ahead, cross, early))
    own_swapped = exchange(kept, cores)
    ahead_swapped = exchange(ahead, cores)
    other_swapped = exchange(other, cores)
    far, other_swapped, own_swapped, ahead_swapped = lax.optimization_barrier(
        (far, other_swapped, own_swapped, ahead_swapped)
    )
    blocks = (own_swapped, ahead_swapped, far, exchange(far, cores), cross,
              exchange(cross, cores), other, other_swapped)
    return product(blocks, early).reshape(lags, channels, NPART)


def solution(mesh):
    return jax.shard_map(
        local,
        mesh=mesh,
        in_specs=(P(("win", "chan"), "tm"), P(("win", "chan")), P("win")),
        out_specs=P("tm", ("win", "chan"), None),
        check_vma=False,
    )
```

```python
import functools
import math

import jax
import jax.numpy as jnp
import ml_dtypes
import numpy as np
from jax import lax
from jax.experimental import pallas as pl
from jax.experimental.pallas import tpu as pltpu
from jax.sharding import PartitionSpec as P

L = 8192
HOP = 4096
H = 128
K0 = 32
NF = 256
WB = 64
NLAG = 32
NPART = 256
EDGE = 512
STEP = 256
GROUP = 512
EPS = 1e-05
TWO_PI = 2.0 * math.pi
BF16 = jnp.bfloat16
F32 = jnp.float32


def split_table(table):
    high = table.astype(ml_dtypes.bfloat16)
    low = (table - high.astype(np.float64)).astype(ml_dtypes.bfloat16)
    return high, low


@functools.cache
def fourier_tables():
    samples = np.arange(GROUP)[:, None]
    bins = K0 + np.arange(NF)[None, :]
    angle = (samples * bins % L) * (TWO_PI / L)
    inner = np.concatenate([np.cos(angle), -np.sin(angle)], axis=1)
    outer = np.zeros((GROUP, 128))
    for lane, k, wave in ((0, K0 - 1, np.cos), (64, K0 - 1, np.sin), (127, K0 + NF, np.cos), (63, K0 + NF, np.sin)):
        sign = 1.0 if wave is np.cos else -1.0
        outer[:, lane] = sign * wave((samples[:, 0] * k % L) * (TWO_PI / L))
    high, low = split_table(inner)
    return np.concatenate([high, outer.astype(ml_dtypes.bfloat16)], axis=1), low


@functools.cache
def packed_tables():
    return np.concatenate(fourier_tables(), axis=1)


@functools.cache
def lag_tables():
    lags = np.arange(NLAG)[:, None] - NLAG // 2
    angle = (lags * (K0 + np.arange(NF))[None, :] % L) * (TWO_PI / L)
    return np.cos(angle).astype(np.float32), np.sin(angle).astype(np.float32)


def split(value):
    high = value.astype(BF16)
    return high, (value - high.astype(F32)).astype(BF16)


def inverse(value):
    guess = pl.reciprocal(value, approx=True)
    return guess * (2.0 - value * guess)


def dot(a, b):
    return jnp.dot(a, b, preferred_element_type=F32)


def spectra_kernel(
    halves, own, halo,
    dead, offs, x_hbm, table_hbm, out, x, absolute, norm_high, norm_low, parts, table, sems,
):
    channels = x.shape[0]
    groups = HOP // GROUP
    bulk = min(own + 1, halves)
    edges = min(own + 2, halves)
    width = halves * HOP
    middle = HOP // 2 + H
    firsts, seconds = [], []
    for j in range(halves):
        firsts.append((j * HOP - (H if j or halo else 0), j * HOP + middle))
        seconds.append((j * HOP + middle, (j + 1) * HOP - H if j + 1 < halves else width + halo))
    copies = [
        pltpu.make_async_copy(
            x_hbm.at[:, pl.ds(halo + begin, end - begin)], x.at[:, pl.ds(H + begin, end - begin)],
            sems.at[i],
        )
        for i, (begin, end) in enumerate(firsts + seconds)
    ]
    table_copy = pltpu.make_async_copy(table_hbm, table, sems.at[2 * halves])
    for copy in copies[:halves] + [table_copy] + copies[halves:]:
        copy.start()
    if not halo:
        for begin in (0, H + width):
            absolute[:, begin:begin + H] = jnp.zeros((channels, H), BF16)

    def arrive(ids):
        for i in ids:
            copies[i].wait()
        for i in ids:
            begin, end = (firsts + seconds)[i]
            here = slice(H + begin, H + end)
            absolute[:, here] = jnp.abs(x[:, here]).astype(BF16)

    high = table.at[:, :2 * NF + 128]
    low = table.at[:, 2 * NF + 128:]
    from_lane = lax.broadcasted_iota(jnp.int32, (2 * H + STEP, STEP), 0)
    to_lane = lax.broadcasted_iota(jnp.int32, (2 * H + STEP, STEP), 1)
    level_band = ((from_lane >= to_lane) & (from_lane <= to_lane + 2 * H)).astype(F32).astype(BF16)
    from_bin = lax.broadcasted_iota(jnp.int32, (NF, NF), 0)
    to_bin = lax.broadcasted_iota(jnp.int32, (NF, NF), 1)
    smooth_band = (jnp.abs(from_bin - to_bin) <= WB).astype(F32).astype(BF16)
    lane = lax.broadcasted_iota(jnp.int32, (1, parts.shape[1]), 1)
    outer_place = lane - 2 * NF
    outer_first = (outer_place == 0) | (outer_place == 64)
    every_bin = jnp.where(
        lane < 2 * NF, jnp.bitwise_and(lane, NF - 1) + K0, jnp.where(outer_first, K0 - 1, K0 + NF)
    )
    real_place = (lane < NF) | (outer_place == 0) | (outer_place == 127)
    group = lax.broadcasted_iota(jnp.int32, (groups, 1), 0) * GROUP
    angle = jnp.bitwise_and(group * every_bin, L - 1).astype(F32) * (TWO_PI / L)
    turn_same = jnp.cos(angle)
    turn_swap = jnp.sin(angle) * jnp.where(real_place, -1.0, 1.0)
    bin_index = lax.broadcasted_iota(jnp.int32, (1, NF), 1)
    below, above = jnp.minimum(bin_index, WB), jnp.minimum(NF - 1 - bin_index, WB)
    inverse_count = 1.0 / (below + above + 1).astype(F32)

    def rows(ref, begin, length, count):
        return [ref[:, begin + j * HOP:begin + j * HOP + length] for j in range(count)]

    def store(place, value):
        here = slice(place, place + value.shape[0])
        norm_high[here, :], norm_low[here, :] = split(value)

    def normalise(group_ids, place):
        blocks = [(g, g * GROUP + part * STEP) for g in group_ids for part in range(GROUP // STEP)]
        counts = [edges if g == 0 else bulk for g, _ in blocks]
        level = dot(
            jnp.concatenate(
                [r for (_, begin), n in zip(blocks, counts)
                 for r in rows(absolute, begin, STEP + 2 * H, n)], axis=0
            ), level_band,
        ) * (1.0 / (2 * H + 1)) + EPS
        values = []
        at = 0
        for (_, begin), n in zip(blocks, counts):
            samples = jnp.concatenate(rows(x, H + begin, STEP, n), axis=0)
            values.append(samples * inverse(level[at:at + n * channels]))
            at += n * channels
        begins = {}
        for index, g in enumerate(group_ids):
            value = jnp.concatenate(values[2 * index:2 * index + 2], axis=1)
            if g == 0:
                lane = lax.broadcasted_iota(jnp.int32, (channels, EDGE), 1)
                merged = []
                for w in range(own):
                    mine = value[w * channels:(w + 1) * channels]
                    other = (
                        value[(w + 2) * channels:(w + 3) * channels]
                        if w + 2 < edges else jnp.zeros_like(mine)
                    )
                    merged.append(jnp.where(lane >= offs[w], mine, other))
                begins["edge"] = place
                store(place, jnp.concatenate(merged, axis=0))
                place += own * channels
                value = value[:bulk * channels]
            begins[g] = place
            store(place, value)
            place += bulk * channels
        return begins, place

    def transform(begin, end):
        first = dot(norm_high[begin:end, :], high[...])
        second = dot(norm_low[begin:end, :], high[:, :2 * NF])
        second = second + dot(norm_high[begin:end, :], low[...])
        parts[begin:end, :2 * NF] = first[:, :2 * NF] + second
        parts[begin:end, 2 * NF:] = first[:, 2 * NF:]

    begins = {}
    place = 0
    waiting = None
    arrive(range(halves))
    table_copy.wait()
    for g in range(0, groups, 2):
        if g == groups // 2:
            arrive(range(halves, 2 * halves))
        start = place
        found, place = normalise([g, g + 1], place)
        begins.update(found)
        if waiting:
            transform(*waiting)
        waiting = (start, place)
    transform(*waiting)

    def piece(name, j):
        return parts[begins[name] + j * channels:begins[name] + (j + 1) * channels, :]

    def bulk_of(j):
        same = jnp.zeros((channels, parts.shape[1]), F32)
        swap = same
        for g in range(1, groups):
            value = piece(g, j)
            same = same + value * turn_same[g:g + 1, :]
            swap = swap + value * turn_swap[g:g + 1, :]
        return same + jnp.concatenate(
            [swap[:, NF:2 * NF], swap[:, :NF], pltpu.roll(swap[:, 2 * NF:], 64, 1)], axis=1
        )

    window = lax.broadcasted_iota(jnp.int32, (own, 1), 0)
    offsets = sum(jnp.where(window == w, offs[w], 0) for w in range(own))
    lane = lax.broadcasted_iota(jnp.int32, (1, NF), 1)
    outer_lane = lax.broadcasted_iota(jnp.int32, (1, 128), 1)
    outer_bin = jnp.where((outer_lane == 0) | (outer_lane == 64), K0 - 1, K0 + NF)

    def turn(bins):
        angle = jnp.bitwise_and(bins * offsets, L - 1).astype(F32) * (TWO_PI / L)
        return jnp.cos(angle), jnp.sin(angle)

    cos_turn, sin_turn = turn(lane + K0)
    cos_outer, sin_outer = turn(outer_bin)
    sign = 1.0 - 2.0 * jnp.bitwise_and(lane + K0, 1).astype(F32)
    sign_outer = 1.0 - 2.0 * jnp.bitwise_and(outer_bin, 1).astype(F32)
    channel = lax.broadcasted_iota(jnp.int32, (channels, 1), 0)
    live = 1.0 - sum(jnp.where(channel == i, dead[i], 0) for i in range(channels)).astype(F32)

    signs = jnp.concatenate([sign, sign, sign_outer], axis=1)
    reals, imags, magnitudes = [], [], []
    following = bulk_of(0)
    for w in range(own):
        spec = following + piece("edge", w)
        if w + 1 < bulk:
            following = bulk_of(w + 1)
            spec = spec + (following + piece(0, w + 1)) * signs
        spec = spec * live
        outer = spec[:, 2 * NF:]
        c, s = cos_turn[w:w + 1], sin_turn[w:w + 1]
        c_outer, s_outer = cos_outer[w:w + 1], sin_outer[w:w + 1]
        outer_imag = pltpu.roll(outer, 64, 1)

        def hann(inner, ends):
            ends = jnp.concatenate([ends, ends], axis=1)
            before = jnp.where(lane == 0, ends, pltpu.roll(inner, 1, 1))
            behind = jnp.where(lane == NF - 1, ends, pltpu.roll(inner, NF - 1, 1))
            return 0.5 * inner - 0.25 * (before + behind)

        real = hann(
            spec[:, :NF] * c - spec[:, NF:2 * NF] * s, outer * c_outer - outer_imag * s_outer
        )
        imag = hann(
            spec[:, :NF] * s + spec[:, NF:2 * NF] * c, outer * s_outer + outer_imag * c_outer
        )
        reals.append(real)
        imags.append(imag)
        magnitudes.append(jnp.sqrt(real * real + imag * imag + 1e-12))
    m_high, m_low = split(jnp.concatenate(magnitudes, axis=0))
    smooth = (dot(m_high, smooth_band) + dot(m_low, smooth_band)) * inverse_count
    scale = 1.0 / (smooth + EPS)
    flip = flip_matrix(channels)
    for w in range(own):
        here = slice(w * channels, (w + 1) * channels)
        white = jnp.concatenate([reals[w] * scale[here], imags[w] * scale[here]], axis=1)
        out[:, w * 2 * NF:(w + 1) * 2 * NF] = dot(flip, white.astype(BF16)).astype(BF16)


def flip_matrix(channels):
    row = lax.broadcasted_iota(jnp.int32, (channels, channels), 0)
    column = lax.broadcasted_iota(jnp.int32, (channels, channels), 1)
    return (row + column == channels - 1).astype(F32).astype(BF16)


def rotate_kernel(lags, own, cos_lag, sin_lag, out):
    channels = own.shape[0]
    straight = dot(flip_matrix(channels), own[...])
    real, imag = straight[:, :NF], straight[:, NF:]
    for t in range(lags):
        c, s = cos_lag[t:t + 1, :], sin_lag[t:t + 1, :]
        here = slice(t * channels, (t + 1) * channels)
        out[here, :NF] = (real * c - imag * s).astype(BF16)
        out[here, NF:] = (real * s + imag * c).astype(BF16)


def put_slots(channels, partners, present, absent):
    last = NPART // channels - 1
    nothing = jnp.zeros((channels, partners.shape[1]), BF16)

    def place(slot):
        return pl.ds(pl.multiple_of((last - slot) * channels, channels), channels)

    for block, slot, valid in present:
        partners[place(slot), :] = block[...]

        @pl.when(jnp.logical_not(valid))
        def _(slot=slot):
            partners[place(slot), :] = nothing

    for slot in absent:
        partners[place(slot), :] = nothing


def early_slots(me, count, channels, blocks, partners):
    own, ahead = blocks
    next_level = me // 4 + 1 < count // 4
    put_slots(
        channels, partners, [(own, 0, me >= 0), (ahead, 4, next_level)], (1, 2, 3, 5, 6, 7)
    )


def late_slots(me, count, channels, blocks, partners):
    core = lax.rem(me, 2)
    side = lax.rem(me // 2, 2)
    (own_swapped, ahead_swapped, far, far_swapped, cross, cross_swapped, other,
     other_swapped) = blocks
    cross_slot = 6 - 4 * side
    other_slot = 8 - cross_slot
    step = 1 - 2 * core
    next_level = me // 4 + 1 < count // 4
    second_level = me // 4 + 2 < count // 4
    other_there = (side == 0) | second_level
    put_slots(channels, partners, [
        (far, 0, second_level), (cross, cross_slot, next_level),
        (other, other_slot, other_there), (ahead_swapped, 4 + step, next_level),
        (cross_swapped, cross_slot + step, next_level),
        (other_swapped, other_slot + step, other_there),
    ], (4,))

    @pl.when(core == 0)
    def _():
        put_slots(channels, partners, [(own_swapped, 1, me >= 0)], ())

    @pl.when(core == 1)
    def _():
        put_slots(channels, partners, [(far_swapped, 7, second_level)], ())


def product_kernel(late, count, norm_scale, place, rotated, *refs):
    refs = list(refs)
    before = refs.pop(0) if late else None
    out, partners, total = refs[-3:]
    blocks = refs[:-3]
    channels = blocks[0].shape[0]
    (late_slots if late else early_slots)(place[0], count, channels, blocks, partners)
    rows, features = rotated.shape
    chunk = 2 * 2 * NF
    for begin in range(0, features, chunk):
        turned = partners[:, begin:begin + chunk].T
        product = dot(rotated[:, begin:begin + chunk], turned)
        if begin == 0:
            total[...] = product
        else:
            total[...] += product

    row = lax.broadcasted_iota(jnp.int32, (channels, NPART), 0)
    column = lax.broadcasted_iota(jnp.int32, (channels, NPART), 1)
    low = row + column >= NPART - 1
    keep = (low | (column < NPART - channels)) if late else jnp.logical_not(low)
    sheared = []
    for begin in range(0, rows, channels):
        here = slice(begin, begin + channels)
        value = jnp.where(keep, total[here, :], 0.0)
        if late:
            value = (value + before[here, :]) * norm_scale
            sheared.append(pltpu.roll(value, 1, 1, stride=1, stride_axis=0).astype(BF16))
        else:
            out[here, :] = value
    if late:
        sheared = jnp.concatenate(sheared, axis=0)
        out[...] = dot(sheared, flip_matrix(NPART)).astype(BF16)


def exchange(value, pairs):
    return lax.ppermute(value, "chan", pairs)


def local(records, dead_mask, offsets):
    channels, samples = records.shape
    tm_count = lax.axis_size("tm")
    tm_index = lax.axis_index("tm")
    chan_count = lax.axis_size("chan")
    own = samples // HOP
    windows = own * tm_count
    halves = own
    halo = 0
    if tm_count > 1:
        reach = 2 * HOP + H
        left = lax.ppermute(
            records[:, samples - H:], "tm", [(i, i + 1) for i in range(tm_count - 1)]
        )
        right = lax.ppermute(
            records[:, :reach], "tm", [(i + 1, i) for i in range(tm_count - 1)]
        )
        records = jnp.concatenate([left, records, right], axis=1)
        halves = own + 2
        halo = H
    table = jnp.asarray(packed_tables())
    own_offsets = lax.dynamic_slice_in_dim(offsets, tm_index * own, own, 0)
    vmem = pl.BlockSpec(memory_space=pltpu.VMEM)
    smem = pl.BlockSpec(memory_space=pltpu.SMEM)
    hbm = pl.BlockSpec(memory_space=pl.ANY)
    params = pltpu.CompilerParams(vmem_limit_bytes=24 * 1024 * 1024)

    bulk = min(own + 1, halves)
    part_rows = (own + bulk * (HOP // GROUP)) * channels
    spectra = pl.pallas_call(
        functools.partial(spectra_kernel, halves, own, halo),
        name="spectra",
        out_shape=jax.ShapeDtypeStruct((channels, own * 2 * NF), BF16),
        in_specs=[smem, smem, hbm, hbm],
        out_specs=vmem,
        scratch_shapes=[
            pltpu.VMEM((channels, halves * HOP + 2 * H), F32),
            pltpu.VMEM((channels, halves * HOP + 2 * H), BF16),
            pltpu.VMEM((part_rows, GROUP), BF16),
            pltpu.VMEM((part_rows, GROUP), BF16),
            pltpu.VMEM((part_rows, 2 * NF + 128), F32),
            pltpu.VMEM(table.shape, BF16),
            pltpu.SemaphoreType.DMA((2 * halves + 1,)),
        ],
        compiler_params=pltpu.CompilerParams(vmem_limit_bytes=60 * 1024 * 1024),
        cost_estimate=pl.CostEstimate(
            flops=7_000_000_000, bytes_accessed=8 * 1024 * 1024, transcendentals=0
        ),
    )(dead_mask, own_offsets, records, table)
    if tm_count > 1:
        spectra = lax.all_gather(spectra, "tm", axis=1, tiled=True)

    lags = NLAG // tm_count
    cos_lag, sin_lag = (
        lax.dynamic_slice_in_dim(jnp.asarray(t), tm_index * lags, lags, 0) for t in lag_tables()
    )
    place = lax.axis_index("chan").astype(jnp.int32).reshape(1)
    norm_scale = 1.0 / math.sqrt(2.0 * NF * windows)

    features = spectra.shape[1]
    rotated = pl.pallas_call(
        functools.partial(rotate_kernel, lags),
        name="rotate",
        grid=(windows,),
        out_shape=jax.ShapeDtypeStruct((lags * channels, features), BF16),
        in_specs=[
            pl.BlockSpec((channels, 2 * NF), lambda w: (0, w)),
            pl.BlockSpec((lags, NF), lambda w: (0, 0)),
            pl.BlockSpec((lags, NF), lambda w: (0, 0)),
        ],
        out_specs=pl.BlockSpec((lags * channels, 2 * NF), lambda w: (0, w)),
        compiler_params=params,
        cost_estimate=pl.CostEstimate(
            flops=4_000_000_000, bytes_accessed=8 * 1024 * 1024, transcendentals=0
        ),
    )(spectra, cos_lag, sin_lag)

    def product(blocks, before):
        late = before is not None
        operands = [place, rotated] + ([before] if late else []) + list(blocks)
        return pl.pallas_call(
            functools.partial(product_kernel, late, chan_count, norm_scale),
            name="late_product" if late else "early_product",
            out_shape=jax.ShapeDtypeStruct((lags * channels, NPART), BF16 if late else F32),
            in_specs=[smem] + [vmem] * (len(operands) - 1),
            out_specs=vmem,
            scratch_shapes=[
                pltpu.VMEM((NPART, features), BF16),
                pltpu.VMEM((lags * channels, NPART), F32),
            ],
            compiler_params=params,
            cost_estimate=pl.CostEstimate(
                flops=2 * lags * channels * features * NPART, bytes_accessed=6 * 1024 * 1024,
                transcendentals=0,
            ),
        )(*operands)

    every = range(chan_count)
    down = [(i, (i - 4) % chan_count) for i in every]
    top = chan_count - 4

    def far_target(i):
        return i if i >= top else (i - 4 if i >= 4 else top - 4 + i)

    def other_target(i):
        if i & 2:
            return i - 2
        return i + 2 if i >= top else (i - 2 if i >= 4 else top - 2 + i)

    far_pairs = [(i, far_target(i)) for i in every]
    other_pairs = [(i, other_target(i)) for i in every]
    across = [(i, i ^ 2) for i in every]
    cores = [(i, i ^ 1) for i in every]
    side = lax.rem(lax.axis_index("chan") // 2, 2)

    ahead = exchange(spectra, down)
    ahead, rotated = lax.optimization_barrier((ahead, rotated))
    cross = exchange(ahead, across)
    other = exchange(jnp.where(side == 0, ahead, spectra), other_pairs)
    far = exchange(ahead, far_pairs)
    early = product((spectra, ahead), None)
    kept, ahead, cross, early = lax.optimization_barrier((spectra, ahead, cross, early))
    own_swapped = exchange(kept, cores)
    ahead_swapped = exchange(ahead, cores)
    other_swapped = exchange(other, cores)
    far, other_swapped, own_swapped, ahead_swapped = lax.optimization_barrier(
        (far, other_swapped, own_swapped, ahead_swapped)
    )
    blocks = (own_swapped, ahead_swapped, far, exchange(far, cores), cross,
              exchange(cross, cores), other, other_swapped)
    return product(blocks, early).reshape(lags, channels, NPART)


def solution(mesh):
    return jax.shard_map(
        local,
        mesh=mesh,
        in_specs=(P(("win", "chan"), "tm"), P(("win", "chan")), P("win")),
        out_specs=P("tm", ("win", "chan"), None),
        check_vma=False,
    )
```

```python
import functools
import math

import jax
import jax.numpy as jnp
import ml_dtypes
import numpy as np
from jax import lax
from jax.experimental import pallas as pl
from jax.experimental.pallas import tpu as pltpu
from jax.sharding import PartitionSpec as P

L = 8192
HOP = 4096
H = 128
K0 = 32
NF = 256
WB = 64
NLAG = 32
NPART = 256
EDGE = 512
STEP = 256
GROUP = 512
EPS = 1e-05
TWO_PI = 2.0 * math.pi
BF16 = jnp.bfloat16
F32 = jnp.float32


def split_table(table):
    high = table.astype(ml_dtypes.bfloat16)
    low = (table - high.astype(np.float64)).astype(ml_dtypes.bfloat16)
    return high, low


@functools.cache
def fourier_tables():
    samples = np.arange(GROUP)[:, None]
    bins = K0 + np.arange(NF)[None, :]
    angle = (samples * bins % L) * (TWO_PI / L)
    inner = np.concatenate([np.cos(angle), -np.sin(angle)], axis=1)
    outer = np.zeros((GROUP, 128))
    for lane, k, wave in ((0, K0 - 1, np.cos), (64, K0 - 1, np.sin), (127, K0 + NF, np.cos), (63, K0 + NF, np.sin)):
        sign = 1.0 if wave is np.cos else -1.0
        outer[:, lane] = sign * wave((samples[:, 0] * k % L) * (TWO_PI / L))
    high, low = split_table(inner)
    return np.concatenate([high, outer.astype(ml_dtypes.bfloat16)], axis=1), low


@functools.cache
def packed_tables():
    return np.concatenate(fourier_tables(), axis=1)


@functools.cache
def lag_tables():
    lags = np.arange(NLAG)[:, None] - NLAG // 2
    angle = (lags * (K0 + np.arange(NF))[None, :] % L) * (TWO_PI / L)
    return np.cos(angle).astype(np.float32), np.sin(angle).astype(np.float32)


def split(value):
    high = value.astype(BF16)
    return high, (value - high.astype(F32)).astype(BF16)


def inverse(value):
    guess = pl.reciprocal(value, approx=True)
    return guess * (2.0 - value * guess)


def dot(a, b):
    return jnp.dot(a, b, preferred_element_type=F32)


def spectra_kernel(
    halves, own, halo,
    dead, offs, x_hbm, table_hbm, out, x, absolute, norm_high, norm_low, parts, table, sems,
):
    channels = x.shape[0]
    groups = HOP // GROUP
    bulk = min(own + 1, halves)
    edges = min(own + 2, halves)
    width = halves * HOP
    middle = HOP // 2 + H
    firsts, seconds = [], []
    for j in range(halves):
        firsts.append((j * HOP - (H if j or halo else 0), j * HOP + middle))
        seconds.append((j * HOP + middle, (j + 1) * HOP - H if j + 1 < halves else width + halo))
    copies = [
        pltpu.make_async_copy(
            x_hbm.at[:, pl.ds(halo + begin, end - begin)], x.at[:, pl.ds(H + begin, end - begin)],
            sems.at[i],
        )
        for i, (begin, end) in enumerate(firsts + seconds)
    ]
    table_copy = pltpu.make_async_copy(table_hbm, table, sems.at[2 * halves])
    for copy in copies[:halves] + [table_copy] + copies[halves:]:
        copy.start()
    if not halo:
        for begin in (0, H + width):
            absolute[:, begin:begin + H] = jnp.zeros((channels, H), BF16)

    def arrive(ids):
        for i in ids:
            copies[i].wait()
        for i in ids:
            begin, end = (firsts + seconds)[i]
            here = slice(H + begin, H + end)
            absolute[:, here] = jnp.abs(x[:, here]).astype(BF16)

    high = table.at[:, :2 * NF + 128]
    low = table.at[:, 2 * NF + 128:]
    from_lane = lax.broadcasted_iota(jnp.int32, (2 * H + STEP, STEP), 0)
    to_lane = lax.broadcasted_iota(jnp.int32, (2 * H + STEP, STEP), 1)
    level_band = ((from_lane >= to_lane) & (from_lane <= to_lane + 2 * H)).astype(F32).astype(BF16)
    from_bin = lax.broadcasted_iota(jnp.int32, (NF, NF), 0)
    to_bin = lax.broadcasted_iota(jnp.int32, (NF, NF), 1)
    smooth_band = (jnp.abs(from_bin - to_bin) <= WB).astype(F32).astype(BF16)
    lane = lax.broadcasted_iota(jnp.int32, (1, parts.shape[1]), 1)
    outer_place = lane - 2 * NF
    outer_first = (outer_place == 0) | (outer_place == 64)
    every_bin = jnp.where(
        lane < 2 * NF, jnp.bitwise_and(lane, NF - 1) + K0, jnp.where(outer_first, K0 - 1, K0 + NF)
    )
    real_place = (lane < NF) | (outer_place == 0) | (outer_place == 127)
    group = lax.broadcasted_iota(jnp.int32, (groups, 1), 0) * GROUP
    angle = jnp.bitwise_and(group * every_bin, L - 1).astype(F32) * (TWO_PI / L)
    turn_same = jnp.cos(angle)
    turn_swap = jnp.sin(angle) * jnp.where(real_place, -1.0, 1.0)
    bin_index = lax.broadcasted_iota(jnp.int32, (1, NF), 1)
    below, above = jnp.minimum(bin_index, WB), jnp.minimum(NF - 1 - bin_index, WB)
    inverse_count = 1.0 / (below + above + 1).astype(F32)

    def rows(ref, begin, length, count):
        return [ref[:, begin + j * HOP:begin + j * HOP + length] for j in range(count)]

    def store(place, value):
        here = slice(place, place + value.shape[0])
        norm_high[here, :], norm_low[here, :] = split(value)

    def normalise(group_ids, place):
        blocks = [(g, g * GROUP + part * STEP) for g in group_ids for part in range(GROUP // STEP)]
        counts = [edges if g == 0 else bulk for g, _ in blocks]
        level = dot(
            jnp.concatenate(
                [r for (_, begin), n in zip(blocks, counts)
                 for r in rows(absolute, begin, STEP + 2 * H, n)], axis=0
            ), level_band,
        ) * (1.0 / (2 * H + 1)) + EPS
        values = []
        at = 0
        for (_, begin), n in zip(blocks, counts):
            samples = jnp.concatenate(rows(x, H + begin, STEP, n), axis=0)
            values.append(samples * inverse(level[at:at + n * channels]))
            at += n * channels
        begins = {}
        for index, g in enumerate(group_ids):
            value = jnp.concatenate(values[2 * index:2 * index + 2], axis=1)
            if g == 0:
                lane = lax.broadcasted_iota(jnp.int32, (channels, EDGE), 1)
                merged = []
                for w in range(own):
                    mine = value[w * channels:(w + 1) * channels]
                    other = (
                        value[(w + 2) * channels:(w + 3) * channels]
                        if w + 2 < edges else jnp.zeros_like(mine)
                    )
                    merged.append(jnp.where(lane >= offs[w], mine, other))
                begins["edge"] = place
                store(place, jnp.concatenate(merged, axis=0))
                place += own * channels
                value = value[:bulk * channels]
            begins[g] = place
            store(place, value)
            place += bulk * channels
        return begins, place

    def transform(begin, end):
        first = dot(norm_high[begin:end, :], high[...])
        second = dot(norm_low[begin:end, :], high[:, :2 * NF])
        second = second + dot(norm_high[begin:end, :], low[...])
        parts[begin:end, :2 * NF] = first[:, :2 * NF] + second
        parts[begin:end, 2 * NF:] = first[:, 2 * NF:]

    begins = {}
    place = 0
    waiting = None
    arrive(range(halves))
    table_copy.wait()
    for g in range(0, groups, 2):
        start = place
        found, place = normalise([g, g + 1], place)
        begins.update(found)
        if g + 2 == groups // 2:
            arrive(range(halves, 2 * halves))
        if waiting:
            transform(*waiting)
        waiting = (start, place)
    transform(*waiting)

    def piece(name, j):
        return parts[begins[name] + j * channels:begins[name] + (j + 1) * channels, :]

    def bulk_of(j):
        same = jnp.zeros((channels, parts.shape[1]), F32)
        swap = same
        for g in range(1, groups):
            value = piece(g, j)
            same = same + value * turn_same[g:g + 1, :]
            swap = swap + value * turn_swap[g:g + 1, :]
        return same + jnp.concatenate(
            [swap[:, NF:2 * NF], swap[:, :NF], pltpu.roll(swap[:, 2 * NF:], 64, 1)], axis=1
        )

    window = lax.broadcasted_iota(jnp.int32, (own, 1), 0)
    offsets = sum(jnp.where(window == w, offs[w], 0) for w in range(own))
    lane = lax.broadcasted_iota(jnp.int32, (1, NF), 1)
    outer_lane = lax.broadcasted_iota(jnp.int32, (1, 128), 1)
    outer_bin = jnp.where((outer_lane == 0) | (outer_lane == 64), K0 - 1, K0 + NF)

    def turn(bins):
        angle = jnp.bitwise_and(bins * offsets, L - 1).astype(F32) * (TWO_PI / L)
        return jnp.cos(angle), jnp.sin(angle)

    cos_turn, sin_turn = turn(lane + K0)
    cos_outer, sin_outer = turn(outer_bin)
    sign = 1.0 - 2.0 * jnp.bitwise_and(lane + K0, 1).astype(F32)
    sign_outer = 1.0 - 2.0 * jnp.bitwise_and(outer_bin, 1).astype(F32)
    channel = lax.broadcasted_iota(jnp.int32, (channels, 1), 0)
    live = 1.0 - sum(jnp.where(channel == i, dead[i], 0) for i in range(channels)).astype(F32)

    signs = jnp.concatenate([sign, sign, sign_outer], axis=1)
    reals, imags, magnitudes = [], [], []
    following = bulk_of(0)
    for w in range(own):
        spec = following + piece("edge", w)
        if w + 1 < bulk:
            following = bulk_of(w + 1)
            spec = spec + (following + piece(0, w + 1)) * signs
        spec = spec * live
        outer = spec[:, 2 * NF:]
        c, s = cos_turn[w:w + 1], sin_turn[w:w + 1]
        c_outer, s_outer = cos_outer[w:w + 1], sin_outer[w:w + 1]
        outer_imag = pltpu.roll(outer, 64, 1)

        def hann(inner, ends):
            ends = jnp.concatenate([ends, ends], axis=1)
            before = jnp.where(lane == 0, ends, pltpu.roll(inner, 1, 1))
            behind = jnp.where(lane == NF - 1, ends, pltpu.roll(inner, NF - 1, 1))
            return 0.5 * inner - 0.25 * (before + behind)

        real = hann(
            spec[:, :NF] * c - spec[:, NF:2 * NF] * s, outer * c_outer - outer_imag * s_outer
        )
        imag = hann(
            spec[:, :NF] * s + spec[:, NF:2 * NF] * c, outer * s_outer + outer_imag * c_outer
        )
        reals.append(real)
        imags.append(imag)
        magnitudes.append(jnp.sqrt(real * real + imag * imag + 1e-12))
    m_high, m_low = split(jnp.concatenate(magnitudes, axis=0))
    smooth = (dot(m_high, smooth_band) + dot(m_low, smooth_band)) * inverse_count
    scale = 1.0 / (smooth + EPS)
    flip = flip_matrix(channels)
    for w in range(own):
        here = slice(w * channels, (w + 1) * channels)
        white = jnp.concatenate([reals[w] * scale[here], imags[w] * scale[here]], axis=1)
        out[:, w * 2 * NF:(w + 1) * 2 * NF] = dot(flip, white.astype(BF16)).astype(BF16)


def flip_matrix(channels):
    row = lax.broadcasted_iota(jnp.int32, (channels, channels), 0)
    column = lax.broadcasted_iota(jnp.int32, (channels, channels), 1)
    return (row + column == channels - 1).astype(F32).astype(BF16)


def rotate_kernel(lags, own, cos_lag, sin_lag, out):
    channels = own.shape[0]
    straight = dot(flip_matrix(channels), own[...])
    real, imag = straight[:, :NF], straight[:, NF:]
    for t in range(lags):
        c, s = cos_lag[t:t + 1, :], sin_lag[t:t + 1, :]
        here = slice(t * channels, (t + 1) * channels)
        out[here, :NF] = (real * c - imag * s).astype(BF16)
        out[here, NF:] = (real * s + imag * c).astype(BF16)


def put_slots(channels, partners, present, absent):
    last = NPART // channels - 1
    nothing = jnp.zeros((channels, partners.shape[1]), BF16)

    def place(slot):
        return pl.ds(pl.multiple_of((last - slot) * channels, channels), channels)

    for block, slot, valid in present:
        partners[place(slot), :] = block[...]

        @pl.when(jnp.logical_not(valid))
        def _(slot=slot):
            partners[place(slot), :] = nothing

    for slot in absent:
        partners[place(slot), :] = nothing


def early_slots(me, count, channels, blocks, partners):
    own, ahead = blocks
    next_level = me // 4 + 1 < count // 4
    put_slots(
        channels, partners, [(own, 0, me >= 0), (ahead, 4, next_level)], (1, 2, 3, 5, 6, 7)
    )


def late_slots(me, count, channels, blocks, partners):
    core = lax.rem(me, 2)
    side = lax.rem(me // 2, 2)
    (own_swapped, ahead_swapped, far, far_swapped, cross, cross_swapped, other,
     other_swapped) = blocks
    cross_slot = 6 - 4 * side
    other_slot = 8 - cross_slot
    step = 1 - 2 * core
    next_level = me // 4 + 1 < count // 4
    second_level = me // 4 + 2 < count // 4
    other_there = (side == 0) | second_level
    put_slots(channels, partners, [
        (far, 0, second_level), (cross, cross_slot, next_level),
        (other, other_slot, other_there), (ahead_swapped, 4 + step, next_level),
        (cross_swapped, cross_slot + step, next_level),
        (other_swapped, other_slot + step, other_there),
    ], (4,))

    @pl.when(core == 0)
    def _():
        put_slots(channels, partners, [(own_swapped, 1, me >= 0)], ())

    @pl.when(core == 1)
    def _():
        put_slots(channels, partners, [(far_swapped, 7, second_level)], ())


def product_kernel(late, count, norm_scale, place, rotated, *refs):
    refs = list(refs)
    before = refs.pop(0) if late else None
    out, partners, total = refs[-3:]
    blocks = refs[:-3]
    channels = blocks[0].shape[0]
    (late_slots if late else early_slots)(place[0], count, channels, blocks, partners)
    rows, features = rotated.shape
    chunk = 2 * 2 * NF
    for begin in range(0, features, chunk):
        turned = partners[:, begin:begin + chunk].T
        product = dot(rotated[:, begin:begin + chunk], turned)
        if begin == 0:
            total[...] = product
        else:
            total[...] += product

    row = lax.broadcasted_iota(jnp.int32, (channels, NPART), 0)
    column = lax.broadcasted_iota(jnp.int32, (channels, NPART), 1)
    low = row + column >= NPART - 1
    keep = (low | (column < NPART - channels)) if late else jnp.logical_not(low)
    sheared = []
    for begin in range(0, rows, channels):
        here = slice(begin, begin + channels)
        value = jnp.where(keep, total[here, :], 0.0)
        if late:
            value = (value + before[here, :]) * norm_scale
            sheared.append(pltpu.roll(value, 1, 1, stride=1, stride_axis=0).astype(BF16))
        else:
            out[here, :] = value
    if late:
        sheared = jnp.concatenate(sheared, axis=0)
        out[...] = dot(sheared, flip_matrix(NPART)).astype(BF16)


def exchange(value, pairs):
    return lax.ppermute(value, "chan", pairs)


def local(records, dead_mask, offsets):
    channels, samples = records.shape
    tm_count = lax.axis_size("tm")
    tm_index = lax.axis_index("tm")
    chan_count = lax.axis_size("chan")
    own = samples // HOP
    windows = own * tm_count
    halves = own
    halo = 0
    if tm_count > 1:
        reach = 2 * HOP + H
        left = lax.ppermute(
            records[:, samples - H:], "tm", [(i, i + 1) for i in range(tm_count - 1)]
        )
        right = lax.ppermute(
            records[:, :reach], "tm", [(i + 1, i) for i in range(tm_count - 1)]
        )
        records = jnp.concatenate([left, records, right], axis=1)
        halves = own + 2
        halo = H
    table = jnp.asarray(packed_tables())
    own_offsets = lax.dynamic_slice_in_dim(offsets, tm_index * own, own, 0)
    vmem = pl.BlockSpec(memory_space=pltpu.VMEM)
    smem = pl.BlockSpec(memory_space=pltpu.SMEM)
    hbm = pl.BlockSpec(memory_space=pl.ANY)
    params = pltpu.CompilerParams(vmem_limit_bytes=24 * 1024 * 1024)

    bulk = min(own + 1, halves)
    part_rows = (own + bulk * (HOP // GROUP)) * channels
    spectra = pl.pallas_call(
        functools.partial(spectra_kernel, halves, own, halo),
        name="spectra",
        out_shape=jax.ShapeDtypeStruct((channels, own * 2 * NF), BF16),
        in_specs=[smem, smem, hbm, hbm],
        out_specs=vmem,
        scratch_shapes=[
            pltpu.VMEM((channels, halves * HOP + 2 * H), F32),
            pltpu.VMEM((channels, halves * HOP + 2 * H), BF16),
            pltpu.VMEM((part_rows, GROUP), BF16),
            pltpu.VMEM((part_rows, GROUP), BF16),
            pltpu.VMEM((part_rows, 2 * NF + 128), F32),
            pltpu.VMEM(table.shape, BF16),
            pltpu.SemaphoreType.DMA((2 * halves + 1,)),
        ],
        compiler_params=pltpu.CompilerParams(vmem_limit_bytes=60 * 1024 * 1024),
        cost_estimate=pl.CostEstimate(
            flops=7_000_000_000, bytes_accessed=8 * 1024 * 1024, transcendentals=0
        ),
    )(dead_mask, own_offsets, records, table)
    if tm_count > 1:
        spectra = lax.all_gather(spectra, "tm", axis=1, tiled=True)

    lags = NLAG // tm_count
    cos_lag, sin_lag = (
        lax.dynamic_slice_in_dim(jnp.asarray(t), tm_index * lags, lags, 0) for t in lag_tables()
    )
    place = lax.axis_index("chan").astype(jnp.int32).reshape(1)
    norm_scale = 1.0 / math.sqrt(2.0 * NF * windows)

    features = spectra.shape[1]
    rotated = pl.pallas_call(
        functools.partial(rotate_kernel, lags),
        name="rotate",
        grid=(windows,),
        out_shape=jax.ShapeDtypeStruct((lags * channels, features), BF16),
        in_specs=[
            pl.BlockSpec((channels, 2 * NF), lambda w: (0, w)),
            pl.BlockSpec((lags, NF), lambda w: (0, 0)),
            pl.BlockSpec((lags, NF), lambda w: (0, 0)),
        ],
        out_specs=pl.BlockSpec((lags * channels, 2 * NF), lambda w: (0, w)),
        compiler_params=params,
        cost_estimate=pl.CostEstimate(
            flops=4_000_000_000, bytes_accessed=8 * 1024 * 1024, transcendentals=0
        ),
    )(spectra, cos_lag, sin_lag)

    def product(blocks, before):
        late = before is not None
        operands = [place, rotated] + ([before] if late else []) + list(blocks)
        return pl.pallas_call(
            functools.partial(product_kernel, late, chan_count, norm_scale),
            name="late_product" if late else "early_product",
            out_shape=jax.ShapeDtypeStruct((lags * channels, NPART), BF16 if late else F32),
            in_specs=[smem] + [vmem] * (len(operands) - 1),
            out_specs=vmem,
            scratch_shapes=[
                pltpu.VMEM((NPART, features), BF16),
                pltpu.VMEM((lags * channels, NPART), F32),
            ],
            compiler_params=params,
            cost_estimate=pl.CostEstimate(
                flops=2 * lags * channels * features * NPART, bytes_accessed=6 * 1024 * 1024,
                transcendentals=0,
            ),
        )(*operands)

    every = range(chan_count)
    down = [(i, (i - 4) % chan_count) for i in every]
    top = chan_count - 4

    def far_target(i):
        return i if i >= top else (i - 4 if i >= 4 else top - 4 + i)

    def other_target(i):
        if i & 2:
            return i - 2
        return i + 2 if i >= top else (i - 2 if i >= 4 else top - 2 + i)

    far_pairs = [(i, far_target(i)) for i in every]
    other_pairs = [(i, other_target(i)) for i in every]
    across = [(i, i ^ 2) for i in every]
    cores = [(i, i ^ 1) for i in every]
    side = lax.rem(lax.axis_index("chan") // 2, 2)

    ahead = exchange(spectra, down)
    ahead, rotated = lax.optimization_barrier((ahead, rotated))
    cross = exchange(ahead, across)
    other = exchange(jnp.where(side == 0, ahead, spectra), other_pairs)
    far = exchange(ahead, far_pairs)
    early = product((spectra, ahead), None)
    cross, other, early = lax.optimization_barrier((cross, other, early))
    own_swapped = exchange(spectra, cores)
    ahead_swapped = exchange(ahead, cores)
    other_swapped = exchange(other, cores)
    far, other_swapped = lax.optimization_barrier((far, other_swapped))
    blocks = (own_swapped, ahead_swapped, far, exchange(far, cores), cross,
              exchange(cross, cores), other, other_swapped)
    return product(blocks, early).reshape(lags, channels, NPART)


def solution(mesh):
    return jax.shard_map(
        local,
        mesh=mesh,
        in_specs=(P(("win", "chan"), "tm"), P(("win", "chan")), P("win")),
        out_specs=P("tm", ("win", "chan"), None),
        check_vma=False,
    )
```

```python
import functools
import math

import jax
import jax.numpy as jnp
import ml_dtypes
import numpy as np
from jax import lax
from jax.experimental import pallas as pl
from jax.experimental.pallas import tpu as pltpu
from jax.sharding import PartitionSpec as P

L = 8192
HOP = 4096
H = 128
K0 = 32
NF = 256
WB = 64
NLAG = 32
NPART = 256
EDGE = 512
STEP = 256
GROUP = 512
EPS = 1e-05
TWO_PI = 2.0 * math.pi
BF16 = jnp.bfloat16
F32 = jnp.float32


def split_table(table):
    high = table.astype(ml_dtypes.bfloat16)
    low = (table - high.astype(np.float64)).astype(ml_dtypes.bfloat16)
    return high, low


@functools.cache
def fourier_tables():
    samples = np.arange(GROUP)[:, None]
    bins = K0 + np.arange(NF)[None, :]
    angle = (samples * bins % L) * (TWO_PI / L)
    inner = np.concatenate([np.cos(angle), -np.sin(angle)], axis=1)
    outer = np.zeros((GROUP, 128))
    for lane, k, wave in ((0, K0 - 1, np.cos), (64, K0 - 1, np.sin), (127, K0 + NF, np.cos), (63, K0 + NF, np.sin)):
        sign = 1.0 if wave is np.cos else -1.0
        outer[:, lane] = sign * wave((samples[:, 0] * k % L) * (TWO_PI / L))
    high, low = split_table(inner)
    return np.concatenate([high, outer.astype(ml_dtypes.bfloat16)], axis=1), low


@functools.cache
def packed_tables():
    return np.concatenate(fourier_tables(), axis=1)


@functools.cache
def lag_tables():
    lags = np.arange(NLAG)[:, None] - NLAG // 2
    angle = (lags * (K0 + np.arange(NF))[None, :] % L) * (TWO_PI / L)
    return np.cos(angle).astype(np.float32), np.sin(angle).astype(np.float32)


def split(value):
    high = value.astype(BF16)
    return high, (value - high.astype(F32)).astype(BF16)


def inverse(value):
    guess = pl.reciprocal(value, approx=True)
    return guess * (2.0 - value * guess)


def dot(a, b):
    return jnp.dot(a, b, preferred_element_type=F32)


def spectra_kernel(
    halves, own, halo,
    dead, offs, x_hbm, table_hbm, out, x, absolute, norm_high, norm_low, parts, table, sems,
):
    channels = x.shape[0]
    groups = HOP // GROUP
    bulk = min(own + 1, halves)
    edges = min(own + 2, halves)
    width = halves * HOP
    cuts = [HOP // 4 + H, HOP // 2 + H]
    pieces = []
    for part in range(3):
        for j in range(halves):
            begin = j * HOP + cuts[part - 1] if part else j * HOP - (H if j or halo else 0)
            end = (j + 1) * HOP - H if j + 1 < halves else width + halo
            pieces.append((begin, j * HOP + cuts[part] if part < 2 else end))
    copies = [
        pltpu.make_async_copy(
            x_hbm.at[:, pl.ds(halo + begin, end - begin)], x.at[:, pl.ds(H + begin, end - begin)],
            sems.at[i],
        )
        for i, (begin, end) in enumerate(pieces)
    ]
    table_copy = pltpu.make_async_copy(table_hbm, table, sems.at[3 * halves])
    for copy in copies[:2 * halves] + [table_copy] + copies[2 * halves:]:
        copy.start()
    if not halo:
        for begin in (0, H + width):
            absolute[:, begin:begin + H] = jnp.zeros((channels, H), BF16)

    def arrive(part):
        ids = range(part * halves, (part + 1) * halves)
        for i in ids:
            copies[i].wait()
        for i in ids:
            begin, end = pieces[i]
            here = slice(H + begin, H + end)
            absolute[:, here] = jnp.abs(x[:, here]).astype(BF16)

    high = table.at[:, :2 * NF + 128]
    low = table.at[:, 2 * NF + 128:]
    from_lane = lax.broadcasted_iota(jnp.int32, (2 * H + STEP, STEP), 0)
    to_lane = lax.broadcasted_iota(jnp.int32, (2 * H + STEP, STEP), 1)
    level_band = ((from_lane >= to_lane) & (from_lane <= to_lane + 2 * H)).astype(F32).astype(BF16)
    from_bin = lax.broadcasted_iota(jnp.int32, (NF, NF), 0)
    to_bin = lax.broadcasted_iota(jnp.int32, (NF, NF), 1)
    smooth_band = (jnp.abs(from_bin - to_bin) <= WB).astype(F32).astype(BF16)
    lane = lax.broadcasted_iota(jnp.int32, (1, parts.shape[1]), 1)
    outer_place = lane - 2 * NF
    outer_first = (outer_place == 0) | (outer_place == 64)
    every_bin = jnp.where(
        lane < 2 * NF, jnp.bitwise_and(lane, NF - 1) + K0, jnp.where(outer_first, K0 - 1, K0 + NF)
    )
    real_place = (lane < NF) | (outer_place == 0) | (outer_place == 127)
    group = lax.broadcasted_iota(jnp.int32, (groups, 1), 0) * GROUP
    angle = jnp.bitwise_and(group * every_bin, L - 1).astype(F32) * (TWO_PI / L)
    turn_same = jnp.cos(angle)
    turn_swap = jnp.sin(angle) * jnp.where(real_place, -1.0, 1.0)
    bin_index = lax.broadcasted_iota(jnp.int32, (1, NF), 1)
    below, above = jnp.minimum(bin_index, WB), jnp.minimum(NF - 1 - bin_index, WB)
    inverse_count = 1.0 / (below + above + 1).astype(F32)

    def rows(ref, begin, length, count):
        return [ref[:, begin + j * HOP:begin + j * HOP + length] for j in range(count)]

    def store(place, value):
        here = slice(place, place + value.shape[0])
        norm_high[here, :], norm_low[here, :] = split(value)

    def normalise(group_ids, place):
        blocks = [(g, g * GROUP + part * STEP) for g in group_ids for part in range(GROUP // STEP)]
        counts = [edges if g == 0 else bulk for g, _ in blocks]
        level = dot(
            jnp.concatenate(
                [r for (_, begin), n in zip(blocks, counts)
                 for r in rows(absolute, begin, STEP + 2 * H, n)], axis=0
            ), level_band,
        ) * (1.0 / (2 * H + 1)) + EPS
        values = []
        at = 0
        for (_, begin), n in zip(blocks, counts):
            samples = jnp.concatenate(rows(x, H + begin, STEP, n), axis=0)
            values.append(samples * inverse(level[at:at + n * channels]))
            at += n * channels
        begins = {}
        for index, g in enumerate(group_ids):
            value = jnp.concatenate(values[2 * index:2 * index + 2], axis=1)
            if g == 0:
                lane = lax.broadcasted_iota(jnp.int32, (channels, EDGE), 1)
                merged = []
                for w in range(own):
                    mine = value[w * channels:(w + 1) * channels]
                    other = (
                        value[(w + 2) * channels:(w + 3) * channels]
                        if w + 2 < edges else jnp.zeros_like(mine)
                    )
                    merged.append(jnp.where(lane >= offs[w], mine, other))
                begins["edge"] = place
                store(place, jnp.concatenate(merged, axis=0))
                place += own * channels
                value = value[:bulk * channels]
            begins[g] = place
            store(place, value)
            place += bulk * channels
        return begins, place

    def transform(begin, end):
        first = dot(norm_high[begin:end, :], high[...])
        second = dot(norm_low[begin:end, :], high[:, :2 * NF])
        second = second + dot(norm_high[begin:end, :], low[...])
        parts[begin:end, :2 * NF] = first[:, :2 * NF] + second
        parts[begin:end, 2 * NF:] = first[:, 2 * NF:]

    begins = {}
    place = 0
    waiting = None
    for g in range(0, groups, 2):
        if g < 4:
            arrive(g // 2)
        start = place
        found, place = normalise([g, g + 1], place)
        begins.update(found)
        if g == 2:
            arrive(2)
            table_copy.wait()
        if waiting:
            transform(*waiting)
        waiting = (start, place)
    transform(*waiting)

    def piece(name, j):
        return parts[begins[name] + j * channels:begins[name] + (j + 1) * channels, :]

    def bulk_of(j):
        same = jnp.zeros((channels, parts.shape[1]), F32)
        swap = same
        for g in range(1, groups):
            value = piece(g, j)
            same = same + value * turn_same[g:g + 1, :]
            swap = swap + value * turn_swap[g:g + 1, :]
        return same + jnp.concatenate(
            [swap[:, NF:2 * NF], swap[:, :NF], pltpu.roll(swap[:, 2 * NF:], 64, 1)], axis=1
        )

    window = lax.broadcasted_iota(jnp.int32, (own, 1), 0)
    offsets = sum(jnp.where(window == w, offs[w], 0) for w in range(own))
    lane = lax.broadcasted_iota(jnp.int32, (1, NF), 1)
    outer_lane = lax.broadcasted_iota(jnp.int32, (1, 128), 1)
    outer_bin = jnp.where((outer_lane == 0) | (outer_lane == 64), K0 - 1, K0 + NF)

    def turn(bins):
        angle = jnp.bitwise_and(bins * offsets, L - 1).astype(F32) * (TWO_PI / L)
        return jnp.cos(angle), jnp.sin(angle)

    cos_turn, sin_turn = turn(lane + K0)
    cos_outer, sin_outer = turn(outer_bin)
    sign = 1.0 - 2.0 * jnp.bitwise_and(lane + K0, 1).astype(F32)
    sign_outer = 1.0 - 2.0 * jnp.bitwise_and(outer_bin, 1).astype(F32)
    channel = lax.broadcasted_iota(jnp.int32, (channels, 1), 0)
    live = 1.0 - sum(jnp.where(channel == i, dead[i], 0) for i in range(channels)).astype(F32)

    signs = jnp.concatenate([sign, sign, sign_outer], axis=1)
    reals, imags, magnitudes = [], [], []
    following = bulk_of(0)
    for w in range(own):
        spec = following + piece("edge", w)
        if w + 1 < bulk:
            following = bulk_of(w + 1)
            spec = spec + (following + piece(0, w + 1)) * signs
        spec = spec * live
        outer = spec[:, 2 * NF:]
        c, s = cos_turn[w:w + 1], sin_turn[w:w + 1]
        c_outer, s_outer = cos_outer[w:w + 1], sin_outer[w:w + 1]
        outer_imag = pltpu.roll(outer, 64, 1)

        def hann(inner, ends):
            ends = jnp.concatenate([ends, ends], axis=1)
            before = jnp.where(lane == 0, ends, pltpu.roll(inner, 1, 1))
            behind = jnp.where(lane == NF - 1, ends, pltpu.roll(inner, NF - 1, 1))
            return 0.5 * inner - 0.25 * (before + behind)

        real = hann(
            spec[:, :NF] * c - spec[:, NF:2 * NF] * s, outer * c_outer - outer_imag * s_outer
        )
        imag = hann(
            spec[:, :NF] * s + spec[:, NF:2 * NF] * c, outer * s_outer + outer_imag * c_outer
        )
        reals.append(real)
        imags.append(imag)
        magnitudes.append(jnp.sqrt(real * real + imag * imag + 1e-12))
    m_high, m_low = split(jnp.concatenate(magnitudes, axis=0))
    smooth = (dot(m_high, smooth_band) + dot(m_low, smooth_band)) * inverse_count
    scale = 1.0 / (smooth + EPS)
    flip = flip_matrix(channels)
    for w in range(own):
        here = slice(w * channels, (w + 1) * channels)
        white = jnp.concatenate([reals[w] * scale[here], imags[w] * scale[here]], axis=1)
        out[:, w * 2 * NF:(w + 1) * 2 * NF] = dot(flip, white.astype(BF16)).astype(BF16)


def flip_matrix(channels):
    row = lax.broadcasted_iota(jnp.int32, (channels, channels), 0)
    column = lax.broadcasted_iota(jnp.int32, (channels, channels), 1)
    return (row + column == channels - 1).astype(F32).astype(BF16)


def rotate_kernel(lags, own, cos_lag, sin_lag, out):
    channels = own.shape[0]
    straight = dot(flip_matrix(channels), own[...])
    real, imag = straight[:, :NF], straight[:, NF:]
    for t in range(lags):
        c, s = cos_lag[t:t + 1, :], sin_lag[t:t + 1, :]
        here = slice(t * channels, (t + 1) * channels)
        out[here, :NF] = (real * c - imag * s).astype(BF16)
        out[here, NF:] = (real * s + imag * c).astype(BF16)


def put_slots(channels, partners, present, absent):
    last = NPART // channels - 1
    nothing = jnp.zeros((channels, partners.shape[1]), BF16)

    def place(slot):
        return pl.ds(pl.multiple_of((last - slot) * channels, channels), channels)

    for block, slot, valid in present:
        partners[place(slot), :] = block[...]

        @pl.when(jnp.logical_not(valid))
        def _(slot=slot):
            partners[place(slot), :] = nothing

    for slot in absent:
        partners[place(slot), :] = nothing


def early_slots(me, count, channels, blocks, partners):
    own, ahead = blocks
    next_level = me // 4 + 1 < count // 4
    put_slots(
        channels, partners, [(own, 0, me >= 0), (ahead, 4, next_level)], (1, 2, 3, 5, 6, 7)
    )


def late_slots(me, count, channels, blocks, partners):
    core = lax.rem(me, 2)
    side = lax.rem(me // 2, 2)
    (own_swapped, ahead_swapped, far, far_swapped, cross, cross_swapped, other,
     other_swapped) = blocks
    cross_slot = 6 - 4 * side
    other_slot = 8 - cross_slot
    step = 1 - 2 * core
    next_level = me // 4 + 1 < count // 4
    second_level = me // 4 + 2 < count // 4
    other_there = (side == 0) | second_level
    put_slots(channels, partners, [
        (far, 0, second_level), (cross, cross_slot, next_level),
        (other, other_slot, other_there), (ahead_swapped, 4 + step, next_level),
        (cross_swapped, cross_slot + step, next_level),
        (other_swapped, other_slot + step, other_there),
    ], (4,))

    @pl.when(core == 0)
    def _():
        put_slots(channels, partners, [(own_swapped, 1, me >= 0)], ())

    @pl.when(core == 1)
    def _():
        put_slots(channels, partners, [(far_swapped, 7, second_level)], ())


def product_kernel(late, count, norm_scale, place, rotated, *refs):
    refs = list(refs)
    before = refs.pop(0) if late else None
    out, partners, total = refs[-3:]
    blocks = refs[:-3]
    channels = blocks[0].shape[0]
    (late_slots if late else early_slots)(place[0], count, channels, blocks, partners)
    rows, features = rotated.shape
    chunk = 2 * 2 * NF
    for begin in range(0, features, chunk):
        turned = partners[:, begin:begin + chunk].T
        product = dot(rotated[:, begin:begin + chunk], turned)
        if begin == 0:
            total[...] = product
        else:
            total[...] += product

    row = lax.broadcasted_iota(jnp.int32, (channels, NPART), 0)
    column = lax.broadcasted_iota(jnp.int32, (channels, NPART), 1)
    low = row + column >= NPART - 1
    keep = (low | (column < NPART - channels)) if late else jnp.logical_not(low)
    sheared = []
    for begin in range(0, rows, channels):
        here = slice(begin, begin + channels)
        value = jnp.where(keep, total[here, :], 0.0)
        if late:
            value = (value + before[here, :]) * norm_scale
            sheared.append(pltpu.roll(value, 1, 1, stride=1, stride_axis=0).astype(BF16))
        else:
            out[here, :] = value
    if late:
        sheared = jnp.concatenate(sheared, axis=0)
        out[...] = dot(sheared, flip_matrix(NPART)).astype(BF16)


def exchange(value, pairs):
    return lax.ppermute(value, "chan", pairs)


def local(records, dead_mask, offsets):
    channels, samples = records.shape
    tm_count = lax.axis_size("tm")
    tm_index = lax.axis_index("tm")
    chan_count = lax.axis_size("chan")
    own = samples // HOP
    windows = own * tm_count
    halves = own
    halo = 0
    if tm_count > 1:
        reach = 2 * HOP + H
        left = lax.ppermute(
            records[:, samples - H:], "tm", [(i, i + 1) for i in range(tm_count - 1)]
        )
        right = lax.ppermute(
            records[:, :reach], "tm", [(i + 1, i) for i in range(tm_count - 1)]
        )
        records = jnp.concatenate([left, records, right], axis=1)
        halves = own + 2
        halo = H
    table = jnp.asarray(packed_tables())
    own_offsets = lax.dynamic_slice_in_dim(offsets, tm_index * own, own, 0)
    vmem = pl.BlockSpec(memory_space=pltpu.VMEM)
    smem = pl.BlockSpec(memory_space=pltpu.SMEM)
    hbm = pl.BlockSpec(memory_space=pl.ANY)
    params = pltpu.CompilerParams(vmem_limit_bytes=24 * 1024 * 1024)

    bulk = min(own + 1, halves)
    part_rows = (own + bulk * (HOP // GROUP)) * channels
    spectra = pl.pallas_call(
        functools.partial(spectra_kernel, halves, own, halo),
        name="spectra",
        out_shape=jax.ShapeDtypeStruct((channels, own * 2 * NF), BF16),
        in_specs=[smem, smem, hbm, hbm],
        out_specs=vmem,
        scratch_shapes=[
            pltpu.VMEM((channels, halves * HOP + 2 * H), F32),
            pltpu.VMEM((channels, halves * HOP + 2 * H), BF16),
            pltpu.VMEM((part_rows, GROUP), BF16),
            pltpu.VMEM((part_rows, GROUP), BF16),
            pltpu.VMEM((part_rows, 2 * NF + 128), F32),
            pltpu.VMEM(table.shape, BF16),
            pltpu.SemaphoreType.DMA((3 * halves + 1,)),
        ],
        compiler_params=pltpu.CompilerParams(vmem_limit_bytes=60 * 1024 * 1024),
        cost_estimate=pl.CostEstimate(
            flops=7_000_000_000, bytes_accessed=8 * 1024 * 1024, transcendentals=0
        ),
    )(dead_mask, own_offsets, records, table)
    if tm_count > 1:
        spectra = lax.all_gather(spectra, "tm", axis=1, tiled=True)

    lags = NLAG // tm_count
    cos_lag, sin_lag = (
        lax.dynamic_slice_in_dim(jnp.asarray(t), tm_index * lags, lags, 0) for t in lag_tables()
    )
    place = lax.axis_index("chan").astype(jnp.int32).reshape(1)
    norm_scale = 1.0 / math.sqrt(2.0 * NF * windows)

    features = spectra.shape[1]
    rotated = pl.pallas_call(
        functools.partial(rotate_kernel, lags),
        name="rotate",
        grid=(windows,),
        out_shape=jax.ShapeDtypeStruct((lags * channels, features), BF16),
        in_specs=[
            pl.BlockSpec((channels, 2 * NF), lambda w: (0, w)),
            pl.BlockSpec((lags, NF), lambda w: (0, 0)),
            pl.BlockSpec((lags, NF), lambda w: (0, 0)),
        ],
        out_specs=pl.BlockSpec((lags * channels, 2 * NF), lambda w: (0, w)),
        compiler_params=params,
        cost_estimate=pl.CostEstimate(
            flops=4_000_000_000, bytes_accessed=8 * 1024 * 1024, transcendentals=0
        ),
    )(spectra, cos_lag, sin_lag)

    def product(blocks, before):
        late = before is not None
        operands = [place, rotated] + ([before] if late else []) + list(blocks)
        return pl.pallas_call(
            functools.partial(product_kernel, late, chan_count, norm_scale),
            name="late_product" if late else "early_product",
            out_shape=jax.ShapeDtypeStruct((lags * channels, NPART), BF16 if late else F32),
            in_specs=[smem] + [vmem] * (len(operands) - 1),
            out_specs=vmem,
            scratch_shapes=[
                pltpu.VMEM((NPART, features), BF16),
                pltpu.VMEM((lags * channels, NPART), F32),
            ],
            compiler_params=params,
            cost_estimate=pl.CostEstimate(
                flops=2 * lags * channels * features * NPART, bytes_accessed=6 * 1024 * 1024,
                transcendentals=0,
            ),
        )(*operands)

    every = range(chan_count)
    down = [(i, (i - 4) % chan_count) for i in every]
    top = chan_count - 4

    def far_target(i):
        return i if i >= top else (i - 4 if i >= 4 else top - 4 + i)

    def other_target(i):
        if i & 2:
            return i - 2
        return i + 2 if i >= top else (i - 2 if i >= 4 else top - 2 + i)

    far_pairs = [(i, far_target(i)) for i in every]
    other_pairs = [(i, other_target(i)) for i in every]
    across = [(i, i ^ 2) for i in every]
    cores = [(i, i ^ 1) for i in every]
    side = lax.rem(lax.axis_index("chan") // 2, 2)

    ahead = exchange(spectra, down)
    ahead, rotated = lax.optimization_barrier((ahead, rotated))
    cross = exchange(ahead, across)
    other = exchange(jnp.where(side == 0, ahead, spectra), other_pairs)
    far = exchange(ahead, far_pairs)
    early = product((spectra, ahead), None)
    kept, ahead, other, early = lax.optimization_barrier((spectra, ahead, other, early))
    own_swapped = exchange(kept, cores)
    ahead_swapped = exchange(ahead, cores)
    cross, own_swapped, ahead_swapped = lax.optimization_barrier(
        (cross, own_swapped, ahead_swapped)
    )
    blocks = (own_swapped, ahead_swapped, far, exchange(far, cores), cross,
              exchange(cross, cores), other, exchange(other, cores))
    return product(blocks, early).reshape(lags, channels, NPART)


def solution(mesh):
    return jax.shard_map(
        local,
        mesh=mesh,
        in_specs=(P(("win", "chan"), "tm"), P(("win", "chan")), P("win")),
        out_specs=P("tm", ("win", "chan"), None),
        check_vma=False,
    )
```

```python
import functools
import math

import jax
import jax.numpy as jnp
import ml_dtypes
import numpy as np
from jax import lax
from jax.experimental import pallas as pl
from jax.experimental.pallas import tpu as pltpu
from jax.sharding import PartitionSpec as P

L = 8192
HOP = 4096
H = 128
K0 = 32
NF = 256
WB = 64
NLAG = 32
NPART = 256
EDGE = 512
STEP = 256
GROUP = 512
EPS = 1e-05
TWO_PI = 2.0 * math.pi
BF16 = jnp.bfloat16
F32 = jnp.float32


def split_table(table):
    high = table.astype(ml_dtypes.bfloat16)
    low = (table - high.astype(np.float64)).astype(ml_dtypes.bfloat16)
    return high, low


@functools.cache
def fourier_tables():
    samples = np.arange(GROUP)[:, None]
    bins = K0 + np.arange(NF)[None, :]
    angle = (samples * bins % L) * (TWO_PI / L)
    inner = np.concatenate([np.cos(angle), -np.sin(angle)], axis=1)
    outer = np.zeros((GROUP, 128))
    for lane, k, wave in ((0, K0 - 1, np.cos), (64, K0 - 1, np.sin), (127, K0 + NF, np.cos), (63, K0 + NF, np.sin)):
        sign = 1.0 if wave is np.cos else -1.0
        outer[:, lane] = sign * wave((samples[:, 0] * k % L) * (TWO_PI / L))
    high, low = split_table(inner)
    return np.concatenate([high, outer.astype(ml_dtypes.bfloat16)], axis=1), low


@functools.cache
def packed_tables():
    return np.concatenate(fourier_tables(), axis=1)


@functools.cache
def lag_tables():
    lags = np.arange(NLAG)[:, None] - NLAG // 2
    angle = (lags * (K0 + np.arange(NF))[None, :] % L) * (TWO_PI / L)
    return np.cos(angle).astype(np.float32), np.sin(angle).astype(np.float32)


def split(value):
    high = value.astype(BF16)
    return high, (value - high.astype(F32)).astype(BF16)


def inverse(value):
    guess = pl.reciprocal(value, approx=True)
    return guess * (2.0 - value * guess)


def dot(a, b):
    return jnp.dot(a, b, preferred_element_type=F32)


def spectra_kernel(
    halves, own, halo,
    dead, offs, x_hbm, table_hbm, out, x, absolute, norm_high, norm_low, parts,
    same_sum, swap_sum, table, sems,
):
    channels = x.shape[0]
    groups = HOP // GROUP
    bulk = min(own + 1, halves)
    edges = min(own + 2, halves)
    width = halves * HOP
    cuts = [HOP // 4 + H, HOP // 2 + H]
    pieces = []
    for part in range(3):
        for j in range(halves):
            begin = j * HOP + cuts[part - 1] if part else j * HOP - (H if j or halo else 0)
            end = (j + 1) * HOP - H if j + 1 < halves else width + halo
            pieces.append((begin, j * HOP + cuts[part] if part < 2 else end))
    copies = [
        pltpu.make_async_copy(
            x_hbm.at[:, pl.ds(halo + begin, end - begin)], x.at[:, pl.ds(H + begin, end - begin)],
            sems.at[i],
        )
        for i, (begin, end) in enumerate(pieces)
    ]
    table_copy = pltpu.make_async_copy(table_hbm, table, sems.at[3 * halves])
    for copy in copies[:2 * halves] + [table_copy] + copies[2 * halves:]:
        copy.start()
    if not halo:
        for begin in (0, H + width):
            absolute[:, begin:begin + H] = jnp.zeros((channels, H), BF16)

    def arrive(part):
        ids = range(part * halves, (part + 1) * halves)
        for i in ids:
            copies[i].wait()
        for i in ids:
            begin, end = pieces[i]
            here = slice(H + begin, H + end)
            absolute[:, here] = jnp.abs(x[:, here]).astype(BF16)

    high = table.at[:, :2 * NF + 128]
    low = table.at[:, 2 * NF + 128:]
    from_lane = lax.broadcasted_iota(jnp.int32, (2 * H + STEP, STEP), 0)
    to_lane = lax.broadcasted_iota(jnp.int32, (2 * H + STEP, STEP), 1)
    level_band = ((from_lane >= to_lane) & (from_lane <= to_lane + 2 * H)).astype(F32).astype(BF16)
    from_bin = lax.broadcasted_iota(jnp.int32, (NF, NF), 0)
    to_bin = lax.broadcasted_iota(jnp.int32, (NF, NF), 1)
    smooth_band = (jnp.abs(from_bin - to_bin) <= WB).astype(F32).astype(BF16)
    lane = lax.broadcasted_iota(jnp.int32, (1, parts.shape[1]), 1)
    outer_place = lane - 2 * NF
    outer_first = (outer_place == 0) | (outer_place == 64)
    every_bin = jnp.where(
        lane < 2 * NF, jnp.bitwise_and(lane, NF - 1) + K0, jnp.where(outer_first, K0 - 1, K0 + NF)
    )
    real_place = (lane < NF) | (outer_place == 0) | (outer_place == 127)
    group = lax.broadcasted_iota(jnp.int32, (groups, 1), 0) * GROUP
    angle = jnp.bitwise_and(group * every_bin, L - 1).astype(F32) * (TWO_PI / L)
    turn_same = jnp.cos(angle)
    turn_swap = jnp.sin(angle) * jnp.where(real_place, -1.0, 1.0)
    bin_index = lax.broadcasted_iota(jnp.int32, (1, NF), 1)
    below, above = jnp.minimum(bin_index, WB), jnp.minimum(NF - 1 - bin_index, WB)
    inverse_count = 1.0 / (below + above + 1).astype(F32)

    def rows(ref, begin, length, count):
        return [ref[:, begin + j * HOP:begin + j * HOP + length] for j in range(count)]

    def store(place, value):
        here = slice(place, place + value.shape[0])
        norm_high[here, :], norm_low[here, :] = split(value)

    def normalise(group_ids, place):
        blocks = [(g, g * GROUP + part * STEP) for g in group_ids for part in range(GROUP // STEP)]
        counts = [edges if g == 0 else bulk for g, _ in blocks]
        level = dot(
            jnp.concatenate(
                [r for (_, begin), n in zip(blocks, counts)
                 for r in rows(absolute, begin, STEP + 2 * H, n)], axis=0
            ), level_band,
        ) * (1.0 / (2 * H + 1)) + EPS
        values = []
        at = 0
        for (_, begin), n in zip(blocks, counts):
            samples = jnp.concatenate(rows(x, H + begin, STEP, n), axis=0)
            values.append(samples * inverse(level[at:at + n * channels]))
            at += n * channels
        begins = {}
        for index, g in enumerate(group_ids):
            value = jnp.concatenate(values[2 * index:2 * index + 2], axis=1)
            if g == 0:
                lane = lax.broadcasted_iota(jnp.int32, (channels, EDGE), 1)
                merged = []
                for w in range(own):
                    mine = value[w * channels:(w + 1) * channels]
                    other = (
                        value[(w + 2) * channels:(w + 3) * channels]
                        if w + 2 < edges else jnp.zeros_like(mine)
                    )
                    merged.append(jnp.where(lane >= offs[w], mine, other))
                begins["edge"] = place
                store(place, jnp.concatenate(merged, axis=0))
                place += own * channels
                value = value[:bulk * channels]
            begins[g] = place
            store(place, value)
            place += bulk * channels
        return begins, place

    def transform(begin, end):
        first = dot(norm_high[begin:end, :], high[...])
        second = dot(norm_low[begin:end, :], high[:, :2 * NF])
        second = second + dot(norm_high[begin:end, :], low[...])
        parts[begin:end, :2 * NF] = first[:, :2 * NF] + second
        parts[begin:end, 2 * NF:] = first[:, 2 * NF:]

    begins = {}
    place = 0
    waiting = None
    for g in range(0, groups, 2):
        if g < 4:
            arrive(g // 2)
        start = place
        found, place = normalise([g, g + 1], place)
        begins.update(found)
        if g == 2:
            arrive(2)
            table_copy.wait()
        if waiting:
            transform(*waiting)
        waiting = (start, place)

    def piece(name, j):
        return parts[begins[name] + j * channels:begins[name] + (j + 1) * channels, :]

    def turned(j, ids):
        same = swap = None
        for g in ids:
            value = piece(g, j)
            first, second = value * turn_same[g:g + 1, :], value * turn_swap[g:g + 1, :]
            same = first if same is None else same + first
            swap = second if swap is None else swap + second
        return same, swap

    def rows_of(j):
        return slice(j * channels, (j + 1) * channels)

    for j in range(bulk):
        same_sum[rows_of(j), :], swap_sum[rows_of(j), :] = turned(j, range(1, groups - 2))
    transform(*waiting)

    def bulk_of(j):
        same, swap = turned(j, range(groups - 2, groups))
        same = same + same_sum[rows_of(j), :]
        swap = swap + swap_sum[rows_of(j), :]
        return same + jnp.concatenate(
            [swap[:, NF:2 * NF], swap[:, :NF], pltpu.roll(swap[:, 2 * NF:], 64, 1)], axis=1
        )

    window = lax.broadcasted_iota(jnp.int32, (own, 1), 0)
    offsets = sum(jnp.where(window == w, offs[w], 0) for w in range(own))
    lane = lax.broadcasted_iota(jnp.int32, (1, NF), 1)
    outer_lane = lax.broadcasted_iota(jnp.int32, (1, 128), 1)
    outer_bin = jnp.where((outer_lane == 0) | (outer_lane == 64), K0 - 1, K0 + NF)

    def turn(bins):
        angle = jnp.bitwise_and(bins * offsets, L - 1).astype(F32) * (TWO_PI / L)
        return jnp.cos(angle), jnp.sin(angle)

    cos_turn, sin_turn = turn(lane + K0)
    cos_outer, sin_outer = turn(outer_bin)
    sign = 1.0 - 2.0 * jnp.bitwise_and(lane + K0, 1).astype(F32)
    sign_outer = 1.0 - 2.0 * jnp.bitwise_and(outer_bin, 1).astype(F32)
    channel = lax.broadcasted_iota(jnp.int32, (channels, 1), 0)
    live = 1.0 - sum(jnp.where(channel == i, dead[i], 0) for i in range(channels)).astype(F32)

    signs = jnp.concatenate([sign, sign, sign_outer], axis=1)
    reals, imags, magnitudes = [], [], []
    following = bulk_of(0)
    for w in range(own):
        spec = following + piece("edge", w)
        if w + 1 < bulk:
            following = bulk_of(w + 1)
            spec = spec + (following + piece(0, w + 1)) * signs
        spec = spec * live
        outer = spec[:, 2 * NF:]
        c, s = cos_turn[w:w + 1], sin_turn[w:w + 1]
        c_outer, s_outer = cos_outer[w:w + 1], sin_outer[w:w + 1]
        outer_imag = pltpu.roll(outer, 64, 1)

        def hann(inner, ends):
            ends = jnp.concatenate([ends, ends], axis=1)
            before = jnp.where(lane == 0, ends, pltpu.roll(inner, 1, 1))
            behind = jnp.where(lane == NF - 1, ends, pltpu.roll(inner, NF - 1, 1))
            return 0.5 * inner - 0.25 * (before + behind)

        real = hann(
            spec[:, :NF] * c - spec[:, NF:2 * NF] * s, outer * c_outer - outer_imag * s_outer
        )
        imag = hann(
            spec[:, :NF] * s + spec[:, NF:2 * NF] * c, outer * s_outer + outer_imag * c_outer
        )
        reals.append(real)
        imags.append(imag)
        magnitudes.append(jnp.sqrt(real * real + imag * imag + 1e-12))
    m_high, m_low = split(jnp.concatenate(magnitudes, axis=0))
    smooth = (dot(m_high, smooth_band) + dot(m_low, smooth_band)) * inverse_count
    scale = 1.0 / (smooth + EPS)
    flip = flip_matrix(channels)
    for w in range(own):
        here = slice(w * channels, (w + 1) * channels)
        white = jnp.concatenate([reals[w] * scale[here], imags[w] * scale[here]], axis=1)
        out[:, w * 2 * NF:(w + 1) * 2 * NF] = dot(flip, white.astype(BF16)).astype(BF16)


def flip_matrix(channels):
    row = lax.broadcasted_iota(jnp.int32, (channels, channels), 0)
    column = lax.broadcasted_iota(jnp.int32, (channels, channels), 1)
    return (row + column == channels - 1).astype(F32).astype(BF16)


def rotate_kernel(lags, own, cos_lag, sin_lag, out):
    channels = own.shape[0]
    straight = dot(flip_matrix(channels), own[...])
    real, imag = straight[:, :NF], straight[:, NF:]
    for t in range(lags):
        c, s = cos_lag[t:t + 1, :], sin_lag[t:t + 1, :]
        here = slice(t * channels, (t + 1) * channels)
        out[here, :NF] = (real * c - imag * s).astype(BF16)
        out[here, NF:] = (real * s + imag * c).astype(BF16)


def put_slots(channels, partners, present, absent):
    last = NPART // channels - 1
    nothing = jnp.zeros((channels, partners.shape[1]), BF16)

    def place(slot):
        return pl.ds(pl.multiple_of((last - slot) * channels, channels), channels)

    for block, slot, valid in present:
        partners[place(slot), :] = block[...]

        @pl.when(jnp.logical_not(valid))
        def _(slot=slot):
            partners[place(slot), :] = nothing

    for slot in absent:
        partners[place(slot), :] = nothing


def early_slots(me, count, channels, blocks, partners):
    own, ahead = blocks
    next_level = me // 4 + 1 < count // 4
    put_slots(
        channels, partners, [(own, 0, me >= 0), (ahead, 4, next_level)], (1, 2, 3, 5, 6, 7)
    )


def late_slots(me, count, channels, blocks, partners):
    core = lax.rem(me, 2)
    side = lax.rem(me // 2, 2)
    (own_swapped, ahead_swapped, far, far_swapped, cross, cross_swapped, other,
     other_swapped) = blocks
    cross_slot = 6 - 4 * side
    other_slot = 8 - cross_slot
    step = 1 - 2 * core
    next_level = me // 4 + 1 < count // 4
    second_level = me // 4 + 2 < count // 4
    other_there = (side == 0) | second_level
    put_slots(channels, partners, [
        (far, 0, second_level), (cross, cross_slot, next_level),
        (other, other_slot, other_there), (ahead_swapped, 4 + step, next_level),
        (cross_swapped, cross_slot + step, next_level),
        (other_swapped, other_slot + step, other_there),
    ], (4,))

    @pl.when(core == 0)
    def _():
        put_slots(channels, partners, [(own_swapped, 1, me >= 0)], ())

    @pl.when(core == 1)
    def _():
        put_slots(channels, partners, [(far_swapped, 7, second_level)], ())


def product_kernel(late, count, norm_scale, place, rotated, *refs):
    refs = list(refs)
    before = refs.pop(0) if late else None
    out, partners, turned, total = refs[-4:]
    blocks = refs[:-4]
    channels = blocks[0].shape[0]
    (late_slots if late else early_slots)(place[0], count, channels, blocks, partners)
    rows, features = rotated.shape
    chunk = 2 * 2 * NF
    for begin in range(0, features, chunk):
        turned[begin:begin + chunk, :] = partners[:, begin:begin + chunk].T
    total[...] = dot(rotated[...], turned[...])

    row = lax.broadcasted_iota(jnp.int32, (channels, NPART), 0)
    column = lax.broadcasted_iota(jnp.int32, (channels, NPART), 1)
    low = row + column >= NPART - 1
    keep = (low | (column < NPART - channels)) if late else jnp.logical_not(low)
    sheared = []
    for begin in range(0, rows, channels):
        here = slice(begin, begin + channels)
        value = jnp.where(keep, total[here, :], 0.0)
        if late:
            value = (value + before[here, :]) * norm_scale
            sheared.append(pltpu.roll(value, 1, 1, stride=1, stride_axis=0).astype(BF16))
        else:
            out[here, :] = value
    if late:
        sheared = jnp.concatenate(sheared, axis=0)
        out[...] = dot(sheared, flip_matrix(NPART)).astype(BF16)


def exchange(value, pairs):
    return lax.ppermute(value, "chan", pairs)


def local(records, dead_mask, offsets):
    channels, samples = records.shape
    tm_count = lax.axis_size("tm")
    tm_index = lax.axis_index("tm")
    chan_count = lax.axis_size("chan")
    own = samples // HOP
    windows = own * tm_count
    halves = own
    halo = 0
    if tm_count > 1:
        reach = 2 * HOP + H
        left = lax.ppermute(
            records[:, samples - H:], "tm", [(i, i + 1) for i in range(tm_count - 1)]
        )
        right = lax.ppermute(
            records[:, :reach], "tm", [(i + 1, i) for i in range(tm_count - 1)]
        )
        records = jnp.concatenate([left, records, right], axis=1)
        halves = own + 2
        halo = H
    table = jnp.asarray(packed_tables())
    own_offsets = lax.dynamic_slice_in_dim(offsets, tm_index * own, own, 0)
    vmem = pl.BlockSpec(memory_space=pltpu.VMEM)
    smem = pl.BlockSpec(memory_space=pltpu.SMEM)
    hbm = pl.BlockSpec(memory_space=pl.ANY)
    params = pltpu.CompilerParams(vmem_limit_bytes=24 * 1024 * 1024)

    bulk = min(own + 1, halves)
    part_rows = (own + bulk * (HOP // GROUP)) * channels
    spectra = pl.pallas_call(
        functools.partial(spectra_kernel, halves, own, halo),
        name="spectra",
        out_shape=jax.ShapeDtypeStruct((channels, own * 2 * NF), BF16),
        in_specs=[smem, smem, hbm, hbm],
        out_specs=vmem,
        scratch_shapes=[
            pltpu.VMEM((channels, halves * HOP + 2 * H), F32),
            pltpu.VMEM((channels, halves * HOP + 2 * H), BF16),
            pltpu.VMEM((part_rows, GROUP), BF16),
            pltpu.VMEM((part_rows, GROUP), BF16),
            pltpu.VMEM((part_rows, 2 * NF + 128), F32),
            pltpu.VMEM((bulk * channels, 2 * NF + 128), F32),
            pltpu.VMEM((bulk * channels, 2 * NF + 128), F32),
            pltpu.VMEM(table.shape, BF16),
            pltpu.SemaphoreType.DMA((3 * halves + 1,)),
        ],
        compiler_params=pltpu.CompilerParams(vmem_limit_bytes=60 * 1024 * 1024),
        cost_estimate=pl.CostEstimate(
            flops=7_000_000_000, bytes_accessed=8 * 1024 * 1024, transcendentals=0
        ),
    )(dead_mask, own_offsets, records, table)
    if tm_count > 1:
        spectra = lax.all_gather(spectra, "tm", axis=1, tiled=True)

    lags = NLAG // tm_count
    cos_lag, sin_lag = (
        lax.dynamic_slice_in_dim(jnp.asarray(t), tm_index * lags, lags, 0) for t in lag_tables()
    )
    place = lax.axis_index("chan").astype(jnp.int32).reshape(1)
    norm_scale = 1.0 / math.sqrt(2.0 * NF * windows)

    features = spectra.shape[1]
    rotated = pl.pallas_call(
        functools.partial(rotate_kernel, lags),
        name="rotate",
        grid=(windows,),
        out_shape=jax.ShapeDtypeStruct((lags * channels, features), BF16),
        in_specs=[
            pl.BlockSpec((channels, 2 * NF), lambda w: (0, w)),
            pl.BlockSpec((lags, NF), lambda w: (0, 0)),
            pl.BlockSpec((lags, NF), lambda w: (0, 0)),
        ],
        out_specs=pl.BlockSpec((lags * channels, 2 * NF), lambda w: (0, w)),
        compiler_params=params,
        cost_estimate=pl.CostEstimate(
            flops=4_000_000_000, bytes_accessed=8 * 1024 * 1024, transcendentals=0
        ),
    )(spectra, cos_lag, sin_lag)

    def product(blocks, before):
        late = before is not None
        operands = [place, rotated] + ([before] if late else []) + list(blocks)
        return pl.pallas_call(
            functools.partial(product_kernel, late, chan_count, norm_scale),
            name="late_product" if late else "early_product",
            out_shape=jax.ShapeDtypeStruct((lags * channels, NPART), BF16 if late else F32),
            in_specs=[smem] + [vmem] * (len(operands) - 1),
            out_specs=vmem,
            scratch_shapes=[
                pltpu.VMEM((NPART, features), BF16),
                pltpu.VMEM((features, NPART), BF16),
                pltpu.VMEM((lags * channels, NPART), F32),
            ],
            compiler_params=params,
            cost_estimate=pl.CostEstimate(
                flops=2 * lags * channels * features * NPART, bytes_accessed=6 * 1024 * 1024,
                transcendentals=0,
            ),
        )(*operands)

    every = range(chan_count)
    down = [(i, (i - 4) % chan_count) for i in every]
    top = chan_count - 4

    def far_target(i):
        return i if i >= top else (i - 4 if i >= 4 else top - 4 + i)

    def other_target(i):
        if i & 2:
            return i - 2
        return i + 2 if i >= top else (i - 2 if i >= 4 else top - 2 + i)

    far_pairs = [(i, far_target(i)) for i in every]
    other_pairs = [(i, other_target(i)) for i in every]
    across = [(i, i ^ 2) for i in every]
    cores = [(i, i ^ 1) for i in every]
    side = lax.rem(lax.axis_index("chan") // 2, 2)

    ahead = exchange(spectra, down)
    ahead, rotated = lax.optimization_barrier((ahead, rotated))
    cross = exchange(ahead, across)
    other = exchange(jnp.where(side == 0, ahead, spectra), other_pairs)
    far = exchange(ahead, far_pairs)
    early = product((spectra, ahead), None)
    kept, ahead, other, early = lax.optimization_barrier((spectra, ahead, other, early))
    own_swapped = exchange(kept, cores)
    ahead_swapped = exchange(ahead, cores)
    cross, own_swapped, ahead_swapped = lax.optimization_barrier(
        (cross, own_swapped, ahead_swapped)
    )
    blocks = (own_swapped, ahead_swapped, far, exchange(far, cores), cross,
              exchange(cross, cores), other, exchange(other, cores))
    return product(blocks, early).reshape(lags, channels, NPART)


def solution(mesh):
    return jax.shard_map(
        local,
        mesh=mesh,
        in_specs=(P(("win", "chan"), "tm"), P(("win", "chan")), P("win")),
        out_specs=P("tm", ("win", "chan"), None),
        check_vma=False,
    )
```

```python
import functools
import math

import jax
import jax.numpy as jnp
import ml_dtypes
import numpy as np
from jax import lax
from jax.experimental import pallas as pl
from jax.experimental.pallas import tpu as pltpu
from jax.sharding import PartitionSpec as P

L = 8192
HOP = 4096
H = 128
K0 = 32
NF = 256
WB = 64
NLAG = 32
NPART = 256
EDGE = 512
STEP = 256
GROUP = 512
EPS = 1e-05
TWO_PI = 2.0 * math.pi
BF16 = jnp.bfloat16
F32 = jnp.float32


def split_table(table):
    high = table.astype(ml_dtypes.bfloat16)
    low = (table - high.astype(np.float64)).astype(ml_dtypes.bfloat16)
    return high, low


@functools.cache
def fourier_tables():
    samples = np.arange(GROUP)[:, None]
    bins = K0 + np.arange(NF)[None, :]
    angle = (samples * bins % L) * (TWO_PI / L)
    inner = np.concatenate([np.cos(angle), -np.sin(angle)], axis=1)
    outer = np.zeros((GROUP, 128))
    for lane, k, wave in ((0, K0 - 1, np.cos), (64, K0 - 1, np.sin), (127, K0 + NF, np.cos), (63, K0 + NF, np.sin)):
        sign = 1.0 if wave is np.cos else -1.0
        outer[:, lane] = sign * wave((samples[:, 0] * k % L) * (TWO_PI / L))
    high, low = split_table(inner)
    return np.concatenate([high, outer.astype(ml_dtypes.bfloat16)], axis=1), low


@functools.cache
def packed_tables():
    return np.concatenate(fourier_tables(), axis=1)


@functools.cache
def lag_tables():
    lags = np.arange(NLAG)[:, None] - NLAG // 2
    angle = (lags * (K0 + np.arange(NF))[None, :] % L) * (TWO_PI / L)
    return np.cos(angle).astype(np.float32), np.sin(angle).astype(np.float32)


def split(value):
    high = value.astype(BF16)
    return high, (value - high.astype(F32)).astype(BF16)


def inverse(value):
    guess = pl.reciprocal(value, approx=True)
    return guess * (2.0 - value * guess)


def dot(a, b):
    return jnp.dot(a, b, preferred_element_type=F32)


def spectra_kernel(
    halves, own, halo,
    dead, offs, x_hbm, table_hbm, out, x, absolute, norm_high, norm_low, parts, table, sems,
):
    channels = x.shape[0]
    groups = HOP // GROUP
    bulk = min(own + 1, halves)
    edges = min(own + 2, halves)
    width = halves * HOP
    cuts = [HOP // 4 + H, HOP // 2 + H]
    pieces = []
    for part in range(3):
        for j in range(halves):
            begin = j * HOP + cuts[part - 1] if part else j * HOP - (H if j or halo else 0)
            end = (j + 1) * HOP - H if j + 1 < halves else width + halo
            pieces.append((begin, j * HOP + cuts[part] if part < 2 else end))
    copies = [
        pltpu.make_async_copy(
            x_hbm.at[:, pl.ds(halo + begin, end - begin)], x.at[:, pl.ds(H + begin, end - begin)],
            sems.at[i],
        )
        for i, (begin, end) in enumerate(pieces)
    ]
    table_copy = pltpu.make_async_copy(table_hbm, table, sems.at[3 * halves])
    for copy in copies[:2 * halves] + [table_copy] + copies[2 * halves:]:
        copy.start()
    if not halo:
        for begin in (0, H + width):
            absolute[:, begin:begin + H] = jnp.zeros((channels, H), BF16)

    def arrive(part):
        ids = range(part * halves, (part + 1) * halves)
        for i in ids:
            copies[i].wait()
        for i in ids:
            begin, end = pieces[i]
            here = slice(H + begin, H + end)
            absolute[:, here] = jnp.abs(x[:, here]).astype(BF16)

    high = table.at[:, :2 * NF + 128]
    low = table.at[:, 2 * NF + 128:]
    from_lane = lax.broadcasted_iota(jnp.int32, (2 * H + STEP, STEP), 0)
    to_lane = lax.broadcasted_iota(jnp.int32, (2 * H + STEP, STEP), 1)
    level_band = ((from_lane >= to_lane) & (from_lane <= to_lane + 2 * H)).astype(F32).astype(BF16)
    from_bin = lax.broadcasted_iota(jnp.int32, (NF, NF), 0)
    to_bin = lax.broadcasted_iota(jnp.int32, (NF, NF), 1)
    smooth_band = (jnp.abs(from_bin - to_bin) <= WB).astype(F32).astype(BF16)
    lane = lax.broadcasted_iota(jnp.int32, (1, parts.shape[1]), 1)
    outer_place = lane - 2 * NF
    outer_first = (outer_place == 0) | (outer_place == 64)
    every_bin = jnp.where(
        lane < 2 * NF, jnp.bitwise_and(lane, NF - 1) + K0, jnp.where(outer_first, K0 - 1, K0 + NF)
    )
    real_place = (lane < NF) | (outer_place == 0) | (outer_place == 127)
    group = lax.broadcasted_iota(jnp.int32, (groups, 1), 0) * GROUP
    angle = jnp.bitwise_and(group * every_bin, L - 1).astype(F32) * (TWO_PI / L)
    turn_same = jnp.cos(angle)
    turn_swap = jnp.sin(angle) * jnp.where(real_place, -1.0, 1.0)
    bin_index = lax.broadcasted_iota(jnp.int32, (1, NF), 1)
    below, above = jnp.minimum(bin_index, WB), jnp.minimum(NF - 1 - bin_index, WB)
    inverse_count = 1.0 / (below + above + 1).astype(F32)

    def rows(ref, begin, length, count):
        return [ref[:, begin + j * HOP:begin + j * HOP + length] for j in range(count)]

    def store(place, value):
        here = slice(place, place + value.shape[0])
        norm_high[here, :], norm_low[here, :] = split(value)

    def normalise(group_ids, place):
        blocks = [(g, g * GROUP + part * STEP) for g in group_ids for part in range(GROUP // STEP)]
        counts = [edges if g == 0 else bulk for g, _ in blocks]
        level = dot(
            jnp.concatenate(
                [r for (_, begin), n in zip(blocks, counts)
                 for r in rows(absolute, begin, STEP + 2 * H, n)], axis=0
            ), level_band,
        ) * (1.0 / (2 * H + 1)) + EPS
        values = []
        at = 0
        for (_, begin), n in zip(blocks, counts):
            samples = jnp.concatenate(rows(x, H + begin, STEP, n), axis=0)
            values.append(samples * inverse(level[at:at + n * channels]))
            at += n * channels
        begins = {}
        for index, g in enumerate(group_ids):
            value = jnp.concatenate(values[2 * index:2 * index + 2], axis=1)
            if g == 0:
                lane = lax.broadcasted_iota(jnp.int32, (channels, EDGE), 1)
                merged = []
                for w in range(own):
                    mine = value[w * channels:(w + 1) * channels]
                    other = (
                        value[(w + 2) * channels:(w + 3) * channels]
                        if w + 2 < edges else jnp.zeros_like(mine)
                    )
                    merged.append(jnp.where(lane >= offs[w], mine, other))
                begins["edge"] = place
                store(place, jnp.concatenate(merged, axis=0))
                place += own * channels
                value = value[:bulk * channels]
            begins[g] = place
            store(place, value)
            place += bulk * channels
        return begins, place

    def transform(begin, end):
        first = dot(norm_high[begin:end, :], high[...])
        second = dot(norm_low[begin:end, :], high[:, :2 * NF])
        second = second + dot(norm_high[begin:end, :], low[...])
        parts[begin:end, :2 * NF] = first[:, :2 * NF] + second
        parts[begin:end, 2 * NF:] = first[:, 2 * NF:]

    begins = {}
    place = 0
    waiting = None
    for g in range(0, groups, 2):
        if g < 4:
            arrive(g // 2)
        start = place
        found, place = normalise([g, g + 1], place)
        begins.update(found)
        if g == 2:
            arrive(2)
            table_copy.wait()
        if waiting:
            transform(*waiting)
        waiting = (start, place)
    transform(*waiting)

    def piece(name, j):
        return parts[begins[name] + j * channels:begins[name] + (j + 1) * channels, :]

    def bulk_of(j):
        same = jnp.zeros((channels, parts.shape[1]), F32)
        swap = same
        for g in range(1, groups):
            value = piece(g, j)
            same = same + value * turn_same[g:g + 1, :]
            swap = swap + value * turn_swap[g:g + 1, :]
        return same + jnp.concatenate(
            [swap[:, NF:2 * NF], swap[:, :NF], pltpu.roll(swap[:, 2 * NF:], 64, 1)], axis=1
        )

    window = lax.broadcasted_iota(jnp.int32, (own, 1), 0)
    offsets = sum(jnp.where(window == w, offs[w], 0) for w in range(own))
    lane = lax.broadcasted_iota(jnp.int32, (1, NF), 1)
    outer_lane = lax.broadcasted_iota(jnp.int32, (1, 128), 1)
    outer_bin = jnp.where((outer_lane == 0) | (outer_lane == 64), K0 - 1, K0 + NF)

    def turn(bins):
        angle = jnp.bitwise_and(bins * offsets, L - 1).astype(F32) * (TWO_PI / L)
        return jnp.cos(angle), jnp.sin(angle)

    cos_turn, sin_turn = turn(lane + K0)
    cos_outer, sin_outer = turn(outer_bin)
    sign = 1.0 - 2.0 * jnp.bitwise_and(lane + K0, 1).astype(F32)
    sign_outer = 1.0 - 2.0 * jnp.bitwise_and(outer_bin, 1).astype(F32)
    channel = lax.broadcasted_iota(jnp.int32, (channels, 1), 0)
    live = 1.0 - sum(jnp.where(channel == i, dead[i], 0) for i in range(channels)).astype(F32)

    signs = jnp.concatenate([sign, sign, sign_outer], axis=1)
    reals, imags, magnitudes = [], [], []
    following = bulk_of(0)
    for w in range(own):
        spec = following + piece("edge", w)
        if w + 1 < bulk:
            following = bulk_of(w + 1)
            spec = spec + (following + piece(0, w + 1)) * signs
        spec = spec * live
        outer = spec[:, 2 * NF:]
        c, s = cos_turn[w:w + 1], sin_turn[w:w + 1]
        c_outer, s_outer = cos_outer[w:w + 1], sin_outer[w:w + 1]
        outer_imag = pltpu.roll(outer, 64, 1)

        def hann(inner, ends):
            ends = jnp.concatenate([ends, ends], axis=1)
            before = jnp.where(lane == 0, ends, pltpu.roll(inner, 1, 1))
            behind = jnp.where(lane == NF - 1, ends, pltpu.roll(inner, NF - 1, 1))
            return 0.5 * inner - 0.25 * (before + behind)

        real = hann(
            spec[:, :NF] * c - spec[:, NF:2 * NF] * s, outer * c_outer - outer_imag * s_outer
        )
        imag = hann(
            spec[:, :NF] * s + spec[:, NF:2 * NF] * c, outer * s_outer + outer_imag * c_outer
        )
        reals.append(real)
        imags.append(imag)
        magnitudes.append(jnp.sqrt(real * real + imag * imag + 1e-12))
    m_high, m_low = split(jnp.concatenate(magnitudes, axis=0))
    smooth = (dot(m_high, smooth_band) + dot(m_low, smooth_band)) * inverse_count
    scale = 1.0 / (smooth + EPS)
    flip = flip_matrix(channels)
    for w in range(own):
        here = slice(w * channels, (w + 1) * channels)
        white = jnp.concatenate([reals[w] * scale[here], imags[w] * scale[here]], axis=1)
        out[:, w * 2 * NF:(w + 1) * 2 * NF] = dot(flip, white.astype(BF16)).astype(BF16)


def flip_matrix(channels):
    row = lax.broadcasted_iota(jnp.int32, (channels, channels), 0)
    column = lax.broadcasted_iota(jnp.int32, (channels, channels), 1)
    return (row + column == channels - 1).astype(F32).astype(BF16)


def rotate_kernel(lags, own, cos_lag, sin_lag, out):
    channels = own.shape[0]
    straight = dot(flip_matrix(channels), own[...])
    real, imag = straight[:, :NF], straight[:, NF:]
    for t in range(lags):
        c, s = cos_lag[t:t + 1, :], sin_lag[t:t + 1, :]
        here = slice(t * channels, (t + 1) * channels)
        out[here, :NF] = (real * c - imag * s).astype(BF16)
        out[here, NF:] = (real * s + imag * c).astype(BF16)


def put_slots(channels, partners, present, absent):
    last = NPART // channels - 1
    nothing = jnp.zeros((channels, partners.shape[1]), BF16)

    def place(slot):
        return pl.ds(pl.multiple_of((last - slot) * channels, channels), channels)

    for block, slot, valid in present:
        partners[place(slot), :] = block[...]

        @pl.when(jnp.logical_not(valid))
        def _(slot=slot):
            partners[place(slot), :] = nothing

    for slot in absent:
        partners[place(slot), :] = nothing


def early_slots(me, count, channels, blocks, partners):
    own, ahead = blocks
    next_level = me // 4 + 1 < count // 4
    put_slots(
        channels, partners, [(own, 0, me >= 0), (ahead, 4, next_level)], (1, 2, 3, 5, 6, 7)
    )


def late_slots(me, count, channels, blocks, partners):
    core = lax.rem(me, 2)
    side = lax.rem(me // 2, 2)
    (own_swapped, ahead_swapped, far, far_swapped, cross, cross_swapped, other,
     other_swapped) = blocks
    cross_slot = 6 - 4 * side
    other_slot = 8 - cross_slot
    step = 1 - 2 * core
    next_level = me // 4 + 1 < count // 4
    second_level = me // 4 + 2 < count // 4
    other_there = (side == 0) | second_level
    put_slots(channels, partners, [
        (far, 0, second_level), (cross, cross_slot, next_level),
        (other, other_slot, other_there), (ahead_swapped, 4 + step, next_level),
        (cross_swapped, cross_slot + step, next_level),
        (other_swapped, other_slot + step, other_there),
    ], (4,))

    @pl.when(core == 0)
    def _():
        put_slots(channels, partners, [(own_swapped, 1, me >= 0)], ())

    @pl.when(core == 1)
    def _():
        put_slots(channels, partners, [(far_swapped, 7, second_level)], ())


def product_kernel(late, count, norm_scale, place, rotated, *refs):
    refs = list(refs)
    before = refs.pop(0) if late else None
    out, partners, total = refs[-3:]
    blocks = refs[:-3]
    channels = blocks[0].shape[0]
    (late_slots if late else early_slots)(place[0], count, channels, blocks, partners)
    rows, features = rotated.shape
    chunk = 2 * 2 * NF
    for begin in range(0, features, chunk):
        turned = partners[:, begin:begin + chunk].T
        product = dot(rotated[:, begin:begin + chunk], turned)
        if begin == 0:
            total[...] = product
        else:
            total[...] += product

    row = lax.broadcasted_iota(jnp.int32, (channels, NPART), 0)
    column = lax.broadcasted_iota(jnp.int32, (channels, NPART), 1)
    low = row + column >= NPART - 1
    keep = (low | (column < NPART - channels)) if late else jnp.logical_not(low)
    sheared = []
    for begin in range(0, rows, channels):
        here = slice(begin, begin + channels)
        value = jnp.where(keep, total[here, :], 0.0)
        if late:
            value = (value + before[here, :]) * norm_scale
            sheared.append(pltpu.roll(value, 1, 1, stride=1, stride_axis=0).astype(BF16))
        else:
            out[here, :] = value
    if late:
        sheared = jnp.concatenate(sheared, axis=0)
        out[...] = dot(sheared, flip_matrix(NPART)).astype(BF16)


def exchange(value, pairs):
    return lax.ppermute(value, "chan", pairs)


def local(records, dead_mask, offsets):
    channels, samples = records.shape
    tm_count = lax.axis_size("tm")
    tm_index = lax.axis_index("tm")
    chan_count = lax.axis_size("chan")
    own = samples // HOP
    windows = own * tm_count
    halves = own
    halo = 0
    if tm_count > 1:
        reach = 2 * HOP + H
        left = lax.ppermute(
            records[:, samples - H:], "tm", [(i, i + 1) for i in range(tm_count - 1)]
        )
        right = lax.ppermute(
            records[:, :reach], "tm", [(i + 1, i) for i in range(tm_count - 1)]
        )
        records = jnp.concatenate([left, records, right], axis=1)
        halves = own + 2
        halo = H
    table = jnp.asarray(packed_tables())
    own_offsets = lax.dynamic_slice_in_dim(offsets, tm_index * own, own, 0)
    vmem = pl.BlockSpec(memory_space=pltpu.VMEM)
    smem = pl.BlockSpec(memory_space=pltpu.SMEM)
    hbm = pl.BlockSpec(memory_space=pl.ANY)
    params = pltpu.CompilerParams(vmem_limit_bytes=24 * 1024 * 1024)

    bulk = min(own + 1, halves)
    part_rows = (own + bulk * (HOP // GROUP)) * channels
    spectra = pl.pallas_call(
        functools.partial(spectra_kernel, halves, own, halo),
        name="spectra",
        out_shape=jax.ShapeDtypeStruct((channels, own * 2 * NF), BF16),
        in_specs=[smem, smem, hbm, hbm],
        out_specs=vmem,
        scratch_shapes=[
            pltpu.VMEM((channels, halves * HOP + 2 * H), F32),
            pltpu.VMEM((channels, halves * HOP + 2 * H), BF16),
            pltpu.VMEM((part_rows, GROUP), BF16),
            pltpu.VMEM((part_rows, GROUP), BF16),
            pltpu.VMEM((part_rows, 2 * NF + 128), F32),
            pltpu.VMEM(table.shape, BF16),
            pltpu.SemaphoreType.DMA((3 * halves + 1,)),
        ],
        compiler_params=pltpu.CompilerParams(vmem_limit_bytes=60 * 1024 * 1024),
        cost_estimate=pl.CostEstimate(
            flops=7_000_000_000, bytes_accessed=8 * 1024 * 1024, transcendentals=0
        ),
    )(dead_mask, own_offsets, records, table)
    if tm_count > 1:
        spectra = lax.all_gather(spectra, "tm", axis=1, tiled=True)

    lags = NLAG // tm_count
    cos_lag, sin_lag = (
        lax.dynamic_slice_in_dim(jnp.asarray(t), tm_index * lags, lags, 0) for t in lag_tables()
    )
    place = lax.axis_index("chan").astype(jnp.int32).reshape(1)
    norm_scale = 1.0 / math.sqrt(2.0 * NF * windows)

    features = spectra.shape[1]
    rotated = pl.pallas_call(
        functools.partial(rotate_kernel, lags),
        name="rotate",
        grid=(windows,),
        out_shape=jax.ShapeDtypeStruct((lags * channels, features), BF16),
        in_specs=[
            pl.BlockSpec((channels, 2 * NF), lambda w: (0, w)),
            pl.BlockSpec((lags, NF), lambda w: (0, 0)),
            pl.BlockSpec((lags, NF), lambda w: (0, 0)),
        ],
        out_specs=pl.BlockSpec((lags * channels, 2 * NF), lambda w: (0, w)),
        compiler_params=params,
        cost_estimate=pl.CostEstimate(
            flops=4_000_000_000, bytes_accessed=8 * 1024 * 1024, transcendentals=0
        ),
    )(spectra, cos_lag, sin_lag)

    def product(blocks, before):
        late = before is not None
        operands = [place, rotated] + ([before] if late else []) + list(blocks)
        return pl.pallas_call(
            functools.partial(product_kernel, late, chan_count, norm_scale),
            name="late_product" if late else "early_product",
            out_shape=jax.ShapeDtypeStruct((lags * channels, NPART), BF16 if late else F32),
            in_specs=[smem] + [vmem] * (len(operands) - 1),
            out_specs=vmem,
            scratch_shapes=[
                pltpu.VMEM((NPART, features), BF16),
                pltpu.VMEM((lags * channels, NPART), F32),
            ],
            compiler_params=params,
            cost_estimate=pl.CostEstimate(
                flops=2 * lags * channels * features * NPART, bytes_accessed=6 * 1024 * 1024,
                transcendentals=0,
            ),
        )(*operands)

    every = range(chan_count)

    def swapped_level(i, odd):
        level = i // 4
        other = level + 1 if level % 2 == odd else level - 1
        return i + 4 * (other - level) if 0 <= 4 * other < chan_count else i

    even_levels, odd_levels = ([(i, swapped_level(i, odd)) for i in every] for odd in (0, 1))
    top = chan_count - 4

    def far_target(i):
        return i if i >= top else (i - 4 if i >= 4 else top - 4 + i)

    def other_target(i):
        if i & 2:
            return i - 2
        return i + 2 if i >= top else (i - 2 if i >= 4 else top - 2 + i)

    far_pairs = [(i, far_target(i)) for i in every]
    other_pairs = [(i, other_target(i)) for i in every]
    across = [(i, i ^ 2) for i in every]
    cores = [(i, i ^ 1) for i in every]
    side = lax.rem(lax.axis_index("chan") // 2, 2)

    from_even = exchange(spectra, even_levels)
    from_odd = exchange(spectra, odd_levels)
    level = lax.axis_index("chan") // 4
    ahead = jnp.where(lax.rem(level, 2) == 0, from_even, from_odd)
    ahead, rotated = lax.optimization_barrier((ahead, rotated))
    cross = exchange(ahead, across)
    other = exchange(jnp.where(side == 0, ahead, spectra), other_pairs)
    far = exchange(ahead, far_pairs)
    early = product((spectra, ahead), None)
    kept, ahead, other, early = lax.optimization_barrier((spectra, ahead, other, early))
    own_swapped = exchange(kept, cores)
    ahead_swapped = exchange(ahead, cores)
    cross, own_swapped, ahead_swapped = lax.optimization_barrier(
        (cross, own_swapped, ahead_swapped)
    )
    blocks = (own_swapped, ahead_swapped, far, exchange(far, cores), cross,
              exchange(cross, cores), other, exchange(other, cores))
    return product(blocks, early).reshape(lags, channels, NPART)


def solution(mesh):
    return jax.shard_map(
        local,
        mesh=mesh,
        in_specs=(P(("win", "chan"), "tm"), P(("win", "chan")), P("win")),
        out_specs=P("tm", ("win", "chan"), None),
        check_vma=False,
    )
```

```python
import functools
import math

import jax
import jax.numpy as jnp
import ml_dtypes
import numpy as np
from jax import lax
from jax.experimental import pallas as pl
from jax.experimental.pallas import tpu as pltpu
from jax.sharding import PartitionSpec as P

L = 8192
HOP = 4096
H = 128
K0 = 32
NF = 256
WB = 64
NLAG = 32
NPART = 256
EDGE = 512
STEP = 256
GROUP = 512
EPS = 1e-05
TWO_PI = 2.0 * math.pi
BF16 = jnp.bfloat16
F32 = jnp.float32


def split_table(table):
    high = table.astype(ml_dtypes.bfloat16)
    low = (table - high.astype(np.float64)).astype(ml_dtypes.bfloat16)
    return high, low


@functools.cache
def fourier_tables():
    samples = np.arange(GROUP)[:, None]
    bins = K0 + np.arange(NF)[None, :]
    angle = (samples * bins % L) * (TWO_PI / L)
    inner = np.concatenate([np.cos(angle), -np.sin(angle)], axis=1)
    outer = np.zeros((GROUP, 128))
    for lane, k, wave in ((0, K0 - 1, np.cos), (64, K0 - 1, np.sin), (127, K0 + NF, np.cos), (63, K0 + NF, np.sin)):
        sign = 1.0 if wave is np.cos else -1.0
        outer[:, lane] = sign * wave((samples[:, 0] * k % L) * (TWO_PI / L))
    high, low = split_table(inner)
    return np.concatenate([high, outer.astype(ml_dtypes.bfloat16)], axis=1), low


@functools.cache
def packed_tables():
    return np.concatenate(fourier_tables(), axis=1)


@functools.cache
def lag_tables():
    lags = np.arange(NLAG)[:, None] - NLAG // 2
    angle = (lags * (K0 + np.arange(NF))[None, :] % L) * (TWO_PI / L)
    return np.cos(angle).astype(np.float32), np.sin(angle).astype(np.float32)


def split(value):
    high = value.astype(BF16)
    return high, (value - high.astype(F32)).astype(BF16)


def inverse(value):
    guess = pl.reciprocal(value, approx=True)
    return guess * (2.0 - value * guess)


def dot(a, b):
    return jnp.dot(a, b, preferred_element_type=F32)


def spectra_kernel(
    halves, own, halo,
    dead, offs, x_hbm, table_hbm, out, x, absolute, norm_high, norm_low, parts, table, sems,
):
    channels = x.shape[0]
    groups = HOP // GROUP
    bulk = min(own + 1, halves)
    edges = min(own + 2, halves)
    width = halves * HOP
    cuts = [HOP // 4 + H, HOP // 2 + H]
    pieces = []
    for part in range(3):
        for j in range(halves):
            begin = j * HOP + cuts[part - 1] if part else j * HOP - (H if j or halo else 0)
            end = (j + 1) * HOP - H if j + 1 < halves else width + halo
            pieces.append((begin, j * HOP + cuts[part] if part < 2 else end))
    copies = [
        pltpu.make_async_copy(
            x_hbm.at[:, pl.ds(halo + begin, end - begin)], x.at[:, pl.ds(H + begin, end - begin)],
            sems.at[i],
        )
        for i, (begin, end) in enumerate(pieces)
    ]
    table_copy = pltpu.make_async_copy(table_hbm, table, sems.at[3 * halves])
    for copy in copies[:2 * halves] + [table_copy] + copies[2 * halves:]:
        copy.start()
    if not halo:
        for begin in (0, H + width):
            absolute[:, begin:begin + H] = jnp.zeros((channels, H), BF16)

    def arrive(part):
        ids = range(part * halves, (part + 1) * halves)
        for i in ids:
            copies[i].wait()
        for i in ids:
            begin, end = pieces[i]
            here = slice(H + begin, H + end)
            absolute[:, here] = jnp.abs(x[:, here]).astype(BF16)

    high = table.at[:, :2 * NF + 128]
    low = table.at[:, 2 * NF + 128:]
    from_lane = lax.broadcasted_iota(jnp.int32, (2 * H + STEP, STEP), 0)
    to_lane = lax.broadcasted_iota(jnp.int32, (2 * H + STEP, STEP), 1)
    level_band = ((from_lane >= to_lane) & (from_lane <= to_lane + 2 * H)).astype(F32).astype(BF16)
    from_bin = lax.broadcasted_iota(jnp.int32, (NF, NF), 0)
    to_bin = lax.broadcasted_iota(jnp.int32, (NF, NF), 1)
    smooth_band = (jnp.abs(from_bin - to_bin) <= WB).astype(F32).astype(BF16)
    lane = lax.broadcasted_iota(jnp.int32, (1, parts.shape[1]), 1)
    outer_place = lane - 2 * NF
    outer_first = (outer_place == 0) | (outer_place == 64)
    every_bin = jnp.where(
        lane < 2 * NF, jnp.bitwise_and(lane, NF - 1) + K0, jnp.where(outer_first, K0 - 1, K0 + NF)
    )
    real_place = (lane < NF) | (outer_place == 0) | (outer_place == 127)
    group = lax.broadcasted_iota(jnp.int32, (groups, 1), 0) * GROUP
    angle = jnp.bitwise_and(group * every_bin, L - 1).astype(F32) * (TWO_PI / L)
    turn_same = jnp.cos(angle)
    turn_swap = jnp.sin(angle) * jnp.where(real_place, -1.0, 1.0)
    bin_index = lax.broadcasted_iota(jnp.int32, (1, NF), 1)
    below, above = jnp.minimum(bin_index, WB), jnp.minimum(NF - 1 - bin_index, WB)
    inverse_count = 1.0 / (below + above + 1).astype(F32)

    def rows(ref, begin, length, count):
        return [ref[:, begin + j * HOP:begin + j * HOP + length] for j in range(count)]

    def store(place, value):
        here = slice(place, place + value.shape[0])
        norm_high[here, :], norm_low[here, :] = split(value)

    def normalise(group_ids, place):
        blocks = [(g, g * GROUP + part * STEP) for g in group_ids for part in range(GROUP // STEP)]
        counts = [edges if g == 0 else bulk for g, _ in blocks]
        level = dot(
            jnp.concatenate(
                [r for (_, begin), n in zip(blocks, counts)
                 for r in rows(absolute, begin, STEP + 2 * H, n)], axis=0
            ), level_band,
        ) * (1.0 / (2 * H + 1)) + EPS
        values = []
        at = 0
        for (_, begin), n in zip(blocks, counts):
            samples = jnp.concatenate(rows(x, H + begin, STEP, n), axis=0)
            values.append(samples * inverse(level[at:at + n * channels]))
            at += n * channels
        begins = {}
        for index, g in enumerate(group_ids):
            value = jnp.concatenate(values[2 * index:2 * index + 2], axis=1)
            if g == 0:
                lane = lax.broadcasted_iota(jnp.int32, (channels, EDGE), 1)
                merged = []
                for w in range(own):
                    mine = value[w * channels:(w + 1) * channels]
                    other = (
                        value[(w + 2) * channels:(w + 3) * channels]
                        if w + 2 < edges else jnp.zeros_like(mine)
                    )
                    merged.append(jnp.where(lane >= offs[w], mine, other))
                begins["edge"] = place
                store(place, jnp.concatenate(merged, axis=0))
                place += own * channels
                value = value[:bulk * channels]
            begins[g] = place
            store(place, value)
            place += bulk * channels
        return begins, place

    def transform(begin, end):
        first = dot(norm_high[begin:end, :], high[...])
        second = dot(norm_low[begin:end, :], high[:, :2 * NF])
        second = second + dot(norm_high[begin:end, :], low[...])
        parts[begin:end, :2 * NF] = first[:, :2 * NF] + second
        parts[begin:end, 2 * NF:] = first[:, 2 * NF:]

    begins = {}
    place = 0
    waiting = None
    for g in range(0, groups, 2):
        if g < 4:
            arrive(g // 2)
        start = place
        found, place = normalise([g, g + 1], place)
        begins.update(found)
        if g == 2:
            arrive(2)
            table_copy.wait()
        if waiting:
            transform(*waiting)
        waiting = (start, place)
    transform(*waiting)

    def piece(name, j):
        return parts[begins[name] + j * channels:begins[name] + (j + 1) * channels, :]

    def bulk_of(j):
        same = jnp.zeros((channels, parts.shape[1]), F32)
        swap = same
        for g in range(1, groups):
            value = piece(g, j)
            same = same + value * turn_same[g:g + 1, :]
            swap = swap + value * turn_swap[g:g + 1, :]
        return same + jnp.concatenate(
            [swap[:, NF:2 * NF], swap[:, :NF], pltpu.roll(swap[:, 2 * NF:], 64, 1)], axis=1
        )

    window = lax.broadcasted_iota(jnp.int32, (own, 1), 0)
    offsets = sum(jnp.where(window == w, offs[w], 0) for w in range(own))
    lane = lax.broadcasted_iota(jnp.int32, (1, NF), 1)
    outer_lane = lax.broadcasted_iota(jnp.int32, (1, 128), 1)
    outer_bin = jnp.where((outer_lane == 0) | (outer_lane == 64), K0 - 1, K0 + NF)

    def turn(bins):
        angle = jnp.bitwise_and(bins * offsets, L - 1).astype(F32) * (TWO_PI / L)
        return jnp.cos(angle), jnp.sin(angle)

    cos_turn, sin_turn = turn(lane + K0)
    cos_outer, sin_outer = turn(outer_bin)
    sign = 1.0 - 2.0 * jnp.bitwise_and(lane + K0, 1).astype(F32)
    sign_outer = 1.0 - 2.0 * jnp.bitwise_and(outer_bin, 1).astype(F32)
    channel = lax.broadcasted_iota(jnp.int32, (channels, 1), 0)
    live = 1.0 - sum(jnp.where(channel == i, dead[i], 0) for i in range(channels)).astype(F32)

    signs = jnp.concatenate([sign, sign, sign_outer], axis=1)
    reals, imags, magnitudes = [], [], []
    following = bulk_of(0)
    for w in range(own):
        spec = following + piece("edge", w)
        if w + 1 < bulk:
            following = bulk_of(w + 1)
            spec = spec + (following + piece(0, w + 1)) * signs
        spec = spec * live
        outer = spec[:, 2 * NF:]
        c, s = cos_turn[w:w + 1], sin_turn[w:w + 1]
        c_outer, s_outer = cos_outer[w:w + 1], sin_outer[w:w + 1]
        outer_imag = pltpu.roll(outer, 64, 1)

        def hann(inner, ends):
            ends = jnp.concatenate([ends, ends], axis=1)
            before = jnp.where(lane == 0, ends, pltpu.roll(inner, 1, 1))
            behind = jnp.where(lane == NF - 1, ends, pltpu.roll(inner, NF - 1, 1))
            return 0.5 * inner - 0.25 * (before + behind)

        real = hann(
            spec[:, :NF] * c - spec[:, NF:2 * NF] * s, outer * c_outer - outer_imag * s_outer
        )
        imag = hann(
            spec[:, :NF] * s + spec[:, NF:2 * NF] * c, outer * s_outer + outer_imag * c_outer
        )
        reals.append(real)
        imags.append(imag)
        magnitudes.append(jnp.sqrt(real * real + imag * imag + 1e-12))
    m_high, m_low = split(jnp.concatenate(magnitudes, axis=0))
    smooth = (dot(m_high, smooth_band) + dot(m_low, smooth_band)) * inverse_count
    scale = 1.0 / (smooth + EPS)
    flip = flip_matrix(channels)
    for w in range(own):
        here = slice(w * channels, (w + 1) * channels)
        white = jnp.concatenate([reals[w] * scale[here], imags[w] * scale[here]], axis=1)
        out[:, w * 2 * NF:(w + 1) * 2 * NF] = dot(flip, white.astype(BF16)).astype(BF16)


def flip_matrix(channels):
    row = lax.broadcasted_iota(jnp.int32, (channels, channels), 0)
    column = lax.broadcasted_iota(jnp.int32, (channels, channels), 1)
    return (row + column == channels - 1).astype(F32).astype(BF16)


def rotate_kernel(lags, own, cos_lag, sin_lag, out):
    channels = own.shape[0]
    straight = dot(flip_matrix(channels), own[...])
    real, imag = straight[:, :NF], straight[:, NF:]
    for t in range(lags):
        c, s = cos_lag[t:t + 1, :], sin_lag[t:t + 1, :]
        here = slice(t * channels, (t + 1) * channels)
        out[here, :NF] = (real * c - imag * s).astype(BF16)
        out[here, NF:] = (real * s + imag * c).astype(BF16)


def put_slots(channels, partners, present, absent):
    last = NPART // channels - 1
    nothing = jnp.zeros((channels, partners.shape[1]), BF16)

    def place(slot):
        return pl.ds(pl.multiple_of((last - slot) * channels, channels), channels)

    for block, slot, valid in present:
        partners[place(slot), :] = block[...]

        @pl.when(jnp.logical_not(valid))
        def _(slot=slot):
            partners[place(slot), :] = nothing

    for slot in absent:
        partners[place(slot), :] = nothing


def early_slots(me, count, channels, blocks, partners):
    own, ahead = blocks
    next_level = me // 4 + 1 < count // 4
    put_slots(
        channels, partners, [(own, 0, me >= 0), (ahead, 4, next_level)], (1, 2, 3, 5, 6, 7)
    )


def late_slots(me, count, channels, blocks, partners):
    core = lax.rem(me, 2)
    side = lax.rem(me // 2, 2)
    (own_swapped, ahead_swapped, far, far_swapped, cross, cross_swapped, other,
     other_swapped) = blocks
    cross_slot = 6 - 4 * side
    other_slot = 8 - cross_slot
    step = 1 - 2 * core
    next_level = me // 4 + 1 < count // 4
    second_level = me // 4 + 2 < count // 4
    other_there = (side == 0) | second_level
    put_slots(channels, partners, [
        (far, 0, second_level), (cross, cross_slot, next_level),
        (other, other_slot, other_there), (ahead_swapped, 4 + step, next_level),
        (cross_swapped, cross_slot + step, next_level),
        (other_swapped, other_slot + step, other_there),
    ], (4,))

    @pl.when(core == 0)
    def _():
        put_slots(channels, partners, [(own_swapped, 1, me >= 0)], ())

    @pl.when(core == 1)
    def _():
        put_slots(channels, partners, [(far_swapped, 7, second_level)], ())


def product_kernel(late, count, norm_scale, place, rotated, *refs):
    refs = list(refs)
    before = refs.pop(0) if late else None
    out, partners, total = refs[-3:]
    blocks = refs[:-3]
    channels = blocks[0].shape[0]
    (late_slots if late else early_slots)(place[0], count, channels, blocks, partners)
    rows, features = rotated.shape
    chunk = 2 * 2 * NF
    for begin in range(0, features, chunk):
        turned = partners[:, begin:begin + chunk].T
        product = dot(rotated[:, begin:begin + chunk], turned)
        if begin == 0:
            total[...] = product
        else:
            total[...] += product

    row = lax.broadcasted_iota(jnp.int32, (channels, NPART), 0)
    column = lax.broadcasted_iota(jnp.int32, (channels, NPART), 1)
    low = row + column >= NPART - 1
    keep = (low | (column < NPART - channels)) if late else jnp.logical_not(low)
    sheared = []
    for begin in range(0, rows, channels):
        here = slice(begin, begin + channels)
        value = jnp.where(keep, total[here, :], 0.0)
        if late:
            value = (value + before[here, :]) * norm_scale
            sheared.append(pltpu.roll(value, 1, 1, stride=1, stride_axis=0).astype(BF16))
        else:
            out[here, :] = value
    if late:
        sheared = jnp.concatenate(sheared, axis=0)
        out[...] = dot(sheared, flip_matrix(NPART)).astype(BF16)


def exchange(value, pairs):
    return lax.ppermute(value, "chan", pairs)


def local(records, dead_mask, offsets):
    channels, samples = records.shape
    tm_count = lax.axis_size("tm")
    tm_index = lax.axis_index("tm")
    chan_count = lax.axis_size("chan")
    own = samples // HOP
    windows = own * tm_count
    halves = own
    halo = 0
    if tm_count > 1:
        reach = 2 * HOP + H
        left = lax.ppermute(
            records[:, samples - H:], "tm", [(i, i + 1) for i in range(tm_count - 1)]
        )
        right = lax.ppermute(
            records[:, :reach], "tm", [(i + 1, i) for i in range(tm_count - 1)]
        )
        records = jnp.concatenate([left, records, right], axis=1)
        halves = own + 2
        halo = H
    table = jnp.asarray(packed_tables())
    own_offsets = lax.dynamic_slice_in_dim(offsets, tm_index * own, own, 0)
    vmem = pl.BlockSpec(memory_space=pltpu.VMEM)
    smem = pl.BlockSpec(memory_space=pltpu.SMEM)
    hbm = pl.BlockSpec(memory_space=pl.ANY)
    params = pltpu.CompilerParams(vmem_limit_bytes=24 * 1024 * 1024)

    bulk = min(own + 1, halves)
    part_rows = (own + bulk * (HOP // GROUP)) * channels
    spectra = pl.pallas_call(
        functools.partial(spectra_kernel, halves, own, halo),
        name="spectra",
        out_shape=jax.ShapeDtypeStruct((channels, own * 2 * NF), BF16),
        in_specs=[smem, smem, hbm, hbm],
        out_specs=vmem,
        scratch_shapes=[
            pltpu.VMEM((channels, halves * HOP + 2 * H), F32),
            pltpu.VMEM((channels, halves * HOP + 2 * H), BF16),
            pltpu.VMEM((part_rows, GROUP), BF16),
            pltpu.VMEM((part_rows, GROUP), BF16),
            pltpu.VMEM((part_rows, 2 * NF + 128), F32),
            pltpu.VMEM(table.shape, BF16),
            pltpu.SemaphoreType.DMA((3 * halves + 1,)),
        ],
        compiler_params=pltpu.CompilerParams(vmem_limit_bytes=60 * 1024 * 1024),
        cost_estimate=pl.CostEstimate(
            flops=7_000_000_000, bytes_accessed=8 * 1024 * 1024, transcendentals=0
        ),
    )(dead_mask, own_offsets, records, table)
    if tm_count > 1:
        spectra = lax.all_gather(spectra, "tm", axis=1, tiled=True)

    lags = NLAG // tm_count
    cos_lag, sin_lag = (
        lax.dynamic_slice_in_dim(jnp.asarray(t), tm_index * lags, lags, 0) for t in lag_tables()
    )
    place = lax.axis_index("chan").astype(jnp.int32).reshape(1)
    norm_scale = 1.0 / math.sqrt(2.0 * NF * windows)

    features = spectra.shape[1]
    rotated = pl.pallas_call(
        functools.partial(rotate_kernel, lags),
        name="rotate",
        grid=(windows,),
        out_shape=jax.ShapeDtypeStruct((lags * channels, features), BF16),
        in_specs=[
            pl.BlockSpec((channels, 2 * NF), lambda w: (0, w)),
            pl.BlockSpec((lags, NF), lambda w: (0, 0)),
            pl.BlockSpec((lags, NF), lambda w: (0, 0)),
        ],
        out_specs=pl.BlockSpec((lags * channels, 2 * NF), lambda w: (0, w)),
        compiler_params=params,
        cost_estimate=pl.CostEstimate(
            flops=4_000_000_000, bytes_accessed=8 * 1024 * 1024, transcendentals=0
        ),
    )(spectra, cos_lag, sin_lag)

    def product(blocks, before):
        late = before is not None
        operands = [place, rotated] + ([before] if late else []) + list(blocks)
        return pl.pallas_call(
            functools.partial(product_kernel, late, chan_count, norm_scale),
            name="late_product" if late else "early_product",
            out_shape=jax.ShapeDtypeStruct((lags * channels, NPART), BF16 if late else F32),
            in_specs=[smem] + [vmem] * (len(operands) - 1),
            out_specs=vmem,
            scratch_shapes=[
                pltpu.VMEM((NPART, features), BF16),
                pltpu.VMEM((lags * channels, NPART), F32),
            ],
            compiler_params=params,
            cost_estimate=pl.CostEstimate(
                flops=2 * lags * channels * features * NPART, bytes_accessed=6 * 1024 * 1024,
                transcendentals=0,
            ),
        )(*operands)

    every = range(chan_count)
    down = [(i, (i - 4) % chan_count) for i in every]
    top = chan_count - 4

    def far_target(i):
        return i ^ 1 if i >= top else (i - 4 if i >= 4 else top - 4 + i)

    def other_target(i):
        if i & 2:
            return i - 2
        return i + 2 if i >= top else (i - 2 if i >= 4 else top - 2 + i)

    far_pairs = [(i, far_target(i)) for i in every]
    other_pairs = [(i, other_target(i)) for i in every]
    across = [(i, i ^ 2) for i in every]
    cores = [(i, i ^ 1) for i in every]
    side = lax.rem(lax.axis_index("chan") // 2, 2)

    ahead = exchange(spectra, down)
    ahead, rotated = lax.optimization_barrier((ahead, rotated))
    other = exchange(jnp.where(side == 0, ahead, spectra), other_pairs)
    cross = exchange(ahead, across)
    far = exchange(ahead, far_pairs)
    early = product((spectra, ahead), None)
    kept, ahead, other, early = lax.optimization_barrier((spectra, ahead, other, early))
    own_swapped = exchange(kept, cores)
    ahead_swapped = exchange(ahead, cores)
    cross, own_swapped, ahead_swapped = lax.optimization_barrier(
        (cross, own_swapped, ahead_swapped)
    )
    blocks = (own_swapped, ahead_swapped, far, exchange(far, cores), cross,
              exchange(cross, cores), other, exchange(other, cores))
    return product(blocks, early).reshape(lags, channels, NPART)


def solution(mesh):
    return jax.shard_map(
        local,
        mesh=mesh,
        in_specs=(P(("win", "chan"), "tm"), P(("win", "chan")), P("win")),
        out_specs=P("tm", ("win", "chan"), None),
        check_vma=False,
    )
```

```python
import functools
import math

import jax
import jax.numpy as jnp
import ml_dtypes
import numpy as np
from jax import lax
from jax.experimental import pallas as pl
from jax.experimental.pallas import tpu as pltpu
from jax.sharding import PartitionSpec as P

L = 8192
HOP = 4096
H = 128
K0 = 32
NF = 256
WB = 64
NLAG = 32
NPART = 256
EDGE = 512
STEP = 256
GROUP = 512
EPS = 1e-05
TWO_PI = 2.0 * math.pi
BF16 = jnp.bfloat16
F32 = jnp.float32


def split_table(table):
    high = table.astype(ml_dtypes.bfloat16)
    low = (table - high.astype(np.float64)).astype(ml_dtypes.bfloat16)
    return high, low


@functools.cache
def fourier_tables():
    samples = np.arange(GROUP)[:, None]
    bins = K0 + np.arange(NF)[None, :]
    angle = (samples * bins % L) * (TWO_PI / L)
    inner = np.concatenate([np.cos(angle), -np.sin(angle)], axis=1)
    outer = np.zeros((GROUP, 128))
    for lane, k, wave in ((0, K0 - 1, np.cos), (64, K0 - 1, np.sin), (127, K0 + NF, np.cos), (63, K0 + NF, np.sin)):
        sign = 1.0 if wave is np.cos else -1.0
        outer[:, lane] = sign * wave((samples[:, 0] * k % L) * (TWO_PI / L))
    high, low = split_table(inner)
    return np.concatenate([high, outer.astype(ml_dtypes.bfloat16)], axis=1), low


@functools.cache
def packed_tables():
    return np.concatenate(fourier_tables(), axis=1)


@functools.cache
def lag_tables():
    lags = np.arange(NLAG)[:, None] - NLAG // 2
    angle = (lags * (K0 + np.arange(NF))[None, :] % L) * (TWO_PI / L)
    return np.cos(angle).astype(np.float32), np.sin(angle).astype(np.float32)


def split(value):
    high = value.astype(BF16)
    return high, (value - high.astype(F32)).astype(BF16)


def inverse(value):
    guess = pl.reciprocal(value, approx=True)
    return guess * (2.0 - value * guess)


def dot(a, b):
    return jnp.dot(a, b, preferred_element_type=F32)


def spectra_kernel(
    halves, own, halo,
    dead, offs, x_hbm, table_hbm, out, x, absolute, norm_high, norm_low, parts, table, sems,
):
    channels = x.shape[0]
    groups = HOP // GROUP
    bulk = min(own + 1, halves)
    edges = min(own + 2, halves)
    width = halves * HOP
    cuts = [HOP // 4 + H, HOP // 2 + H]
    pieces = []
    for part in range(3):
        for j in range(halves):
            begin = j * HOP + cuts[part - 1] if part else j * HOP - (H if j or halo else 0)
            end = (j + 1) * HOP - H if j + 1 < halves else width + halo
            pieces.append((begin, j * HOP + cuts[part] if part < 2 else end))
    copies = [
        pltpu.make_async_copy(
            x_hbm.at[:, pl.ds(halo + begin, end - begin)], x.at[:, pl.ds(H + begin, end - begin)],
            sems.at[i],
        )
        for i, (begin, end) in enumerate(pieces)
    ]
    table_copy = pltpu.make_async_copy(table_hbm, table, sems.at[3 * halves])
    for copy in copies[:2 * halves] + [table_copy] + copies[2 * halves:]:
        copy.start()
    if not halo:
        for begin in (0, H + width):
            absolute[:, begin:begin + H] = jnp.zeros((channels, H), BF16)

    def arrive(part):
        ids = range(part * halves, (part + 1) * halves)
        for i in ids:
            copies[i].wait()
        for i in ids:
            begin, end = pieces[i]
            here = slice(H + begin, H + end)
            absolute[:, here] = jnp.abs(x[:, here]).astype(BF16)

    high = table.at[:, :2 * NF + 128]
    low = table.at[:, 2 * NF + 128:]
    from_lane = lax.broadcasted_iota(jnp.int32, (2 * H + STEP, STEP), 0)
    to_lane = lax.broadcasted_iota(jnp.int32, (2 * H + STEP, STEP), 1)
    level_band = ((from_lane >= to_lane) & (from_lane <= to_lane + 2 * H)).astype(F32).astype(BF16)
    from_bin = lax.broadcasted_iota(jnp.int32, (NF, NF), 0)
    to_bin = lax.broadcasted_iota(jnp.int32, (NF, NF), 1)
    smooth_band = (jnp.abs(from_bin - to_bin) <= WB).astype(F32).astype(BF16)
    lane = lax.broadcasted_iota(jnp.int32, (1, parts.shape[1]), 1)
    outer_place = lane - 2 * NF
    outer_first = (outer_place == 0) | (outer_place == 64)
    every_bin = jnp.where(
        lane < 2 * NF, jnp.bitwise_and(lane, NF - 1) + K0, jnp.where(outer_first, K0 - 1, K0 + NF)
    )
    real_place = (lane < NF) | (outer_place == 0) | (outer_place == 127)
    group = lax.broadcasted_iota(jnp.int32, (groups, 1), 0) * GROUP
    angle = jnp.bitwise_and(group * every_bin, L - 1).astype(F32) * (TWO_PI / L)
    turn_same = jnp.cos(angle)
    turn_swap = jnp.sin(angle) * jnp.where(real_place, -1.0, 1.0)
    bin_index = lax.broadcasted_iota(jnp.int32, (1, NF), 1)
    below, above = jnp.minimum(bin_index, WB), jnp.minimum(NF - 1 - bin_index, WB)
    inverse_count = 1.0 / (below + above + 1).astype(F32)

    def rows(ref, begin, length, count):
        return [ref[:, begin + j * HOP:begin + j * HOP + length] for j in range(count)]

    def store(place, value):
        here = slice(place, place + value.shape[0])
        norm_high[here, :], norm_low[here, :] = split(value)

    def normalise(group_ids, place):
        blocks = [(g, g * GROUP + part * STEP) for g in group_ids for part in range(GROUP // STEP)]
        counts = [edges if g == 0 else bulk for g, _ in blocks]
        level = dot(
            jnp.concatenate(
                [r for (_, begin), n in zip(blocks, counts)
                 for r in rows(absolute, begin, STEP + 2 * H, n)], axis=0
            ), level_band,
        ) * (1.0 / (2 * H + 1)) + EPS
        values = []
        at = 0
        for (_, begin), n in zip(blocks, counts):
            samples = jnp.concatenate(rows(x, H + begin, STEP, n), axis=0)
            values.append(samples * inverse(level[at:at + n * channels]))
            at += n * channels
        begins = {}
        for index, g in enumerate(group_ids):
            value = jnp.concatenate(values[2 * index:2 * index + 2], axis=1)
            if g == 0:
                lane = lax.broadcasted_iota(jnp.int32, (channels, EDGE), 1)
                merged = []
                for w in range(own):
                    mine = value[w * channels:(w + 1) * channels]
                    other = (
                        value[(w + 2) * channels:(w + 3) * channels]
                        if w + 2 < edges else jnp.zeros_like(mine)
                    )
                    merged.append(jnp.where(lane >= offs[w], mine, other))
                begins["edge"] = place
                store(place, jnp.concatenate(merged, axis=0))
                place += own * channels
                value = value[:bulk * channels]
            begins[g] = place
            store(place, value)
            place += bulk * channels
        return begins, place

    def transform(begin, end):
        first = dot(norm_high[begin:end, :], high[...])
        second = dot(norm_low[begin:end, :], high[:, :2 * NF])
        second = second + dot(norm_high[begin:end, :], low[...])
        parts[begin:end, :2 * NF] = first[:, :2 * NF] + second
        parts[begin:end, 2 * NF:] = first[:, 2 * NF:]

    begins = {}
    place = 0
    waiting = None
    for g in range(0, groups, 2):
        if g < 4:
            arrive(g // 2)
        start = place
        found, place = normalise([g, g + 1], place)
        begins.update(found)
        if g == 2:
            arrive(2)
            table_copy.wait()
        if waiting:
            transform(*waiting)
        waiting = (start, place)
    transform(*waiting)

    def piece(name, j):
        return parts[begins[name] + j * channels:begins[name] + (j + 1) * channels, :]

    def bulk_of(j):
        same = jnp.zeros((channels, parts.shape[1]), F32)
        swap = same
        for g in range(1, groups):
            value = piece(g, j)
            same = same + value * turn_same[g:g + 1, :]
            swap = swap + value * turn_swap[g:g + 1, :]
        return same + jnp.concatenate(
            [swap[:, NF:2 * NF], swap[:, :NF], pltpu.roll(swap[:, 2 * NF:], 64, 1)], axis=1
        )

    window = lax.broadcasted_iota(jnp.int32, (own, 1), 0)
    offsets = sum(jnp.where(window == w, offs[w], 0) for w in range(own))
    lane = lax.broadcasted_iota(jnp.int32, (1, NF), 1)
    outer_lane = lax.broadcasted_iota(jnp.int32, (1, 128), 1)
    outer_bin = jnp.where((outer_lane == 0) | (outer_lane == 64), K0 - 1, K0 + NF)

    def turn(bins):
        angle = jnp.bitwise_and(bins * offsets, L - 1).astype(F32) * (TWO_PI / L)
        return jnp.cos(angle), jnp.sin(angle)

    cos_turn, sin_turn = turn(lane + K0)
    cos_outer, sin_outer = turn(outer_bin)
    sign = 1.0 - 2.0 * jnp.bitwise_and(lane + K0, 1).astype(F32)
    sign_outer = 1.0 - 2.0 * jnp.bitwise_and(outer_bin, 1).astype(F32)
    channel = lax.broadcasted_iota(jnp.int32, (channels, 1), 0)
    live = 1.0 - sum(jnp.where(channel == i, dead[i], 0) for i in range(channels)).astype(F32)

    signs = jnp.concatenate([sign, sign, sign_outer], axis=1)
    reals, imags, magnitudes = [], [], []
    following = bulk_of(0)
    for w in range(own):
        spec = following + piece("edge", w)
        if w + 1 < bulk:
            following = bulk_of(w + 1)
            spec = spec + (following + piece(0, w + 1)) * signs
        spec = spec * live
        outer = spec[:, 2 * NF:]
        c, s = cos_turn[w:w + 1], sin_turn[w:w + 1]
        c_outer, s_outer = cos_outer[w:w + 1], sin_outer[w:w + 1]
        outer_imag = pltpu.roll(outer, 64, 1)

        def hann(inner, ends):
            ends = jnp.concatenate([ends, ends], axis=1)
            before = jnp.where(lane == 0, ends, pltpu.roll(inner, 1, 1))
            behind = jnp.where(lane == NF - 1, ends, pltpu.roll(inner, NF - 1, 1))
            return 0.5 * inner - 0.25 * (before + behind)

        real = hann(
            spec[:, :NF] * c - spec[:, NF:2 * NF] * s, outer * c_outer - outer_imag * s_outer
        )
        imag = hann(
            spec[:, :NF] * s + spec[:, NF:2 * NF] * c, outer * s_outer + outer_imag * c_outer
        )
        reals.append(real)
        imags.append(imag)
        magnitudes.append(jnp.sqrt(real * real + imag * imag + 1e-12))
    m_high, m_low = split(jnp.concatenate(magnitudes, axis=0))
    smooth = (dot(m_high, smooth_band) + dot(m_low, smooth_band)) * inverse_count
    scale = 1.0 / (smooth + EPS)
    flip = flip_matrix(channels)
    for w in range(own):
        here = slice(w * channels, (w + 1) * channels)
        white = jnp.concatenate([reals[w] * scale[here], imags[w] * scale[here]], axis=1)
        out[:, w * 2 * NF:(w + 1) * 2 * NF] = dot(flip, white.astype(BF16)).astype(BF16)


def flip_matrix(channels):
    row = lax.broadcasted_iota(jnp.int32, (channels, channels), 0)
    column = lax.broadcasted_iota(jnp.int32, (channels, channels), 1)
    return (row + column == channels - 1).astype(F32).astype(BF16)


def rotate_kernel(lags, own, cos_lag, sin_lag, out):
    channels = own.shape[0]
    straight = dot(flip_matrix(channels), own[...])
    real, imag = straight[:, :NF], straight[:, NF:]
    for t in range(lags):
        c, s = cos_lag[t:t + 1, :], sin_lag[t:t + 1, :]
        here = slice(t * channels, (t + 1) * channels)
        out[here, :NF] = (real * c - imag * s).astype(BF16)
        out[here, NF:] = (real * s + imag * c).astype(BF16)


def put_slots(channels, partners, present, absent):
    last = NPART // channels - 1
    nothing = jnp.zeros((channels, partners.shape[1]), BF16)

    def place(slot):
        return pl.ds(pl.multiple_of((last - slot) * channels, channels), channels)

    for block, slot, valid in present:
        partners[place(slot), :] = block[...]

        @pl.when(jnp.logical_not(valid))
        def _(slot=slot):
            partners[place(slot), :] = nothing

    for slot in absent:
        partners[place(slot), :] = nothing


def early_slots(me, count, channels, blocks, partners):
    own, ahead = blocks
    next_level = me // 4 + 1 < count // 4
    put_slots(
        channels, partners, [(own, 0, me >= 0), (ahead, 4, next_level)], (1, 2, 3, 5, 6, 7)
    )


def late_slots(me, count, channels, blocks, partners):
    core = lax.rem(me, 2)
    side = lax.rem(me // 2, 2)
    (own_swapped, ahead_swapped, far, far_swapped, cross, cross_swapped, other,
     other_swapped) = blocks
    cross_slot = 6 - 4 * side
    other_slot = 8 - cross_slot
    step = 1 - 2 * core
    next_level = me // 4 + 1 < count // 4
    second_level = me // 4 + 2 < count // 4
    other_there = (side == 0) | second_level
    put_slots(channels, partners, [
        (far, 0, second_level), (cross, cross_slot, next_level),
        (other, other_slot, other_there), (ahead_swapped, 4 + step, next_level),
        (cross_swapped, cross_slot + step, next_level),
        (other_swapped, other_slot + step, other_there),
    ], (4,))

    @pl.when(core == 0)
    def _():
        put_slots(channels, partners, [(own_swapped, 1, me >= 0)], ())

    @pl.when(core == 1)
    def _():
        put_slots(channels, partners, [(far_swapped, 7, second_level)], ())


def product_kernel(late, count, norm_scale, place, rotated, *refs):
    refs = list(refs)
    before = refs.pop(0) if late else None
    out, partners, total = refs[-3:]
    blocks = refs[:-3]
    channels = blocks[0].shape[0]
    (late_slots if late else early_slots)(place[0], count, channels, blocks, partners)
    rows, features = rotated.shape
    chunk = 2 * 2 * NF
    for begin in range(0, features, chunk):
        turned = partners[:, begin:begin + chunk].T
        product = dot(rotated[:, begin:begin + chunk], turned)
        if begin == 0:
            total[...] = product
        else:
            total[...] += product

    row = lax.broadcasted_iota(jnp.int32, (channels, NPART), 0)
    column = lax.broadcasted_iota(jnp.int32, (channels, NPART), 1)
    low = row + column >= NPART - 1
    keep = (low | (column < NPART - channels)) if late else jnp.logical_not(low)
    sheared = []
    for begin in range(0, rows, channels):
        here = slice(begin, begin + channels)
        value = jnp.where(keep, total[here, :], 0.0)
        if late:
            value = (value + before[here, :]) * norm_scale
            sheared.append(pltpu.roll(value, 1, 1, stride=1, stride_axis=0).astype(BF16))
        else:
            out[here, :] = value
    if late:
        sheared = jnp.concatenate(sheared, axis=0)
        out[...] = dot(sheared, flip_matrix(NPART)).astype(BF16)


def exchange(value, pairs):
    return lax.ppermute(value, "chan", pairs)


def local(records, dead_mask, offsets):
    channels, samples = records.shape
    tm_count = lax.axis_size("tm")
    tm_index = lax.axis_index("tm")
    chan_count = lax.axis_size("chan")
    own = samples // HOP
    windows = own * tm_count
    halves = own
    halo = 0
    if tm_count > 1:
        reach = 2 * HOP + H
        left = lax.ppermute(
            records[:, samples - H:], "tm", [(i, i + 1) for i in range(tm_count - 1)]
        )
        right = lax.ppermute(
            records[:, :reach], "tm", [(i + 1, i) for i in range(tm_count - 1)]
        )
        records = jnp.concatenate([left, records, right], axis=1)
        halves = own + 2
        halo = H
    table = jnp.asarray(packed_tables())
    own_offsets = lax.dynamic_slice_in_dim(offsets, tm_index * own, own, 0)
    vmem = pl.BlockSpec(memory_space=pltpu.VMEM)
    smem = pl.BlockSpec(memory_space=pltpu.SMEM)
    hbm = pl.BlockSpec(memory_space=pl.ANY)
    params = pltpu.CompilerParams(vmem_limit_bytes=24 * 1024 * 1024)

    bulk = min(own + 1, halves)
    part_rows = (own + bulk * (HOP // GROUP)) * channels
    spectra = pl.pallas_call(
        functools.partial(spectra_kernel, halves, own, halo),
        name="spectra",
        out_shape=jax.ShapeDtypeStruct((channels, own * 2 * NF), BF16),
        in_specs=[smem, smem, hbm, hbm],
        out_specs=vmem,
        scratch_shapes=[
            pltpu.VMEM((channels, halves * HOP + 2 * H), F32),
            pltpu.VMEM((channels, halves * HOP + 2 * H), BF16),
            pltpu.VMEM((part_rows, GROUP), BF16),
            pltpu.VMEM((part_rows, GROUP), BF16),
            pltpu.VMEM((part_rows, 2 * NF + 128), F32),
            pltpu.VMEM(table.shape, BF16),
            pltpu.SemaphoreType.DMA((3 * halves + 1,)),
        ],
        compiler_params=pltpu.CompilerParams(vmem_limit_bytes=60 * 1024 * 1024),
        cost_estimate=pl.CostEstimate(
            flops=7_000_000_000, bytes_accessed=8 * 1024 * 1024, transcendentals=0
        ),
    )(dead_mask, own_offsets, records, table)
    if tm_count > 1:
        spectra = lax.all_gather(spectra, "tm", axis=1, tiled=True)

    lags = NLAG // tm_count
    cos_lag, sin_lag = (
        lax.dynamic_slice_in_dim(jnp.asarray(t), tm_index * lags, lags, 0) for t in lag_tables()
    )
    place = lax.axis_index("chan").astype(jnp.int32).reshape(1)
    norm_scale = 1.0 / math.sqrt(2.0 * NF * windows)

    features = spectra.shape[1]
    rotated = pl.pallas_call(
        functools.partial(rotate_kernel, lags),
        name="rotate",
        grid=(windows,),
        out_shape=jax.ShapeDtypeStruct((lags * channels, features), BF16),
        in_specs=[
            pl.BlockSpec((channels, 2 * NF), lambda w: (0, w)),
            pl.BlockSpec((lags, NF), lambda w: (0, 0)),
            pl.BlockSpec((lags, NF), lambda w: (0, 0)),
        ],
        out_specs=pl.BlockSpec((lags * channels, 2 * NF), lambda w: (0, w)),
        compiler_params=params,
        cost_estimate=pl.CostEstimate(
            flops=4_000_000_000, bytes_accessed=8 * 1024 * 1024, transcendentals=0
        ),
    )(spectra, cos_lag, sin_lag)

    def product(blocks, before):
        late = before is not None
        operands = [place, rotated] + ([before] if late else []) + list(blocks)
        return pl.pallas_call(
            functools.partial(product_kernel, late, chan_count, norm_scale),
            name="late_product" if late else "early_product",
            out_shape=jax.ShapeDtypeStruct((lags * channels, NPART), BF16 if late else F32),
            in_specs=[smem] + [vmem] * (len(operands) - 1),
            out_specs=vmem,
            scratch_shapes=[
                pltpu.VMEM((NPART, features), BF16),
                pltpu.VMEM((lags * channels, NPART), F32),
            ],
            compiler_params=params,
            cost_estimate=pl.CostEstimate(
                flops=2 * lags * channels * features * NPART, bytes_accessed=6 * 1024 * 1024,
                transcendentals=0,
            ),
        )(*operands)

    every = range(chan_count)
    down = [(i, (i - 4) % chan_count) for i in every]
    top = chan_count - 4

    def far_target(i):
        return i ^ 1 if i >= top else (i - 4 if i >= 4 else top - 4 + i)

    def other_target(i):
        if i & 2:
            return i - 2
        return i + 2 if i >= top else (i - 2 if i >= 4 else top - 2 + i)

    far_pairs = [(i, far_target(i)) for i in every]
    other_pairs = [(i, other_target(i)) for i in every]
    across = [(i, i ^ 2) for i in every]
    cores = [(i, i ^ 1) for i in every]
    side = lax.rem(lax.axis_index("chan") // 2, 2)

    ahead = exchange(spectra, down)
    ahead, rotated = lax.optimization_barrier((ahead, rotated))
    other = exchange(jnp.where(side == 0, ahead, spectra), other_pairs)
    cross = exchange(ahead, across)
    far = exchange(ahead, far_pairs)
    early = product((spectra, ahead), None)
    kept, ahead, other, early = lax.optimization_barrier((spectra, ahead, other, early))
    own_swapped = exchange(kept, cores)
    ahead_swapped = exchange(ahead, cores)
    far, own_swapped, ahead_swapped = lax.optimization_barrier(
        (far, own_swapped, ahead_swapped)
    )
    blocks = (own_swapped, ahead_swapped, far, exchange(far, cores), cross,
              exchange(cross, cores), other, exchange(other, cores))
    return product(blocks, early).reshape(lags, channels, NPART)


def solution(mesh):
    return jax.shard_map(
        local,
        mesh=mesh,
        in_specs=(P(("win", "chan"), "tm"), P(("win", "chan")), P("win")),
        out_specs=P("tm", ("win", "chan"), None),
        check_vma=False,
    )
```

```python
import functools
import math

import jax
import jax.numpy as jnp
import ml_dtypes
import numpy as np
from jax import lax
from jax.experimental import pallas as pl
from jax.experimental.pallas import tpu as pltpu
from jax.sharding import PartitionSpec as P

L = 8192
HOP = 4096
H = 128
K0 = 32
NF = 256
WB = 64
NLAG = 32
NPART = 256
EDGE = 512
STEP = 256
GROUP = 512
EPS = 1e-05
TWO_PI = 2.0 * math.pi
BF16 = jnp.bfloat16
F32 = jnp.float32


def split_table(table):
    high = table.astype(ml_dtypes.bfloat16)
    low = (table - high.astype(np.float64)).astype(ml_dtypes.bfloat16)
    return high, low


@functools.cache
def fourier_tables():
    samples = np.arange(GROUP)[:, None]
    bins = K0 + np.arange(NF)[None, :]
    angle = (samples * bins % L) * (TWO_PI / L)
    inner = np.concatenate([np.cos(angle), -np.sin(angle)], axis=1)
    outer = np.zeros((GROUP, 128))
    for lane, k, wave in ((0, K0 - 1, np.cos), (64, K0 - 1, np.sin), (127, K0 + NF, np.cos), (63, K0 + NF, np.sin)):
        sign = 1.0 if wave is np.cos else -1.0
        outer[:, lane] = sign * wave((samples[:, 0] * k % L) * (TWO_PI / L))
    high, low = split_table(inner)
    return np.concatenate([high, outer.astype(ml_dtypes.bfloat16)], axis=1), low


@functools.cache
def packed_tables():
    return np.concatenate(fourier_tables(), axis=1)


@functools.cache
def lag_tables():
    lags = np.arange(NLAG)[:, None] - NLAG // 2
    angle = (lags * (K0 + np.arange(NF))[None, :] % L) * (TWO_PI / L)
    return np.cos(angle).astype(np.float32), np.sin(angle).astype(np.float32)


def split(value):
    high = value.astype(BF16)
    return high, (value - high.astype(F32)).astype(BF16)


def inverse(value):
    guess = pl.reciprocal(value, approx=True)
    return guess * (2.0 - value * guess)


def dot(a, b):
    return jnp.dot(a, b, preferred_element_type=F32)


def spectra_kernel(
    halves, own, halo,
    dead, offs, x_hbm, table_hbm, out, x, absolute, norm_high, norm_low, parts, table, sems,
):
    channels = x.shape[0]
    groups = HOP // GROUP
    bulk = min(own + 1, halves)
    edges = min(own + 2, halves)
    width = halves * HOP
    cuts = [HOP // 4 + H, HOP // 2 + H]
    pieces = []
    for part in range(3):
        for j in range(halves):
            begin = j * HOP + cuts[part - 1] if part else j * HOP - (H if j or halo else 0)
            end = (j + 1) * HOP - H if j + 1 < halves else width + halo
            pieces.append((begin, j * HOP + cuts[part] if part < 2 else end))
    copies = [
        pltpu.make_async_copy(
            x_hbm.at[:, pl.ds(halo + begin, end - begin)], x.at[:, pl.ds(H + begin, end - begin)],
            sems.at[i],
        )
        for i, (begin, end) in enumerate(pieces)
    ]
    table_copy = pltpu.make_async_copy(table_hbm, table, sems.at[3 * halves])
    for copy in copies[:2 * halves] + [table_copy] + copies[2 * halves:]:
        copy.start()
    if not halo:
        for begin in (0, H + width):
            absolute[:, begin:begin + H] = jnp.zeros((channels, H), BF16)

    def arrive(part):
        ids = range(part * halves, (part + 1) * halves)
        for i in ids:
            copies[i].wait()
        for i in ids:
            begin, end = pieces[i]
            here = slice(H + begin, H + end)
            absolute[:, here] = jnp.abs(x[:, here]).astype(BF16)

    high = table.at[:, :2 * NF + 128]
    low = table.at[:, 2 * NF + 128:]
    from_lane = lax.broadcasted_iota(jnp.int32, (2 * H + STEP, STEP), 0)
    to_lane = lax.broadcasted_iota(jnp.int32, (2 * H + STEP, STEP), 1)
    level_band = ((from_lane >= to_lane) & (from_lane <= to_lane + 2 * H)).astype(F32).astype(BF16)
    from_bin = lax.broadcasted_iota(jnp.int32, (NF, NF), 0)
    to_bin = lax.broadcasted_iota(jnp.int32, (NF, NF), 1)
    smooth_band = (jnp.abs(from_bin - to_bin) <= WB).astype(F32).astype(BF16)
    lane = lax.broadcasted_iota(jnp.int32, (1, parts.shape[1]), 1)
    outer_place = lane - 2 * NF
    outer_first = (outer_place == 0) | (outer_place == 64)
    every_bin = jnp.where(
        lane < 2 * NF, jnp.bitwise_and(lane, NF - 1) + K0, jnp.where(outer_first, K0 - 1, K0 + NF)
    )
    real_place = (lane < NF) | (outer_place == 0) | (outer_place == 127)
    group = lax.broadcasted_iota(jnp.int32, (groups, 1), 0) * GROUP
    angle = jnp.bitwise_and(group * every_bin, L - 1).astype(F32) * (TWO_PI / L)
    turn_same = jnp.cos(angle)
    turn_swap = jnp.sin(angle) * jnp.where(real_place, -1.0, 1.0)
    bin_index = lax.broadcasted_iota(jnp.int32, (1, NF), 1)
    below, above = jnp.minimum(bin_index, WB), jnp.minimum(NF - 1 - bin_index, WB)
    inverse_count = 1.0 / (below + above + 1).astype(F32)

    def rows(ref, begin, length, count):
        return [ref[:, begin + j * HOP:begin + j * HOP + length] for j in range(count)]

    def store(place, value):
        here = slice(place, place + value.shape[0])
        norm_high[here, :], norm_low[here, :] = split(value)

    def normalise(group_ids, place):
        blocks = [(g, g * GROUP + part * STEP) for g in group_ids for part in range(GROUP // STEP)]
        counts = [edges if g == 0 else bulk for g, _ in blocks]
        level = dot(
            jnp.concatenate(
                [r for (_, begin), n in zip(blocks, counts)
                 for r in rows(absolute, begin, STEP + 2 * H, n)], axis=0
            ), level_band,
        ) * (1.0 / (2 * H + 1)) + EPS
        values = []
        at = 0
        for (_, begin), n in zip(blocks, counts):
            samples = jnp.concatenate(rows(x, H + begin, STEP, n), axis=0)
            values.append(samples * inverse(level[at:at + n * channels]))
            at += n * channels
        begins = {}
        for index, g in enumerate(group_ids):
            value = jnp.concatenate(values[2 * index:2 * index + 2], axis=1)
            if g == 0:
                lane = lax.broadcasted_iota(jnp.int32, (channels, EDGE), 1)
                merged = []
                for w in range(own):
                    mine = value[w * channels:(w + 1) * channels]
                    other = (
                        value[(w + 2) * channels:(w + 3) * channels]
                        if w + 2 < edges else jnp.zeros_like(mine)
                    )
                    merged.append(jnp.where(lane >= offs[w], mine, other))
                begins["edge"] = place
                store(place, jnp.concatenate(merged, axis=0))
                place += own * channels
                value = value[:bulk * channels]
            begins[g] = place
            store(place, value)
            place += bulk * channels
        return begins, place

    def transform(begin, end):
        first = dot(norm_high[begin:end, :], high[...])
        second = dot(norm_low[begin:end, :], high[:, :2 * NF])
        second = second + dot(norm_high[begin:end, :], low[...])
        parts[begin:end, :2 * NF] = first[:, :2 * NF] + second
        parts[begin:end, 2 * NF:] = first[:, 2 * NF:]

    begins = {}
    place = 0
    waiting = None
    for g in range(0, groups, 2):
        if g < 4:
            arrive(g // 2)
        start = place
        found, place = normalise([g, g + 1], place)
        begins.update(found)
        if g == 2:
            arrive(2)
            table_copy.wait()
        if waiting:
            transform(*waiting)
        waiting = (start, place)
    transform(*waiting)

    def piece(name, j):
        return parts[begins[name] + j * channels:begins[name] + (j + 1) * channels, :]

    def bulk_of(j):
        same = jnp.zeros((channels, parts.shape[1]), F32)
        swap = same
        for g in range(1, groups):
            value = piece(g, j)
            same = same + value * turn_same[g:g + 1, :]
            swap = swap + value * turn_swap[g:g + 1, :]
        return same + jnp.concatenate(
            [swap[:, NF:2 * NF], swap[:, :NF], pltpu.roll(swap[:, 2 * NF:], 64, 1)], axis=1
        )

    window = lax.broadcasted_iota(jnp.int32, (own, 1), 0)
    offsets = sum(jnp.where(window == w, offs[w], 0) for w in range(own))
    lane = lax.broadcasted_iota(jnp.int32, (1, NF), 1)
    outer_lane = lax.broadcasted_iota(jnp.int32, (1, 128), 1)
    outer_bin = jnp.where((outer_lane == 0) | (outer_lane == 64), K0 - 1, K0 + NF)

    def turn(bins):
        angle = jnp.bitwise_and(bins * offsets, L - 1).astype(F32) * (TWO_PI / L)
        return jnp.cos(angle), jnp.sin(angle)

    cos_turn, sin_turn = turn(lane + K0)
    cos_outer, sin_outer = turn(outer_bin)
    sign = 1.0 - 2.0 * jnp.bitwise_and(lane + K0, 1).astype(F32)
    sign_outer = 1.0 - 2.0 * jnp.bitwise_and(outer_bin, 1).astype(F32)
    channel = lax.broadcasted_iota(jnp.int32, (channels, 1), 0)
    live = 1.0 - sum(jnp.where(channel == i, dead[i], 0) for i in range(channels)).astype(F32)

    signs = jnp.concatenate([sign, sign, sign_outer], axis=1)
    reals, imags, magnitudes = [], [], []
    following = bulk_of(0)
    for w in range(own):
        spec = following + piece("edge", w)
        if w + 1 < bulk:
            following = bulk_of(w + 1)
            spec = spec + (following + piece(0, w + 1)) * signs
        spec = spec * live
        outer = spec[:, 2 * NF:]
        c, s = cos_turn[w:w + 1], sin_turn[w:w + 1]
        c_outer, s_outer = cos_outer[w:w + 1], sin_outer[w:w + 1]
        outer_imag = pltpu.roll(outer, 64, 1)

        def hann(inner, ends):
            ends = jnp.concatenate([ends, ends], axis=1)
            before = jnp.where(lane == 0, ends, pltpu.roll(inner, 1, 1))
            behind = jnp.where(lane == NF - 1, ends, pltpu.roll(inner, NF - 1, 1))
            return 0.5 * inner - 0.25 * (before + behind)

        real = hann(
            spec[:, :NF] * c - spec[:, NF:2 * NF] * s, outer * c_outer - outer_imag * s_outer
        )
        imag = hann(
            spec[:, :NF] * s + spec[:, NF:2 * NF] * c, outer * s_outer + outer_imag * c_outer
        )
        reals.append(real)
        imags.append(imag)
        magnitudes.append(jnp.sqrt(real * real + imag * imag + 1e-12))
    m_high, m_low = split(jnp.concatenate(magnitudes, axis=0))
    smooth = (dot(m_high, smooth_band) + dot(m_low, smooth_band)) * inverse_count
    scale = 1.0 / (smooth + EPS)
    flip = flip_matrix(channels)
    for w in range(own):
        here = slice(w * channels, (w + 1) * channels)
        white = jnp.concatenate([reals[w] * scale[here], imags[w] * scale[here]], axis=1)
        out[:, w * 2 * NF:(w + 1) * 2 * NF] = dot(flip, white.astype(BF16)).astype(BF16)


def flip_matrix(channels):
    row = lax.broadcasted_iota(jnp.int32, (channels, channels), 0)
    column = lax.broadcasted_iota(jnp.int32, (channels, channels), 1)
    return (row + column == channels - 1).astype(F32).astype(BF16)


def rotate_kernel(lags, own, cos_lag, sin_lag, out):
    channels = own.shape[0]
    straight = dot(flip_matrix(channels), own[...])
    real, imag = straight[:, :NF], straight[:, NF:]
    for t in range(lags):
        c, s = cos_lag[t:t + 1, :], sin_lag[t:t + 1, :]
        here = slice(t * channels, (t + 1) * channels)
        out[here, :NF] = (real * c - imag * s).astype(BF16)
        out[here, NF:] = (real * s + imag * c).astype(BF16)


def put_slots(channels, partners, present, absent):
    last = NPART // channels - 1
    nothing = jnp.zeros((channels, partners.shape[1]), BF16)

    def place(slot):
        return pl.ds(pl.multiple_of((last - slot) * channels, channels), channels)

    for block, slot, valid in present:
        partners[place(slot), :] = block[...]

        @pl.when(jnp.logical_not(valid))
        def _(slot=slot):
            partners[place(slot), :] = nothing

    for slot in absent:
        partners[place(slot), :] = nothing


def early_slots(me, count, channels, blocks, partners):
    own, ahead = blocks
    next_level = me // 4 + 1 < count // 4
    put_slots(
        channels, partners, [(own, 0, me >= 0), (ahead, 4, next_level)], (1, 2, 3, 5, 6, 7)
    )


def late_slots(me, count, channels, blocks, partners):
    core = lax.rem(me, 2)
    side = lax.rem(me // 2, 2)
    (own_swapped, ahead_swapped, far, far_swapped, cross, cross_swapped, other,
     other_swapped) = blocks
    cross_slot = 6 - 4 * side
    other_slot = 8 - cross_slot
    step = 1 - 2 * core
    next_level = me // 4 + 1 < count // 4
    second_level = me // 4 + 2 < count // 4
    other_there = (side == 0) | second_level
    put_slots(channels, partners, [
        (far, 0, second_level), (cross, cross_slot, next_level),
        (other, other_slot, other_there), (ahead_swapped, 4 + step, next_level),
        (cross_swapped, cross_slot + step, next_level),
        (other_swapped, other_slot + step, other_there),
    ], (4,))

    @pl.when(core == 0)
    def _():
        put_slots(channels, partners, [(own_swapped, 1, me >= 0)], ())

    @pl.when(core == 1)
    def _():
        put_slots(channels, partners, [(far_swapped, 7, second_level)], ())


def product_kernel(late, count, norm_scale, place, rotated, *refs):
    refs = list(refs)
    before = refs.pop(0) if late else None
    out, partners, total = refs[-3:]
    blocks = refs[:-3]
    channels = blocks[0].shape[0]
    (late_slots if late else early_slots)(place[0], count, channels, blocks, partners)
    rows, features = rotated.shape
    chunk = 2 * 2 * NF
    for begin in range(0, features, chunk):
        turned = partners[:, begin:begin + chunk].T
        product = dot(rotated[:, begin:begin + chunk], turned)
        if begin == 0:
            total[...] = product
        else:
            total[...] += product

    row = lax.broadcasted_iota(jnp.int32, (channels, NPART), 0)
    column = lax.broadcasted_iota(jnp.int32, (channels, NPART), 1)
    low = row + column >= NPART - 1
    keep = (low | (column < NPART - channels)) if late else jnp.logical_not(low)
    sheared = []
    for begin in range(0, rows, channels):
        here = slice(begin, begin + channels)
        value = jnp.where(keep, total[here, :], 0.0)
        if late:
            value = (value + before[here, :]) * norm_scale
            sheared.append(pltpu.roll(value, 1, 1, stride=1, stride_axis=0).astype(BF16))
        else:
            out[here, :] = value
    if late:
        sheared = jnp.concatenate(sheared, axis=0)
        out[...] = dot(sheared, flip_matrix(NPART)).astype(BF16)


def exchange(value, pairs):
    return lax.ppermute(value, "chan", pairs)


def local(records, dead_mask, offsets):
    channels, samples = records.shape
    tm_count = lax.axis_size("tm")
    tm_index = lax.axis_index("tm")
    chan_count = lax.axis_size("chan")
    own = samples // HOP
    windows = own * tm_count
    halves = own
    halo = 0
    if tm_count > 1:
        reach = 2 * HOP + H
        left = lax.ppermute(
            records[:, samples - H:], "tm", [(i, i + 1) for i in range(tm_count - 1)]
        )
        right = lax.ppermute(
            records[:, :reach], "tm", [(i + 1, i) for i in range(tm_count - 1)]
        )
        records = jnp.concatenate([left, records, right], axis=1)
        halves = own + 2
        halo = H
    table = jnp.asarray(packed_tables())
    own_offsets = lax.dynamic_slice_in_dim(offsets, tm_index * own, own, 0)
    vmem = pl.BlockSpec(memory_space=pltpu.VMEM)
    smem = pl.BlockSpec(memory_space=pltpu.SMEM)
    hbm = pl.BlockSpec(memory_space=pl.ANY)
    params = pltpu.CompilerParams(vmem_limit_bytes=24 * 1024 * 1024)

    bulk = min(own + 1, halves)
    part_rows = (own + bulk * (HOP // GROUP)) * channels
    spectra = pl.pallas_call(
        functools.partial(spectra_kernel, halves, own, halo),
        name="spectra",
        out_shape=jax.ShapeDtypeStruct((channels, own * 2 * NF), BF16),
        in_specs=[smem, smem, hbm, hbm],
        out_specs=vmem,
        scratch_shapes=[
            pltpu.VMEM((channels, halves * HOP + 2 * H), F32),
            pltpu.VMEM((channels, halves * HOP + 2 * H), BF16),
            pltpu.VMEM((part_rows, GROUP), BF16),
            pltpu.VMEM((part_rows, GROUP), BF16),
            pltpu.VMEM((part_rows, 2 * NF + 128), F32),
            pltpu.VMEM(table.shape, BF16),
            pltpu.SemaphoreType.DMA((3 * halves + 1,)),
        ],
        compiler_params=pltpu.CompilerParams(vmem_limit_bytes=60 * 1024 * 1024),
        cost_estimate=pl.CostEstimate(
            flops=7_000_000_000, bytes_accessed=8 * 1024 * 1024, transcendentals=0
        ),
    )(dead_mask, own_offsets, records, table)
    if tm_count > 1:
        spectra = lax.all_gather(spectra, "tm", axis=1, tiled=True)

    lags = NLAG // tm_count
    cos_lag, sin_lag = (
        lax.dynamic_slice_in_dim(jnp.asarray(t), tm_index * lags, lags, 0) for t in lag_tables()
    )
    place = lax.axis_index("chan").astype(jnp.int32).reshape(1)
    norm_scale = 1.0 / math.sqrt(2.0 * NF * windows)

    features = spectra.shape[1]
    rotated = pl.pallas_call(
        functools.partial(rotate_kernel, lags),
        name="rotate",
        grid=(windows,),
        out_shape=jax.ShapeDtypeStruct((lags * channels, features), BF16),
        in_specs=[
            pl.BlockSpec((channels, 2 * NF), lambda w: (0, w)),
            pl.BlockSpec((lags, NF), lambda w: (0, 0)),
            pl.BlockSpec((lags, NF), lambda w: (0, 0)),
        ],
        out_specs=pl.BlockSpec((lags * channels, 2 * NF), lambda w: (0, w)),
        compiler_params=params,
        cost_estimate=pl.CostEstimate(
            flops=4_000_000_000, bytes_accessed=8 * 1024 * 1024, transcendentals=0
        ),
    )(spectra, cos_lag, sin_lag)

    def product(blocks, before):
        late = before is not None
        operands = [place, rotated] + ([before] if late else []) + list(blocks)
        return pl.pallas_call(
            functools.partial(product_kernel, late, chan_count, norm_scale),
            name="late_product" if late else "early_product",
            out_shape=jax.ShapeDtypeStruct((lags * channels, NPART), BF16 if late else F32),
            in_specs=[smem] + [vmem] * (len(operands) - 1),
            out_specs=vmem,
            scratch_shapes=[
                pltpu.VMEM((NPART, features), BF16),
                pltpu.VMEM((lags * channels, NPART), F32),
            ],
            compiler_params=params,
            cost_estimate=pl.CostEstimate(
                flops=2 * lags * channels * features * NPART, bytes_accessed=6 * 1024 * 1024,
                transcendentals=0,
            ),
        )(*operands)

    every = range(chan_count)

    def swapped_level(i, odd):
        level = i // 4
        other = level + 1 if level % 2 == odd else level - 1
        return i + 4 * (other - level) if 0 <= 4 * other < chan_count else i ^ 1

    even_levels, odd_levels = ([(i, swapped_level(i, odd)) for i in every] for odd in (0, 1))
    top = chan_count - 4

    def far_target(i):
        return i ^ 1 if i >= top else (i - 4 if i >= 4 else top - 4 + i)

    def other_target(i):
        if i & 2:
            return i - 2
        return i + 2 if i >= top else (i - 2 if i >= 4 else top - 2 + i)

    far_pairs = [(i, far_target(i)) for i in every]
    other_pairs = [(i, other_target(i)) for i in every]
    across = [(i, i ^ 2) for i in every]
    cores = [(i, i ^ 1) for i in every]
    side = lax.rem(lax.axis_index("chan") // 2, 2)

    from_even = exchange(spectra, even_levels)
    from_odd = exchange(spectra, odd_levels)
    level = lax.axis_index("chan") // 4
    ahead = jnp.where(lax.rem(level, 2) == 0, from_even, from_odd)
    ahead, rotated = lax.optimization_barrier((ahead, rotated))
    other = exchange(jnp.where(side == 0, ahead, spectra), other_pairs)
    cross = exchange(ahead, across)
    far = exchange(ahead, far_pairs)
    early = product((spectra, ahead), None)
    kept, ahead, other, early = lax.optimization_barrier((spectra, ahead, other, early))
    own_swapped = exchange(kept, cores)
    ahead_swapped = exchange(ahead, cores)
    far, own_swapped, ahead_swapped = lax.optimization_barrier(
        (far, own_swapped, ahead_swapped)
    )
    blocks = (own_swapped, ahead_swapped, far, exchange(far, cores), cross,
              exchange(cross, cores), other, exchange(other, cores))
    return product(blocks, early).reshape(lags, channels, NPART)


def solution(mesh):
    return jax.shard_map(
        local,
        mesh=mesh,
        in_specs=(P(("win", "chan"), "tm"), P(("win", "chan")), P("win")),
        out_specs=P("tm", ("win", "chan"), None),
        check_vma=False,
    )
```

```python
import functools
import math

import jax
import jax.numpy as jnp
import ml_dtypes
import numpy as np
from jax import lax
from jax.experimental import pallas as pl
from jax.experimental.pallas import tpu as pltpu
from jax.sharding import PartitionSpec as P

L = 8192
HOP = 4096
H = 128
K0 = 32
NF = 256
WB = 64
NLAG = 32
NPART = 256
EDGE = 512
STEP = 256
GROUP = 512
EPS = 1e-05
TWO_PI = 2.0 * math.pi
BF16 = jnp.bfloat16
F32 = jnp.float32


def split_table(table):
    high = table.astype(ml_dtypes.bfloat16)
    low = (table - high.astype(np.float64)).astype(ml_dtypes.bfloat16)
    return high, low


@functools.cache
def fourier_tables():
    samples = np.arange(GROUP)[:, None]
    bins = K0 + np.arange(NF)[None, :]
    angle = (samples * bins % L) * (TWO_PI / L)
    inner = np.concatenate([np.cos(angle), -np.sin(angle)], axis=1)
    outer = np.zeros((GROUP, 128))
    for lane, k, wave in ((0, K0 - 1, np.cos), (64, K0 - 1, np.sin), (127, K0 + NF, np.cos), (63, K0 + NF, np.sin)):
        sign = 1.0 if wave is np.cos else -1.0
        outer[:, lane] = sign * wave((samples[:, 0] * k % L) * (TWO_PI / L))
    high, low = split_table(inner)
    return np.concatenate([high, outer.astype(ml_dtypes.bfloat16)], axis=1), low


@functools.cache
def packed_tables():
    return np.concatenate(fourier_tables(), axis=1)


@functools.cache
def lag_tables():
    lags = np.arange(NLAG)[:, None] - NLAG // 2
    angle = (lags * (K0 + np.arange(NF))[None, :] % L) * (TWO_PI / L)
    return np.cos(angle).astype(np.float32), np.sin(angle).astype(np.float32)


def split(value):
    high = value.astype(BF16)
    return high, (value - high.astype(F32)).astype(BF16)


def inverse(value):
    guess = pl.reciprocal(value, approx=True)
    return guess * (2.0 - value * guess)


def dot(a, b):
    return jnp.dot(a, b, preferred_element_type=F32)


def spectra_kernel(
    halves, own, halo,
    dead, offs, x_hbm, table_hbm, out, x, absolute, norm_high, norm_low, parts, table, sems,
):
    channels = x.shape[0]
    groups = HOP // GROUP
    bulk = min(own + 1, halves)
    edges = min(own + 2, halves)
    width = halves * HOP
    cuts = [HOP // 4 + H, HOP // 2 + H]
    pieces = []
    for part in range(3):
        for j in range(halves):
            begin = j * HOP + cuts[part - 1] if part else j * HOP - (H if j or halo else 0)
            end = (j + 1) * HOP - H if j + 1 < halves else width + halo
            pieces.append((begin, j * HOP + cuts[part] if part < 2 else end))
    copies = [
        pltpu.make_async_copy(
            x_hbm.at[:, pl.ds(halo + begin, end - begin)], x.at[:, pl.ds(H + begin, end - begin)],
            sems.at[i],
        )
        for i, (begin, end) in enumerate(pieces)
    ]
    table_copy = pltpu.make_async_copy(table_hbm, table, sems.at[3 * halves])
    for copy in copies[:2 * halves] + [table_copy] + copies[2 * halves:]:
        copy.start()
    if not halo:
        for begin in (0, H + width):
            absolute[:, begin:begin + H] = jnp.zeros((channels, H), BF16)

    def arrive(part):
        ids = range(part * halves, (part + 1) * halves)
        for i in ids:
            copies[i].wait()
        for i in ids:
            begin, end = pieces[i]
            here = slice(H + begin, H + end)
            absolute[:, here] = jnp.abs(x[:, here]).astype(BF16)

    high = table.at[:, :2 * NF + 128]
    low = table.at[:, 2 * NF + 128:]
    from_lane = lax.broadcasted_iota(jnp.int32, (2 * H + STEP, STEP), 0)
    to_lane = lax.broadcasted_iota(jnp.int32, (2 * H + STEP, STEP), 1)
    level_band = ((from_lane >= to_lane) & (from_lane <= to_lane + 2 * H)).astype(F32).astype(BF16)
    from_bin = lax.broadcasted_iota(jnp.int32, (NF, NF), 0)
    to_bin = lax.broadcasted_iota(jnp.int32, (NF, NF), 1)
    smooth_band = (jnp.abs(from_bin - to_bin) <= WB).astype(F32).astype(BF16)
    lane = lax.broadcasted_iota(jnp.int32, (1, parts.shape[1]), 1)
    outer_place = lane - 2 * NF
    outer_first = (outer_place == 0) | (outer_place == 64)
    every_bin = jnp.where(
        lane < 2 * NF, jnp.bitwise_and(lane, NF - 1) + K0, jnp.where(outer_first, K0 - 1, K0 + NF)
    )
    real_place = (lane < NF) | (outer_place == 0) | (outer_place == 127)
    group = lax.broadcasted_iota(jnp.int32, (groups, 1), 0) * GROUP
    angle = jnp.bitwise_and(group * every_bin, L - 1).astype(F32) * (TWO_PI / L)
    turn_same = jnp.cos(angle)
    turn_swap = jnp.sin(angle) * jnp.where(real_place, -1.0, 1.0)
    bin_index = lax.broadcasted_iota(jnp.int32, (1, NF), 1)
    below, above = jnp.minimum(bin_index, WB), jnp.minimum(NF - 1 - bin_index, WB)
    inverse_count = 1.0 / (below + above + 1).astype(F32)

    def rows(ref, begin, length, count):
        return [ref[:, begin + j * HOP:begin + j * HOP + length] for j in range(count)]

    def store(place, value):
        here = slice(place, place + value.shape[0])
        norm_high[here, :], norm_low[here, :] = split(value)

    def normalise(group_ids, place):
        blocks = [(g, g * GROUP + part * STEP) for g in group_ids for part in range(GROUP // STEP)]
        counts = [edges if g == 0 else bulk for g, _ in blocks]
        level = dot(
            jnp.concatenate(
                [r for (_, begin), n in zip(blocks, counts)
                 for r in rows(absolute, begin, STEP + 2 * H, n)], axis=0
            ), level_band,
        ) * (1.0 / (2 * H + 1)) + EPS
        values = []
        at = 0
        for (_, begin), n in zip(blocks, counts):
            samples = jnp.concatenate(rows(x, H + begin, STEP, n), axis=0)
            values.append(samples * inverse(level[at:at + n * channels]))
            at += n * channels
        begins = {}
        for index, g in enumerate(group_ids):
            value = jnp.concatenate(values[2 * index:2 * index + 2], axis=1)
            if g == 0:
                lane = lax.broadcasted_iota(jnp.int32, (channels, EDGE), 1)
                merged = []
                for w in range(own):
                    mine = value[w * channels:(w + 1) * channels]
                    other = (
                        value[(w + 2) * channels:(w + 3) * channels]
                        if w + 2 < edges else jnp.zeros_like(mine)
                    )
                    merged.append(jnp.where(lane >= offs[w], mine, other))
                begins["edge"] = place
                store(place, jnp.concatenate(merged, axis=0))
                place += own * channels
                value = value[:bulk * channels]
            begins[g] = place
            store(place, value)
            place += bulk * channels
        return begins, place

    def transform(begin, end):
        first = dot(norm_high[begin:end, :], high[...])
        second = dot(norm_low[begin:end, :], high[:, :2 * NF])
        second = second + dot(norm_high[begin:end, :], low[...])
        parts[begin:end, :2 * NF] = first[:, :2 * NF] + second
        parts[begin:end, 2 * NF:] = first[:, 2 * NF:]

    begins = {}
    place = 0
    waiting = None
    for g in range(0, groups, 2):
        if g < 4:
            arrive(g // 2)
        start = place
        found, place = normalise([g, g + 1], place)
        begins.update(found)
        if g == 2:
            arrive(2)
            table_copy.wait()
        if waiting:
            transform(*waiting)
        waiting = (start, place)
    transform(*waiting)

    def piece(name, j):
        return parts[begins[name] + j * channels:begins[name] + (j + 1) * channels, :]

    def bulk_of(j):
        same = jnp.zeros((channels, parts.shape[1]), F32)
        swap = same
        for g in range(1, groups):
            value = piece(g, j)
            same = same + value * turn_same[g:g + 1, :]
            swap = swap + value * turn_swap[g:g + 1, :]
        return same + jnp.concatenate(
            [swap[:, NF:2 * NF], swap[:, :NF], pltpu.roll(swap[:, 2 * NF:], 64, 1)], axis=1
        )

    window = lax.broadcasted_iota(jnp.int32, (own, 1), 0)
    offsets = sum(jnp.where(window == w, offs[w], 0) for w in range(own))
    lane = lax.broadcasted_iota(jnp.int32, (1, NF), 1)
    outer_lane = lax.broadcasted_iota(jnp.int32, (1, 128), 1)
    outer_bin = jnp.where((outer_lane == 0) | (outer_lane == 64), K0 - 1, K0 + NF)

    def turn(bins):
        angle = jnp.bitwise_and(bins * offsets, L - 1).astype(F32) * (TWO_PI / L)
        return jnp.cos(angle), jnp.sin(angle)

    cos_turn, sin_turn = turn(lane + K0)
    cos_outer, sin_outer = turn(outer_bin)
    sign = 1.0 - 2.0 * jnp.bitwise_and(lane + K0, 1).astype(F32)
    sign_outer = 1.0 - 2.0 * jnp.bitwise_and(outer_bin, 1).astype(F32)
    channel = lax.broadcasted_iota(jnp.int32, (channels, 1), 0)
    live = 1.0 - sum(jnp.where(channel == i, dead[i], 0) for i in range(channels)).astype(F32)

    signs = jnp.concatenate([sign, sign, sign_outer], axis=1)
    reals, imags, magnitudes = [], [], []
    following = bulk_of(0)
    for w in range(own):
        spec = following + piece("edge", w)
        if w + 1 < bulk:
            following = bulk_of(w + 1)
            spec = spec + (following + piece(0, w + 1)) * signs
        spec = spec * live
        outer = spec[:, 2 * NF:]
        c, s = cos_turn[w:w + 1], sin_turn[w:w + 1]
        c_outer, s_outer = cos_outer[w:w + 1], sin_outer[w:w + 1]
        outer_imag = pltpu.roll(outer, 64, 1)

        def hann(inner, ends):
            ends = jnp.concatenate([ends, ends], axis=1)
            before = jnp.where(lane == 0, ends, pltpu.roll(inner, 1, 1))
            behind = jnp.where(lane == NF - 1, ends, pltpu.roll(inner, NF - 1, 1))
            return 0.5 * inner - 0.25 * (before + behind)

        real = hann(
            spec[:, :NF] * c - spec[:, NF:2 * NF] * s, outer * c_outer - outer_imag * s_outer
        )
        imag = hann(
            spec[:, :NF] * s + spec[:, NF:2 * NF] * c, outer * s_outer + outer_imag * c_outer
        )
        reals.append(real)
        imags.append(imag)
        magnitudes.append(jnp.sqrt(real * real + imag * imag + 1e-12))
    m_high, m_low = split(jnp.concatenate(magnitudes, axis=0))
    smooth = (dot(m_high, smooth_band) + dot(m_low, smooth_band)) * inverse_count
    scale = 1.0 / (smooth + EPS)
    flip = flip_matrix(channels)
    for w in range(own):
        here = slice(w * channels, (w + 1) * channels)
        white = jnp.concatenate([reals[w] * scale[here], imags[w] * scale[here]], axis=1)
        out[:, w * 2 * NF:(w + 1) * 2 * NF] = dot(flip, white.astype(BF16)).astype(BF16)


def flip_matrix(channels):
    row = lax.broadcasted_iota(jnp.int32, (channels, channels), 0)
    column = lax.broadcasted_iota(jnp.int32, (channels, channels), 1)
    return (row + column == channels - 1).astype(F32).astype(BF16)


def rotate_kernel(lags, own, cos_lag, sin_lag, out):
    channels = own.shape[0]
    straight = dot(flip_matrix(channels), own[...])
    real, imag = straight[:, :NF], straight[:, NF:]
    for t in range(lags):
        c, s = cos_lag[t:t + 1, :], sin_lag[t:t + 1, :]
        here = slice(t * channels, (t + 1) * channels)
        out[here, :NF] = (real * c - imag * s).astype(BF16)
        out[here, NF:] = (real * s + imag * c).astype(BF16)


def put_slots(channels, partners, present, absent):
    last = NPART // channels - 1
    nothing = jnp.zeros((channels, partners.shape[1]), BF16)

    def place(slot):
        return pl.ds(pl.multiple_of((last - slot) * channels, channels), channels)

    for block, slot, valid in present:
        partners[place(slot), :] = block[...]

        @pl.when(jnp.logical_not(valid))
        def _(slot=slot):
            partners[place(slot), :] = nothing

    for slot in absent:
        partners[place(slot), :] = nothing


def early_slots(me, count, channels, blocks, partners):
    own, ahead = blocks
    next_level = me // 4 + 1 < count // 4
    put_slots(
        channels, partners, [(own, 0, me >= 0), (ahead, 4, next_level)], (1, 2, 3, 5, 6, 7)
    )


def late_slots(me, count, channels, blocks, partners):
    core = lax.rem(me, 2)
    side = lax.rem(me // 2, 2)
    (own_swapped, ahead_swapped, far, far_swapped, cross, cross_swapped, other,
     other_swapped) = blocks
    cross_slot = 6 - 4 * side
    other_slot = 8 - cross_slot
    step = 1 - 2 * core
    next_level = me // 4 + 1 < count // 4
    second_level = me // 4 + 2 < count // 4
    other_there = (side == 0) | second_level
    put_slots(channels, partners, [
        (far, 0, second_level), (cross, cross_slot, next_level),
        (other, other_slot, other_there), (ahead_swapped, 4 + step, next_level),
        (cross_swapped, cross_slot + step, next_level),
        (other_swapped, other_slot + step, other_there),
    ], (4,))

    @pl.when(core == 0)
    def _():
        put_slots(channels, partners, [(own_swapped, 1, me >= 0)], ())

    @pl.when(core == 1)
    def _():
        put_slots(channels, partners, [(far_swapped, 7, second_level)], ())


def product_kernel(late, count, norm_scale, place, rotated, *refs):
    refs = list(refs)
    before = refs.pop(0) if late else None
    out, partners, total = refs[-3:]
    blocks = refs[:-3]
    channels = blocks[0].shape[0]
    (late_slots if late else early_slots)(place[0], count, channels, blocks, partners)
    rows, features = rotated.shape
    chunk = 2 * 2 * NF
    for begin in range(0, features, chunk):
        turned = partners[:, begin:begin + chunk].T
        product = dot(rotated[:, begin:begin + chunk], turned)
        if begin == 0:
            total[...] = product
        else:
            total[...] += product

    row = lax.broadcasted_iota(jnp.int32, (channels, NPART), 0)
    column = lax.broadcasted_iota(jnp.int32, (channels, NPART), 1)
    low = row + column >= NPART - 1
    keep = (low | (column < NPART - channels)) if late else jnp.logical_not(low)
    sheared = []
    for begin in range(0, rows, channels):
        here = slice(begin, begin + channels)
        value = jnp.where(keep, total[here, :], 0.0)
        if late:
            value = (value + before[here, :]) * norm_scale
            sheared.append(pltpu.roll(value, 1, 1, stride=1, stride_axis=0).astype(BF16))
        else:
            out[here, :] = value
    if late:
        sheared = jnp.concatenate(sheared, axis=0)
        out[...] = dot(sheared, flip_matrix(NPART)).astype(BF16)


def exchange(value, pairs):
    return lax.ppermute(value, "chan", pairs)


def local(records, dead_mask, offsets):
    channels, samples = records.shape
    tm_count = lax.axis_size("tm")
    tm_index = lax.axis_index("tm")
    chan_count = lax.axis_size("chan")
    own = samples // HOP
    windows = own * tm_count
    halves = own
    halo = 0
    if tm_count > 1:
        reach = 2 * HOP + H
        left = lax.ppermute(
            records[:, samples - H:], "tm", [(i, i + 1) for i in range(tm_count - 1)]
        )
        right = lax.ppermute(
            records[:, :reach], "tm", [(i + 1, i) for i in range(tm_count - 1)]
        )
        records = jnp.concatenate([left, records, right], axis=1)
        halves = own + 2
        halo = H
    table = jnp.asarray(packed_tables())
    own_offsets = lax.dynamic_slice_in_dim(offsets, tm_index * own, own, 0)
    vmem = pl.BlockSpec(memory_space=pltpu.VMEM)
    smem = pl.BlockSpec(memory_space=pltpu.SMEM)
    hbm = pl.BlockSpec(memory_space=pl.ANY)
    params = pltpu.CompilerParams(vmem_limit_bytes=24 * 1024 * 1024)

    bulk = min(own + 1, halves)
    part_rows = (own + bulk * (HOP // GROUP)) * channels
    spectra = pl.pallas_call(
        functools.partial(spectra_kernel, halves, own, halo),
        name="spectra",
        out_shape=jax.ShapeDtypeStruct((channels, own * 2 * NF), BF16),
        in_specs=[smem, smem, hbm, hbm],
        out_specs=vmem,
        scratch_shapes=[
            pltpu.VMEM((channels, halves * HOP + 2 * H), F32),
            pltpu.VMEM((channels, halves * HOP + 2 * H), BF16),
            pltpu.VMEM((part_rows, GROUP), BF16),
            pltpu.VMEM((part_rows, GROUP), BF16),
            pltpu.VMEM((part_rows, 2 * NF + 128), F32),
            pltpu.VMEM(table.shape, BF16),
            pltpu.SemaphoreType.DMA((3 * halves + 1,)),
        ],
        compiler_params=pltpu.CompilerParams(vmem_limit_bytes=60 * 1024 * 1024),
        cost_estimate=pl.CostEstimate(
            flops=7_000_000_000, bytes_accessed=8 * 1024 * 1024, transcendentals=0
        ),
    )(dead_mask, own_offsets, records, table)
    if tm_count > 1:
        spectra = lax.all_gather(spectra, "tm", axis=1, tiled=True)

    lags = NLAG // tm_count
    cos_lag, sin_lag = (
        lax.dynamic_slice_in_dim(jnp.asarray(t), tm_index * lags, lags, 0) for t in lag_tables()
    )
    place = lax.axis_index("chan").astype(jnp.int32).reshape(1)
    norm_scale = 1.0 / math.sqrt(2.0 * NF * windows)

    features = spectra.shape[1]
    rotated = pl.pallas_call(
        functools.partial(rotate_kernel, lags),
        name="rotate",
        grid=(windows,),
        out_shape=jax.ShapeDtypeStruct((lags * channels, features), BF16),
        in_specs=[
            pl.BlockSpec((channels, 2 * NF), lambda w: (0, w)),
            pl.BlockSpec((lags, NF), lambda w: (0, 0)),
            pl.BlockSpec((lags, NF), lambda w: (0, 0)),
        ],
        out_specs=pl.BlockSpec((lags * channels, 2 * NF), lambda w: (0, w)),
        compiler_params=params,
        cost_estimate=pl.CostEstimate(
            flops=4_000_000_000, bytes_accessed=8 * 1024 * 1024, transcendentals=0
        ),
    )(spectra, cos_lag, sin_lag)

    def product(blocks, before):
        late = before is not None
        operands = [place, rotated] + ([before] if late else []) + list(blocks)
        return pl.pallas_call(
            functools.partial(product_kernel, late, chan_count, norm_scale),
            name="late_product" if late else "early_product",
            out_shape=jax.ShapeDtypeStruct((lags * channels, NPART), BF16 if late else F32),
            in_specs=[smem] + [vmem] * (len(operands) - 1),
            out_specs=vmem,
            scratch_shapes=[
                pltpu.VMEM((NPART, features), BF16),
                pltpu.VMEM((lags * channels, NPART), F32),
            ],
            compiler_params=params,
            cost_estimate=pl.CostEstimate(
                flops=2 * lags * channels * features * NPART, bytes_accessed=6 * 1024 * 1024,
                transcendentals=0,
            ),
        )(*operands)

    every = range(chan_count)

    def swapped_level(i, odd):
        level = i // 4
        other = level + 1 if level % 2 == odd else level - 1
        return i + 4 * (other - level) if 0 <= 4 * other < chan_count else i ^ 1

    even_levels, odd_levels = ([(i, swapped_level(i, odd)) for i in every] for odd in (0, 1))
    top = chan_count - 4

    def far_target(i):
        return i ^ 1 if i >= top else (i - 4 if i >= 4 else top - 4 + i)

    def other_target(i):
        if i & 2:
            return i - 2
        return i + 2 if i >= top else (i - 2 if i >= 4 else top - 2 + i)

    far_pairs = [(i, far_target(i)) for i in every]
    other_pairs = [(i, other_target(i)) for i in every]
    across = [(i, i ^ 2) for i in every]
    cores = [(i, i ^ 1) for i in every]
    side = lax.rem(lax.axis_index("chan") // 2, 2)

    from_even = exchange(spectra, even_levels)
    from_odd = exchange(lax.optimization_barrier(spectra), odd_levels)
    level = lax.axis_index("chan") // 4
    ahead = jnp.where(lax.rem(level, 2) == 0, from_even, from_odd)
    ahead, rotated = lax.optimization_barrier((ahead, rotated))
    other = exchange(jnp.where(side == 0, ahead, spectra), other_pairs)
    cross = exchange(ahead, across)
    far = exchange(ahead, far_pairs)
    early = product((spectra, ahead), None)
    kept, ahead, other, early = lax.optimization_barrier((spectra, ahead, other, early))
    own_swapped = exchange(kept, cores)
    ahead_swapped = exchange(ahead, cores)
    far, own_swapped, ahead_swapped = lax.optimization_barrier(
        (far, own_swapped, ahead_swapped)
    )
    blocks = (own_swapped, ahead_swapped, far, exchange(far, cores), cross,
              exchange(cross, cores), other, exchange(other, cores))
    return product(blocks, early).reshape(lags, channels, NPART)


def solution(mesh):
    return jax.shard_map(
        local,
        mesh=mesh,
        in_specs=(P(("win", "chan"), "tm"), P(("win", "chan")), P("win")),
        out_specs=P("tm", ("win", "chan"), None),
        check_vma=False,
    )
```
